128 devices in a mesh: ctx: 8 (over y, z_lo), fsdp: 16 (over x, z_hi, core).
Axes of the slice: x: 4, y: 4, z: 4 (z_hi: 2, z_lo: 2; z = z_hi * 2 + z_lo), core: 2. Of those that a mesh axis runs over, the one named last changes fastest.
Arguments:
- tokens: bfloat16 [16, 1024, 2048], P('fsdp', 'ctx'), may hold values from -6 to 6
- block_deal: int32 [16, 8, 2], replicated, may hold values from 0 to 15, as said below
- attn_gain: bfloat16 [2048], P('fsdp'), may hold values from 0.5 to 1.5
- query_weight: bfloat16 [2048, 2048], P('fsdp'), may hold values from -0.125 to 0.125
- key_weight: bfloat16 [2048, 256], P('fsdp'), may hold values from -0.125 to 0.125
- value_weight: bfloat16 [2048, 256], P('fsdp'), may hold values from -0.125 to 0.125
- output_weight: bfloat16 [2048, 2048], P('fsdp'), may hold values from -2 to 2
- mlp_gain: bfloat16 [2048], P('fsdp'), may hold values from 0.5 to 1.5
- gate_weight: bfloat16 [2048, 5632], P('fsdp'), may hold values from -0.125 to 0.125
- up_weight: bfloat16 [2048, 5632], P('fsdp'), may hold values from -0.125 to 0.125
- down_weight: bfloat16 [5632, 2048], P('fsdp'), may hold values from -0.078125 to 0.078125
- cotangent: bfloat16 [16, 1024, 2048], P('fsdp', 'ctx'), may hold values from -6 to 6
Outputs:
- mixed: bfloat16 [16, 1024, 2048], P('fsdp', 'ctx')
- tokens_grad: bfloat16 [16, 1024, 2048], P('fsdp', 'ctx')
- attn_gain_grad: float32 [2048], P('fsdp')
- query_grad: float32 [2048, 2048], P('fsdp')
- key_grad: float32 [2048, 256], P('fsdp')
- value_grad: float32 [2048, 256], P('fsdp')
- output_grad: float32 [2048, 2048], P('fsdp')
- mlp_gain_grad: float32 [2048], P('fsdp')
- gate_grad: float32 [2048, 5632], P('fsdp')
- up_grad: float32 [2048, 5632], P('fsdp')
- down_grad: float32 [5632, 2048], P('fsdp')
The draws below stay inside these ranges and needn't reach their ends.
Inputs may be any that keep to these rules, and one draw needn't show every extreme that they name: In each group, block_deal[g, :, 0] is a permutation of 0 to 8 - 1 (prompt blocks) and block_deal[g, :, 1] one of 8 to 2 * 8 - 1 (continuation blocks).
All inputs are finite; a program needn't handle non-finite values.
Results may differ from the reference program's by a relative error of at most 0.025.
Values may be sent and summed in bfloat16 or wider, within the bound.
A program may use at most 320 MiB of HBM per device.

```python
import jax
import jax.numpy as jnp
from jax import lax

D = 2048
HEADS = 32
KV_HEADS = 4
HEAD_DIM = 64
FF = 5632
TOK_DEV = 128
GROUP_HEADS = 8
GLEN = 1024
GROUPS = 16
N_CTX = 8


def draw_block_deal(key, part):
    key = jax.random.fold_in(key, 7)

    def one_group(group_key):
        first = jax.random.permutation(jax.random.fold_in(group_key, 1), N_CTX)
        second = jax.random.permutation(jax.random.fold_in(group_key, 2), N_CTX) + N_CTX
        return jnp.stack([first, second], axis=1).astype(jnp.int32)
    return jax.vmap(one_group)(jax.random.split(key, GROUPS))


def block_scale(rng, dims, cuts, least, largest):
    level = 1.0
    for dim, parts in cuts:
        draws = jax.random.uniform(jax.random.fold_in(jax.random.fold_in(rng, 6), dim), (parts,), jnp.float32, least / len(cuts), largest / len(cuts))
        level = level * jnp.repeat(jnp.exp(draws), dims[dim] // parts).reshape((-1,) + (1,) * (len(dims) - 1 - dim))
    return level


def bell_draw(rng, dims, scale, reach, shards=(), held_as=jnp.bfloat16):
    result = scale * jax.random.normal(rng, dims, jnp.float32)
    if shards:
        result = result * block_scale(rng, dims, shards, -0.22, 0.18)
    return jnp.clip(result, -reach, reach).astype(held_as)


def setup_inputs(seed: int = 0) -> dict:
    key_of = jax.random.split(jax.random.key(seed), 13)
    return {
        "tokens": bell_draw(key_of[0], (GROUPS, GLEN, D), 1.0, 6.0, ((0, 16), (1, 8))),
        "block_deal": draw_block_deal(jax.random.fold_in(key_of[12], 71), 0),
        "attn_gain": jnp.clip(1.0 + 0.1 * jax.random.normal(key_of[2], (D,), jnp.float32), 0.5, 1.5).astype(jnp.bfloat16),
        "query_weight": bell_draw(key_of[3], (D, HEADS * HEAD_DIM), D ** -0.5, 0.125, ((0, 16),)),
        "key_weight": bell_draw(key_of[4], (D, KV_HEADS * HEAD_DIM), D ** -0.5, 0.125, ((0, 16),)),
        "value_weight": bell_draw(key_of[5], (D, KV_HEADS * HEAD_DIM), D ** -0.5, 0.125, ((0, 16),)),
        "output_weight": bell_draw(key_of[6], (HEADS * HEAD_DIM, D), 8 ** -0.5, 2.0, ((0, 16),)),
        "mlp_gain": jnp.clip(1.0 + 0.1 * jax.random.normal(key_of[7], (D,), jnp.float32), 0.5, 1.5).astype(jnp.bfloat16),
        "gate_weight": bell_draw(key_of[8], (D, FF), D ** -0.5, 0.125, ((0, 16),)),
        "up_weight": bell_draw(key_of[9], (D, FF), D ** -0.5, 0.125, ((0, 16),)),
        "down_weight": bell_draw(key_of[10], (FF, D), FF ** -0.5, 0.078125, ((0, 16),)),
        "cotangent": bell_draw(key_of[11], (GROUPS, GLEN, D), 1.0, 6.0, ((0, 16), (1, 8))),
    }


EPS = 1e-05
SCALE = 0.125
BASE = 10000.0

@jax.custom_vjp
def low(v):
    return lax.optimization_barrier(v.astype(jnp.bfloat16)).astype(jnp.float32)

@jax.custom_vjp
def low_back(v):
    return v

def low_keep(v):
    return (low(v), None)

def low_pass(kept, grad):
    return (grad,)

def back_keep(v):
    return (v, None)

def back_low(kept, grad):
    return (low(grad),)
low.defvjp(low_keep, low_pass)
low_back.defvjp(back_keep, back_low)

def matmul(left, right):
    return jnp.dot(left, right, precision=lax.Precision.HIGHEST)

def rms_norm(values, gain):
    return values * lax.rsqrt(lax.optimization_barrier(jnp.mean(values * values, axis=-1, keepdims=True)) + EPS) * gain

def tables(position):
    freq = BASE ** (-(jnp.arange(HEAD_DIM // 2, dtype=jnp.float32) * 2.0) / HEAD_DIM)
    angle = position.astype(jnp.float32)[:, None] * freq[None, :]
    angle = jnp.concatenate([angle, angle], axis=-1)
    return (jnp.cos(angle), jnp.sin(angle))

def rotate(values, cosine, sine):
    half_dim = values.shape[-1] // 2
    turned = jnp.concatenate([-values[..., half_dim:], values[..., :half_dim]], axis=-1)
    return values * cosine[:, None, :] + turned * sine[:, None, :]

def timeline(table_flat, total_len, row_count):
    everywhere = jnp.arange(total_len, dtype=jnp.int32)
    half_len = row_count // 2
    slot = everywhere // row_count * 2 + everywhere % row_count // half_len
    moment = jnp.take(table_flat, slot) * half_len + everywhere % half_len
    prompt_len = total_len // 2
    cont_len = total_len // 8
    later = moment >= prompt_len
    segment = jnp.where(later, 1 + (moment - prompt_len) // cont_len, 0).astype(jnp.int32)
    position = jnp.where(later, prompt_len + (moment - prompt_len) % cont_len, moment).astype(jnp.int32)
    return (segment, position)

def visibility(seg_query, pos_query, seg_key, pos_key):
    same = (seg_key[None, :] == 0) | (seg_key[None, :] == seg_query[:, None])
    return same & (pos_key[None, :] <= pos_query[:, None])

def layer(inputs, weights, cosine, sine, visible):
    attn_gain, query_weight, key_weight, value_weight, output_weight, mlp_gain, gate_weight, up_weight, down_weight = weights
    length = inputs.shape[0]
    normed = low(rms_norm(inputs, attn_gain))
    query_raw = low_back(matmul(normed, query_weight))
    queries = low(rotate(query_raw.reshape(length, HEADS, HEAD_DIM), cosine, sine))
    queries = queries.reshape(length, KV_HEADS, GROUP_HEADS, HEAD_DIM)
    key_raw = low_back(matmul(normed, key_weight))
    keys = low(rotate(key_raw.reshape(length, KV_HEADS, HEAD_DIM), cosine, sine))
    values = low(low_back(matmul(normed, value_weight))).reshape(length, KV_HEADS, HEAD_DIM)
    scores = jnp.einsum('qcgd,kcd->cgqk', queries, keys, precision=lax.Precision.HIGHEST) * SCALE
    scores = jnp.where(visible, low_back(scores), -1e+30)
    probs = low(jax.nn.softmax(scores, axis=-1))
    heads_out = jnp.einsum('cgqk,kcd->qcgd', probs, values, precision=lax.Precision.HIGHEST)
    attended = low(low_back(heads_out)).reshape(length, HEADS * HEAD_DIM)
    hidden_state = inputs + low_back(matmul(attended, output_weight))
    normed_two = low(rms_norm(hidden_state, mlp_gain))
    gate_act = low_back(matmul(normed_two, gate_weight))
    up_act = low_back(matmul(normed_two, up_weight))
    inner = low(jax.nn.silu(gate_act) * up_act)
    return hidden_state + low_back(matmul(inner, down_weight))

def reference(tokens, block_deal, attn_gain, query_weight, key_weight, value_weight, output_weight, mlp_gain, gate_weight, up_weight, down_weight, cotangent):
    weights = tuple((item.astype(jnp.float32) for item in (attn_gain, query_weight, key_weight, value_weight, output_weight, mlp_gain, gate_weight, up_weight, down_weight)))

    def one_group(totals, item):
        group_tokens, group_deal, group_cot = item
        segment, position = timeline(group_deal.reshape(-1), GLEN, TOK_DEV)
        cosine, sine = tables(position)
        visible = visibility(segment, position, segment, position)

        def forward(inputs, *params):
            return layer(inputs, params, cosine, sine, visible)
        output, backward = jax.vjp(forward, group_tokens.astype(jnp.float32), *weights)
        grads = backward(group_cot.astype(jnp.float32))
        totals = tuple((total + grad for total, grad in zip(totals, grads[1:])))
        return (totals, (output.astype(jnp.bfloat16), grads[0].astype(jnp.bfloat16)))
    zeros = tuple((jnp.zeros(item.shape, jnp.float32) for item in weights))
    totals, (mixed, tokens_grad) = lax.scan(one_group, zeros, (tokens, block_deal, cotangent))
    return (mixed, tokens_grad, totals[0], totals[1], totals[2], totals[3], totals[4], totals[5], totals[6], totals[7], totals[8])
```

```python
import jax
import jax.numpy as jnp
from jax import lax
from jax.sharding import PartitionSpec as P

HEADS = 32
KV_HEADS = 4
HEAD_DIM = 64
GROUP_HEADS = 8


EPS = 1e-05
SCALE = 0.125
BASE = 10000.0


def mult(left, right):
    return jnp.dot(left, right, preferred_element_type=jnp.float32)


def mult_back(left, right):
    return lax.dot_general(
        left, right, (((1,), (1,)), ((), ())), preferred_element_type=jnp.float32
    )


def mult_rows(left, right):
    return lax.dot_general(
        left, right, (((0,), (0,)), ((), ())), preferred_element_type=jnp.float32
    )


def rms_norm(values, gain):
    return values * lax.rsqrt(jnp.mean(values * values, axis=-1, keepdims=True) + EPS) * gain


def tables(position):
    freq = BASE ** (-(jnp.arange(HEAD_DIM // 2, dtype=jnp.float32) * 2.0) / HEAD_DIM)
    angle = position.astype(jnp.float32)[:, None] * freq[None, :]
    angle = jnp.concatenate([angle, angle], axis=-1)
    return (jnp.cos(angle), jnp.sin(angle))


def rotate(values, cosine, sine):
    half_dim = values.shape[-1] // 2
    turned = jnp.concatenate([-values[..., half_dim:], values[..., :half_dim]], axis=-1)
    return values * cosine[:, None, :] + turned * sine[:, None, :]


def unrotate(values, cosine, sine):
    half_dim = values.shape[-1] // 2
    scaled = values * sine[:, None, :]
    turned = jnp.concatenate([scaled[..., half_dim:], -scaled[..., :half_dim]], axis=-1)
    return values * cosine[:, None, :] + turned


def timeline(table_flat, total_len, row_count):
    everywhere = jnp.arange(total_len, dtype=jnp.int32)
    half_len = row_count // 2
    slot = everywhere // row_count * 2 + everywhere % row_count // half_len
    moment = jnp.take(table_flat, slot) * half_len + everywhere % half_len
    prompt_len = total_len // 2
    cont_len = total_len // 8
    later = moment >= prompt_len
    segment = jnp.where(later, 1 + (moment - prompt_len) // cont_len, 0)
    position = jnp.where(later, prompt_len + (moment - prompt_len) % cont_len, moment)
    return (segment, position)


def fetch_attention(attn_gain, mlp_gain, query_weight, key_weight, value_weight, output_weight):
    return (
        lax.all_gather(attn_gain, "fsdp", axis=0, tiled=True),
        lax.all_gather(mlp_gain, "fsdp", axis=0, tiled=True),
        lax.all_gather(query_weight, "fsdp", axis=0, tiled=True),
        lax.all_gather(key_weight, "fsdp", axis=0, tiled=True),
        lax.all_gather(value_weight, "fsdp", axis=0, tiled=True),
        lax.all_gather(output_weight, "fsdp", axis=0, tiled=True),
    )


def swap_pairs():
    pairs = []
    for c in range(8):
        for f in range(16):
            pairs.append((c * 16 + f, (f // 2) * 16 + 2 * c + f % 2))
    return pairs


def fetch_mlp(gate_weight, up_weight, down_weight):
    c = lax.axis_index("ctx")
    width = gate_weight.shape[1] // 8
    gate_own = lax.dynamic_slice_in_dim(gate_weight, c * width, width, 1)
    up_own = lax.dynamic_slice_in_dim(up_weight, c * width, width, 1)
    span = down_weight.shape[1] // 8
    rows = down_weight.shape[0]
    down_own = lax.dynamic_slice_in_dim(down_weight, c * span, span, 1)
    down_own = lax.ppermute(down_own, ("ctx", "fsdp"), swap_pairs())
    down_all = lax.all_gather(down_own, "fsdp", axis=0, tiled=False)
    down_all = down_all.reshape(8, 2, rows, span).transpose(1, 2, 0, 3).reshape(2 * rows, 8 * span)
    return (
        lax.all_gather(gate_own, "fsdp", axis=0, tiled=True),
        lax.all_gather(up_own, "fsdp", axis=0, tiled=True),
        down_all,
    )


def sliced_share(grad):
    part = lax.psum_scatter(grad.astype(jnp.bfloat16), "fsdp", scatter_dimension=0, tiled=True)
    return lax.all_gather(part, "ctx", axis=1, tiled=True).astype(jnp.float32)


def down_share(grad):
    rows, span = grad.shape[0] // 2, grad.shape[1] // 8
    grad = grad.astype(jnp.bfloat16).reshape(2, rows, 8, span).transpose(2, 0, 1, 3)
    grad = grad.reshape(16, rows, span)
    part = lax.psum_scatter(grad, "fsdp", scatter_dimension=0, tiled=False)
    part = lax.ppermute(part, ("ctx", "fsdp"), swap_pairs())
    return lax.all_gather(part, "ctx", axis=1, tiled=True).astype(jnp.float32)


def weight_share(left, right):
    return lax.psum_scatter(
        mult_rows(left, right).astype(jnp.bfloat16), "fsdp", scatter_dimension=0, tiled=True
    ).astype(jnp.float32)


def softmax_parts(masked):
    peak = jnp.max(masked, axis=-1, keepdims=True)
    unscaled = jnp.exp(masked - peak)
    total = jnp.sum(unscaled, axis=-1, keepdims=True)
    return ((unscaled / total).astype(jnp.bfloat16), peak + jnp.log(total))


def on_device(
    tokens,
    block_deal,
    attn_gain,
    query_weight,
    key_weight,
    value_weight,
    output_weight,
    mlp_gain,
    gate_weight,
    up_weight,
    down_weight,
    cotangent,
):
    inputs = tokens[0].astype(jnp.float32)
    grad_out = cotangent[0].astype(jnp.float32)
    row_count = inputs.shape[0]
    ctx_index = lax.axis_index("ctx")
    group_index = lax.axis_index("fsdp")
    full_len = row_count * lax.axis_size("ctx")
    seg_all, pos_all = jax.vmap(lambda table: timeline(table.reshape(-1), full_len, row_count))(
        block_deal
    )
    own_seg_all = lax.dynamic_slice_in_dim(seg_all, ctx_index * row_count, row_count, 1)
    own_pos_all = lax.dynamic_slice_in_dim(pos_all, ctx_index * row_count, row_count, 1)
    own_position = lax.dynamic_index_in_dim(own_pos_all, group_index, 0, keepdims=False)
    cosine, sine = tables(own_position)
    segment = lax.dynamic_index_in_dim(seg_all, group_index, 0, keepdims=False)
    position = lax.dynamic_index_in_dim(pos_all, group_index, 0, keepdims=False)
    own_segment = lax.dynamic_index_in_dim(own_seg_all, group_index, 0, keepdims=False)
    same = (segment[None, :] == 0) | (segment[None, :] == own_segment[:, None])
    visible = same & (position[None, :] <= own_position[:, None])
    gain_one, gain_two, query_full, key_full, value_full, output_full = fetch_attention(
        attn_gain, mlp_gain, query_weight, key_weight, value_weight, output_weight
    )
    gain_first = gain_one.astype(jnp.float32)
    gain_second = gain_two.astype(jnp.float32)
    normed = rms_norm(inputs, gain_first).astype(jnp.bfloat16)
    query_raw = mult(normed, query_full).reshape(row_count, HEADS, HEAD_DIM)
    key_raw = mult(normed, key_full).reshape(row_count, KV_HEADS, HEAD_DIM)
    queries = rotate(query_raw, cosine, sine).astype(jnp.bfloat16)
    queries = queries.reshape(row_count, KV_HEADS, GROUP_HEADS, HEAD_DIM)
    keys_own = (
        rotate(key_raw, cosine, sine).astype(jnp.bfloat16).reshape(row_count, KV_HEADS * HEAD_DIM)
    )
    values_own = mult(normed, value_full).astype(jnp.bfloat16)
    keys_flat, values_flat = (
        lax.all_gather(keys_own, "ctx", axis=0, tiled=True),
        lax.all_gather(values_own, "ctx", axis=0, tiled=True),
    )
    keys_all = keys_flat.reshape(full_len, KV_HEADS, HEAD_DIM)
    values_all = values_flat.reshape(full_len, KV_HEADS, HEAD_DIM)
    scores = (
        jnp.einsum("qcgd,kcd->cgqk", queries, keys_all, preferred_element_type=jnp.float32) * SCALE
    )
    probs_low, log_total = softmax_parts(jnp.where(visible, scores, -1e30))
    heads_out = jnp.einsum(
        "cgqk,kcd->qcgd", probs_low, values_all, preferred_element_type=jnp.float32
    )
    attended = heads_out.astype(jnp.bfloat16).reshape(row_count, HEADS * HEAD_DIM)
    hidden_state = inputs + mult(attended, output_full)
    gate_part, up_part, down_part = fetch_mlp(gate_weight, up_weight, down_weight)
    normed_two = rms_norm(hidden_state, gain_second).astype(jnp.bfloat16)
    normed_two_all = lax.all_gather(normed_two, "ctx", axis=0, tiled=True)
    grad_mlp_all = lax.all_gather(cotangent[0], "ctx", axis=0, tiled=True)
    gate_act = mult(normed_two_all, gate_part)
    up_act = mult(normed_two_all, up_part)
    inner = (jax.nn.silu(gate_act) * up_act).astype(jnp.bfloat16)
    mixed = (
        hidden_state
        + lax.psum_scatter(
            mult(inner, down_part).astype(jnp.bfloat16), "ctx", scatter_dimension=0, tiled=True
        ).astype(jnp.float32)
    ).astype(jnp.bfloat16)
    grad_inner = mult_back(grad_mlp_all, down_part)
    _, swiglu_back = jax.vjp(lambda first, second: jax.nn.silu(first) * second, gate_act, up_act)
    grad_gate, grad_up = swiglu_back(grad_inner)
    grad_gate = grad_gate.astype(jnp.bfloat16)
    grad_up = grad_up.astype(jnp.bfloat16)
    grad_normed_two = lax.psum_scatter(
        (mult_back(grad_gate, gate_part) + mult_back(grad_up, up_part)).astype(jnp.bfloat16),
        "ctx",
        scatter_dimension=0,
        tiled=True,
    ).astype(jnp.float32)
    _, norm_two_back = jax.vjp(rms_norm, hidden_state, gain_second)
    grad_hidden_norm, grad_gain_two = norm_two_back(grad_normed_two)
    grad_hidden = grad_out + grad_hidden_norm
    grad_att = grad_hidden.astype(jnp.bfloat16)
    grad_heads = mult_back(grad_att, output_full).astype(jnp.bfloat16)
    grad_heads = grad_heads.reshape(row_count, KV_HEADS, GROUP_HEADS, HEAD_DIM)
    scores_again = (
        jnp.einsum("qcgd,kcd->cgqk", queries, keys_all, preferred_element_type=jnp.float32) * SCALE
    )
    probs = jnp.exp(jnp.where(visible, scores_again, -1e30) - log_total)
    probs_again = probs.astype(jnp.bfloat16)
    grad_probs = jnp.einsum(
        "qcgd,kcd->cgqk", grad_heads, values_all, preferred_element_type=jnp.float32
    )
    grad_values_all = jnp.einsum(
        "cgqk,qcgd->kcd", probs_again, grad_heads, preferred_element_type=jnp.float32
    )
    grad_scores = probs * (grad_probs - jnp.sum(probs * grad_probs, axis=-1, keepdims=True))
    grad_scores = grad_scores.astype(jnp.bfloat16)
    grad_queries = (
        jnp.einsum("cgqk,kcd->qcgd", grad_scores, keys_all, preferred_element_type=jnp.float32)
        * SCALE
    )
    grad_keys_all = (
        jnp.einsum("cgqk,qcgd->kcd", grad_scores, queries, preferred_element_type=jnp.float32)
        * SCALE
    )
    grad_keys_own, grad_values_own = (
        lax.psum_scatter(
            grad_keys_all.reshape(full_len, KV_HEADS * HEAD_DIM).astype(jnp.bfloat16),
            "ctx",
            scatter_dimension=0,
            tiled=True,
        ).astype(jnp.float32),
        lax.psum_scatter(
            grad_values_all.reshape(full_len, KV_HEADS * HEAD_DIM).astype(jnp.bfloat16),
            "ctx",
            scatter_dimension=0,
            tiled=True,
        ).astype(jnp.float32),
    )
    grad_query_raw = unrotate(grad_queries.reshape(row_count, HEADS, HEAD_DIM), cosine, sine)
    grad_query_raw = grad_query_raw.reshape(row_count, HEADS * HEAD_DIM).astype(jnp.bfloat16)
    grad_key_raw = unrotate(grad_keys_own.reshape(row_count, KV_HEADS, HEAD_DIM), cosine, sine)
    grad_key_raw = grad_key_raw.reshape(row_count, KV_HEADS * HEAD_DIM).astype(jnp.bfloat16)
    grad_value_raw = grad_values_own.astype(jnp.bfloat16)
    grad_normed = (
        mult_back(grad_query_raw, query_full)
        + mult_back(grad_key_raw, key_full)
        + mult_back(grad_value_raw, value_full)
    )
    _, norm_one_back = jax.vjp(rms_norm, inputs, gain_first)
    grad_inputs_norm, grad_gain_one = norm_one_back(grad_normed)
    tokens_grad = (grad_hidden + grad_inputs_norm).astype(jnp.bfloat16)
    query_part = weight_share(normed, grad_query_raw)
    key_part = weight_share(normed, grad_key_raw)
    value_part = weight_share(normed, grad_value_raw)
    output_part = weight_share(attended, grad_att)
    gate_part = sliced_share(mult_rows(normed_two_all, grad_gate))
    up_part = sliced_share(mult_rows(normed_two_all, grad_up))
    down_part = down_share(mult_rows(inner, grad_mlp_all))
    gain_one_part, gain_two_part = (
        lax.psum_scatter(grad_gain_one, "fsdp", scatter_dimension=0, tiled=True),
        lax.psum_scatter(grad_gain_two, "fsdp", scatter_dimension=0, tiled=True),
    )
    summed = (
        lax.psum(gain_one_part.astype(jnp.bfloat16), "ctx").astype(jnp.float32),
        lax.psum(query_part.astype(jnp.bfloat16), "ctx").astype(jnp.float32),
        lax.psum(key_part.astype(jnp.bfloat16), "ctx").astype(jnp.float32),
        lax.psum(value_part.astype(jnp.bfloat16), "ctx").astype(jnp.float32),
        lax.psum(output_part.astype(jnp.bfloat16), "ctx").astype(jnp.float32),
        lax.psum(gain_two_part.astype(jnp.bfloat16), "ctx").astype(jnp.float32),
        gate_part,
        up_part,
        down_part,
    )
    return (
        mixed[None],
        tokens_grad[None],
        summed[0],
        summed[1],
        summed[2],
        summed[3],
        summed[4],
        summed[5],
        summed[6],
        summed[7],
        summed[8],
    )


def solution(mesh):
    return jax.shard_map(
        on_device,
        mesh=mesh,
        in_specs=(
            P("fsdp", "ctx", None),
            P(),
            P("fsdp"),
            P("fsdp", None),
            P("fsdp", None),
            P("fsdp", None),
            P("fsdp", None),
            P("fsdp"),
            P("fsdp", None),
            P("fsdp", None),
            P("fsdp", None),
            P("fsdp", "ctx", None),
        ),
        out_specs=(
            P("fsdp", "ctx", None),
            P("fsdp", "ctx", None),
            P("fsdp"),
            P("fsdp", None),
            P("fsdp", None),
            P("fsdp", None),
            P("fsdp", None),
            P("fsdp"),
            P("fsdp", None),
            P("fsdp", None),
            P("fsdp", None),
        ),
        check_vma=False,
    )
```

```python
import functools

import jax
import jax.numpy as jnp
from jax import lax
from jax.experimental import pallas as pl
from jax.experimental.pallas import tpu as pltpu
from jax.sharding import PartitionSpec as P

MESH = pl.DeviceIdType.MESH
BF = jnp.bfloat16
F32 = jnp.float32
ANY = pl.BlockSpec(memory_space=pl.ANY)
VMEM = pl.BlockSpec(memory_space=pltpu.VMEM)

SLOT = {(0, 0): 0, (0, 1): 1, (1, 0): 2, (3, 0): 3, (1, 1): 4, (3, 1): 5, (2, 0): 6, (2, 1): 7}
STEPS = (0, 0, 1, 3, 1, 3, 2, 2)
PAIRS = (0, 1, 0, 0, 1, 1, 0, 1)


def slot_of(dr, dp):
    return SLOT[(dr % 4, dp % 2)]


class Place:
    def __init__(self):
        self.c = lax.axis_index("ctx")
        self.f = lax.axis_index("fsdp")
        self.y, self.zl = lax.div(self.c, 2), lax.rem(self.c, 2)
        self.j, self.co = lax.div(self.f, 2), lax.rem(self.f, 2)
        self.x, self.zh = lax.div(self.j, 2), lax.rem(self.j, 2)

    def ctx_at(self, dr, dp):
        return lax.rem(self.y + dr % 4, 4) * 2 + lax.rem(self.zl + dp, 2)

    def chip_at(self, dr, dp):
        return lax.rem(self.x + dr % 4, 4) * 2 + lax.rem(self.zh + dp, 2)

    def fsdp_at(self, dr, dp):
        return self.chip_at(dr, dp) * 2 + self.co

    def across_y(self, dr, dp):
        return {"ctx": self.ctx_at(dr, dp), "fsdp": self.f}

    def across_x(self, dr, dp):
        return {"ctx": self.c, "fsdp": self.fsdp_at(dr, dp)}

    def sibling(self):
        return {"ctx": self.c, "fsdp": self.f + 1 - 2 * self.co}


def greet(devices):
    barrier = pltpu.get_barrier_semaphore()
    for device in devices:
        pl.semaphore_signal(barrier, 1, device_id=device, device_id_type=MESH)
    pl.semaphore_wait(barrier, len(devices))


def near(dev):
    return [dev(1, 0), dev(-1, 0), dev(0, 1)]


def send(src, dst, sems, index, device):
    return pltpu.make_async_remote_copy(
        src, dst, sems[0].at[index], sems[1].at[index], device_id=device, device_id_type=MESH
    )


class Gather:
    MOVES = (
        ((0, 0), (0, 1), None),
        ((0, 0), (1, 0), None),
        ((0, 0), (-1, 0), None),
        ((0, 1), (1, 0), None),
        ((0, 1), (-1, 0), None),
        ((-1, 0), (1, 0), 0),
        ((-1, 1), (1, 0), 0),
        ((1, 0), (-1, 0), 1),
        ((1, 1), (-1, 0), 1),
    )

    def __init__(self, dev, own, loc, sems, row, sibling=None, sibling_sems=None):
        self.loc = loc
        self.copies = []
        for index, (block, to, half) in enumerate(self.MOVES):
            src = own if block == (0, 0) else loc(*block, 0, 0, half)
            dst = loc(*block, *to, half)
            self.copies.append(send(src, dst, sems, (row, index), dev(*to)))
        self.passed = []
        self.sibling = sibling
        self.sibling_sems = sibling_sems
        self.row = row
        self.own = own

    def _pass(self, index, src, dst):
        if self.sibling is not None:
            copy = send(src, dst, self.sibling_sems, (self.row, index), self.sibling)
            copy.start()
            self.passed.append(copy)

    def _got(self, index):
        self.copies[index].wait_recv()
        (dr, dp), (er, ep), half = self.MOVES[index]
        ref = self.loc(dr - er, dp + ep, 0, 0, half)
        self._pass(index, ref, ref)

    def start(self):
        for index in (0, 1, 2):
            self.copies[index].start()
        self._pass(9, self.own, self.loc(0, 0, 0, 0, None))

    def pair(self):
        self._got(0)
        self.copies[3].start()
        self.copies[4].start()

    def turn(self, dp):
        for got, on in (((1, 5), (2, 7)) if dp == 0 else ((3, 6), (4, 8))):
            self._got(got)
            self.copies[on].start()

    def last(self, dp):
        for got in ((5, 7) if dp == 0 else (6, 8)):
            self._got(got)

    def end(self):
        for copy in self.copies:
            copy.wait_send()
        for copy in self.passed:
            copy.wait()

    def all(self):
        self.start()
        self.pair()
        self.turn(0)
        self.turn(1)
        self.last(0)
        self.last(1)
        self.end()


def row_half(half, rows):
    return pl.ds(0, rows) if half is None else pl.ds(half * (rows // 2), rows // 2)


def add_into(ref, rows, others, step=16):
    step = min(step, rows)

    @pl.loop(0, rows // step)
    def _(i):
        at = pl.ds(pl.multiple_of(i * step, step), step)
        total = ref[at].astype(F32)
        for other in others:
            total = total + other[at].astype(F32)
        ref[at] = total.astype(ref.dtype)


class Scatter:
    def __init__(self, dev, part, rows, halves, fulls, paired, sems, row, cut=None):
        self.part, self.rows, self.cut = part, rows, cut
        self.halves, self.fulls, self.paired = halves, fulls, paired
        self.first, self.second = {}, {}
        for dp in (0, 1):
            for way, sign in ((0, 1), (1, -1)):
                self.first[way, dp] = send(
                    self._half(part(slot_of(2, dp)), way), halves.at[way, dp], sems, (row, way * 2 + dp), dev(sign, 0)
                )
                self.second[way, dp] = send(
                    part(slot_of(sign, dp)), fulls.at[way, dp], sems, (row, 4 + way * 2 + dp), dev(sign, 0)
                )
        self.third = send(part(slot_of(0, 1)), paired, sems, (row, 8), dev(0, 1))

    def _half(self, ref, way):
        if self.cut is None:
            return ref.at[pl.ds(way * (self.rows // 2), self.rows // 2)]
        return ref.at[:, pl.ds(way * (self.cut // 2), self.cut // 2)]

    def start(self):
        for dp in (1, 0):
            for way in (0, 1):
                self.first[way, dp].start()

    def turn(self, dp):
        for way, sign in ((0, 1), (1, -1)):
            self.first[way, dp].wait_recv()
            block = self._half(self.part(slot_of(sign, dp)), way)
            add_into(block, block.shape[0], [self.halves.at[way, dp]])
            self.second[way, dp].start()

    def pair(self):
        for way in (0, 1):
            self.second[way, 1].wait_recv()
        add_into(self.part(slot_of(0, 1)), self.rows, [self.fulls.at[0, 1], self.fulls.at[1, 1]])
        self.third.start()

    def finish(self, out, extra=()):
        for way in (0, 1):
            self.second[way, 0].wait_recv()
        self.third.wait_recv()
        own = self.part(0)
        terms = [own, self.fulls.at[0, 0], self.fulls.at[1, 0], self.paired, *extra]

        @pl.loop(0, self.rows // 16)
        def _(i):
            at = pl.ds(pl.multiple_of(i * 16, 16), 16)
            total = terms[0][at].astype(F32)
            for term in terms[1:]:
                total = total + term[at].astype(F32)
            out[at] = total.astype(out.dtype)

    def end(self):
        for copy in (*self.first.values(), *self.second.values(), self.third):
            copy.wait_send()


def scatter_buffers(rows, columns, dtype=BF, cut=False):
    half = (rows, columns // 2) if cut else (rows // 2, columns)
    return [
        pltpu.VMEM((2, 2, *half), dtype),
        pltpu.VMEM((2, 2, rows, columns), dtype),
        pltpu.VMEM((rows, columns), dtype),
    ]


def dma_sems(rows, count):
    return [pltpu.SemaphoreType.DMA((rows, count)), pltpu.SemaphoreType.DMA((rows, count))]


def params(collective_id, vmem=56):
    return pltpu.CompilerParams(
        collective_id=collective_id, has_side_effects=True, vmem_limit_bytes=vmem << 20
    )


def dot_in(left, right):
    return jnp.dot(left, right, preferred_element_type=F32)


def dot_back(left, right):
    return lax.dot_general(left, right, (((1,), (1,)), ((), ())), preferred_element_type=F32)


def dot_rows(left, right):
    return lax.dot_general(left, right, (((0,), (0,)), ((), ())), preferred_element_type=F32)


def weights_kernel(
    gains, qkv, wo, gu, dn, dy, gains_all, qkv_all, wo_all, gu_all, dn_all, dy_all, s0, s1, t0, t1, y0, y1, local
):
    me = Place()
    greet(near(me.across_x) + near(me.across_y) + [me.sibling()])

    def rows_at(ref, rows):
        def loc(dr, dp, er, ep, half):
            size = rows if half is None else rows // 2
            first = me.fsdp_at(dr, dp) * rows + (0 if half is None else half * size)
            return ref.at[pl.ds(pl.multiple_of(first, size), size)]

        return loc

    def gains_at(dr, dp, er, ep, half):
        return gains_all.at[me.fsdp_at(dr, dp), row_half(half, 16)]

    def dn_at(dr, dp, er, ep, half):
        size = 352 if half is None else 176
        first = me.co * 352 + (0 if half is None else half * size)
        return dn_all.at[
            pl.ds(pl.multiple_of(first, 16), size),
            pl.ds(pl.multiple_of(me.chip_at(dr, dp) * 256, 256), 256),
        ]

    def dy_at(dr, dp, er, ep, half):
        return dy_all.at[slot_of(dr - er, dp + ep), row_half(half, 128)]

    def over_x(own, loc, row):
        return Gather(me.across_x, own, loc, (s0, s1), row, me.sibling(), (t0, t1))

    tasks = [
        over_x(gains, gains_at, 0),
        over_x(qkv, rows_at(qkv_all, 128), 1),
        over_x(wo, rows_at(wo_all, 128), 2),
        over_x(gu, rows_at(gu_all, 128), 3),
        over_x(dn, dn_at, 4),
    ]
    grad = Gather(me.across_y, dy, dy_at, (y0, y1), 0)
    kept = []
    for index, task in enumerate([*tasks, grad]):
        copy = pltpu.make_async_copy(task.own, task.loc(0, 0, 0, 0, None), local.at[index])
        copy.start()
        kept.append(copy)
    g, q, o, m, d = tasks
    g.start()
    q.start()
    grad.start()
    g.pair()
    q.pair()
    grad.pair()
    g.turn(0)
    q.turn(0)
    grad.turn(0)
    o.start()
    g.turn(1)
    q.turn(1)
    grad.turn(1)
    o.pair()
    o.turn(0)
    m.start()
    d.start()
    for task in (g, q, grad):
        task.last(0)
        task.last(1)
    o.turn(1)
    m.pair()
    d.pair()
    m.turn(0)
    d.turn(0)
    o.last(0)
    o.last(1)
    m.turn(1)
    d.turn(1)
    for task in (m, d):
        task.last(0)
        task.last(1)
    for task in [*tasks, grad]:
        task.end()
    for copy in kept:
        copy.wait()


def gather_weights(gains, qkv, wo, gu, dn, dy):
    return pl.pallas_call(
        weights_kernel,
        out_shape=(
            jax.ShapeDtypeStruct((16, 16, 128), F32),
            jax.ShapeDtypeStruct((2048, 2560), BF),
            jax.ShapeDtypeStruct((2048, 2048), BF),
            jax.ShapeDtypeStruct((2048, 1536), BF),
            jax.ShapeDtypeStruct((704, 2048), BF),
            jax.ShapeDtypeStruct((8, 128, 2048), BF),
        ),
        in_specs=[ANY] * 6,
        out_specs=[ANY] * 6,
        scratch_shapes=dma_sems(5, 9) + dma_sems(5, 10) + dma_sems(1, 9) + [pltpu.SemaphoreType.DMA((6,))],
        compiler_params=params(1),
        name="gather_weights",
    )(gains, qkv, wo, gu, dn, dy)


def kv_kernel(own, everyone, y0, y1, local):
    me = Place()
    greet(near(me.across_y))

    def loc(dr, dp, er, ep, half):
        return everyone.at[me.ctx_at(dr, dp), row_half(half, 128)]

    task = Gather(me.across_y, own, loc, (y0, y1), 0)
    copy = pltpu.make_async_copy(own, loc(0, 0, 0, 0, None), local)
    copy.start()
    task.all()
    copy.wait()


def gather_kv(own):
    rows, columns = own.shape
    return pl.pallas_call(
        kv_kernel,
        out_shape=jax.ShapeDtypeStruct((8, rows, columns), BF),
        in_specs=[VMEM],
        out_specs=VMEM,
        scratch_shapes=dma_sems(1, 9) + [pltpu.SemaphoreType.DMA],
        compiler_params=params(2),
        name="gather_kv",
    )(own)


def kv_back_kernel(parts, out, halves, fulls, paired, work, y0, y1):
    me = Place()
    greet(near(me.across_y))
    for slot in range(8):
        work[slot] = parts[me.ctx_at(STEPS[slot], PAIRS[slot])]
    task = Scatter(me.across_y, lambda slot: work.at[slot], 128, halves, fulls, paired, (y0, y1), 0)
    task.start()
    task.turn(1)
    task.turn(0)
    task.pair()
    task.finish(out)
    task.end()


def scatter_kv(parts):
    return pl.pallas_call(
        kv_back_kernel,
        out_shape=jax.ShapeDtypeStruct((128, 512), F32),
        in_specs=[VMEM],
        out_specs=VMEM,
        scratch_shapes=scatter_buffers(128, 512) + [pltpu.VMEM((8, 128, 512), BF)] + dma_sems(1, 9),
        compiler_params=params(3),
        name="scatter_kv",
    )(parts)


def mlp_kernel(
    a2, gu_in, dn_in, dy_in,
    da2_out, mpart, gu_out, dn_out,
    acts, gu, wd, dy, hid, dgu, dpart,
    d_half, d_full, d_pair,
    gsib, grecv, gown, gd, gdrecv, gdown,
    g_half, g_full, g_pair, n_half, n_full, n_pair,
    ag0, ag1, rs0, rs1, sib0, sib1, local,
):
    me = Place()
    greet(near(me.across_x) + near(me.across_y) + [me.sibling()])

    def acts_at(dr, dp, er, ep, half):
        return acts.at[slot_of(dr - er, dp + ep), row_half(half, 128)]

    task = Gather(me.across_y, a2, acts_at, (ag0, ag1), 0)
    task.start()
    loads = [
        pltpu.make_async_copy(gu_in, gu, local.at[0]),
        pltpu.make_async_copy(dn_in, wd.at[pl.ds(0, 704)], local.at[1]),
        pltpu.make_async_copy(dy_in, dy, local.at[2]),
    ]
    for load in loads:
        load.start()
    acts[0] = a2[...]
    wd[pl.ds(704, 64)] = jnp.zeros((64, 2048), BF)
    for load in loads:
        load.wait()

    def group(g):
        at = pl.ds(2 * g, 2)
        rows = pl.ds(pl.multiple_of(256 * g, 256), 256)
        for h in range(3):
            first, second = pl.ds(256 * h, 256), pl.ds(768 + 256 * h, 256)
            here = acts[at].reshape(256, 2048)
            gate = dot_in(here, gu[:, first])
            up = dot_in(here, gu[:, second])
            back = dot_back(dy[at].reshape(256, 2048), wd[first, :])
            curve = 1.0 / (1.0 + jnp.exp(-gate))
            silu = gate * curve
            hid[rows, first] = (silu * up).astype(BF)
            dgu[rows, first] = (back * up * (curve + silu * (1.0 - curve))).astype(BF)
            dgu[rows, second] = (back * silu).astype(BF)
        for n in range(4):
            wide = pl.ds(512 * n, 512)
            mpart[at, :, wide] = dot_in(hid[rows, :], wd[:, wide]).astype(BF).reshape(2, 128, 512)
            dpart[at, :, wide] = dot_back(dgu[rows, :], gu[wide, :]).astype(BF).reshape(2, 128, 512)

    @pl.loop(0, 4)
    def _(g):
        @pl.when(g == 0)
        def _():
            task.pair()

        @pl.when(g == 1)
        def _():
            task.turn(0)

        @pl.when(g == 2)
        def _():
            task.turn(1)

        @pl.when(g == 3)
        def _():
            task.last(0)
            task.last(1)

        group(g)

    grad = Scatter(me.across_y, lambda slot: dpart.at[slot], 128, d_half, d_full, d_pair, (rs0, rs1), 0)
    grad.start()

    def chip_of(t):
        dr = jnp.where(t < 2, 0, jnp.where(t >= 6, 2, 1 + 2 * lax.rem(t, 2)))
        dp = jnp.where(t < 2, t, jnp.where(t >= 6, t - 6, lax.div(t, 4)))
        return lax.rem(me.x + dr, 4) * 2 + lax.rem(me.zh + dp, 2)

    def weight_terms(t, core, out):
        first = pl.multiple_of((chip_of(t) * 2 + core) * 128, 128)
        left = acts[:, :, pl.ds(first, 128)].reshape(1024, 128)
        out[t] = dot_rows(left, dgu[...]).astype(BF)

    down_to = [
        send(gd.at[t, pl.ds(pl.multiple_of((1 - me.co) * 352, 16), 352)], gdrecv.at[t], (sib0, sib1), t, me.sibling())
        for t in range(8)
    ]
    gu_to = [send(gsib.at[t], grecv.at[t], (sib0, sib1), 8 + t, me.sibling()) for t in range(8)]

    @pl.loop(0, 8)
    def _(t):
        first = pl.multiple_of(chip_of(t) * 256, 256)
        gd[t] = dot_rows(hid[...], dy[:, :, pl.ds(first, 256)].reshape(1024, 256)).astype(BF)

    for copy in down_to:
        copy.start()

    @pl.loop(0, 8)
    def _(t):
        weight_terms(t, 1 - me.co, gsib)

    for copy in gu_to:
        copy.start()
    grad.turn(1)
    grad.turn(0)

    @pl.loop(0, 8)
    def _(t):
        weight_terms(t, me.co, gown)

    for copy in down_to:
        copy.wait_recv()

    @pl.loop(0, 8 * 22)
    def _(i):
        t, row = lax.div(i, 22), lax.rem(i, 22) * 16
        mine = gd[t, pl.ds(pl.multiple_of(me.co * 352 + row, 16), 16)].astype(F32)
        at = pl.ds(pl.multiple_of(row, 16), 16)
        gdown[t, at] = (mine + gdrecv[t, at].astype(F32)).astype(BF)

    for copy in gu_to:
        copy.wait_recv()

    @pl.loop(0, 8 * 8)
    def _(i):
        t, at = lax.div(i, 8), pl.ds(pl.multiple_of(lax.rem(i, 8) * 16, 16), 16)
        gown[t, at] = (gown[t, at].astype(F32) + grecv[t, at].astype(F32)).astype(BF)

    first = Scatter(me.across_x, lambda slot: gown.at[slot], 128, g_half, g_full, g_pair, (rs0, rs1), 1)
    second = Scatter(me.across_x, lambda slot: gdown.at[slot], 352, n_half, n_full, n_pair, (rs0, rs1), 2)
    first.start()
    second.start()
    grad.pair()
    for dp in (1, 0):
        first.turn(dp)
        second.turn(dp)
    grad.finish(da2_out)
    first.pair()
    second.pair()
    first.finish(gu_out)
    second.finish(dn_out)
    for job in (task, grad, first, second):
        job.end()
    for copy in (*down_to, *gu_to):
        copy.wait_send()


def feed_forward(a2, gu, dn, dy):
    scratch = [
        pltpu.VMEM((8, 128, 2048), BF),
        pltpu.VMEM((2048, 1536), BF),
        pltpu.VMEM((768, 2048), BF),
        pltpu.VMEM((8, 128, 2048), BF),
        pltpu.VMEM((1024, 768), BF),
        pltpu.VMEM((1024, 1536), BF),
        pltpu.VMEM((8, 128, 2048), BF),
        *scatter_buffers(128, 2048),
        pltpu.VMEM((8, 128, 1536), BF),
        pltpu.VMEM((8, 128, 1536), BF),
        pltpu.VMEM((8, 128, 1536), BF),
        pltpu.VMEM((8, 768, 256), BF),
        pltpu.VMEM((8, 352, 256), BF),
        pltpu.VMEM((8, 352, 256), BF),
        *scatter_buffers(128, 1536),
        *scatter_buffers(352, 256),
        *dma_sems(1, 9),
        *dma_sems(3, 9),
        pltpu.SemaphoreType.DMA((16,)),
        pltpu.SemaphoreType.DMA((16,)),
        pltpu.SemaphoreType.DMA((3,)),
    ]
    return pl.pallas_call(
        mlp_kernel,
        out_shape=(
            jax.ShapeDtypeStruct((128, 2048), F32),
            jax.ShapeDtypeStruct((8, 128, 2048), BF),
            jax.ShapeDtypeStruct((128, 1536), BF),
            jax.ShapeDtypeStruct((352, 256), BF),
        ),
        in_specs=[VMEM, ANY, ANY, ANY],
        out_specs=[VMEM] * 4,
        scratch_shapes=scratch,
        compiler_params=params(4, 62),
        name="feed_forward",
    )(a2, gu, dn, dy)


def grads_kernel(
    a1, att, dqkv, datt, gains, mpart_in, h1, gu, dn,
    mixed, q_out, o_out, gains_out, gu_all, dn_all,
    a1s, atts, dqkvs, datts, gsib, mpart,
    qp, op, gp, ggot,
    q_half, q_full, q_pair, o_half, o_full, o_pair, e_half, e_full, e_pair,
    m_half, m_full, m_pair,
    q_sum, o_sum, g_sum,
    qr_half, qr_full, qr_pair, or_half, or_full, or_pair,
    sib0, sib1, x0, x1, y0, y1, ag0, ag1, local,
):
    me = Place()
    greet(near(me.across_x) + near(me.across_y) + [me.sibling()])
    swaps = []
    for index, (own, both) in enumerate(((att, atts), (datt, datts), (a1, a1s), (dqkv, dqkvs))):
        swaps.append(send(own, both.at[pl.ds(128, 128)], (sib0, sib1), index, me.sibling()))
    swaps.append(send(gains, gsib, (sib0, sib1), 4, me.sibling()))
    for copy in swaps:
        copy.start()
    load = pltpu.make_async_copy(mpart_in, mpart, local.at[0])
    load.start()

    def at_ctx(ref):
        def loc(dr, dp, er, ep, half):
            rows = ref.shape[1]
            return ref.at[me.ctx_at(dr, dp), row_half(half, rows)]

        return loc

    gu_task = Gather(me.across_y, gu, at_ctx(gu_all), (ag0, ag1), 0)
    dn_task = Gather(me.across_y, dn, at_ctx(dn_all), (ag0, ag1), 1)
    kept = [
        pltpu.make_async_copy(gu, gu_all.at[me.c], local.at[1]),
        pltpu.make_async_copy(dn, dn_all.at[me.c], local.at[2]),
    ]
    for copy in kept:
        copy.start()
    gu_task.start()
    dn_task.start()
    for own, both in ((att, atts), (datt, datts), (a1, a1s), (dqkv, dqkvs)):
        both[pl.ds(0, 128)] = own[...]

    def chip_of(t):
        dr = jnp.where(t < 2, 0, jnp.where(t >= 6, 2, 1 + 2 * lax.rem(t, 2)))
        dp = jnp.where(t < 2, t, jnp.where(t >= 6, t - 6, lax.div(t, 4)))
        return lax.rem(me.x + dr, 4) * 2 + lax.rem(me.zh + dp, 2)

    swaps[0].wait_recv()
    swaps[1].wait_recv()

    def terms(left, right, out):
        @pl.loop(0, 8)
        def _(i):
            t = 7 - i
            first = pl.multiple_of((chip_of(t) * 2 + me.co) * 128, 128)
            out[t] = dot_rows(left[:, pl.ds(first, 128)], right[...]).astype(BF)

    over_x = (x0, x1)
    over_y = (y0, y1)
    o_job = Scatter(me.across_x, lambda slot: op.at[slot], 128, o_half, o_full, o_pair, over_x, 0)
    q_job = Scatter(me.across_x, lambda slot: qp.at[slot], 128, q_half, q_full, q_pair, over_x, 1)
    e_job = Scatter(me.across_x, lambda slot: gp.at[slot], 16, e_half, e_full, e_pair, over_x, 2)
    m_job = Scatter(me.across_y, lambda slot: mpart.at[slot], 128, m_half, m_full, m_pair, over_y, 0)
    terms(atts, datts, op)
    o_job.start()
    swaps[4].wait_recv()
    for slot in range(8):
        block = me.fsdp_at(STEPS[slot], PAIRS[slot])
        gp[slot] = gains[block] + gsib[block]
    e_job.start()
    swaps[2].wait_recv()
    swaps[3].wait_recv()
    terms(a1s, dqkvs, qp)
    gu_task.pair()
    dn_task.pair()
    for dp in (1, 0):
        o_job.turn(dp)
        e_job.turn(dp)
    q_job.start()
    gu_task.turn(0)
    dn_task.turn(0)
    gu_task.turn(1)
    dn_task.turn(1)
    load.wait()
    m_job.start()
    o_job.pair()
    e_job.pair()
    o_job.finish(o_sum)
    e_job.finish(g_sum)
    for dp in (1, 0):
        q_job.turn(dp)
        m_job.turn(dp)

    def sum_over_ctx(total, columns, halves, fulls, paired, row):
        def part(slot):
            first = pl.multiple_of(me.ctx_at(STEPS[slot], PAIRS[slot]) * 16, 16)
            return total.at[pl.ds(first, 16)]

        return Scatter(me.across_y, part, 16, halves, fulls, paired, over_y, row, cut=columns)

    def spread(out, columns, row):
        def loc(dr, dp, er, ep, half):
            first = pl.multiple_of(me.ctx_at(dr, dp) * 16, 16)
            if half is None:
                return out.at[pl.ds(first, 16)]
            return out.at[pl.ds(first, 16), pl.ds(half * (columns // 2), columns // 2)]

        return Gather(me.across_y, loc(0, 0, 0, 0, None), loc, (ag0, ag1), row)

    e_task = Gather(me.across_y, g_sum, at_ctx(ggot), (ag0, ag1), 2)
    e_task.start()
    o_sums = sum_over_ctx(o_sum, 2048, or_half, or_full, or_pair, 1)
    o_sums.start()
    o_spread = spread(o_out, 2048, 3)
    q_spread = spread(q_out, 2560, 4)
    ggot[me.c] = g_sum[...]
    e_task.pair()
    e_task.turn(0)
    e_task.turn(1)
    o_sums.turn(1)
    o_sums.turn(0)
    m_job.pair()
    o_sums.pair()
    m_job.finish(mixed, (h1,))
    own_rows = pl.ds(pl.multiple_of(me.c * 16, 16), 16)
    o_sums.finish(o_out.at[own_rows])
    o_spread.start()
    for task in (gu_task, dn_task, e_task):
        task.last(0)
        task.last(1)
    total = ggot[0]
    for index in range(1, 8):
        total = total + ggot[index]
    gains_out[...] = total
    q_job.pair()
    q_job.finish(q_sum)
    q_sums = sum_over_ctx(q_sum, 2560, qr_half, qr_full, qr_pair, 2)
    q_sums.start()
    o_spread.pair()
    o_spread.turn(0)
    o_spread.turn(1)
    q_sums.turn(1)
    q_sums.turn(0)
    q_sums.pair()
    q_sums.finish(q_out.at[own_rows])
    q_spread.start()
    q_spread.pair()
    q_spread.turn(0)
    q_spread.turn(1)
    for task in (o_spread, q_spread):
        task.last(0)
        task.last(1)
    for job in (o_job, q_job, e_job, m_job, o_sums, q_sums, gu_task, dn_task, e_task, o_spread, q_spread):
        job.end()
    for copy in swaps:
        copy.wait_send()
    for copy in kept:
        copy.wait()


def weight_grads(a1, att, dqkv, datt, gains, mpart, h1, gu, dn):
    scratch = [
        pltpu.VMEM((256, 2048), BF),
        pltpu.VMEM((256, 2048), BF),
        pltpu.VMEM((256, 2560), BF),
        pltpu.VMEM((256, 2048), BF),
        pltpu.VMEM((16, 16, 128), F32),
        pltpu.VMEM((8, 128, 2048), BF),
        pltpu.VMEM((8, 128, 2560), BF),
        pltpu.VMEM((8, 128, 2048), BF),
        pltpu.VMEM((8, 16, 128), F32),
        pltpu.VMEM((8, 16, 128), F32),
        *scatter_buffers(128, 2560),
        *scatter_buffers(128, 2048),
        *scatter_buffers(16, 128, F32),
        *scatter_buffers(128, 2048),
        pltpu.VMEM((128, 2560), BF),
        pltpu.VMEM((128, 2048), BF),
        pltpu.VMEM((16, 128), F32),
        *scatter_buffers(16, 2560, cut=True),
        *scatter_buffers(16, 2048, cut=True),
        pltpu.SemaphoreType.DMA((5,)),
        pltpu.SemaphoreType.DMA((5,)),
        *dma_sems(3, 9),
        *dma_sems(3, 9),
        *dma_sems(5, 9),
        pltpu.SemaphoreType.DMA((3,)),
    ]
    return pl.pallas_call(
        grads_kernel,
        out_shape=(
            jax.ShapeDtypeStruct((128, 2048), BF),
            jax.ShapeDtypeStruct((128, 2560), BF),
            jax.ShapeDtypeStruct((128, 2048), BF),
            jax.ShapeDtypeStruct((16, 128), F32),
            jax.ShapeDtypeStruct((8, 128, 1536), BF),
            jax.ShapeDtypeStruct((8, 352, 256), BF),
        ),
        in_specs=[VMEM] * 5 + [ANY, VMEM, ANY, ANY],
        out_specs=[VMEM] * 4 + [ANY, ANY],
        scratch_shapes=scratch,
        compiler_params=params(5, 60),
        name="weight_grads",
    )(a1, att, dqkv, datt, gains, mpart, h1, gu, dn)


HEADS = 32
KV_HEADS = 4
HEAD_DIM = 64
GROUP_HEADS = 8
EPS = 1e-05
SCALE = 0.125
BASE = 10000.0


def rms_norm(values, gain):
    return values * lax.rsqrt(jnp.mean(values * values, axis=-1, keepdims=True) + EPS) * gain


def tables(position):
    freq = BASE ** (-(jnp.arange(HEAD_DIM // 2, dtype=jnp.float32) * 2.0) / HEAD_DIM)
    angle = position.astype(jnp.float32)[:, None] * freq[None, :]
    angle = jnp.concatenate([angle, angle], axis=-1)
    return (jnp.cos(angle), jnp.sin(angle))


def rotate(values, cosine, sine):
    half_dim = values.shape[-1] // 2
    turned = jnp.concatenate([-values[..., half_dim:], values[..., :half_dim]], axis=-1)
    return values * cosine[:, None, :] + turned * sine[:, None, :]


def unrotate(values, cosine, sine):
    half_dim = values.shape[-1] // 2
    scaled = values * sine[:, None, :]
    turned = jnp.concatenate([scaled[..., half_dim:], -scaled[..., :half_dim]], axis=-1)
    return values * cosine[:, None, :] + turned


def timeline(table_flat, total_len, row_count):
    everywhere = jnp.arange(total_len, dtype=jnp.int32)
    half_len = row_count // 2
    moment = jnp.repeat(table_flat, half_len) * half_len + everywhere % half_len
    prompt_len = total_len // 2
    cont_len = total_len // 8
    later = moment >= prompt_len
    segment = jnp.where(later, 1 + (moment - prompt_len) // cont_len, 0)
    position = jnp.where(later, prompt_len + (moment - prompt_len) % cont_len, moment)
    return (segment, position)


def swap_pairs():
    pairs = []
    for c in range(8):
        for f in range(16):
            pairs.append((c * 16 + f, (f // 2) * 16 + 2 * c + f % 2))
    return pairs


def softmax_parts(masked):
    peak = jnp.max(masked, axis=-1, keepdims=True)
    unscaled = jnp.exp(masked - peak)
    total = jnp.sum(unscaled, axis=-1, keepdims=True)
    return ((unscaled / total).astype(jnp.bfloat16), peak + jnp.log(total))


def on_device(
    tokens,
    block_deal,
    attn_gain,
    query_weight,
    key_weight,
    value_weight,
    output_weight,
    mlp_gain,
    gate_weight,
    up_weight,
    down_weight,
    cotangent,
):
    inputs = tokens[0].astype(F32)
    grad_out = cotangent[0].astype(F32)
    row_count = inputs.shape[0]
    c = lax.axis_index("ctx")
    f = lax.axis_index("fsdp")
    full_len = row_count * 8

    def sliced(weight):
        return jnp.pad(lax.dynamic_slice_in_dim(weight, c * 704, 704, 1), ((0, 0), (0, 64)))

    none = jnp.zeros((7, 128), F32)
    gains = jnp.concatenate([attn_gain.astype(F32)[None], none, mlp_gain.astype(F32)[None], none])
    qkv = jnp.concatenate([query_weight, key_weight, value_weight], axis=1)
    gu = jnp.concatenate([sliced(gate_weight), sliced(up_weight)], axis=1)
    dn = lax.dynamic_slice_in_dim(down_weight, c * 256, 256, 1)
    dn = lax.ppermute(dn, ("ctx", "fsdp"), swap_pairs())
    gains_all, qkv_all, wo_all, gu_all, dn_all, dy_all = gather_weights(
        gains, qkv, output_weight, gu, dn, cotangent[0]
    )
    gain_first = gains_all[:, 0].reshape(2048)
    gain_second = gains_all[:, 8].reshape(2048)

    deal = lax.dynamic_index_in_dim(block_deal, f, 0, keepdims=False)
    segment, position = timeline(deal.reshape(-1), full_len, row_count)
    own_segment = lax.dynamic_slice_in_dim(segment, c * row_count, row_count, 0)
    own_position = lax.dynamic_slice_in_dim(position, c * row_count, row_count, 0)
    cosine, sine = tables(own_position)
    same = (segment[None, :] == 0) | (segment[None, :] == own_segment[:, None])
    visible = same & (position[None, :] <= own_position[:, None])

    normed = rms_norm(inputs, gain_first).astype(BF)
    raw = dot_in(normed, qkv_all)
    query_raw = raw[:, :2048].reshape(row_count, HEADS, HEAD_DIM)
    key_raw = raw[:, 2048:2304].reshape(row_count, KV_HEADS, HEAD_DIM)
    queries = rotate(query_raw, cosine, sine).astype(BF)
    queries = queries.reshape(row_count, KV_HEADS, GROUP_HEADS, HEAD_DIM)
    keys_own = rotate(key_raw, cosine, sine).astype(BF).reshape(row_count, KV_HEADS * HEAD_DIM)
    values_own = raw[:, 2304:].astype(BF)
    kv_all = gather_kv(jnp.concatenate([keys_own, values_own], axis=1)).reshape(full_len, 512)
    keys_all = kv_all[:, :256].reshape(full_len, KV_HEADS, HEAD_DIM)
    values_all = kv_all[:, 256:].reshape(full_len, KV_HEADS, HEAD_DIM)
    scores = jnp.einsum("qcgd,kcd->cgqk", queries, keys_all, preferred_element_type=F32) * SCALE
    probs_low, log_total = softmax_parts(jnp.where(visible, scores, -1e30))
    heads_out = jnp.einsum("cgqk,kcd->qcgd", probs_low, values_all, preferred_element_type=F32)
    attended = heads_out.astype(BF).reshape(row_count, HEADS * HEAD_DIM)
    hidden_state = inputs + dot_in(attended, wo_all)

    normed_two = rms_norm(hidden_state, gain_second).astype(BF)
    grad_normed_two, mixed_parts, gu_sum, dn_sum = feed_forward(normed_two, gu_all, dn_all, dy_all)
    dn_sum = lax.ppermute(dn_sum, ("ctx", "fsdp"), swap_pairs())
    _, norm_two_back = jax.vjp(rms_norm, hidden_state, gain_second)
    grad_hidden_norm, grad_gain_two = norm_two_back(grad_normed_two)
    grad_hidden = grad_out + grad_hidden_norm
    grad_att = grad_hidden.astype(BF)

    grad_heads = dot_back(grad_att, wo_all).astype(BF)
    grad_heads = grad_heads.reshape(row_count, KV_HEADS, GROUP_HEADS, HEAD_DIM)
    scores_again = jnp.einsum("qcgd,kcd->cgqk", queries, keys_all, preferred_element_type=F32) * SCALE
    probs = jnp.exp(jnp.where(visible, scores_again, -1e30) - log_total)
    probs_again = probs.astype(BF)
    grad_probs = jnp.einsum("qcgd,kcd->cgqk", grad_heads, values_all, preferred_element_type=F32)
    grad_values_all = jnp.einsum("cgqk,qcgd->kcd", probs_again, grad_heads, preferred_element_type=F32)
    grad_scores = probs * (grad_probs - jnp.sum(probs * grad_probs, axis=-1, keepdims=True))
    grad_scores = grad_scores.astype(BF)
    grad_queries = jnp.einsum("cgqk,kcd->qcgd", grad_scores, keys_all, preferred_element_type=F32) * SCALE
    grad_keys_all = jnp.einsum("cgqk,qcgd->kcd", grad_scores, queries, preferred_element_type=F32) * SCALE
    kv_parts = jnp.concatenate(
        [grad_keys_all.reshape(full_len, 256), grad_values_all.reshape(full_len, 256)], axis=1
    ).astype(BF)
    grad_kv = scatter_kv(kv_parts.reshape(8, 128, 512))
    grad_query_raw = unrotate(grad_queries.reshape(row_count, HEADS, HEAD_DIM), cosine, sine)
    grad_query_raw = grad_query_raw.reshape(row_count, HEADS * HEAD_DIM).astype(BF)
    grad_key_raw = unrotate(grad_kv[:, :256].reshape(row_count, KV_HEADS, HEAD_DIM), cosine, sine)
    grad_key_raw = grad_key_raw.reshape(row_count, KV_HEADS * HEAD_DIM).astype(BF)
    grad_raw = jnp.concatenate([grad_query_raw, grad_key_raw, grad_kv[:, 256:].astype(BF)], axis=1)
    grad_normed = dot_back(grad_raw, qkv_all)
    _, norm_one_back = jax.vjp(rms_norm, inputs, gain_first)
    grad_inputs_norm, grad_gain_one = norm_one_back(grad_normed)
    tokens_grad = (grad_hidden + grad_inputs_norm).astype(BF)

    gain_terms = jnp.zeros((16, 16, 128), F32)
    gain_terms = gain_terms.at[:, 0].set(grad_gain_one.reshape(16, 128))
    gain_terms = gain_terms.at[:, 8].set(grad_gain_two.reshape(16, 128))
    mixed, qkv_grad, o_grad, gain_grads, gu_grads, dn_grads = weight_grads(
        normed, attended, grad_raw, grad_att, gain_terms, mixed_parts, hidden_state, gu_sum, dn_sum
    )

    def joined(parts):
        return parts.transpose(1, 0, 2).reshape(parts.shape[1], -1).astype(F32)

    return (
        mixed[None],
        tokens_grad[None],
        gain_grads[0],
        qkv_grad[:, :2048].astype(F32),
        qkv_grad[:, 2048:2304].astype(F32),
        qkv_grad[:, 2304:].astype(F32),
        o_grad.astype(F32),
        gain_grads[8],
        joined(gu_grads[:, :, :704]),
        joined(gu_grads[:, :, 768:1472]),
        joined(dn_grads),
    )


def solution(mesh):
    held = P("fsdp", "ctx", None)
    rows = P("fsdp", None)
    return jax.shard_map(
        on_device,
        mesh=mesh,
        in_specs=(held, P(), P("fsdp"), rows, rows, rows, rows, P("fsdp"), rows, rows, rows, held),
        out_specs=(held, held, P("fsdp"), rows, rows, rows, rows, P("fsdp"), rows, rows, rows),
        check_vma=False,
    )
```

```python
import functools

import jax
import jax.numpy as jnp
from jax import lax
from jax.experimental import pallas as pl
from jax.experimental.pallas import tpu as pltpu
from jax.sharding import PartitionSpec as P

MESH = pl.DeviceIdType.MESH
BF = jnp.bfloat16
F32 = jnp.float32
ANY = pl.BlockSpec(memory_space=pl.ANY)
VMEM = pl.BlockSpec(memory_space=pltpu.VMEM)

HEAD_DIM = 64
EPS = 1e-05
SCALE = 0.125
BASE = 10000.0

SLOT = {(0, 0): 0, (0, 1): 1, (1, 0): 2, (3, 0): 3, (1, 1): 4, (3, 1): 5, (2, 0): 6, (2, 1): 7}
STEPS = (0, 0, 1, 3, 1, 3, 2, 2)
PAIRS = (0, 1, 0, 0, 1, 1, 0, 1)


def slot_of(dr, dp):
    return SLOT[(dr % 4, dp % 2)]


class Place:
    def __init__(self):
        self.c = lax.axis_index("ctx")
        self.f = lax.axis_index("fsdp")
        self.y, self.zl = lax.div(self.c, 2), lax.rem(self.c, 2)
        self.j, self.co = lax.div(self.f, 2), lax.rem(self.f, 2)
        self.x, self.zh = lax.div(self.j, 2), lax.rem(self.j, 2)

    def ctx_at(self, dr, dp):
        return lax.rem(self.y + dr % 4, 4) * 2 + lax.rem(self.zl + dp, 2)

    def chip_at(self, dr, dp):
        return lax.rem(self.x + dr % 4, 4) * 2 + lax.rem(self.zh + dp, 2)

    def fsdp_at(self, dr, dp):
        return self.chip_at(dr, dp) * 2 + self.co

    def across_y(self, dr, dp):
        return {"ctx": self.ctx_at(dr, dp), "fsdp": self.f}

    def across_x(self, dr, dp):
        return {"ctx": self.c, "fsdp": self.fsdp_at(dr, dp)}

    def sibling(self):
        return {"ctx": self.c, "fsdp": self.f + 1 - 2 * self.co}


def greet(devices):
    barrier = pltpu.get_barrier_semaphore()
    for device in devices:
        pl.semaphore_signal(barrier, 1, device_id=device, device_id_type=MESH)
    pl.semaphore_wait(barrier, len(devices))


def near(dev):
    return [dev(1, 0), dev(-1, 0), dev(0, 1)]


def send(src, dst, sems, index, device):
    return pltpu.make_async_remote_copy(
        src, dst, sems[0].at[index], sems[1].at[index], device_id=device, device_id_type=MESH
    )


class Gather:
    MOVES = (
        ((0, 0), (0, 1), None),
        ((0, 0), (1, 0), None),
        ((0, 0), (-1, 0), None),
        ((0, 1), (1, 0), None),
        ((0, 1), (-1, 0), None),
        ((-1, 0), (1, 0), 0),
        ((-1, 1), (1, 0), 0),
        ((1, 0), (-1, 0), 1),
        ((1, 1), (-1, 0), 1),
    )

    def __init__(self, dev, own, loc, sems, row, sibling=None, sibling_sems=None):
        self.loc = loc
        self.copies = []
        for index, (block, to, half) in enumerate(self.MOVES):
            src = own if block == (0, 0) else loc(*block, 0, 0, half)
            dst = loc(*block, *to, half)
            self.copies.append(send(src, dst, sems, (row, index), dev(*to)))
        self.passed = {}
        if sibling is not None:
            self.passed[9] = send(own, loc(0, 0, 0, 0, None), sibling_sems, (row, 9), sibling)
            for index, ((dr, dp), (er, ep), half) in enumerate(self.MOVES):
                ref = loc(dr - er, dp + ep, 0, 0, half)
                self.passed[index] = send(ref, ref, sibling_sems, (row, index), sibling)
        self.own = own

    def _pass(self, index):
        if self.passed:
            self.passed[index].start()

    def _got(self, index):
        self.copies[index].wait_recv()
        self._pass(index)

    def start(self):
        for index in (0, 1, 2):
            self.copies[index].start()
        self._pass(9)

    def pair(self):
        self._got(0)
        self.copies[3].start()
        self.copies[4].start()

    def turn(self, dp):
        for got, on in (((1, 5), (2, 7)) if dp == 0 else ((3, 6), (4, 8))):
            self._got(got)
            self.copies[on].start()

    def last(self, dp):
        for got in ((5, 7) if dp == 0 else (6, 8)):
            self._got(got)

    def end(self):
        for copy in self.copies:
            copy.wait_send()
        for copy in self.passed.values():
            copy.wait()

    def all(self):
        self.start()
        self.pair()
        self.turn(0)
        self.turn(1)
        self.last(0)
        self.last(1)
        self.end()


def row_half(half, rows):
    return pl.ds(0, rows) if half is None else pl.ds(half * (rows // 2), rows // 2)


def add_into(ref, rows, others, step=16):
    step = min(step, rows)

    @pl.loop(0, rows // step)
    def _(i):
        at = pl.ds(pl.multiple_of(i * step, step), step)
        total = ref[at].astype(F32)
        for other in others:
            total = total + other[at].astype(F32)
        ref[at] = total.astype(ref.dtype)


class Scatter:
    def __init__(self, dev, part, rows, halves, fulls, paired, sems, row, cut=None):
        self.part, self.rows, self.cut = part, rows, cut
        self.halves, self.fulls, self.paired = halves, fulls, paired
        self.first, self.second = {}, {}
        for dp in (0, 1):
            for way, sign in ((0, 1), (1, -1)):
                self.first[way, dp] = send(
                    self._half(part(slot_of(2, dp)), way), halves.at[way, dp], sems, (row, way * 2 + dp), dev(sign, 0)
                )
                self.second[way, dp] = send(
                    part(slot_of(sign, dp)), fulls.at[way, dp], sems, (row, 4 + way * 2 + dp), dev(sign, 0)
                )
        self.third = send(part(slot_of(0, 1)), paired, sems, (row, 8), dev(0, 1))

    def _half(self, ref, way):
        if self.cut is None:
            return ref.at[pl.ds(way * (self.rows // 2), self.rows // 2)]
        return ref.at[:, pl.ds(way * (self.cut // 2), self.cut // 2)]

    def start(self):
        for dp in (1, 0):
            for way in (0, 1):
                self.first[way, dp].start()

    def turn(self, dp):
        for way, sign in ((0, 1), (1, -1)):
            self.first[way, dp].wait_recv()
            block = self._half(self.part(slot_of(sign, dp)), way)
            add_into(block, block.shape[0], [self.halves.at[way, dp]])
            self.second[way, dp].start()

    def pair(self):
        for way in (0, 1):
            self.second[way, 1].wait_recv()
        add_into(self.part(slot_of(0, 1)), self.rows, [self.fulls.at[0, 1], self.fulls.at[1, 1]])
        self.third.start()

    def finish(self, out, extra=()):
        for way in (0, 1):
            self.second[way, 0].wait_recv()
        self.third.wait_recv()
        own = self.part(0)
        terms = [own, self.fulls.at[0, 0], self.fulls.at[1, 0], self.paired, *extra]

        @pl.loop(0, self.rows // 16)
        def _(i):
            at = pl.ds(pl.multiple_of(i * 16, 16), 16)
            total = terms[0][at].astype(F32)
            for term in terms[1:]:
                total = total + term[at].astype(F32)
            out[at] = total.astype(out.dtype)

    def end(self):
        for copy in (*self.first.values(), *self.second.values(), self.third):
            copy.wait_send()


def scatter_buffers(rows, columns, dtype=BF, cut=False):
    half = (rows, columns // 2) if cut else (rows // 2, columns)
    return [
        pltpu.VMEM((2, 2, *half), dtype),
        pltpu.VMEM((2, 2, rows, columns), dtype),
        pltpu.VMEM((rows, columns), dtype),
    ]


def dma_sems(rows, count):
    return [pltpu.SemaphoreType.DMA((rows, count)), pltpu.SemaphoreType.DMA((rows, count))]


def params(collective_id, vmem=56):
    return pltpu.CompilerParams(
        collective_id=collective_id, has_side_effects=True, vmem_limit_bytes=vmem << 20
    )


def dot_in(left, right):
    return jnp.dot(left, right, preferred_element_type=F32)


def dot_back(left, right):
    return lax.dot_general(left, right, (((1,), (1,)), ((), ())), preferred_element_type=F32)


def dot_rows(left, right):
    return lax.dot_general(left, right, (((0,), (0,)), ((), ())), preferred_element_type=F32)


def mlp_kernel(
    a2, gu_in, dn_in, dy_in,
    da2_out, mpart, gu_out, dn_out,
    acts, gu, wd, dy, hid, dgu, dpart,
    d_half, d_full, d_pair,
    gsib, grecv, gown, gd, gdrecv, gdown,
    g_half, g_full, g_pair, n_half, n_full, n_pair,
    ag0, ag1, rs0, rs1, sib0, sib1, local,
):
    me = Place()
    greet(near(me.across_x) + near(me.across_y) + [me.sibling()])

    def acts_at(dr, dp, er, ep, half):
        return acts.at[slot_of(dr - er, dp + ep), row_half(half, 128)]

    task = Gather(me.across_y, a2, acts_at, (ag0, ag1), 0)
    task.start()
    loads = [
        pltpu.make_async_copy(gu_in, gu, local.at[0]),
        pltpu.make_async_copy(dn_in, wd.at[pl.ds(0, 704)], local.at[1]),
        pltpu.make_async_copy(dy_in, dy, local.at[2]),
    ]
    for load in loads:
        load.start()
    acts[0] = a2[...]
    wd[pl.ds(704, 64)] = jnp.zeros((64, 2048), BF)
    for load in loads:
        load.wait()

    def group(g):
        at = pl.ds(2 * g, 2)
        rows = pl.ds(pl.multiple_of(256 * g, 256), 256)
        for h in range(3):
            first, second = pl.ds(256 * h, 256), pl.ds(768 + 256 * h, 256)
            here = acts[at].reshape(256, 2048)
            gate = dot_in(here, gu[:, first])
            up = dot_in(here, gu[:, second])
            back = dot_back(dy[at].reshape(256, 2048), wd[first, :])
            curve = 1.0 / (1.0 + jnp.exp(-gate))
            silu = gate * curve
            hid[rows, first] = (silu * up).astype(BF)
            dgu[rows, first] = (back * up * (curve + silu * (1.0 - curve))).astype(BF)
            dgu[rows, second] = (back * silu).astype(BF)
        for n in range(4):
            wide = pl.ds(512 * n, 512)
            mpart[at, :, wide] = dot_in(hid[rows, :], wd[:, wide]).astype(BF).reshape(2, 128, 512)
            dpart[at, :, wide] = dot_back(dgu[rows, :], gu[wide, :]).astype(BF).reshape(2, 128, 512)

    @pl.loop(0, 4)
    def _(g):
        @pl.when(g == 0)
        def _():
            task.pair()

        @pl.when(g == 1)
        def _():
            task.turn(0)

        @pl.when(g == 2)
        def _():
            task.turn(1)

        @pl.when(g == 3)
        def _():
            task.last(0)
            task.last(1)

        group(g)

    grad = Scatter(me.across_y, lambda slot: dpart.at[slot], 128, d_half, d_full, d_pair, (rs0, rs1), 0)
    grad.start()

    def chip_of(t):
        dr = jnp.where(t < 2, 0, jnp.where(t >= 6, 2, 1 + 2 * lax.rem(t, 2)))
        dp = jnp.where(t < 2, t, jnp.where(t >= 6, t - 6, lax.div(t, 4)))
        return lax.rem(me.x + dr, 4) * 2 + lax.rem(me.zh + dp, 2)

    def weight_terms(t, core, out):
        first = pl.multiple_of((chip_of(t) * 2 + core) * 128, 128)
        left = acts[:, :, pl.ds(first, 128)].reshape(1024, 128)
        out[t] = dot_rows(left, dgu[...]).astype(BF)

    down_to = [
        send(gd.at[t, pl.ds(pl.multiple_of((1 - me.co) * 352, 16), 352)], gdrecv.at[t], (sib0, sib1), t, me.sibling())
        for t in range(8)
    ]
    gu_to = [send(gsib.at[t], grecv.at[t], (sib0, sib1), 8 + t, me.sibling()) for t in range(8)]

    @pl.loop(0, 8)
    def _(t):
        first = pl.multiple_of(chip_of(t) * 256, 256)
        gd[t] = dot_rows(hid[...], dy[:, :, pl.ds(first, 256)].reshape(1024, 256)).astype(BF)

    for copy in down_to:
        copy.start()

    @pl.loop(0, 8)
    def _(t):
        weight_terms(t, 1 - me.co, gsib)

    for copy in gu_to:
        copy.start()
    grad.turn(1)
    grad.turn(0)

    @pl.loop(0, 8)
    def _(t):
        weight_terms(t, me.co, gown)

    for copy in down_to:
        copy.wait_recv()

    @pl.loop(0, 8 * 22)
    def _(i):
        t, row = lax.div(i, 22), lax.rem(i, 22) * 16
        mine = gd[t, pl.ds(pl.multiple_of(me.co * 352 + row, 16), 16)].astype(F32)
        at = pl.ds(pl.multiple_of(row, 16), 16)
        gdown[t, at] = (mine + gdrecv[t, at].astype(F32)).astype(BF)

    for copy in gu_to:
        copy.wait_recv()

    @pl.loop(0, 8 * 8)
    def _(i):
        t, at = lax.div(i, 8), pl.ds(pl.multiple_of(lax.rem(i, 8) * 16, 16), 16)
        gown[t, at] = (gown[t, at].astype(F32) + grecv[t, at].astype(F32)).astype(BF)

    first = Scatter(me.across_x, lambda slot: gown.at[slot], 128, g_half, g_full, g_pair, (rs0, rs1), 1)
    second = Scatter(me.across_x, lambda slot: gdown.at[slot], 352, n_half, n_full, n_pair, (rs0, rs1), 2)
    first.start()
    second.start()
    grad.pair()
    for dp in (1, 0):
        first.turn(dp)
        second.turn(dp)
    grad.finish(da2_out)
    first.pair()
    second.pair()
    first.finish(gu_out)
    second.finish(dn_out)
    for job in (task, grad, first, second):
        job.end()
    for copy in (*down_to, *gu_to):
        copy.wait_send()


def feed_forward(a2, gu, dn, dy):
    scratch = [
        pltpu.VMEM((8, 128, 2048), BF),
        pltpu.VMEM((2048, 1536), BF),
        pltpu.VMEM((768, 2048), BF),
        pltpu.VMEM((8, 128, 2048), BF),
        pltpu.VMEM((1024, 768), BF),
        pltpu.VMEM((1024, 1536), BF),
        pltpu.VMEM((8, 128, 2048), BF),
        *scatter_buffers(128, 2048),
        pltpu.VMEM((8, 128, 1536), BF),
        pltpu.VMEM((8, 128, 1536), BF),
        pltpu.VMEM((8, 128, 1536), BF),
        pltpu.VMEM((8, 768, 256), BF),
        pltpu.VMEM((8, 352, 256), BF),
        pltpu.VMEM((8, 352, 256), BF),
        *scatter_buffers(128, 1536),
        *scatter_buffers(352, 256),
        *dma_sems(1, 9),
        *dma_sems(3, 9),
        pltpu.SemaphoreType.DMA((16,)),
        pltpu.SemaphoreType.DMA((16,)),
        pltpu.SemaphoreType.DMA((3,)),
    ]
    return pl.pallas_call(
        mlp_kernel,
        out_shape=(
            jax.ShapeDtypeStruct((128, 2048), F32),
            jax.ShapeDtypeStruct((8, 128, 2048), BF),
            jax.ShapeDtypeStruct((128, 1536), BF),
            jax.ShapeDtypeStruct((352, 256), BF),
        ),
        in_specs=[VMEM, ANY, ANY, ANY],
        out_specs=[VMEM] * 4,
        scratch_shapes=scratch,
        compiler_params=params(4, 62),
        name="feed_forward",
    )(a2, gu, dn, dy)


def load(src, dst, sem):
    copy = pltpu.make_async_copy(src, dst, sem)
    copy.start()
    return copy


def turned(values):
    lane = lax.broadcasted_iota(jnp.int32, values.shape, 1)
    low = lax.rem(lane, 64) < 32
    return jnp.where(low, pltpu.roll(values, 96, 1), pltpu.roll(values, 32, 1))


def pile(out, values, half):
    for h in range(8):
        out[pl.ds(64 * h, 64), :] = values[64 * half : 64 * half + 64, 64 * h : 64 * h + 64]


def unpile(values):
    flat = values.T
    return [
        jnp.concatenate([flat[128 * m : 128 * m + 64], flat[128 * m + 64 : 128 * m + 128]], axis=1)
        for m in range(4)
    ]


def norm_scale(ref, out):
    values = ref[...].astype(F32)
    out[...] = lax.rsqrt(jnp.mean(values * values, axis=1, keepdims=True) + EPS)


def front_kernel(
    x, gains_in, qkv_in, wo_in, gu_in, dn_in, dy_in, cosine, sine, bias_p, bias_c, partner,
    gains, qkv_out, wo_out, gu_all, dn_all, dy_all, a1, qst, kst, vst, att, lse, h1, a2,
    qkv, wo, kv_own, kv, sT, pT, scale,
    s0, s1, t0, t1, y0, y1, u0, u1, local,
):
    me = Place()
    greet(near(me.across_x) + near(me.across_y) + [me.sibling()])

    def rows_at(ref, rows):
        def loc(dr, dp, er, ep, half):
            size = rows if half is None else rows // 2
            first = me.fsdp_at(dr, dp) * rows + (0 if half is None else half * size)
            return ref.at[pl.ds(pl.multiple_of(first, size), size)]

        return loc

    def gains_at(dr, dp, er, ep, half):
        return gains.at[me.fsdp_at(dr, dp), row_half(half, 16)]

    def dn_at(dr, dp, er, ep, half):
        size = 352 if half is None else 176
        first = me.co * 352 + (0 if half is None else half * size)
        return dn_all.at[
            pl.ds(pl.multiple_of(first, 16), size),
            pl.ds(pl.multiple_of(me.chip_at(dr, dp) * 256, 256), 256),
        ]

    def slot_at(ref, rows):
        def loc(dr, dp, er, ep, half):
            return ref.at[slot_of(dr - er, dp + ep), row_half(half, rows)]

        return loc

    def columns(index):
        return pl.ds(pl.multiple_of(index * 256, 256), 256)

    def wo_x_at(dr, dp, er, ep, half):
        return wo.at[me.chip_at(dr, dp), me.co, row_half(half, 128), columns(me.c)]

    def wo_y_at(dr, dp, er, ep, half):
        chips = pl.ds(0, 8) if half is None else pl.ds(4 * half, 4)
        return wo.at[chips, me.co, :, columns(me.ctx_at(dr, dp))]

    def over_x(own, loc, row, both=True):
        return Gather(me.across_x, own, loc, (s0, s1), row, me.sibling() if both else None, (t0, t1))

    wo_own = wo_in.at[:, columns(me.c)]
    g = over_x(gains_in, gains_at, 0)
    q = over_x(qkv_in, rows_at(qkv, 128), 1)
    o = over_x(wo_own, wo_x_at, 2, both=False)
    m = over_x(gu_in, rows_at(gu_all, 128), 3)
    d = over_x(dn_in, dn_at, 4)
    dy = Gather(me.across_y, dy_in, slot_at(dy_all, 128), (y0, y1), 0)
    oy = Gather(me.across_y, wo_y_at(0, 0, 0, 0, None), wo_y_at, (y0, y1), 1, me.sibling(), (u0, u1))
    kv_task = Gather(me.across_y, kv_own, slot_at(kv, 128), (y0, y1), 2)
    kept = [load(task.own, task.loc(0, 0, 0, 0, None), local.at[i]) for i, task in enumerate((g, q, o, m, d, dy))]

    g.start()
    q.start()
    o.start()
    norm_scale(x, scale)
    g.pair()
    o.pair()
    q.pair()
    for task in (g, o, q):
        task.turn(0)
    for task in (g, o, q):
        task.turn(1)
    m.start()
    d.start()
    for task in (g, o):
        task.last(0)
        task.last(1)
    kept[2].wait()
    oy.start()
    kept[0].wait()
    g.end()

    @pl.loop(0, 16)
    def _(i):
        at = pl.ds(pl.multiple_of(i * 128, 128), 128)
        a1[:, at] = (x[:, at].astype(F32) * scale[...] * gains[i, pl.ds(0, 1), :]).astype(BF)

    q.last(0)
    q.last(1)
    oy.pair()
    kept[1].wait()
    q.end()
    saved = [load(qkv, qkv_out, local.at[6])]

    @pl.loop(0, 4)
    def _(n):
        raw = dot_in(a1[...], qkv[:, pl.ds(pl.multiple_of(512 * n, 512), 512)])
        for i in range(4):
            part = raw[:, 128 * i : 128 * i + 128]
            part = ((part * cosine[...] + turned(part) * sine[...]) .astype(BF).astype(F32) * SCALE).astype(BF)
            for half in (0, 1):
                for e in (0, 1):
                    qst[n, half, pl.ds(64 * (2 * i + e), 64), :] = part[64 * half : 64 * half + 64, 64 * e : 64 * e + 64]

    raw = dot_in(a1[...], qkv[:, pl.ds(2048, 512)])
    for i in range(2):
        part = raw[:, 128 * i : 128 * i + 128]
        kv_own[:, 128 * i : 128 * i + 128] = (part * cosine[...] + turned(part) * sine[...]).astype(BF)
    kv_own[:, 256:] = raw[:, 256:].astype(BF)
    kv_task.start()
    kv[0] = kv_own[...]
    m.pair()
    d.pair()
    kv_task.pair()
    kv_task.turn(0)
    kv_task.turn(1)
    m.turn(0)
    d.turn(0)
    oy.turn(0)
    kv_task.last(0)
    kv_task.last(1)
    kv_task.end()
    dy.start()
    oy.turn(1)

    mate = partner[0]
    beside = kv[mate]
    for out, base in ((kst, 0), (vst, 256)):
        for n in range(4):
            first = base + 64 * n
            for slot in range(8):
                out[n, pl.ds(64 * slot, 64), :] = kv[slot, 0:64, first : first + 64]
            out[n, pl.ds(512, 64), :] = beside[64:128, first : first + 64]
            out[n, pl.ds(576, 64), :] = kv_own[64:128, first : first + 64]

    def attend(n, half):
        count = 512 if half == 0 else 640
        keys = pl.ds(0, count)
        sT[keys] = dot_back(kst[n, keys, :], qst[n, half])
        for i in range(4):
            at = pl.ds(128 * i, 128)
            if half == 0:
                scores = sT[keys, at] + bias_p[...]
                peak = jnp.max(scores, axis=0, keepdims=True)
                raised = jnp.exp(scores - peak)
                total = jnp.sum(raised, axis=0, keepdims=True)
                pT[keys, at] = (raised * (1.0 / total)).astype(BF)
            else:
                first = sT[0:512, at]
                rest = sT[512:640, at] + bias_c[...]
                peak = jnp.maximum(
                    jnp.max(first, axis=0, keepdims=True), jnp.max(rest, axis=0, keepdims=True)
                )
                first = jnp.exp(first - peak)
                rest = jnp.exp(rest - peak)
                total = jnp.sum(first, axis=0, keepdims=True) + jnp.sum(rest, axis=0, keepdims=True)
                pT[0:512, at] = (first * (1.0 / total)).astype(BF)
                pT[512:640, at] = (rest * (1.0 / total)).astype(BF)
            lse[2 * n + half, :, at] = peak + jnp.log(total)
        for i, block in enumerate(unpile(dot_rows(vst[n, keys, :], pT[keys]))):
            first = pl.multiple_of(512 * n + 128 * i, 128)
            att[pl.ds(64 * half, 64), pl.ds(first, 128)] = block.astype(BF)

    @pl.loop(0, 4)
    def _(n):
        attend(n, 0)
        attend(n, 1)

        @pl.when(n == 0)
        def _():
            m.turn(1)
            d.turn(1)
            dy.pair()

        @pl.when(n == 1)
        def _():
            oy.last(0)
            dy.turn(0)

        @pl.when(n == 2)
        def _():
            oy.last(1)
            dy.turn(1)

    o.end()
    oy.end()
    saved.append(load(wo, wo_out, local.at[7]))

    @pl.loop(0, 4)
    def _(n):
        at = pl.ds(pl.multiple_of(512 * n, 512), 512)
        h1[:, at] = x[:, at].astype(F32) + dot_in(att[...], wo[:, :, :, at].reshape(2048, 512))

    norm_scale(h1, scale)

    @pl.loop(0, 16)
    def _(i):
        at = pl.ds(pl.multiple_of(i * 128, 128), 128)
        a2[:, at] = (h1[:, at] * scale[...] * gains[i, pl.ds(8, 1), :]).astype(BF)

    for task in (m, d, dy):
        task.last(0)
        task.last(1)
        task.end()
    for copy in (*kept[3:], *saved):
        copy.wait()


def front(x, gains, qkv, wo, gu, dn, dy, cosine, sine, bias_p, bias_c, partner):
    return pl.pallas_call(
        front_kernel,
        out_shape=(
            jax.ShapeDtypeStruct((16, 16, 128), F32),
            jax.ShapeDtypeStruct((2048, 2560), BF),
            jax.ShapeDtypeStruct((8, 2, 128, 2048), BF),
            jax.ShapeDtypeStruct((2048, 1536), BF),
            jax.ShapeDtypeStruct((704, 2048), BF),
            jax.ShapeDtypeStruct((8, 128, 2048), BF),
            jax.ShapeDtypeStruct((128, 2048), BF),
            jax.ShapeDtypeStruct((4, 2, 512, 64), BF),
            jax.ShapeDtypeStruct((4, 640, 64), BF),
            jax.ShapeDtypeStruct((4, 640, 64), BF),
            jax.ShapeDtypeStruct((128, 2048), BF),
            jax.ShapeDtypeStruct((8, 1, 512), F32),
            jax.ShapeDtypeStruct((128, 2048), F32),
            jax.ShapeDtypeStruct((128, 2048), BF),
        ),
        in_specs=[VMEM] + [ANY] * 6 + [VMEM] * 4 + [pl.BlockSpec(memory_space=pltpu.SMEM)],
        out_specs=[VMEM] + [ANY] * 5 + [VMEM] * 8,
        scratch_shapes=[
            pltpu.VMEM((2048, 2560), BF),
            pltpu.VMEM((8, 2, 128, 2048), BF),
            pltpu.VMEM((128, 512), BF),
            pltpu.VMEM((8, 128, 512), BF),
            pltpu.VMEM((640, 512), F32),
            pltpu.VMEM((640, 512), BF),
            pltpu.VMEM((128, 1), F32),
            *dma_sems(5, 9),
            *dma_sems(5, 10),
            *dma_sems(3, 9),
            *dma_sems(2, 10),
            pltpu.SemaphoreType.DMA((8,)),
        ],
        compiler_params=params(1, 50),
        name="front",
    )(x, gains, qkv, wo, gu, dn, dy, cosine, sine, bias_p, bias_c, partner)


def back_kernel(
    da2, h1, dy, x, gains, wo_in, qkv_in, qst, kst, vst, lse, cosine, sine, bias_p, bias_c, partner,
    a1_in, att_in, mpart_in, gu, dn,
    mixed, tokens_grad, q_out, kv_out, o_out, gains_out, gu_all, dn_all,
    a1s, atts, dqkvs, datts, grow, dh1, gown, gsib, mpart, stream, dost, sT, dT, pT, dsT,
    kgrad, vgrad, kvp, dkv, da1, dnp,
    qp, op, kp, gp, ggot, q_sum, o_sum, kv_sum, g_sum,
    q_half, q_full, q_pair, o_half, o_full, o_pair, k_half, k_full, k_pair, e_half, e_full, e_pair,
    m_half, m_full, m_pair, d_half, d_full, d_pair,
    or_half, or_full, or_pair, qr_half, qr_full, qr_pair, kr_half, kr_full, kr_pair,
    sib0, sib1, x0, x1, y0, y1, ag0, ag1, swap0, swap1, local,
):
    me = Place()
    moved = me.c != me.j
    swapped = {"ctx": me.j, "fsdp": 2 * me.c + me.co}
    barrier = pltpu.get_barrier_semaphore()
    others = near(me.across_x) + near(me.across_y) + [me.sibling()]
    for device in others:
        pl.semaphore_signal(barrier, 1, device_id=device, device_id_type=MESH)

    @pl.when(moved)
    def _():
        pl.semaphore_signal(barrier, 1, device_id=swapped, device_id_type=MESH)

    pl.semaphore_wait(barrier, len(others) + jnp.where(moved, 1, 0))

    dn_move = pltpu.make_async_remote_copy(dn, dnp, swap0, swap1, device_id=swapped, device_id_type=MESH)
    dn_keep = pltpu.make_async_copy(dn, dnp, local.at[0])

    @pl.when(moved)
    def _():
        dn_move.start()

    @pl.when(jnp.logical_not(moved))
    def _():
        dn_keep.start()

    own, other = pl.ds(0, 128), pl.ds(128, 128)
    mload = load(mpart_in, mpart, local.at[1])
    a1load = load(a1_in, a1s.at[own], local.at[2])
    attload = load(att_in, atts.at[own], local.at[3])

    def wo_load(n):
        return pltpu.make_async_copy(
            wo_in.at[pl.ds(512 * n, 512)], stream.at[n % 2, :, pl.ds(0, 2048)], local.at[4 + n % 2]
        )

    def qkv_load(n):
        return pltpu.make_async_copy(qkv_in.at[pl.ds(512 * n, 512)], stream.at[n % 2], local.at[4 + n % 2])

    wo_load(0).start()
    wo_load(1).start()

    over_x, over_y, over_ag = (x0, x1), (y0, y1), (ag0, ag1)
    o_job = Scatter(me.across_x, lambda slot: op.at[slot], 128, o_half, o_full, o_pair, over_x, 0)
    q_job = Scatter(me.across_x, lambda slot: qp.at[slot], 128, q_half, q_full, q_pair, over_x, 1)
    k_job = Scatter(me.across_x, lambda slot: kp.at[slot], 128, k_half, k_full, k_pair, over_x, 2)
    e_job = Scatter(me.across_x, lambda slot: gp.at[slot], 16, e_half, e_full, e_pair, over_x, 3)
    m_job = Scatter(me.across_y, lambda slot: mpart.at[slot], 128, m_half, m_full, m_pair, over_y, 0)
    d_job = Scatter(me.across_y, lambda slot: kvp.at[slot], 128, d_half, d_full, d_pair, over_y, 1)

    def at_ctx(ref):
        def loc(dr, dp, er, ep, half):
            return ref.at[me.ctx_at(dr, dp), row_half(half, ref.shape[1])]

        return loc

    def dn_at(dr, dp, er, ep, half):
        first = pl.multiple_of(me.ctx_at(dr, dp) * 256, 256)
        return dn_all.at[row_half(half, 352), pl.ds(first, 256)]

    gu_task = Gather(me.across_y, gu, at_ctx(gu_all), over_ag, 0)
    dn_task = Gather(me.across_y, dnp, dn_at, over_ag, 1)
    e_task = Gather(me.across_y, g_sum, at_ctx(ggot), over_ag, 2)

    def sum_over_ctx(total, columns, halves, fulls, paired, row):
        def part(slot):
            first = pl.multiple_of(me.ctx_at(STEPS[slot], PAIRS[slot]) * 16, 16)
            return total.at[pl.ds(first, 16)]

        return Scatter(me.across_y, part, 16, halves, fulls, paired, over_y, row, cut=columns)

    def spread(out, columns, row):
        def loc(dr, dp, er, ep, half):
            first = pl.multiple_of(me.ctx_at(dr, dp) * 16, 16)
            if half is None:
                return out.at[pl.ds(first, 16)]
            return out.at[pl.ds(first, 16), pl.ds(half * (columns // 2), columns // 2)]

        return Gather(me.across_y, loc(0, 0, 0, 0, None), loc, over_ag, row)

    o_sums = sum_over_ctx(o_sum, 2048, or_half, or_full, or_pair, 2)
    q_sums = sum_over_ctx(q_sum, 2048, qr_half, qr_full, qr_pair, 3)
    kv_sums = sum_over_ctx(kv_sum, 512, kr_half, kr_full, kr_pair, 4)
    o_spread = spread(o_out, 2048, 3)
    q_spread = spread(q_out, 2048, 4)
    kv_spread = spread(kv_out, 512, 5)
    own_rows = pl.ds(pl.multiple_of(me.c * 16, 16), 16)

    swap = lambda src, dst, index: send(src, dst, (sib0, sib1), index, me.sibling())
    att_swap = swap(atts.at[own], atts.at[other], 0)
    datt_swap = swap(datts.at[own], datts.at[other], 1)
    a1_swap = swap(a1s.at[own], a1s.at[other], 2)
    queries = pl.ds(0, 2048)
    dq_swap = swap(dqkvs.at[own, queries], dqkvs.at[other, queries], 3)
    rest = pl.ds(2048, 512)
    dkv_swap = swap(dqkvs.at[own, rest], dqkvs.at[other, rest], 4)
    gain_swap = swap(gown, gsib, 5)

    attload.wait()
    att_swap.start()
    a1load.wait()
    a1_swap.start()
    mload.wait()
    m_job.start()

    gown[...] = jnp.zeros((16, 16, 128), F32)
    for i in range(16):
        grow[0, :, 128 * i : 128 * i + 128] = gains[i, 0:1, :]
        grow[1, :, 128 * i : 128 * i + 128] = gains[i, 8:9, :]
    grow[2] = jnp.zeros((1, 2048), F32)
    grow[3] = jnp.zeros((1, 2048), F32)

    @pl.loop(0, 8)
    def _(i):
        at = pl.ds(pl.multiple_of(16 * i, 16), 16)
        values, grad = h1[at], da2[at]
        scale = lax.rsqrt(jnp.mean(values * values, axis=1, keepdims=True) + EPS)
        grow[3] += jnp.sum(grad * values * scale, axis=0, keepdims=True)
        grad = grad * grow[1]
        level = jnp.mean(grad * values, axis=1, keepdims=True) * scale * scale * scale
        total = dy[at].astype(F32) + scale * grad - values * level
        dh1[at] = total
        datts[at] = total.astype(BF)

    datt_swap.start()
    for n in range(4):
        wo_load(n).wait()
        part = dot_back(datts[own], stream[n % 2, :, 0:2048]).astype(BF)
        for half in (0, 1):
            pile(dost.at[n, half], part, half)
        if n < 2:
            wo_load(n + 2).start()
    qkv_load(0).start()
    qkv_load(1).start()

    def chip_of(t):
        dr = jnp.where(t < 2, 0, jnp.where(t >= 6, 2, 1 + 2 * lax.rem(t, 2)))
        dp = jnp.where(t < 2, t, jnp.where(t >= 6, t - 6, lax.div(t, 4)))
        return lax.rem(me.x + dr, 4) * 2 + lax.rem(me.zh + dp, 2)

    def terms(left, right, out):
        @pl.loop(0, 8)
        def _(i):
            t = 7 - i
            first = pl.multiple_of((chip_of(t) * 2 + me.co) * 128, 128)
            out[t] = dot_rows(left[:, pl.ds(first, 128)], right).astype(BF)

    att_swap.wait_recv()
    datt_swap.wait_recv()
    terms(atts, datts[...], op)
    o_job.start()
    m_job.turn(1)
    m_job.turn(0)

    def attend(n, half):
        count = 512 if half == 0 else 640
        keys = pl.ds(0, count)
        key, query, out = kst[n, keys, :], qst[n, half], dost[n, half]
        sT[keys] = dot_back(key, query)
        dT[keys] = dot_back(vst[n, keys, :], out)
        for i in range(4):
            at = pl.ds(128 * i, 128)
            parts = []
            for first, size in ((0, 512), (512, 128))[: 1 + half]:
                scores = sT[first : first + size, at]
                if half == 0:
                    scores = scores + bias_p[...]
                elif first:
                    scores = scores + bias_c[...]
                probs = jnp.exp(scores - lse[2 * n + half, :, at])
                grad = dT[first : first + size, at]
                parts.append((first, size, probs, grad))
            level = sum(jnp.sum(probs * grad, axis=0, keepdims=True) for _, _, probs, grad in parts)
            for first, size, probs, grad in parts:
                pT[first : first + size, at] = probs.astype(BF)
                dsT[first : first + size, at] = (probs * (grad - level)).astype(BF)
        rows = slice(64 * half, 64 * half + 64)
        for i, block in enumerate(unpile(dot_rows(key, dsT[keys]) * SCALE)):
            block = block * cosine[rows] - turned(block) * sine[rows]
            first = pl.multiple_of(512 * n + 128 * i, 128)
            dqkvs[rows, pl.ds(first, 128)] = block.astype(BF)
        return dot_in(dsT[keys], query), dot_in(pT[keys], out)

    @pl.loop(0, 4)
    def _(n):
        key_one, value_one = attend(n, 0)
        key_two, value_two = attend(n, 1)
        for out, one, two in ((kgrad, key_one, key_two), (vgrad, value_one, value_two)):
            out[n, 0:512] = (one + two[0:512]).astype(BF)
            out[n, 512:640] = two[512:640].astype(BF)

        @pl.when(n == 0)
        def _():
            o_job.turn(1)
            o_job.turn(0)

        @pl.when(n == 1)
        def _():
            m_job.pair()

        @pl.when(n == 2)
        def _():
            o_job.pair()

    dq_swap.start()
    mate = partner[0]
    for out, base in ((kgrad, 0), (vgrad, 256)):
        for n in range(4):
            first = base + 64 * n
            for slot in range(8):
                kvp[slot, 0:64, first : first + 64] = out[n, 64 * slot : 64 * slot + 64, :]
                if slot == 0:
                    late = out[n, 576:640, :]
                else:
                    late = jnp.where(mate == slot, out[n, 512:576, :], jnp.zeros((64, 64), BF))
                kvp[slot, 64:128, first : first + 64] = late
    d_job.start()
    a1_swap.wait_recv()
    dq_swap.wait_recv()
    terms(a1s, dqkvs[:, 0:2048], qp)
    q_job.start()
    d_job.turn(1)
    d_job.turn(0)
    m_job.finish(mixed, (h1,))
    o_job.finish(o_sum)
    d_job.pair()
    d_job.finish(dkv)
    for i in range(2):
        at = slice(128 * i, 128 * i + 128)
        block = dkv[:, at]
        dqkvs[own, 2048 + 128 * i : 2176 + 128 * i] = (block * cosine[...] - turned(block) * sine[...]).astype(BF)
    dqkvs[own, 2304:2560] = dkv[:, 256:512].astype(BF)
    dkv_swap.start()
    o_sums.start()
    kept = [load(gu, gu_all.at[me.c], local.at[6])]
    gu_task.start()

    @pl.when(moved)
    def _():
        dn_move.wait()

    @pl.when(jnp.logical_not(moved))
    def _():
        dn_keep.wait()

    dn_task.start()
    kept.append(load(dnp, dn_at(0, 0, 0, 0, None), local.at[7]))
    dkv_swap.wait_recv()
    terms(a1s, dqkvs[:, 2048:2560], kp)
    k_job.start()
    q_job.turn(1)
    q_job.turn(0)

    for n in range(4):
        qkv_load(n).wait()
        da1[:, 512 * n : 512 * n + 512] = dot_back(dqkvs[own], stream[n % 2])
        if n < 2:
            qkv_load(n + 2).start()

    @pl.loop(0, 8)
    def _(i):
        at = pl.ds(pl.multiple_of(16 * i, 16), 16)
        values, grad = x[at].astype(F32), da1[at]
        scale = lax.rsqrt(jnp.mean(values * values, axis=1, keepdims=True) + EPS)
        grow[2] += jnp.sum(grad * values * scale, axis=0, keepdims=True)
        grad = grad * grow[0]
        level = jnp.mean(grad * values, axis=1, keepdims=True) * scale * scale * scale
        tokens_grad[at] = (dh1[at] + scale * grad - values * level).astype(BF)

    for i in range(16):
        gown[i, 0:1, :] = grow[2, :, 128 * i : 128 * i + 128]
        gown[i, 8:9, :] = grow[3, :, 128 * i : 128 * i + 128]
    gain_swap.start()
    o_sums.turn(1)
    o_sums.turn(0)
    gain_swap.wait_recv()
    for slot in range(8):
        block = me.fsdp_at(STEPS[slot], PAIRS[slot])
        gp[slot] = gown[block] + gsib[block]
    e_job.start()
    gu_task.pair()
    dn_task.pair()
    o_sums.pair()
    o_sums.finish(o_out.at[own_rows])
    o_spread.start()
    gu_task.turn(0)
    dn_task.turn(0)
    k_job.turn(1)
    k_job.turn(0)
    q_job.pair()
    e_job.turn(1)
    e_job.turn(0)
    gu_task.turn(1)
    dn_task.turn(1)
    o_spread.pair()
    o_spread.turn(0)
    o_spread.turn(1)
    k_job.pair()
    e_job.pair()
    q_job.finish(q_sum)
    q_sums.start()
    k_job.finish(kv_sum)
    kv_sums.start()
    e_job.finish(g_sum)
    e_task.start()
    ggot[me.c] = g_sum[...]
    for job in (q_sums, kv_sums):
        job.turn(1)
        job.turn(0)
    e_task.pair()
    e_task.turn(0)
    e_task.turn(1)
    for job, out, task in ((q_sums, q_out, q_spread), (kv_sums, kv_out, kv_spread)):
        job.pair()
        job.finish(out.at[own_rows])
        task.start()
    for task in (q_spread, kv_spread):
        task.pair()
    for task in (q_spread, kv_spread):
        task.turn(0)
        task.turn(1)
    e_task.last(0)
    e_task.last(1)
    total = ggot[0]
    for index in range(1, 8):
        total = total + ggot[index]
    gains_out[...] = total
    for task in (gu_task, dn_task, o_spread, q_spread, kv_spread):
        task.last(0)
        task.last(1)
    jobs = (o_job, q_job, k_job, e_job, m_job, d_job, o_sums, q_sums, kv_sums)
    for job in (*jobs, gu_task, dn_task, e_task, o_spread, q_spread, kv_spread):
        job.end()
    for copy in (att_swap, datt_swap, a1_swap, dq_swap, dkv_swap, gain_swap):
        copy.wait_send()
    for copy in kept:
        copy.wait()


def back(da2, h1, dy, x, gains, wo, qkv, qst, kst, vst, lse, cosine, sine, bias_p, bias_c, partner, a1, att, mpart, gu, dn):
    scratch = [
        pltpu.VMEM((256, 2048), BF),
        pltpu.VMEM((256, 2048), BF),
        pltpu.VMEM((256, 2560), BF),
        pltpu.VMEM((256, 2048), BF),
        pltpu.VMEM((4, 1, 2048), F32),
        pltpu.VMEM((128, 2048), F32),
        pltpu.VMEM((16, 16, 128), F32),
        pltpu.VMEM((16, 16, 128), F32),
        pltpu.VMEM((8, 128, 2048), BF),
        pltpu.VMEM((2, 512, 2560), BF),
        pltpu.VMEM((4, 2, 512, 64), BF),
        pltpu.VMEM((640, 512), F32),
        pltpu.VMEM((640, 512), F32),
        pltpu.VMEM((640, 512), BF),
        pltpu.VMEM((640, 512), BF),
        pltpu.VMEM((4, 640, 64), BF),
        pltpu.VMEM((4, 640, 64), BF),
        pltpu.VMEM((8, 128, 512), BF),
        pltpu.VMEM((128, 512), F32),
        pltpu.VMEM((128, 2048), F32),
        pltpu.VMEM((352, 256), BF),
        pltpu.VMEM((8, 128, 2048), BF),
        pltpu.VMEM((8, 128, 2048), BF),
        pltpu.VMEM((8, 128, 512), BF),
        pltpu.VMEM((8, 16, 128), F32),
        pltpu.VMEM((8, 16, 128), F32),
        pltpu.VMEM((128, 2048), BF),
        pltpu.VMEM((128, 2048), BF),
        pltpu.VMEM((128, 512), BF),
        pltpu.VMEM((16, 128), F32),
        *scatter_buffers(128, 2048),
        *scatter_buffers(128, 2048),
        *scatter_buffers(128, 512),
        *scatter_buffers(16, 128, F32),
        *scatter_buffers(128, 2048),
        *scatter_buffers(128, 512),
        *scatter_buffers(16, 2048, cut=True),
        *scatter_buffers(16, 2048, cut=True),
        *scatter_buffers(16, 512, cut=True),
        pltpu.SemaphoreType.DMA((6,)),
        pltpu.SemaphoreType.DMA((6,)),
        *dma_sems(4, 9),
        *dma_sems(5, 9),
        *dma_sems(6, 9),
        pltpu.SemaphoreType.DMA,
        pltpu.SemaphoreType.DMA,
        pltpu.SemaphoreType.DMA((8,)),
    ]
    return pl.pallas_call(
        back_kernel,
        out_shape=(
            jax.ShapeDtypeStruct((128, 2048), BF),
            jax.ShapeDtypeStruct((128, 2048), BF),
            jax.ShapeDtypeStruct((128, 2048), BF),
            jax.ShapeDtypeStruct((128, 512), BF),
            jax.ShapeDtypeStruct((128, 2048), BF),
            jax.ShapeDtypeStruct((16, 128), F32),
            jax.ShapeDtypeStruct((8, 128, 1536), BF),
            jax.ShapeDtypeStruct((352, 2048), BF),
        ),
        in_specs=[VMEM] * 5 + [ANY] * 2 + [VMEM] * 8 + [pl.BlockSpec(memory_space=pltpu.SMEM)] + [ANY] * 5,
        out_specs=[VMEM] * 6 + [ANY] * 2,
        scratch_shapes=scratch,
        compiler_params=params(5, 62),
        name="back",
    )(da2, h1, dy, x, gains, wo, qkv, qst, kst, vst, lse, cosine, sine, bias_p, bias_c, partner, a1, att, mpart, gu, dn)


def tables(position):
    freq = BASE ** (-(jnp.arange(HEAD_DIM // 2, dtype=jnp.float32) * 2.0) / HEAD_DIM)
    angle = position.astype(jnp.float32)[:, None] * freq[None, :]
    angle = jnp.concatenate([angle, angle], axis=-1)
    return (jnp.cos(angle), jnp.sin(angle))


def timeline(table_flat, total_len, row_count):
    everywhere = jnp.arange(total_len, dtype=jnp.int32)
    half_len = row_count // 2
    moment = jnp.repeat(table_flat, half_len) * half_len + everywhere % half_len
    prompt_len = total_len // 2
    cont_len = total_len // 8
    later = moment >= prompt_len
    segment = jnp.where(later, 1 + (moment - prompt_len) // cont_len, 0)
    position = jnp.where(later, prompt_len + (moment - prompt_len) % cont_len, moment)
    return (segment, position)


def swap_pairs():
    pairs = []
    for c in range(8):
        for f in range(16):
            pairs.append((c * 16 + f, (f // 2) * 16 + 2 * c + f % 2))
    return pairs


def on_device(
    tokens,
    block_deal,
    attn_gain,
    query_weight,
    key_weight,
    value_weight,
    output_weight,
    mlp_gain,
    gate_weight,
    up_weight,
    down_weight,
    cotangent,
):
    row_count = tokens.shape[1]
    c = lax.axis_index("ctx")
    f = lax.axis_index("fsdp")
    full_len = row_count * 8

    def sliced(weight):
        return jnp.pad(lax.dynamic_slice_in_dim(weight, c * 704, 704, 1), ((0, 0), (0, 64)))

    none = jnp.zeros((7, 128), F32)
    gains = jnp.concatenate([attn_gain.astype(F32)[None], none, mlp_gain.astype(F32)[None], none])
    qkv = jnp.concatenate([query_weight, key_weight, value_weight], axis=1)
    gu = jnp.concatenate([sliced(gate_weight), sliced(up_weight)], axis=1)
    dn = lax.dynamic_slice_in_dim(down_weight, c * 256, 256, 1)
    dn = lax.ppermute(dn, ("ctx", "fsdp"), swap_pairs())

    y, zl = c // 2, c % 2
    order = jnp.stack([((y + STEPS[s]) % 4) * 2 + (zl + PAIRS[s]) % 2 for s in range(8)])
    deal = jnp.take(lax.dynamic_index_in_dim(block_deal, f, 0, keepdims=False), order, axis=0)
    mate_block = 8 + (deal[0, 1] - 8 + 1 - 2 * ((deal[0, 1] - 8) % 2))
    mate = jnp.argmax((deal[:, 1] == mate_block).astype(jnp.int32)).astype(jnp.int32)
    segment, position = timeline(deal.reshape(-1), full_len, row_count)
    own_segment, own_position = segment[:row_count], position[:row_count]
    cosine, sine = tables(own_position)
    sign = jnp.where(jnp.arange(HEAD_DIM) < 32, -1.0, 1.0)
    cosine_two = jnp.concatenate([cosine, cosine], axis=1)
    sine_two = jnp.concatenate([sine * sign, sine * sign], axis=1)
    prompt_position = position.reshape(8, 2, 64)[:, 0].reshape(512)
    bias_p = jnp.where(prompt_position[:, None] <= own_position[None, :64], 0.0, -1e30)
    mate_seen = deal[0, 1] > mate_block
    step = jnp.arange(64)
    bias_c = jnp.concatenate(
        [
            jnp.broadcast_to(jnp.where(mate_seen, 0.0, -1e30), (64, 64)),
            jnp.where(step[:, None] <= step[None, :], 0.0, -1e30),
        ]
    )
    bias_p = jnp.concatenate([bias_p, bias_p], axis=1).astype(F32)
    bias_c = jnp.concatenate([bias_c, bias_c], axis=1).astype(F32)

    gains_all, qkv_all, wo_all, gu_all, dn_all, dy_all, normed, qst, kst, vst, attended, lse, hidden_state, normed_two = front(
        tokens[0], gains, qkv, output_weight, gu, dn, cotangent[0], cosine_two, sine_two, bias_p, bias_c, mate[None]
    )
    wo_all = wo_all.reshape(2048, 2048)

    grad_normed_two, mixed_parts, gu_sum, dn_sum = feed_forward(normed_two, gu_all, dn_all, dy_all)

    mixed, tokens_grad, query_grad, kv_grad, o_grad, gain_grads, gu_grads, dn_grad = back(
        grad_normed_two, hidden_state, cotangent[0], tokens[0], gains_all, wo_all, qkv_all, qst, kst, vst, lse,
        cosine_two, sine_two, bias_p, bias_c, mate[None], normed, attended, mixed_parts, gu_sum, dn_sum,
    )

    def joined(parts):
        return parts.transpose(1, 0, 2).reshape(parts.shape[1], -1).astype(F32)

    return (
        mixed[None],
        tokens_grad[None],
        gain_grads[0],
        query_grad.astype(F32),
        kv_grad[:, :256].astype(F32),
        kv_grad[:, 256:].astype(F32),
        o_grad.astype(F32),
        gain_grads[8],
        joined(gu_grads[:, :, :704]),
        joined(gu_grads[:, :, 768:1472]),
        dn_grad.astype(F32),
    )


def solution(mesh):
    held = P("fsdp", "ctx", None)
    rows = P("fsdp", None)
    return jax.shard_map(
        on_device,
        mesh=mesh,
        in_specs=(held, P(), P("fsdp"), rows, rows, rows, rows, P("fsdp"), rows, rows, rows, held),
        out_specs=(held, held, P("fsdp"), rows, rows, rows, rows, P("fsdp"), rows, rows, rows),
        check_vma=False,
    )
```

```python
import functools

import jax
import jax.numpy as jnp
from jax import lax
from jax.experimental import pallas as pl
from jax.experimental.pallas import tpu as pltpu
from jax.sharding import PartitionSpec as P

MESH = pl.DeviceIdType.MESH
BF = jnp.bfloat16
F32 = jnp.float32
ANY = pl.BlockSpec(memory_space=pl.ANY)
VMEM = pl.BlockSpec(memory_space=pltpu.VMEM)

HEAD_DIM = 64
EPS = 1e-05
SCALE = 0.125
BASE = 10000.0

SLOT = {(0, 0): 0, (0, 1): 1, (1, 0): 2, (3, 0): 3, (1, 1): 4, (3, 1): 5, (2, 0): 6, (2, 1): 7}
STEPS = (0, 0, 1, 3, 1, 3, 2, 2)
PAIRS = (0, 1, 0, 0, 1, 1, 0, 1)


def slot_of(dr, dp):
    return SLOT[(dr % 4, dp % 2)]


class Place:
    def __init__(self):
        self.c = lax.axis_index("ctx")
        self.f = lax.axis_index("fsdp")
        self.y, self.zl = lax.div(self.c, 2), lax.rem(self.c, 2)
        self.j, self.co = lax.div(self.f, 2), lax.rem(self.f, 2)
        self.x, self.zh = lax.div(self.j, 2), lax.rem(self.j, 2)

    def ctx_at(self, dr, dp):
        return lax.rem(self.y + dr % 4, 4) * 2 + lax.rem(self.zl + dp, 2)

    def chip_at(self, dr, dp):
        return lax.rem(self.x + dr % 4, 4) * 2 + lax.rem(self.zh + dp, 2)

    def fsdp_at(self, dr, dp):
        return self.chip_at(dr, dp) * 2 + self.co

    def across_y(self, dr, dp):
        return {"ctx": self.ctx_at(dr, dp), "fsdp": self.f}

    def across_x(self, dr, dp):
        return {"ctx": self.c, "fsdp": self.fsdp_at(dr, dp)}

    def sibling(self):
        return {"ctx": self.c, "fsdp": self.f + 1 - 2 * self.co}


def chip_of(me, t):
    dr = jnp.where(t < 2, 0, jnp.where(t >= 6, 2, 1 + 2 * lax.rem(t, 2)))
    dp = jnp.where(t < 2, t, jnp.where(t >= 6, t - 6, lax.div(t, 4)))
    return lax.rem(me.x + dr, 4) * 2 + lax.rem(me.zh + dp, 2)


def greet(devices):
    barrier = pltpu.get_barrier_semaphore()
    for device in devices:
        pl.semaphore_signal(barrier, 1, device_id=device, device_id_type=MESH)
    pl.semaphore_wait(barrier, len(devices))


class Swap:
    def __init__(self, me, src, dst, sems, local):
        self.moved = me.c != me.j
        self.to = {"ctx": me.j, "fsdp": 2 * me.c + me.co}
        self.copy = pltpu.make_async_remote_copy(
            src, dst, sems[0], sems[1], device_id=self.to, device_id_type=MESH
        )
        self.keep = pltpu.make_async_copy(src, dst, local)

    def start(self):
        pl.when(self.moved)(self.copy.start)
        pl.when(jnp.logical_not(self.moved))(self.keep.start)

    def wait(self):
        pl.when(self.moved)(self.copy.wait)
        pl.when(jnp.logical_not(self.moved))(self.keep.wait)


def greet_all(me):
    barrier = pltpu.get_barrier_semaphore()
    others = near(me.across_x) + near(me.across_y) + [me.sibling()]
    for device in others:
        pl.semaphore_signal(barrier, 1, device_id=device, device_id_type=MESH)
    moved = me.c != me.j

    @pl.when(moved)
    def _():
        to = {"ctx": me.j, "fsdp": 2 * me.c + me.co}
        pl.semaphore_signal(barrier, 1, device_id=to, device_id_type=MESH)

    pl.semaphore_wait(barrier, len(others) + jnp.where(moved, 1, 0))


def near(dev):
    return [dev(1, 0), dev(-1, 0), dev(0, 1)]


def send(src, dst, sems, index, device):
    return pltpu.make_async_remote_copy(
        src, dst, sems[0].at[index], sems[1].at[index], device_id=device, device_id_type=MESH
    )


class Gather:
    MOVES = (
        ((0, 0), (0, 1), None),
        ((0, 0), (1, 0), None),
        ((0, 0), (-1, 0), None),
        ((0, 1), (1, 0), None),
        ((0, 1), (-1, 0), None),
        ((-1, 0), (1, 0), 0),
        ((-1, 1), (1, 0), 0),
        ((1, 0), (-1, 0), 1),
        ((1, 1), (-1, 0), 1),
    )

    def __init__(self, dev, own, loc, sems, row, sibling=None, sibling_sems=None):
        self.loc = loc
        self.copies = []
        for index, (block, to, half) in enumerate(self.MOVES):
            src = own if block == (0, 0) else loc(*block, 0, 0, half)
            dst = loc(*block, *to, half)
            self.copies.append(send(src, dst, sems, (row, index), dev(*to)))
        self.passed = {}
        if sibling is not None:
            self.passed[9] = send(own, loc(0, 0, 0, 0, None), sibling_sems, (row, 9), sibling)
            for index, ((dr, dp), (er, ep), half) in enumerate(self.MOVES):
                ref = loc(dr - er, dp + ep, 0, 0, half)
                self.passed[index] = send(ref, ref, sibling_sems, (row, index), sibling)
        self.own = own

    def _pass(self, index):
        if self.passed:
            self.passed[index].start()

    def _got(self, index):
        self.copies[index].wait_recv()
        self._pass(index)

    def start(self):
        for index in (0, 1, 2):
            self.copies[index].start()
        self._pass(9)

    def pair(self):
        self._got(0)
        self.copies[3].start()
        self.copies[4].start()

    def turn(self, dp):
        for got, on in (((1, 5), (2, 7)) if dp == 0 else ((3, 6), (4, 8))):
            self._got(got)
            self.copies[on].start()

    def last(self, dp):
        for got in ((5, 7) if dp == 0 else (6, 8)):
            self._got(got)

    def end(self):
        for copy in self.copies:
            copy.wait_send()
        for copy in self.passed.values():
            copy.wait()

    def all(self):
        self.start()
        self.pair()
        self.turn(0)
        self.turn(1)
        self.last(0)
        self.last(1)
        self.end()


def row_half(half, rows):
    return pl.ds(0, rows) if half is None else pl.ds(half * (rows // 2), rows // 2)


def add_into(ref, rows, others, step=16):
    step = min(step, rows)

    @pl.loop(0, rows // step)
    def _(i):
        at = pl.ds(pl.multiple_of(i * step, step), step)
        total = ref[at].astype(F32)
        for other in others:
            total = total + other[at].astype(F32)
        ref[at] = total.astype(ref.dtype)


class Scatter:
    def __init__(self, dev, part, rows, halves, fulls, paired, sems, row, cut=None):
        self.part, self.rows, self.cut = part, rows, cut
        self.halves, self.fulls, self.paired = halves, fulls, paired
        self.first, self.second = {}, {}
        for dp in (0, 1):
            for way, sign in ((0, 1), (1, -1)):
                self.first[way, dp] = send(
                    self._half(part(slot_of(2, dp)), way), halves.at[way, dp], sems, (row, way * 2 + dp), dev(sign, 0)
                )
                self.second[way, dp] = send(
                    part(slot_of(sign, dp)), fulls.at[way, dp], sems, (row, 4 + way * 2 + dp), dev(sign, 0)
                )
        self.third = send(part(slot_of(0, 1)), paired, sems, (row, 8), dev(0, 1))

    def _half(self, ref, way):
        if self.cut is None:
            return ref.at[pl.ds(way * (self.rows // 2), self.rows // 2)]
        return ref.at[:, pl.ds(way * (self.cut // 2), self.cut // 2)]

    def start(self):
        for dp in (1, 0):
            for way in (0, 1):
                self.first[way, dp].start()

    def turn(self, dp):
        for way, sign in ((0, 1), (1, -1)):
            self.first[way, dp].wait_recv()
            block = self._half(self.part(slot_of(sign, dp)), way)
            add_into(block, block.shape[0], [self.halves.at[way, dp]])
            self.second[way, dp].start()

    def pair(self):
        for way in (0, 1):
            self.second[way, 1].wait_recv()
        add_into(self.part(slot_of(0, 1)), self.rows, [self.fulls.at[0, 1], self.fulls.at[1, 1]])
        self.third.start()

    def finish(self, out, extra=()):
        for way in (0, 1):
            self.second[way, 0].wait_recv()
        self.third.wait_recv()
        own = self.part(0)
        terms = [own, self.fulls.at[0, 0], self.fulls.at[1, 0], self.paired, *extra]

        @pl.loop(0, self.rows // 16)
        def _(i):
            at = pl.ds(pl.multiple_of(i * 16, 16), 16)
            total = terms[0][at].astype(F32)
            for term in terms[1:]:
                total = total + term[at].astype(F32)
            out[at] = total.astype(out.dtype)

    def end(self):
        for copy in (*self.first.values(), *self.second.values(), self.third):
            copy.wait_send()


def scatter_buffers(rows, columns, dtype=BF, cut=False):
    half = (rows, columns // 2) if cut else (rows // 2, columns)
    return [
        pltpu.VMEM((2, 2, *half), dtype),
        pltpu.VMEM((2, 2, rows, columns), dtype),
        pltpu.VMEM((rows, columns), dtype),
    ]


def dma_sems(rows, count):
    return [pltpu.SemaphoreType.DMA((rows, count)), pltpu.SemaphoreType.DMA((rows, count))]


def params(collective_id, vmem=56):
    return pltpu.CompilerParams(
        collective_id=collective_id, has_side_effects=True, vmem_limit_bytes=vmem << 20
    )


def dot_in(left, right):
    return jnp.dot(left, right, preferred_element_type=F32)


def dot_back(left, right):
    return lax.dot_general(left, right, (((1,), (1,)), ((), ())), preferred_element_type=F32)


def dot_rows(left, right):
    return lax.dot_general(left, right, (((0,), (0,)), ((), ())), preferred_element_type=F32)


def mlp_kernel(
    a2, gu_in, dn_in, dy_in,
    da2_out, mpart, gu_out, gdown,
    acts, gu, wd, dy, hid, dgu, dpart,
    d_half, d_full, d_pair,
    gsib, grecv, gown, gd, gdrecv,
    g_half, g_full, g_pair,
    ag0, ag1, rs0, rs1, sib0, sib1, local,
):
    me = Place()
    greet(near(me.across_x) + near(me.across_y) + [me.sibling()])

    def acts_at(dr, dp, er, ep, half):
        return acts.at[slot_of(dr - er, dp + ep), row_half(half, 128)]

    task = Gather(me.across_y, a2, acts_at, (ag0, ag1), 0)
    task.start()
    loads = [
        pltpu.make_async_copy(gu_in, gu, local.at[0]),
        pltpu.make_async_copy(dn_in, wd.at[pl.ds(0, 704)], local.at[1]),
        pltpu.make_async_copy(dy_in, dy, local.at[2]),
    ]
    for load in loads:
        load.start()
    acts[0] = a2[...]
    wd[pl.ds(704, 64)] = jnp.zeros((64, 2048), BF)
    for load in loads:
        load.wait()

    def group(g):
        at = pl.ds(2 * g, 2)
        rows = pl.ds(pl.multiple_of(256 * g, 256), 256)
        for h in range(3):
            first, second = pl.ds(256 * h, 256), pl.ds(768 + 256 * h, 256)
            here = acts[at].reshape(256, 2048)
            gate = dot_in(here, gu[:, first])
            up = dot_in(here, gu[:, second])
            back = dot_back(dy[at].reshape(256, 2048), wd[first, :])
            curve = 1.0 / (1.0 + jnp.exp(-gate))
            silu = gate * curve
            hid[rows, first] = (silu * up).astype(BF)
            dgu[rows, first] = (back * up * (curve + silu * (1.0 - curve))).astype(BF)
            dgu[rows, second] = (back * silu).astype(BF)
        for n in range(4):
            wide = pl.ds(512 * n, 512)
            mpart[at, :, wide] = dot_in(hid[rows, :], wd[:, wide]).astype(BF).reshape(2, 128, 512)
            dpart[at, :, wide] = dot_back(dgu[rows, :], gu[wide, :]).astype(BF).reshape(2, 128, 512)

    @pl.loop(0, 4)
    def _(g):
        @pl.when(g == 0)
        def _():
            task.pair()

        @pl.when(g == 1)
        def _():
            task.turn(0)

        @pl.when(g == 2)
        def _():
            task.turn(1)

        @pl.when(g == 3)
        def _():
            task.last(0)
            task.last(1)

        group(g)

    grad = Scatter(me.across_y, lambda slot: dpart.at[slot], 128, d_half, d_full, d_pair, (rs0, rs1), 0)
    first = Scatter(me.across_x, lambda slot: gown.at[slot], 128, g_half, g_full, g_pair, (rs0, rs1), 1)
    grad.start()

    def weight_terms(t, core):
        at = pl.multiple_of((chip_of(me, t) * 2 + core) * 128, 128)
        left = acts[:, :, pl.ds(at, 128)].reshape(1024, 128)
        return dot_rows(left, dgu[...])

    def gu_to(t):
        return send(gsib.at[t], grecv.at[t], (sib0, sib1), 8 + t, me.sibling())

    @pl.loop(0, 8)
    def _(i):
        gsib[7 - i] = weight_terms(7 - i, 1 - me.co).astype(BF)
        gu_to(7 - i).start()

    grad.turn(1)

    @pl.loop(0, 8)
    def _(i):
        gu_to(7 - i).wait_recv()
        gown[7 - i] = (weight_terms(7 - i, me.co) + grecv[7 - i].astype(F32)).astype(BF)

        @pl.when(i == 1)
        def _():
            first.start()

    grad.turn(0)
    first.turn(1)

    def down_to(t):
        mine = pl.ds(pl.multiple_of((1 - me.co) * 352, 16), 352)
        return send(gd.at[t, mine], gdrecv.at[t], (sib0, sib1), t, me.sibling())

    @pl.loop(0, 8)
    def _(t):
        at = pl.multiple_of(chip_of(me, t) * 256, 256)
        gd[t] = dot_rows(hid[...], dy[:, :, pl.ds(at, 256)].reshape(1024, 256)).astype(BF)
        down_to(t).start()

    first.turn(0)
    grad.pair()
    first.pair()

    @pl.loop(0, 8)
    def _(t):
        down_to(t).wait_recv()

        @pl.loop(0, 22)
        def _(i):
            mine = gd[t, pl.ds(pl.multiple_of(me.co * 352 + i * 16, 16), 16)].astype(F32)
            at = pl.ds(pl.multiple_of(i * 16, 16), 16)
            gdown[t, at] = (mine + gdrecv[t, at].astype(F32)).astype(BF)

    first.finish(gu_out)
    grad.finish(da2_out)
    for job in (task, grad, first):
        job.end()

    @pl.loop(0, 8)
    def _(t):
        gu_to(t).wait_send()
        down_to(t).wait_send()


def feed_forward(a2, gu, dn, dy):
    scratch = [
        pltpu.VMEM((8, 128, 2048), BF),
        pltpu.VMEM((2048, 1536), BF),
        pltpu.VMEM((768, 2048), BF),
        pltpu.VMEM((8, 128, 2048), BF),
        pltpu.VMEM((1024, 768), BF),
        pltpu.VMEM((1024, 1536), BF),
        pltpu.VMEM((8, 128, 2048), BF),
        *scatter_buffers(128, 2048),
        pltpu.VMEM((8, 128, 1536), BF),
        pltpu.VMEM((8, 128, 1536), BF),
        pltpu.VMEM((8, 128, 1536), BF),
        pltpu.VMEM((8, 768, 256), BF),
        pltpu.VMEM((8, 352, 256), BF),
        *scatter_buffers(128, 1536),
        *dma_sems(1, 9),
        *dma_sems(2, 9),
        pltpu.SemaphoreType.DMA((16,)),
        pltpu.SemaphoreType.DMA((16,)),
        pltpu.SemaphoreType.DMA((3,)),
    ]
    return pl.pallas_call(
        mlp_kernel,
        out_shape=(
            jax.ShapeDtypeStruct((128, 2048), F32),
            jax.ShapeDtypeStruct((8, 128, 2048), BF),
            jax.ShapeDtypeStruct((128, 1536), BF),
            jax.ShapeDtypeStruct((8, 352, 256), BF),
        ),
        in_specs=[VMEM, ANY, ANY, ANY],
        out_specs=[VMEM] * 4,
        scratch_shapes=scratch,
        compiler_params=params(4, 62),
        name="feed_forward",
    )(a2, gu, dn, dy)


def load(src, dst, sem):
    copy = pltpu.make_async_copy(src, dst, sem)
    copy.start()
    return copy


def turned(values):
    lane = lax.broadcasted_iota(jnp.int32, values.shape, 1)
    low = lax.rem(lane, 64) < 32
    return jnp.where(low, pltpu.roll(values, 96, 1), pltpu.roll(values, 32, 1))


def pile(out, values, half):
    for h in range(8):
        out[pl.ds(64 * h, 64), :] = values[64 * half : 64 * half + 64, 64 * h : 64 * h + 64]


def unpile(values):
    flat = values.T
    return [
        jnp.concatenate([flat[128 * m : 128 * m + 64], flat[128 * m + 64 : 128 * m + 128]], axis=1)
        for m in range(4)
    ]


def norm_scale(ref, out):
    values = ref[...].astype(F32)
    out[...] = lax.rsqrt(jnp.mean(values * values, axis=1, keepdims=True) + EPS)


def front_kernel(
    x, gains_in, qkv_in, wo_in, gu_in, dn_in, dy_in, cosine, sine, bias_p, bias_c, partner,
    gains, qkv_out, wo_out, gu_all, dn_all, dy_all, a1, qst, kst, vst, att, lse, h1, a2,
    qkv, wo, kv_own, kv, sT, pT, scale, dnp,
    s0, s1, t0, t1, y0, y1, u0, u1, w0, w1, local,
):
    me = Place()
    greet_all(me)
    swap = Swap(me, dn_in.at[:, pl.ds(pl.multiple_of(me.c * 256, 256), 256)], dnp, (w0, w1), local.at[8])
    swap.start()

    def rows_at(ref, rows):
        def loc(dr, dp, er, ep, half):
            size = rows if half is None else rows // 2
            first = me.fsdp_at(dr, dp) * rows + (0 if half is None else half * size)
            return ref.at[pl.ds(pl.multiple_of(first, size), size)]

        return loc

    def gains_at(dr, dp, er, ep, half):
        return gains.at[me.fsdp_at(dr, dp), row_half(half, 16)]

    def dn_at(dr, dp, er, ep, half):
        size = 352 if half is None else 176
        first = me.co * 352 + (0 if half is None else half * size)
        return dn_all.at[
            pl.ds(pl.multiple_of(first, 16), size),
            pl.ds(pl.multiple_of(me.chip_at(dr, dp) * 256, 256), 256),
        ]

    def slot_at(ref, rows):
        def loc(dr, dp, er, ep, half):
            return ref.at[slot_of(dr - er, dp + ep), row_half(half, rows)]

        return loc

    def columns(index):
        return pl.ds(pl.multiple_of(index * 256, 256), 256)

    def wo_x_at(dr, dp, er, ep, half):
        return wo.at[me.chip_at(dr, dp), me.co, row_half(half, 128), columns(me.c)]

    def wo_y_at(dr, dp, er, ep, half):
        chips = pl.ds(0, 8) if half is None else pl.ds(4 * half, 4)
        return wo.at[chips, me.co, :, columns(me.ctx_at(dr, dp))]

    def over_x(own, loc, row, both=True):
        return Gather(me.across_x, own, loc, (s0, s1), row, me.sibling() if both else None, (t0, t1))

    wo_own = wo_in.at[:, columns(me.c)]
    g = over_x(gains_in, gains_at, 0)
    q = over_x(qkv_in, rows_at(qkv, 128), 1)
    o = over_x(wo_own, wo_x_at, 2, both=False)
    m = over_x(gu_in, rows_at(gu_all, 128), 3)
    d = over_x(dnp, dn_at, 4)
    dy = Gather(me.across_y, dy_in, slot_at(dy_all, 128), (y0, y1), 0)
    oy = Gather(me.across_y, wo_y_at(0, 0, 0, 0, None), wo_y_at, (y0, y1), 1, me.sibling(), (u0, u1))
    kv_task = Gather(me.across_y, kv_own, slot_at(kv, 128), (y0, y1), 2)
    kept = [load(task.own, task.loc(0, 0, 0, 0, None), local.at[i]) for i, task in enumerate((g, q, o, m, dy))]

    g.start()
    o.start()
    q.start()
    dy.start()
    norm_scale(x, scale)
    swap.wait()
    kept.append(load(dnp, d.loc(0, 0, 0, 0, None), local.at[5]))
    for task in (g, o):
        task.pair()
        task.turn(0)
    dy.pair()
    dy.turn(0)
    q.pair()
    g.turn(1)
    o.turn(1)
    q.turn(0)
    dy.turn(1)
    q.turn(1)
    m.start()
    d.start()
    for task in (g, o):
        task.last(0)
        task.last(1)
    kept[2].wait()
    oy.start()
    dy.last(0)
    dy.last(1)
    kept[0].wait()
    g.end()

    @pl.loop(0, 16)
    def _(i):
        at = pl.ds(pl.multiple_of(i * 128, 128), 128)
        a1[:, at] = (x[:, at].astype(F32) * scale[...] * gains[i, pl.ds(0, 1), :]).astype(BF)

    q.last(0)
    q.last(1)
    m.pair()
    d.pair()
    oy.pair()
    kept[1].wait()
    q.end()
    saved = [load(qkv, qkv_out, local.at[6])]

    @pl.loop(0, 4)
    def _(n):
        raw = dot_in(a1[...], qkv[:, pl.ds(pl.multiple_of(512 * n, 512), 512)])
        for i in range(4):
            part = raw[:, 128 * i : 128 * i + 128]
            part = ((part * cosine[...] + turned(part) * sine[...]) .astype(BF).astype(F32) * SCALE).astype(BF)
            for half in (0, 1):
                for e in (0, 1):
                    qst[n, half, pl.ds(64 * (2 * i + e), 64), :] = part[64 * half : 64 * half + 64, 64 * e : 64 * e + 64]

    raw = dot_in(a1[...], qkv[:, pl.ds(2048, 512)])
    for i in range(2):
        part = raw[:, 128 * i : 128 * i + 128]
        kv_own[:, 128 * i : 128 * i + 128] = (part * cosine[...] + turned(part) * sine[...]).astype(BF)
    kv_own[:, 256:] = raw[:, 256:].astype(BF)
    kv_task.start()
    kv[0] = kv_own[...]
    m.turn(0)
    kv_task.pair()
    kv_task.turn(0)
    d.turn(0)
    kv_task.turn(1)
    oy.turn(0)
    kv_task.last(0)
    kv_task.last(1)
    kv_task.end()

    mate = partner[0]
    beside = kv[mate]
    for out, base in ((kst, 0), (vst, 256)):
        for n in range(4):
            first = base + 64 * n
            for slot in range(8):
                out[n, pl.ds(64 * slot, 64), :] = kv[slot, 0:64, first : first + 64]
            out[n, pl.ds(512, 64), :] = beside[64:128, first : first + 64]
            out[n, pl.ds(576, 64), :] = kv_own[64:128, first : first + 64]

    def attend(n, half):
        count = 512 if half == 0 else 640
        keys = pl.ds(0, count)
        sT[keys] = dot_back(kst[n, keys, :], qst[n, half])
        for i in range(4):
            at = pl.ds(128 * i, 128)
            if half == 0:
                scores = sT[keys, at] + bias_p[...]
                peak = jnp.max(scores, axis=0, keepdims=True)
                raised = jnp.exp(scores - peak)
                total = jnp.sum(raised, axis=0, keepdims=True)
                pT[keys, at] = (raised * (1.0 / total)).astype(BF)
            else:
                first = sT[0:512, at]
                rest = sT[512:640, at] + bias_c[...]
                peak = jnp.maximum(
                    jnp.max(first, axis=0, keepdims=True), jnp.max(rest, axis=0, keepdims=True)
                )
                first = jnp.exp(first - peak)
                rest = jnp.exp(rest - peak)
                total = jnp.sum(first, axis=0, keepdims=True) + jnp.sum(rest, axis=0, keepdims=True)
                pT[0:512, at] = (first * (1.0 / total)).astype(BF)
                pT[512:640, at] = (rest * (1.0 / total)).astype(BF)
            lse[2 * n + half, :, at] = peak + jnp.log(total)
        for i, block in enumerate(unpile(dot_rows(vst[n, keys, :], pT[keys]))):
            first = pl.multiple_of(512 * n + 128 * i, 128)
            att[pl.ds(64 * half, 64), pl.ds(first, 128)] = block.astype(BF)

    @pl.loop(0, 4)
    def _(n):
        attend(n, 0)
        attend(n, 1)

        @pl.when(n == 0)
        def _():
            oy.turn(1)
            m.turn(1)

        @pl.when(n == 1)
        def _():
            d.turn(1)

    oy.last(0)
    oy.last(1)
    o.end()
    oy.end()
    saved.append(load(wo, wo_out, local.at[7]))

    @pl.loop(0, 4)
    def _(n):
        at = pl.ds(pl.multiple_of(512 * n, 512), 512)
        h1[:, at] = x[:, at].astype(F32) + dot_in(att[...], wo[:, :, :, at].reshape(2048, 512))

    norm_scale(h1, scale)

    @pl.loop(0, 16)
    def _(i):
        at = pl.ds(pl.multiple_of(i * 128, 128), 128)
        a2[:, at] = (h1[:, at] * scale[...] * gains[i, pl.ds(8, 1), :]).astype(BF)

    for task in (m, d):
        task.last(0)
        task.last(1)
    for task in (m, d, dy):
        task.end()
    for copy in (*kept[3:], *saved):
        copy.wait()


def front(x, gains, qkv, wo, gu, dn, dy, cosine, sine, bias_p, bias_c, partner):
    return pl.pallas_call(
        front_kernel,
        out_shape=(
            jax.ShapeDtypeStruct((16, 16, 128), F32),
            jax.ShapeDtypeStruct((2048, 2560), BF),
            jax.ShapeDtypeStruct((8, 2, 128, 2048), BF),
            jax.ShapeDtypeStruct((2048, 1536), BF),
            jax.ShapeDtypeStruct((704, 2048), BF),
            jax.ShapeDtypeStruct((8, 128, 2048), BF),
            jax.ShapeDtypeStruct((128, 2048), BF),
            jax.ShapeDtypeStruct((4, 2, 512, 64), BF),
            jax.ShapeDtypeStruct((4, 640, 64), BF),
            jax.ShapeDtypeStruct((4, 640, 64), BF),
            jax.ShapeDtypeStruct((128, 2048), BF),
            jax.ShapeDtypeStruct((8, 1, 512), F32),
            jax.ShapeDtypeStruct((128, 2048), F32),
            jax.ShapeDtypeStruct((128, 2048), BF),
        ),
        in_specs=[VMEM] + [ANY] * 6 + [VMEM] * 4 + [pl.BlockSpec(memory_space=pltpu.SMEM)],
        out_specs=[VMEM] + [ANY] * 5 + [VMEM] * 8,
        scratch_shapes=[
            pltpu.VMEM((2048, 2560), BF),
            pltpu.VMEM((8, 2, 128, 2048), BF),
            pltpu.VMEM((128, 512), BF),
            pltpu.VMEM((8, 128, 512), BF),
            pltpu.VMEM((640, 512), F32),
            pltpu.VMEM((640, 512), BF),
            pltpu.VMEM((128, 1), F32),
            pltpu.VMEM((352, 256), BF),
            *dma_sems(5, 9),
            *dma_sems(5, 10),
            *dma_sems(3, 9),
            *dma_sems(2, 10),
            pltpu.SemaphoreType.DMA,
            pltpu.SemaphoreType.DMA,
            pltpu.SemaphoreType.DMA((9,)),
        ],
        compiler_params=params(1, 50),
        name="front",
    )(x, gains, qkv, wo, gu, dn, dy, cosine, sine, bias_p, bias_c, partner)


def back_kernel(
    da2, h1, dy, x, gains, wo_in, qkv_in, qst, kst, vst, lse, cosine, sine, bias_p, bias_c, partner,
    a1_in, att_in, mpart_in, gu, gdown_in,
    mixed, tokens_grad, q_out, kv_out, o_out, gains_out, gu_all, dn_all,
    a1s, atts, dqkvs, datts, grow, dh1, gown, gsib, mpart, stream, dost, sT, dT, pT, dsT,
    kgrad, vgrad, kvp, dkv, da1, gdown, dn_sum, dnp,
    qp, op, kp, gp, ggot, q_sum, o_sum, kv_sum, g_sum,
    q_half, q_full, q_pair, o_half, o_full, o_pair, k_half, k_full, k_pair, e_half, e_full, e_pair,
    m_half, m_full, m_pair, d_half, d_full, d_pair, n_half, n_full, n_pair,
    or_half, or_full, or_pair, qr_half, qr_full, qr_pair, kr_half, kr_full, kr_pair,
    sib0, sib1, x0, x1, y0, y1, ag0, ag1, swap0, swap1, local,
):
    me = Place()
    greet_all(me)
    nload = load(gdown_in, gdown, local.at[0])
    own, other = pl.ds(0, 128), pl.ds(128, 128)
    mload = load(mpart_in, mpart, local.at[1])
    a1load = load(a1_in, a1s.at[own], local.at[2])
    attload = load(att_in, atts.at[own], local.at[3])

    def wo_load(n):
        return pltpu.make_async_copy(
            wo_in.at[pl.ds(512 * n, 512)], stream.at[n % 2, :, pl.ds(0, 2048)], local.at[4 + n % 2]
        )

    def qkv_load(n):
        return pltpu.make_async_copy(qkv_in.at[pl.ds(512 * n, 512)], stream.at[n % 2], local.at[4 + n % 2])

    wo_load(0).start()
    wo_load(1).start()

    over_x, over_y, over_ag = (x0, x1), (y0, y1), (ag0, ag1)
    o_job = Scatter(me.across_x, lambda slot: op.at[slot], 128, o_half, o_full, o_pair, over_x, 0)
    q_job = Scatter(me.across_x, lambda slot: qp.at[slot], 128, q_half, q_full, q_pair, over_x, 1)
    k_job = Scatter(me.across_x, lambda slot: kp.at[slot], 128, k_half, k_full, k_pair, over_x, 2)
    e_job = Scatter(me.across_x, lambda slot: gp.at[slot], 16, e_half, e_full, e_pair, over_x, 3)
    n_job = Scatter(me.across_x, lambda slot: gdown.at[slot], 352, n_half, n_full, n_pair, over_x, 4)
    dn_swap = Swap(me, dn_sum, dnp, (swap0, swap1), local.at[8])
    m_job = Scatter(me.across_y, lambda slot: mpart.at[slot], 128, m_half, m_full, m_pair, over_y, 0)
    d_job = Scatter(me.across_y, lambda slot: kvp.at[slot], 128, d_half, d_full, d_pair, over_y, 1)

    def at_ctx(ref):
        def loc(dr, dp, er, ep, half):
            return ref.at[me.ctx_at(dr, dp), row_half(half, ref.shape[1])]

        return loc

    def dn_at(dr, dp, er, ep, half):
        first = pl.multiple_of(me.ctx_at(dr, dp) * 256, 256)
        return dn_all.at[row_half(half, 352), pl.ds(first, 256)]

    gu_task = Gather(me.across_y, gu, at_ctx(gu_all), over_ag, 0)
    dn_task = Gather(me.across_y, dnp, dn_at, over_ag, 1)
    e_task = Gather(me.across_y, g_sum, at_ctx(ggot), over_ag, 2)

    def sum_over_ctx(total, columns, halves, fulls, paired, row):
        def part(slot):
            first = pl.multiple_of(me.ctx_at(STEPS[slot], PAIRS[slot]) * 16, 16)
            return total.at[pl.ds(first, 16)]

        return Scatter(me.across_y, part, 16, halves, fulls, paired, over_y, row, cut=columns)

    def spread(out, columns, row):
        def loc(dr, dp, er, ep, half):
            first = pl.multiple_of(me.ctx_at(dr, dp) * 16, 16)
            if half is None:
                return out.at[pl.ds(first, 16)]
            return out.at[pl.ds(first, 16), pl.ds(half * (columns // 2), columns // 2)]

        return Gather(me.across_y, loc(0, 0, 0, 0, None), loc, over_ag, row)

    o_sums = sum_over_ctx(o_sum, 2048, or_half, or_full, or_pair, 2)
    q_sums = sum_over_ctx(q_sum, 2048, qr_half, qr_full, qr_pair, 3)
    kv_sums = sum_over_ctx(kv_sum, 512, kr_half, kr_full, kr_pair, 4)
    o_spread = spread(o_out, 2048, 3)
    q_spread = spread(q_out, 2048, 4)
    kv_spread = spread(kv_out, 512, 5)
    own_rows = pl.ds(pl.multiple_of(me.c * 16, 16), 16)

    swap = lambda src, dst, index: send(src, dst, (sib0, sib1), index, me.sibling())
    att_swap = swap(atts.at[own], atts.at[other], 0)
    datt_swap = swap(datts.at[own], datts.at[other], 1)
    a1_swap = swap(a1s.at[own], a1s.at[other], 2)
    queries = pl.ds(0, 2048)
    dq_swap = swap(dqkvs.at[own, queries], dqkvs.at[other, queries], 3)
    rest = pl.ds(2048, 512)
    dkv_swap = swap(dqkvs.at[own, rest], dqkvs.at[other, rest], 4)
    gain_swap = swap(gown, gsib, 5)

    attload.wait()
    att_swap.start()
    a1load.wait()
    a1_swap.start()
    nload.wait()
    n_job.start()
    mload.wait()
    m_job.start()

    gown[...] = jnp.zeros((16, 16, 128), F32)
    for i in range(16):
        grow[0, :, 128 * i : 128 * i + 128] = gains[i, 0:1, :]
        grow[1, :, 128 * i : 128 * i + 128] = gains[i, 8:9, :]
    grow[2] = jnp.zeros((1, 2048), F32)
    grow[3] = jnp.zeros((1, 2048), F32)

    @pl.loop(0, 8)
    def _(i):
        at = pl.ds(pl.multiple_of(16 * i, 16), 16)
        values, grad = h1[at], da2[at]
        scale = lax.rsqrt(jnp.mean(values * values, axis=1, keepdims=True) + EPS)
        grow[3] += jnp.sum(grad * values * scale, axis=0, keepdims=True)
        grad = grad * grow[1]
        level = jnp.mean(grad * values, axis=1, keepdims=True) * scale * scale * scale
        total = dy[at].astype(F32) + scale * grad - values * level
        dh1[at] = total
        datts[at] = total.astype(BF)

    datt_swap.start()
    n_job.turn(1)
    n_job.turn(0)
    for n in range(4):
        wo_load(n).wait()
        part = dot_back(datts[own], stream[n % 2, :, 0:2048]).astype(BF)
        for half in (0, 1):
            pile(dost.at[n, half], part, half)
        if n < 2:
            wo_load(n + 2).start()
    qkv_load(0).start()
    qkv_load(1).start()

    def terms(left, right, out, job):
        @pl.loop(0, 8)
        def _(i):
            at = pl.multiple_of((chip_of(me, 7 - i) * 2 + me.co) * 128, 128)
            out[7 - i] = dot_rows(left[:, pl.ds(at, 128)], right[...]).astype(BF)

            @pl.when(i == 1)
            def _():
                job.start()

    m_job.turn(1)
    att_swap.wait_recv()
    datt_swap.wait_recv()
    terms(atts, datts, op, o_job)
    m_job.turn(0)
    n_job.pair()

    def attend(n, half):
        count = 512 if half == 0 else 640
        keys = pl.ds(0, count)
        key, query, out = kst[n, keys, :], qst[n, half], dost[n, half]
        sT[keys] = dot_back(key, query)
        dT[keys] = dot_back(vst[n, keys, :], out)
        for i in range(4):
            at = pl.ds(128 * i, 128)
            parts = []
            for first, size in ((0, 512), (512, 128))[: 1 + half]:
                scores = sT[first : first + size, at]
                if half == 0:
                    scores = scores + bias_p[...]
                elif first:
                    scores = scores + bias_c[...]
                probs = jnp.exp(scores - lse[2 * n + half, :, at])
                grad = dT[first : first + size, at]
                parts.append((first, size, probs, grad))
            level = sum(jnp.sum(probs * grad, axis=0, keepdims=True) for _, _, probs, grad in parts)
            for first, size, probs, grad in parts:
                pT[first : first + size, at] = probs.astype(BF)
                dsT[first : first + size, at] = (probs * (grad - level)).astype(BF)
        rows = slice(64 * half, 64 * half + 64)
        for i, block in enumerate(unpile(dot_rows(key, dsT[keys]) * SCALE)):
            block = block * cosine[rows] - turned(block) * sine[rows]
            first = pl.multiple_of(512 * n + 128 * i, 128)
            dqkvs[rows, pl.ds(first, 128)] = block.astype(BF)
        return dot_in(dsT[keys], query), dot_in(pT[keys], out)

    @pl.loop(0, 4)
    def _(n):
        key_one, value_one = attend(n, 0)
        key_two, value_two = attend(n, 1)
        for out, one, two in ((kgrad, key_one, key_two), (vgrad, value_one, value_two)):
            out[n, 0:512] = (one + two[0:512]).astype(BF)
            out[n, 512:640] = two[512:640].astype(BF)

        @pl.when(n == 0)
        def _():
            n_job.finish(dn_sum)
            dn_swap.start()

        @pl.when(n == 1)
        def _():
            o_job.turn(1)

    dq_swap.start()
    o_job.turn(0)
    mate = partner[0]
    for out, base in ((kgrad, 0), (vgrad, 256)):
        for n in range(4):
            first = base + 64 * n
            for slot in range(8):
                kvp[slot, 0:64, first : first + 64] = out[n, 64 * slot : 64 * slot + 64, :]
                if slot == 0:
                    late = out[n, 576:640, :]
                else:
                    late = jnp.where(mate == slot, out[n, 512:576, :], jnp.zeros((64, 64), BF))
                kvp[slot, 64:128, first : first + 64] = late
    d_job.start()
    m_job.pair()
    a1_swap.wait_recv()
    dq_swap.wait_recv()
    terms(a1s, dqkvs.at[:, pl.ds(0, 2048)], qp, q_job)
    m_job.finish(mixed, (h1,))
    o_job.pair()
    d_job.turn(1)
    d_job.turn(0)
    kept = [load(gu, gu_all.at[me.c], local.at[6])]
    gu_task.start()
    dn_swap.wait()
    dn_task.start()
    kept.append(load(dnp, dn_at(0, 0, 0, 0, None), local.at[7]))
    d_job.pair()
    d_job.finish(dkv)
    for i in range(2):
        at = slice(128 * i, 128 * i + 128)
        block = dkv[:, at]
        dqkvs[own, 2048 + 128 * i : 2176 + 128 * i] = (block * cosine[...] - turned(block) * sine[...]).astype(BF)
    dqkvs[own, 2304:2560] = dkv[:, 256:512].astype(BF)
    dkv_swap.start()
    o_job.finish(o_sum)
    o_sums.start()

    for n in range(4):
        qkv_load(n).wait()
        da1[:, 512 * n : 512 * n + 512] = dot_back(dqkvs[own], stream[n % 2])
        if n < 2:
            qkv_load(n + 2).start()
    q_job.turn(1)
    dkv_swap.wait_recv()
    terms(a1s, dqkvs.at[:, pl.ds(2048, 512)], kp, k_job)

    @pl.loop(0, 8)
    def _(i):
        at = pl.ds(pl.multiple_of(16 * i, 16), 16)
        values, grad = x[at].astype(F32), da1[at]
        scale = lax.rsqrt(jnp.mean(values * values, axis=1, keepdims=True) + EPS)
        grow[2] += jnp.sum(grad * values * scale, axis=0, keepdims=True)
        grad = grad * grow[0]
        level = jnp.mean(grad * values, axis=1, keepdims=True) * scale * scale * scale
        tokens_grad[at] = (dh1[at] + scale * grad - values * level).astype(BF)

    for i in range(16):
        gown[i, 0:1, :] = grow[2, :, 128 * i : 128 * i + 128]
        gown[i, 8:9, :] = grow[3, :, 128 * i : 128 * i + 128]
    gain_swap.start()
    gu_task.pair()
    dn_task.pair()
    q_job.turn(0)
    gu_task.turn(0)
    dn_task.turn(0)
    gain_swap.wait_recv()
    for slot in range(8):
        block = me.fsdp_at(STEPS[slot], PAIRS[slot])
        gp[slot] = gown[block] + gsib[block]
    e_job.start()
    o_sums.turn(1)
    o_sums.turn(0)
    gu_task.turn(1)
    dn_task.turn(1)
    o_sums.pair()
    o_sums.finish(o_out.at[own_rows])
    o_spread.start()
    q_job.pair()
    k_job.turn(1)
    k_job.turn(0)
    e_job.turn(1)
    e_job.turn(0)
    o_spread.pair()
    o_spread.turn(0)
    o_spread.turn(1)
    q_job.finish(q_sum)
    q_sums.start()
    k_job.pair()
    e_job.pair()
    q_sums.turn(1)
    q_sums.turn(0)
    k_job.finish(kv_sum)
    kv_sums.start()
    e_job.finish(g_sum)
    e_task.start()
    ggot[me.c] = g_sum[...]
    q_sums.pair()
    kv_sums.turn(1)
    kv_sums.turn(0)
    e_task.pair()
    e_task.turn(0)
    q_sums.finish(q_out.at[own_rows])
    q_spread.start()
    e_task.turn(1)
    kv_sums.pair()
    q_spread.pair()
    q_spread.turn(0)
    kv_sums.finish(kv_out.at[own_rows])
    kv_spread.start()
    q_spread.turn(1)
    kv_spread.pair()
    kv_spread.turn(0)
    kv_spread.turn(1)
    e_task.last(0)
    e_task.last(1)
    total = ggot[0]
    for index in range(1, 8):
        total = total + ggot[index]
    gains_out[...] = total
    for task in (gu_task, dn_task, o_spread, q_spread, kv_spread):
        task.last(0)
        task.last(1)
    jobs = (o_job, q_job, k_job, e_job, m_job, d_job, n_job, o_sums, q_sums, kv_sums)
    for job in (*jobs, gu_task, dn_task, e_task, o_spread, q_spread, kv_spread):
        job.end()
    for copy in (att_swap, datt_swap, a1_swap, dq_swap, dkv_swap, gain_swap):
        copy.wait_send()
    for copy in kept:
        copy.wait()


def back(da2, h1, dy, x, gains, wo, qkv, qst, kst, vst, lse, cosine, sine, bias_p, bias_c, partner, a1, att, mpart, gu, gdown):
    scratch = [
        pltpu.VMEM((256, 2048), BF),
        pltpu.VMEM((256, 2048), BF),
        pltpu.VMEM((256, 2560), BF),
        pltpu.VMEM((256, 2048), BF),
        pltpu.VMEM((4, 1, 2048), F32),
        pltpu.VMEM((128, 2048), F32),
        pltpu.VMEM((16, 16, 128), F32),
        pltpu.VMEM((16, 16, 128), F32),
        pltpu.VMEM((8, 128, 2048), BF),
        pltpu.VMEM((2, 512, 2560), BF),
        pltpu.VMEM((4, 2, 512, 64), BF),
        pltpu.VMEM((640, 512), F32),
        pltpu.VMEM((640, 512), F32),
        pltpu.VMEM((640, 512), BF),
        pltpu.VMEM((640, 512), BF),
        pltpu.VMEM((4, 640, 64), BF),
        pltpu.VMEM((4, 640, 64), BF),
        pltpu.VMEM((8, 128, 512), BF),
        pltpu.VMEM((128, 512), F32),
        pltpu.VMEM((128, 2048), F32),
        pltpu.VMEM((8, 352, 256), BF),
        pltpu.VMEM((352, 256), BF),
        pltpu.VMEM((352, 256), BF),
        pltpu.VMEM((8, 128, 2048), BF),
        pltpu.VMEM((8, 128, 2048), BF),
        pltpu.VMEM((8, 128, 512), BF),
        pltpu.VMEM((8, 16, 128), F32),
        pltpu.VMEM((8, 16, 128), F32),
        pltpu.VMEM((128, 2048), BF),
        pltpu.VMEM((128, 2048), BF),
        pltpu.VMEM((128, 512), BF),
        pltpu.VMEM((16, 128), F32),
        *scatter_buffers(128, 2048),
        *scatter_buffers(128, 2048),
        *scatter_buffers(128, 512),
        *scatter_buffers(16, 128, F32),
        *scatter_buffers(128, 2048),
        *scatter_buffers(128, 512),
        *scatter_buffers(352, 256),
        *scatter_buffers(16, 2048, cut=True),
        *scatter_buffers(16, 2048, cut=True),
        *scatter_buffers(16, 512, cut=True),
        pltpu.SemaphoreType.DMA((6,)),
        pltpu.SemaphoreType.DMA((6,)),
        *dma_sems(5, 9),
        *dma_sems(5, 9),
        *dma_sems(6, 9),
        pltpu.SemaphoreType.DMA,
        pltpu.SemaphoreType.DMA,
        pltpu.SemaphoreType.DMA((9,)),
    ]
    return pl.pallas_call(
        back_kernel,
        out_shape=(
            jax.ShapeDtypeStruct((128, 2048), BF),
            jax.ShapeDtypeStruct((128, 2048), BF),
            jax.ShapeDtypeStruct((128, 2048), BF),
            jax.ShapeDtypeStruct((128, 512), BF),
            jax.ShapeDtypeStruct((128, 2048), BF),
            jax.ShapeDtypeStruct((16, 128), F32),
            jax.ShapeDtypeStruct((8, 128, 1536), BF),
            jax.ShapeDtypeStruct((352, 2048), BF),
        ),
        in_specs=[VMEM] * 5 + [ANY] * 2 + [VMEM] * 8 + [pl.BlockSpec(memory_space=pltpu.SMEM)] + [ANY] * 5,
        out_specs=[VMEM] * 6 + [ANY] * 2,
        scratch_shapes=scratch,
        compiler_params=params(5, 62),
        name="back",
    )(da2, h1, dy, x, gains, wo, qkv, qst, kst, vst, lse, cosine, sine, bias_p, bias_c, partner, a1, att, mpart, gu, gdown)


def widen_kernel(parts, gate, up):
    for out, base in ((gate, 0), (up, 768)):
        for pair in range(4):
            even = parts[2 * pair, :, base : base + 768].astype(F32)
            odd = pltpu.roll(parts[2 * pair + 1, :, base : base + 768].astype(F32), 64, 1)
            first = 1408 * pair
            out[:, first : first + 640] = even[:, 0:640]
            out[:, first + 640 : first + 768] = even[:, 640:768] + odd[:, 0:128]
            out[:, first + 768 : first + 1408] = odd[:, 128:768]


def widen(parts):
    out = jax.ShapeDtypeStruct((128, 5632), F32)
    block = pl.BlockSpec((16, 5632), lambda i: (i, 0))
    return pl.pallas_call(
        widen_kernel,
        grid=(8,),
        out_shape=(out, out),
        in_specs=[pl.BlockSpec((8, 16, 1536), lambda i: (0, i, 0))],
        out_specs=[block, block],
        name="widen",
    )(parts)


def tables(position):
    freq = BASE ** (-(jnp.arange(HEAD_DIM // 2, dtype=jnp.float32) * 2.0) / HEAD_DIM)
    angle = position.astype(jnp.float32)[:, None] * freq[None, :]
    angle = jnp.concatenate([angle, angle], axis=-1)
    return (jnp.cos(angle), jnp.sin(angle))


def timeline(table_flat, total_len, row_count):
    everywhere = jnp.arange(total_len, dtype=jnp.int32)
    half_len = row_count // 2
    moment = jnp.repeat(table_flat, half_len) * half_len + everywhere % half_len
    prompt_len = total_len // 2
    cont_len = total_len // 8
    later = moment >= prompt_len
    segment = jnp.where(later, 1 + (moment - prompt_len) // cont_len, 0)
    position = jnp.where(later, prompt_len + (moment - prompt_len) % cont_len, moment)
    return (segment, position)


def on_device(
    tokens,
    block_deal,
    attn_gain,
    query_weight,
    key_weight,
    value_weight,
    output_weight,
    mlp_gain,
    gate_weight,
    up_weight,
    down_weight,
    cotangent,
):
    row_count = tokens.shape[1]
    c = lax.axis_index("ctx")
    f = lax.axis_index("fsdp")
    full_len = row_count * 8

    def sliced(weight):
        return jnp.pad(lax.dynamic_slice_in_dim(weight, c * 704, 704, 1), ((0, 0), (0, 64)))

    none = jnp.zeros((7, 128), F32)
    gains = jnp.concatenate([attn_gain.astype(F32)[None], none, mlp_gain.astype(F32)[None], none])
    qkv = jnp.concatenate([query_weight, key_weight, value_weight], axis=1)
    gu = jnp.concatenate([sliced(gate_weight), sliced(up_weight)], axis=1)

    y, zl = c // 2, c % 2
    order = jnp.stack([((y + STEPS[s]) % 4) * 2 + (zl + PAIRS[s]) % 2 for s in range(8)])
    deal = jnp.take(lax.dynamic_index_in_dim(block_deal, f, 0, keepdims=False), order, axis=0)
    mate_block = 8 + (deal[0, 1] - 8 + 1 - 2 * ((deal[0, 1] - 8) % 2))
    mate = jnp.argmax((deal[:, 1] == mate_block).astype(jnp.int32)).astype(jnp.int32)
    segment, position = timeline(deal.reshape(-1), full_len, row_count)
    own_segment, own_position = segment[:row_count], position[:row_count]
    cosine, sine = tables(own_position)
    sign = jnp.where(jnp.arange(HEAD_DIM) < 32, -1.0, 1.0)
    cosine_two = jnp.concatenate([cosine, cosine], axis=1)
    sine_two = jnp.concatenate([sine * sign, sine * sign], axis=1)
    prompt_position = position.reshape(8, 2, 64)[:, 0].reshape(512)
    bias_p = jnp.where(prompt_position[:, None] <= own_position[None, :64], 0.0, -1e30)
    mate_seen = deal[0, 1] > mate_block
    step = jnp.arange(64)
    bias_c = jnp.concatenate(
        [
            jnp.broadcast_to(jnp.where(mate_seen, 0.0, -1e30), (64, 64)),
            jnp.where(step[:, None] <= step[None, :], 0.0, -1e30),
        ]
    )
    bias_p = jnp.concatenate([bias_p, bias_p], axis=1).astype(F32)
    bias_c = jnp.concatenate([bias_c, bias_c], axis=1).astype(F32)

    gains_all, qkv_all, wo_all, gu_all, dn_all, dy_all, normed, qst, kst, vst, attended, lse, hidden_state, normed_two = front(
        tokens[0], gains, qkv, output_weight, gu, down_weight, cotangent[0], cosine_two, sine_two, bias_p, bias_c, mate[None]
    )
    wo_all = wo_all.reshape(2048, 2048)

    grad_normed_two, mixed_parts, gu_sum, dn_parts = feed_forward(normed_two, gu_all, dn_all, dy_all)

    mixed, tokens_grad, query_grad, kv_grad, o_grad, gain_grads, gu_grads, dn_grad = back(
        grad_normed_two, hidden_state, cotangent[0], tokens[0], gains_all, wo_all, qkv_all, qst, kst, vst, lse,
        cosine_two, sine_two, bias_p, bias_c, mate[None], normed, attended, mixed_parts, gu_sum, dn_parts,
    )

    gate_grad, up_grad = widen(gu_grads)
    return (
        mixed[None],
        tokens_grad[None],
        gain_grads[0],
        query_grad.astype(F32),
        kv_grad[:, :256].astype(F32),
        kv_grad[:, 256:].astype(F32),
        o_grad.astype(F32),
        gain_grads[8],
        gate_grad,
        up_grad,
        dn_grad.astype(F32),
    )


def solution(mesh):
    held = P("fsdp", "ctx", None)
    rows = P("fsdp", None)
    return jax.shard_map(
        on_device,
        mesh=mesh,
        in_specs=(held, P(), P("fsdp"), rows, rows, rows, rows, P("fsdp"), rows, rows, rows, held),
        out_specs=(held, held, P("fsdp"), rows, rows, rows, rows, P("fsdp"), rows, rows, rows),
        check_vma=False,
    )
```

```python
import functools

import jax
import jax.numpy as jnp
from jax import lax
from jax.experimental import pallas as pl
from jax.experimental.pallas import tpu as pltpu
from jax.sharding import PartitionSpec as P

MESH = pl.DeviceIdType.MESH
BF = jnp.bfloat16
F32 = jnp.float32
ANY = pl.BlockSpec(memory_space=pl.ANY)
VMEM = pl.BlockSpec(memory_space=pltpu.VMEM)

HEAD_DIM = 64
EPS = 1e-05
SCALE = 0.125
BASE = 10000.0

SLOT = {(0, 0): 0, (0, 1): 1, (1, 0): 2, (3, 0): 3, (1, 1): 4, (3, 1): 5, (2, 0): 6, (2, 1): 7}
STEPS = (0, 0, 1, 3, 1, 3, 2, 2)
PAIRS = (0, 1, 0, 0, 1, 1, 0, 1)


def slot_of(dr, dp):
    return SLOT[(dr % 4, dp % 2)]


class Place:
    def __init__(self):
        self.c = lax.axis_index("ctx")
        self.f = lax.axis_index("fsdp")
        self.y, self.zl = lax.div(self.c, 2), lax.rem(self.c, 2)
        self.j, self.co = lax.div(self.f, 2), lax.rem(self.f, 2)
        self.x, self.zh = lax.div(self.j, 2), lax.rem(self.j, 2)

    def ctx_at(self, dr, dp):
        return lax.rem(self.y + dr % 4, 4) * 2 + lax.rem(self.zl + dp, 2)

    def chip_at(self, dr, dp):
        return lax.rem(self.x + dr % 4, 4) * 2 + lax.rem(self.zh + dp, 2)

    def fsdp_at(self, dr, dp):
        return self.chip_at(dr, dp) * 2 + self.co

    def across_y(self, dr, dp):
        return {"ctx": self.ctx_at(dr, dp), "fsdp": self.f}

    def across_x(self, dr, dp):
        return {"ctx": self.c, "fsdp": self.fsdp_at(dr, dp)}

    def sibling(self):
        return {"ctx": self.c, "fsdp": self.f + 1 - 2 * self.co}


def chip_of(me, t):
    dr = jnp.where(t < 2, 0, jnp.where(t >= 6, 2, 1 + 2 * lax.rem(t, 2)))
    dp = jnp.where(t < 2, t, jnp.where(t >= 6, t - 6, lax.div(t, 4)))
    return lax.rem(me.x + dr, 4) * 2 + lax.rem(me.zh + dp, 2)


def greet(devices):
    barrier = pltpu.get_barrier_semaphore()
    for device in devices:
        pl.semaphore_signal(barrier, 1, device_id=device, device_id_type=MESH)
    pl.semaphore_wait(barrier, len(devices))


class Swap:
    def __init__(self, me, src, dst, sems, local):
        self.moved = me.c != me.j
        self.to = {"ctx": me.j, "fsdp": 2 * me.c + me.co}
        self.copy = pltpu.make_async_remote_copy(
            src, dst, sems[0], sems[1], device_id=self.to, device_id_type=MESH
        )
        self.keep = pltpu.make_async_copy(src, dst, local)

    def start(self):
        pl.when(self.moved)(self.copy.start)
        pl.when(jnp.logical_not(self.moved))(self.keep.start)

    def wait(self):
        pl.when(self.moved)(self.copy.wait)
        pl.when(jnp.logical_not(self.moved))(self.keep.wait)


def greet_all(me, plane=False):
    barrier = pltpu.get_barrier_semaphore()
    others = near(me.across_x) + [me.sibling()]
    others += [me.across_y(STEPS[s], PAIRS[s]) for s in range(1, 8)] if plane else near(me.across_y)
    for device in others:
        pl.semaphore_signal(barrier, 1, device_id=device, device_id_type=MESH)
    moved = me.c != me.j

    @pl.when(moved)
    def _():
        to = {"ctx": me.j, "fsdp": 2 * me.c + me.co}
        pl.semaphore_signal(barrier, 1, device_id=to, device_id_type=MESH)

    pl.semaphore_wait(barrier, len(others) + jnp.where(moved, 1, 0))


def near(dev):
    return [dev(1, 0), dev(-1, 0), dev(0, 1)]


def send(src, dst, sems, index, device):
    return pltpu.make_async_remote_copy(
        src, dst, sems[0].at[index], sems[1].at[index], device_id=device, device_id_type=MESH
    )


class Gather:
    MOVES = (
        ((0, 0), (0, 1), None),
        ((0, 0), (1, 0), None),
        ((0, 0), (-1, 0), None),
        ((0, 1), (1, 0), None),
        ((0, 1), (-1, 0), None),
        ((-1, 0), (1, 0), 0),
        ((-1, 1), (1, 0), 0),
        ((1, 0), (-1, 0), 1),
        ((1, 1), (-1, 0), 1),
    )

    def __init__(self, dev, own, loc, sems, row, sibling=None, sibling_sems=None):
        self.loc = loc
        self.copies = []
        for index, (block, to, half) in enumerate(self.MOVES):
            src = own if block == (0, 0) else loc(*block, 0, 0, half)
            dst = loc(*block, *to, half)
            self.copies.append(send(src, dst, sems, (row, index), dev(*to)))
        self.passed = {}
        if sibling is not None:
            self.passed[9] = send(own, loc(0, 0, 0, 0, None), sibling_sems, (row, 9), sibling)
            for index, ((dr, dp), (er, ep), half) in enumerate(self.MOVES):
                ref = loc(dr - er, dp + ep, 0, 0, half)
                self.passed[index] = send(ref, ref, sibling_sems, (row, index), sibling)
        self.own = own

    def _pass(self, index):
        if self.passed:
            self.passed[index].start()

    def _got(self, index):
        self.copies[index].wait_recv()
        self._pass(index)

    def start(self):
        for index in (0, 1, 2):
            self.copies[index].start()
        self._pass(9)

    def pair(self):
        self._got(0)
        self.copies[3].start()
        self.copies[4].start()

    def turn(self, dp):
        for got, on in (((1, 5), (2, 7)) if dp == 0 else ((3, 6), (4, 8))):
            self._got(got)
            self.copies[on].start()

    def last(self, dp):
        for got in ((5, 7) if dp == 0 else (6, 8)):
            self._got(got)

    def sync(self):
        for copy in self.passed.values():
            copy.wait()

    def end(self):
        for copy in self.copies:
            copy.wait_send()


def row_half(half, rows):
    return pl.ds(0, rows) if half is None else pl.ds(half * (rows // 2), rows // 2)


def add_into(ref, rows, others, step=16):
    step = min(step, rows)

    @pl.loop(0, rows // step)
    def _(i):
        at = pl.ds(pl.multiple_of(i * step, step), step)
        total = ref[at].astype(F32)
        for other in others:
            total = total + other[at].astype(F32)
        ref[at] = total.astype(ref.dtype)


class Scatter:
    def __init__(self, dev, part, rows, halves, fulls, paired, sems, row, cut=None):
        self.part, self.rows, self.cut = part, rows, cut
        self.halves, self.fulls, self.paired = halves, fulls, paired
        self.first, self.second = {}, {}
        for dp in (0, 1):
            for way, sign in ((0, 1), (1, -1)):
                self.first[way, dp] = send(
                    self._half(part(slot_of(2, dp)), way), halves.at[way, dp], sems, (row, way * 2 + dp), dev(sign, 0)
                )
                self.second[way, dp] = send(
                    part(slot_of(sign, dp)), fulls.at[way, dp], sems, (row, 4 + way * 2 + dp), dev(sign, 0)
                )
        self.third = send(part(slot_of(0, 1)), paired, sems, (row, 8), dev(0, 1))

    def _half(self, ref, way):
        if self.cut is None:
            return ref.at[pl.ds(way * (self.rows // 2), self.rows // 2)]
        return ref.at[:, pl.ds(way * (self.cut // 2), self.cut // 2)]

    def start(self):
        for dp in (1, 0):
            for way in (0, 1):
                self.first[way, dp].start()

    def turn(self, dp):
        for way, sign in ((0, 1), (1, -1)):
            self.first[way, dp].wait_recv()
            block = self._half(self.part(slot_of(sign, dp)), way)
            add_into(block, block.shape[0], [self.halves.at[way, dp]])
            self.second[way, dp].start()

    def pair(self):
        for way in (0, 1):
            self.second[way, 1].wait_recv()
        add_into(self.part(slot_of(0, 1)), self.rows, [self.fulls.at[0, 1], self.fulls.at[1, 1]])
        self.third.start()

    def finish(self, out, extra=()):
        for way in (0, 1):
            self.second[way, 0].wait_recv()
        self.third.wait_recv()
        own = self.part(0)
        terms = [own, self.fulls.at[0, 0], self.fulls.at[1, 0], self.paired, *extra]

        @pl.loop(0, self.rows // 16)
        def _(i):
            at = pl.ds(pl.multiple_of(i * 16, 16), 16)
            total = terms[0][at].astype(F32)
            for term in terms[1:]:
                total = total + term[at].astype(F32)
            out[at] = total.astype(out.dtype)

    def end(self):
        for copy in (*self.first.values(), *self.second.values(), self.third):
            copy.wait_send()


def mirror(slot):
    return slot_of(-STEPS[slot], PAIRS[slot])


class Trade:
    def __init__(self, dev, what, where, sems, row):
        self.copies = [
            pltpu.make_async_remote_copy(
                what(slot), where(slot), sems[0].at[row, slot], sems[1].at[row, mirror(slot)],
                device_id=dev(STEPS[slot], PAIRS[slot]), device_id_type=MESH,
            )
            for slot in range(1, 8)
        ]

    def start(self):
        for copy in self.copies:
            copy.start()

    def got(self):
        for copy in self.copies:
            copy.wait_recv()

    def end(self):
        for copy in self.copies:
            copy.wait_send()


def scatter_buffers(rows, columns, dtype=BF, cut=False):
    half = (rows, columns // 2) if cut else (rows // 2, columns)
    return [
        pltpu.VMEM((2, 2, *half), dtype),
        pltpu.VMEM((2, 2, rows, columns), dtype),
        pltpu.VMEM((rows, columns), dtype),
    ]


def dma_sems(rows, count):
    return [pltpu.SemaphoreType.DMA((rows, count)), pltpu.SemaphoreType.DMA((rows, count))]


def params(collective_id, vmem=56):
    return pltpu.CompilerParams(
        collective_id=collective_id, has_side_effects=True, vmem_limit_bytes=vmem << 20
    )


def dot_in(left, right):
    return jnp.dot(left, right, preferred_element_type=F32)


def dot_back(left, right):
    return lax.dot_general(left, right, (((1,), (1,)), ((), ())), preferred_element_type=F32)


def dot_rows(left, right):
    return lax.dot_general(left, right, (((0,), (0,)), ((), ())), preferred_element_type=F32)


def mlp_kernel(
    a2, gu_in, dn_in, dy_in, dy_own,
    da2_out, mpart, gu_out, gdown,
    acts, gu, wd, dy, hid, dgu, dpart,
    d_half, d_full, d_pair,
    gsib, grecv, gown, gd, gdrecv,
    g_half, g_full, g_pair,
    ag0, ag1, dn0, dn1, dp0, dp1, rs0, rs1, sib0, sib1, local,
):
    me = Place()
    greet(near(me.across_x) + near(me.across_y) + [me.sibling()])

    def wd_at(dr, dp, er, ep, half):
        size = 352 if half is None else 176
        first = me.co * 352 + (0 if half is None else half * size)
        return wd.at[
            pl.ds(pl.multiple_of(first, 16), size),
            pl.ds(pl.multiple_of(me.chip_at(dr, dp) * 256, 256), 256),
        ]

    def acts_at(dr, dp, er, ep, half):
        return acts.at[slot_of(dr - er, dp + ep), row_half(half, 128)]

    task = Gather(me.across_y, a2, acts_at, (ag0, ag1), 0)
    down = Gather(me.across_x, dn_in, wd_at, (dn0, dn1), 0, me.sibling(), (dp0, dp1))
    down.start()
    task.start()
    loads = [
        pltpu.make_async_copy(gu_in, gu, local.at[0]),
        pltpu.make_async_copy(dn_in, wd_at(0, 0, 0, 0, None), local.at[1]),
        pltpu.make_async_copy(dy_in.at[pl.ds(1, 7)], dy.at[pl.ds(1, 7)], local.at[2]),
        pltpu.make_async_copy(dy_own, dy.at[0], local.at[3]),
    ]
    for load in loads:
        load.start()
    acts[0] = a2[...]
    wd[pl.ds(704, 64)] = jnp.zeros((64, 2048), BF)
    down.turn(0)
    down.pair()
    down.last(0)
    task.turn(0)
    down.turn(1)
    task.pair()
    for load in loads:
        load.wait()
    down.last(1)
    down.sync()

    def group(g):
        at = pl.ds(2 * g, 2)
        rows = pl.ds(pl.multiple_of(256 * g, 256), 256)
        for h in range(3):
            first, second = pl.ds(256 * h, 256), pl.ds(768 + 256 * h, 256)
            here = acts[at].reshape(256, 2048)
            gate = dot_in(here, gu[:, first])
            up = dot_in(here, gu[:, second])
            back = dot_back(dy[at].reshape(256, 2048), wd[first, :])
            curve = 1.0 / (1.0 + jnp.exp(-gate))
            silu = gate * curve
            hid[rows, first] = (silu * up).astype(BF)
            dgu[rows, first] = (back * up * (curve + silu * (1.0 - curve))).astype(BF)
            dgu[rows, second] = (back * silu).astype(BF)
        for n in range(4):
            wide = pl.ds(512 * n, 512)
            mpart[at, :, wide] = dot_in(hid[rows, :], wd[:, wide]).astype(BF).reshape(2, 128, 512)
            dpart[at, :, wide] = dot_back(dgu[rows, :], gu[wide, :]).astype(BF).reshape(2, 128, 512)

    @pl.loop(0, 4)
    def _(g):
        @pl.when(g == 2)
        def _():
            task.turn(1)

        @pl.when(g == 3)
        def _():
            task.last(0)
            task.last(1)

        group(g)

    grad = Scatter(me.across_y, lambda slot: dpart.at[slot], 128, d_half, d_full, d_pair, (rs0, rs1), 0)
    first = Scatter(me.across_x, lambda slot: gown.at[slot], 128, g_half, g_full, g_pair, (rs0, rs1), 1)
    grad.start()

    def weight_terms(t, core):
        at = pl.multiple_of((chip_of(me, t) * 2 + core) * 128, 128)
        left = acts[:, :, pl.ds(at, 128)].reshape(1024, 128)
        return dot_rows(left, dgu[...])

    def gu_to(t):
        return send(gsib.at[t], grecv.at[t], (sib0, sib1), 8 + t, me.sibling())

    @pl.loop(0, 8)
    def _(i):
        gsib[7 - i] = weight_terms(7 - i, 1 - me.co).astype(BF)
        gu_to(7 - i).start()

    grad.turn(1)

    @pl.loop(0, 8)
    def _(i):
        gu_to(7 - i).wait_recv()
        gown[7 - i] = (weight_terms(7 - i, me.co) + grecv[7 - i].astype(F32)).astype(BF)

        @pl.when(i == 1)
        def _():
            first.start()

    grad.turn(0)
    first.turn(1)

    def down_to(t):
        mine = pl.ds(pl.multiple_of((1 - me.co) * 352, 16), 352)
        return send(gd.at[t, mine], gdrecv.at[t], (sib0, sib1), t, me.sibling())

    @pl.loop(0, 8)
    def _(t):
        at = pl.multiple_of(chip_of(me, t) * 256, 256)
        gd[t] = dot_rows(hid[...], dy[:, :, pl.ds(at, 256)].reshape(1024, 256)).astype(BF)
        down_to(t).start()

    first.turn(0)
    grad.pair()
    first.pair()

    @pl.loop(0, 8)
    def _(t):
        down_to(t).wait_recv()

        @pl.loop(0, 22)
        def _(i):
            mine = gd[t, pl.ds(pl.multiple_of(me.co * 352 + i * 16, 16), 16)].astype(F32)
            at = pl.ds(pl.multiple_of(i * 16, 16), 16)
            gdown[t, at] = (mine + gdrecv[t, at].astype(F32)).astype(BF)

    first.finish(gu_out)
    grad.finish(da2_out)
    for job in (task, down, grad, first):
        job.end()

    @pl.loop(0, 8)
    def _(t):
        gu_to(t).wait_send()
        down_to(t).wait_send()


def feed_forward(a2, gu, dn, dy, dy_own):
    scratch = [
        pltpu.VMEM((8, 128, 2048), BF),
        pltpu.VMEM((2048, 1536), BF),
        pltpu.VMEM((768, 2048), BF),
        pltpu.VMEM((8, 128, 2048), BF),
        pltpu.VMEM((1024, 768), BF),
        pltpu.VMEM((1024, 1536), BF),
        pltpu.VMEM((8, 128, 2048), BF),
        *scatter_buffers(128, 2048),
        pltpu.VMEM((8, 128, 1536), BF),
        pltpu.VMEM((8, 128, 1536), BF),
        pltpu.VMEM((8, 128, 1536), BF),
        pltpu.VMEM((8, 768, 256), BF),
        pltpu.VMEM((8, 352, 256), BF),
        *scatter_buffers(128, 1536),
        *dma_sems(1, 9),
        *dma_sems(1, 9),
        *dma_sems(1, 10),
        *dma_sems(2, 9),
        pltpu.SemaphoreType.DMA((16,)),
        pltpu.SemaphoreType.DMA((16,)),
        pltpu.SemaphoreType.DMA((4,)),
    ]
    return pl.pallas_call(
        mlp_kernel,
        out_shape=(
            jax.ShapeDtypeStruct((128, 2048), F32),
            jax.ShapeDtypeStruct((8, 128, 2048), BF),
            jax.ShapeDtypeStruct((128, 1536), BF),
            jax.ShapeDtypeStruct((8, 352, 256), BF),
        ),
        in_specs=[VMEM, ANY, ANY, ANY, ANY],
        out_specs=[VMEM] * 4,
        scratch_shapes=scratch,
        compiler_params=params(4, 62),
        name="feed_forward",
    )(a2, gu, dn, dy, dy_own)


def load(src, dst, sem):
    copy = pltpu.make_async_copy(src, dst, sem)
    copy.start()
    return copy


def turned(values):
    lane = lax.broadcasted_iota(jnp.int32, values.shape, 1)
    low = lax.rem(lane, 64) < 32
    return jnp.where(low, pltpu.roll(values, 96, 1), pltpu.roll(values, 32, 1))


def pile(out, values, half):
    for h in range(8):
        out[pl.ds(64 * h, 64), :] = values[64 * half : 64 * half + 64, 64 * h : 64 * h + 64]


def unpile(values):
    flat = values.T
    return [
        jnp.concatenate([flat[128 * m : 128 * m + 64], flat[128 * m + 64 : 128 * m + 128]], axis=1)
        for m in range(4)
    ]


def norm_scale(ref, out):
    values = ref[...].astype(F32)
    out[...] = lax.rsqrt(jnp.mean(values * values, axis=1, keepdims=True) + EPS)


def front_kernel(
    x, gains_in, q_in, kw_in, wo_in, gu_in, dn_in, dy_in, cosine, sine, bias_p, bias_c, partner,
    gains, q_out, kw_out, wo_out, gu_all, dn_out, dy_all, a1, qst, kst, vst, att, lse, h1, a2,
    qw, kw, wo, kv_own, kv, sT, pT, scale, gu_own,
    s0, s1, t0, t1, y0, y1, u0, u1, w0, w1, local,
):
    me = Place()
    greet_all(me)
    swap = Swap(me, dn_in.at[:, pl.ds(pl.multiple_of(me.c * 256, 256), 256)], dn_out, (w0, w1), local.at[10])

    def rows_at(ref, rows):
        def loc(dr, dp, er, ep, half):
            size = rows if half is None else rows // 2
            first = me.fsdp_at(dr, dp) * rows + (0 if half is None else half * size)
            return ref.at[pl.ds(pl.multiple_of(first, size), size)]

        return loc

    def gains_at(dr, dp, er, ep, half):
        return gains.at[me.fsdp_at(dr, dp), row_half(half, 16)]

    def slot_at(ref, rows):
        def loc(dr, dp, er, ep, half):
            return ref.at[slot_of(dr - er, dp + ep), row_half(half, rows)]

        return loc

    def columns(first, index):
        return pl.ds(pl.multiple_of(first + index * 128, 128), 128)

    def plain(ref, count):
        def loc(dr, dp, er, ep, half):
            return ref.at[me.chip_at(dr, dp), me.co, row_half(half, 128), pl.ds(0, count)]

        return loc

    def strip_x(ref, first):
        def loc(dr, dp, er, ep, half):
            return ref.at[me.chip_at(dr, dp), me.co, row_half(half, 128), columns(first, me.c)]

        return loc

    def strip_y(ref, first):
        def loc(dr, dp, er, ep, half):
            chips = pl.ds(0, 8) if half is None else pl.ds(4 * half, 4)
            return ref.at[chips, me.co, :, columns(first, me.ctx_at(dr, dp))]

        return loc

    def over_x(own, loc, row, both=True):
        return Gather(me.across_x, own, loc, (s0, s1), row, me.sibling() if both else None, (t0, t1))

    def over_y(loc, row):
        own = loc(0, 0, 0, 0, None)
        return Gather(me.across_y, own, loc, (y0, y1), row, me.sibling(), (u0, u1))

    g = over_x(gains_in, gains_at, 0)
    k = over_x(kw_in, plain(kw, 512), 6)
    q = over_x(q_in.at[:, pl.ds(0, 1024)], plain(qw, 1024), 1)
    qx = over_x(q_in.at[:, columns(1024, me.c)], strip_x(qw, 1024), 2, both=False)
    o = over_x(wo_in.at[:, pl.ds(0, 1024)], plain(wo, 1024), 3)
    ox = over_x(wo_in.at[:, columns(1024, me.c)], strip_x(wo, 1024), 4, both=False)
    m = over_x(gu_in, rows_at(gu_all, 128), 5)
    qy = over_y(strip_y(qw, 1024), 0)
    oy = over_y(strip_y(wo, 1024), 1)
    dy = Gather(me.across_y, dy_in, slot_at(dy_all, 128), (y0, y1), 2)
    kv_task = Gather(me.across_y, kv_own, slot_at(kv, 128), (y0, y1), 3)
    kept = [load(task.own, task.loc(0, 0, 0, 0, None), local.at[i]) for i, task in enumerate((g, q, qx, o, ox, k))]
    kept.append(load(gu_in, gu_own, local.at[6]))

    def normed():
        norm_scale(x, scale)
        kept[0].wait()

        @pl.loop(0, 16)
        def _(i):
            at = pl.ds(pl.multiple_of(i * 128, 128), 128)
            a1[:, at] = (x[:, at].astype(F32) * scale[...] * gains[i, pl.ds(0, 1), :]).astype(BF)

    def project_kv():
        kept[5].wait()
        raw = dot_in(a1[...], kw[...].reshape(2048, 512))
        for i in range(2):
            part = raw[:, 128 * i : 128 * i + 128]
            kv_own[:, 128 * i : 128 * i + 128] = (part * cosine[...] + turned(part) * sine[...]).astype(BF)
        kv_own[:, 256:] = raw[:, 256:].astype(BF)
        kv[0] = kv_own[...]

    def project_q():
        @pl.loop(0, 4)
        def _(n):
            raw = dot_in(a1[...], qw[:, :, :, pl.ds(pl.multiple_of(512 * n, 512), 512)].reshape(2048, 512))
            for i in range(4):
                part = raw[:, 128 * i : 128 * i + 128]
                part = ((part * cosine[...] + turned(part) * sine[...]).astype(BF).astype(F32) * SCALE).astype(BF)
                for half in (0, 1):
                    for e in (0, 1):
                        rows = pl.ds(64 * (2 * i + e), 64)
                        qst[n, half, rows, :] = part[64 * half : 64 * half + 64, 64 * e : 64 * e + 64]

    def collect_kv():
        mate = partner[0]
        beside = kv[mate]
        for out, base in ((kst, 0), (vst, 256)):
            for n in range(4):
                first = base + 64 * n
                for slot in range(8):
                    out[n, pl.ds(64 * slot, 64), :] = kv[slot, 0:64, first : first + 64]
                out[n, pl.ds(512, 64), :] = beside[64:128, first : first + 64]
                out[n, pl.ds(576, 64), :] = kv_own[64:128, first : first + 64]

    def attend(n, half):
        count = 512 if half == 0 else 640
        keys = pl.ds(0, count)
        sT[keys] = dot_back(kst[n, keys, :], qst[n, half])
        for i in range(4):
            at = pl.ds(128 * i, 128)
            if half == 0:
                scores = sT[keys, at] + bias_p[...]
                peak = jnp.max(scores, axis=0, keepdims=True)
                raised = jnp.exp(scores - peak)
                total = jnp.sum(raised, axis=0, keepdims=True)
                pT[keys, at] = (raised * (1.0 / total)).astype(BF)
            else:
                first = sT[0:512, at]
                rest = sT[512:640, at] + bias_c[...]
                peak = jnp.maximum(
                    jnp.max(first, axis=0, keepdims=True), jnp.max(rest, axis=0, keepdims=True)
                )
                first = jnp.exp(first - peak)
                rest = jnp.exp(rest - peak)
                total = jnp.sum(first, axis=0, keepdims=True) + jnp.sum(rest, axis=0, keepdims=True)
                pT[0:512, at] = (first * (1.0 / total)).astype(BF)
                pT[512:640, at] = (rest * (1.0 / total)).astype(BF)
            lse[2 * n + half, :, at] = peak + jnp.log(total)
        for i, block in enumerate(unpile(dot_rows(vst[n, keys, :], pT[keys]))):
            first = pl.multiple_of(512 * n + 128 * i, 128)
            att[pl.ds(64 * half, 64), pl.ds(first, 128)] = block.astype(BF)

    def project_o():
        @pl.loop(0, 4)
        def _(n):
            at = pl.ds(pl.multiple_of(512 * n, 512), 512)
            h1[:, at] = x[:, at].astype(F32) + dot_in(att[...], wo[:, :, :, at].reshape(2048, 512))

    def normed_two():
        norm_scale(h1, scale)

        @pl.loop(0, 16)
        def _(i):
            at = pl.ds(pl.multiple_of(i * 128, 128), 128)
            a2[:, at] = (h1[:, at] * scale[...] * gains[i, pl.ds(8, 1), :]).astype(BF)

    qx.start()
    k.start()
    g.start()
    ox.start()
    dy.start()
    qx.pair()
    qx.turn(0)
    k.turn(0)
    g.pair()
    qx.turn(1)
    ox.pair()
    k.pair()
    k.last(0)
    qx.last(0)
    g.turn(0)
    g.turn(1)
    ox.turn(0)
    qx.last(1)
    ox.turn(1)
    kept[2].wait()
    qy.start()
    q.start()
    dy.pair()
    k.turn(1)
    o.start()
    g.last(0)
    m.start()
    g.last(1)
    ox.last(0)
    k.last(1)
    ox.last(1)
    g.sync()
    qy.pair()
    k.sync()
    q.turn(0)
    normed()
    project_kv()
    qy.turn(0)
    o.turn(0)
    kept[4].wait()
    oy.start()
    o.pair()
    qy.turn(1)
    q.pair()
    kv_task.start()
    o.last(0)
    qy.last(0)
    oy.pair()
    q.last(0)
    o.turn(1)
    q.turn(1)
    m.pair()
    kv_task.pair()
    oy.turn(0)
    q.last(1)
    qy.last(1)
    kv_task.turn(1)
    kv_task.turn(0)
    o.last(1)
    oy.turn(1)
    m.turn(0)
    dy.turn(0)
    dy.turn(1)
    q.sync()
    qy.sync()
    kept[1].wait()
    kept[6].wait()
    saved = [load(qw, q_out, local.at[7]), load(kw, kw_out, local.at[8])]
    saved.append(load(gu_own, m.loc(0, 0, 0, 0, None), local.at[6]))
    project_q()
    swap.start()
    kv_task.last(1)
    kv_task.last(0)
    oy.last(0)
    collect_kv()
    m.turn(1)

    @pl.loop(0, 4)
    def _(n):
        attend(n, 0)
        attend(n, 1)

        @pl.when(n == 1)
        def _():
            oy.last(1)

        @pl.when(n == 2)
        def _():
            o.sync()

    oy.sync()
    m.last(0)
    m.last(1)
    dy.last(0)
    kept[3].wait()
    saved.append(load(wo, wo_out, local.at[9]))
    project_o()
    normed_two()
    m.sync()
    dy.last(1)
    for task in (g, k, q, qx, o, ox, m, qy, oy, dy, kv_task):
        task.end()
    swap.wait()
    for copy in saved:
        copy.wait()


def front(x, gains, q, kw, wo, gu, dn, dy, cosine, sine, bias_p, bias_c, partner):
    return pl.pallas_call(
        front_kernel,
        out_shape=(
            jax.ShapeDtypeStruct((16, 16, 128), F32),
            jax.ShapeDtypeStruct((8, 2, 128, 2048), BF),
            jax.ShapeDtypeStruct((8, 2, 128, 512), BF),
            jax.ShapeDtypeStruct((8, 2, 128, 2048), BF),
            jax.ShapeDtypeStruct((2048, 1536), BF),
            jax.ShapeDtypeStruct((352, 256), BF),
            jax.ShapeDtypeStruct((8, 128, 2048), BF),
            jax.ShapeDtypeStruct((128, 2048), BF),
            jax.ShapeDtypeStruct((4, 2, 512, 64), BF),
            jax.ShapeDtypeStruct((4, 640, 64), BF),
            jax.ShapeDtypeStruct((4, 640, 64), BF),
            jax.ShapeDtypeStruct((128, 2048), BF),
            jax.ShapeDtypeStruct((8, 1, 512), F32),
            jax.ShapeDtypeStruct((128, 2048), F32),
            jax.ShapeDtypeStruct((128, 2048), BF),
        ),
        in_specs=[VMEM] + [ANY] * 7 + [VMEM] * 4 + [pl.BlockSpec(memory_space=pltpu.SMEM)],
        out_specs=[VMEM] + [ANY] * 6 + [VMEM] * 8,
        scratch_shapes=[
            pltpu.VMEM((8, 2, 128, 2048), BF),
            pltpu.VMEM((8, 2, 128, 512), BF),
            pltpu.VMEM((8, 2, 128, 2048), BF),
            pltpu.VMEM((128, 512), BF),
            pltpu.VMEM((8, 128, 512), BF),
            pltpu.VMEM((640, 512), F32),
            pltpu.VMEM((640, 512), BF),
            pltpu.VMEM((128, 1), F32),
            pltpu.VMEM((128, 1536), BF),
            *dma_sems(7, 9),
            *dma_sems(7, 10),
            *dma_sems(4, 9),
            *dma_sems(2, 10),
            pltpu.SemaphoreType.DMA,
            pltpu.SemaphoreType.DMA,
            pltpu.SemaphoreType.DMA((11,)),
        ],
        compiler_params=params(1, 62),
        name="front",
    )(x, gains, q, kw, wo, gu, dn, dy, cosine, sine, bias_p, bias_c, partner)


def back_kernel(
    da2, h1, dy, x, gains, wo_in, q_in, kw_in, qst, kst, vst, lse, cosine, sine, bias_p, bias_c, partner,
    a1_in, att_in, mpart_in, gu, gdown_in,
    mixed, tokens_grad, q_out, kv_out, o_out, gains_out, gu_all, dn_all,
    a1s, atts, dqkvs, datts, grow, dh1, gown, gsib, mpart, stream, dost, sT, dT, pT, dsT,
    kgrad, vgrad, kvp, dkv, da1, gdown, dn_sum, dnp, gu_own,
    qp, op, kp, gp, ggot, q_sum, o_sum, kv_sum, g_sum,
    q_half, q_full, q_pair, o_half, o_full, o_pair, k_half, k_full, k_pair, e_half, e_full, e_pair,
    m_half, m_full, m_pair, d_half, d_full, d_pair, n_half, n_full, n_pair,
    o_got, q_got, k_got,
    sib0, sib1, x0, x1, y0, y1, ag0, ag1, z0, z1, swap0, swap1, local,
):
    me = Place()
    greet_all(me, plane=True)
    nload = load(gdown_in, gdown, local.at[0])
    own, other = pl.ds(0, 128), pl.ds(128, 128)
    mload = load(mpart_in, mpart, local.at[1])
    guload = load(gu, gu_own, local.at[6])
    a1load = load(a1_in, a1s.at[own], local.at[2])
    attload = load(att_in, atts.at[own], local.at[3])

    def wo_load(n):
        return pltpu.make_async_copy(
            wo_in.at[pl.ds(512 * n, 512)], stream.at[n % 2, :, pl.ds(0, 2048)], local.at[4 + n % 2]
        )

    def qkv_load(n):
        rows = pl.ds(512 * n, 512)
        return (
            pltpu.make_async_copy(q_in.at[rows], stream.at[n % 2, :, pl.ds(0, 2048)], local.at[4 + n % 2]),
            pltpu.make_async_copy(kw_in.at[rows], stream.at[n % 2, :, pl.ds(2048, 512)], local.at[9 + n % 2]),
        )

    wo_load(0).start()
    wo_load(1).start()

    over_x, over_y, over_ag, over_sum = (x0, x1), (y0, y1), (ag0, ag1), (z0, z1)
    o_job = Scatter(me.across_x, lambda slot: op.at[slot], 128, o_half, o_full, o_pair, over_x, 0)
    q_job = Scatter(me.across_x, lambda slot: qp.at[slot], 128, q_half, q_full, q_pair, over_x, 1)
    k_job = Scatter(me.across_x, lambda slot: kp.at[slot], 128, k_half, k_full, k_pair, over_x, 2)
    e_job = Scatter(me.across_x, lambda slot: gp.at[slot], 16, e_half, e_full, e_pair, over_x, 3)
    n_job = Scatter(me.across_x, lambda slot: gdown.at[slot], 352, n_half, n_full, n_pair, over_x, 4)
    dn_swap = Swap(me, dn_sum, dnp, (swap0, swap1), local.at[8])
    m_job = Scatter(me.across_y, lambda slot: mpart.at[slot], 128, m_half, m_full, m_pair, over_y, 0)
    d_job = Scatter(me.across_y, lambda slot: kvp.at[slot], 128, d_half, d_full, d_pair, over_y, 1)

    def at_ctx(ref):
        def loc(dr, dp, er, ep, half):
            return ref.at[me.ctx_at(dr, dp), row_half(half, ref.shape[1])]

        return loc

    def dn_at(dr, dp, er, ep, half):
        first = pl.multiple_of(me.ctx_at(dr, dp) * 256, 256)
        return dn_all.at[row_half(half, 352), pl.ds(first, 256)]

    gu_task = Gather(me.across_y, gu_own, at_ctx(gu_all), over_ag, 0)
    dn_task = Gather(me.across_y, dnp, dn_at, over_ag, 1)
    def block_at(ref, slot):
        first = pl.multiple_of(me.ctx_at(STEPS[slot], PAIRS[slot]) * 16, 16)
        return ref.at[pl.ds(first, 16)]

    def sum_over_ctx(total, got, row):
        return Trade(
            me.across_y, lambda slot: block_at(total, slot), lambda slot: got.at[mirror(slot)], over_sum, row
        )

    def spread(out, row):
        return Trade(me.across_y, lambda slot: block_at(out, 0), lambda slot: block_at(out, 0), over_sum, row)

    def sum_up(total, got, out):
        value = block_at(total, 0)[...].astype(F32)
        for slot in range(1, 8):
            value = value + got[slot].astype(F32)
        block_at(out, 0)[...] = value.astype(BF)

    o_sums = sum_over_ctx(o_sum, o_got, 0)
    q_sums = sum_over_ctx(q_sum, q_got, 1)
    k_sums = sum_over_ctx(kv_sum, k_got, 2)
    o_spread = spread(o_out, 3)
    q_spread = spread(q_out, 4)
    k_spread = spread(kv_out, 5)
    e_task = Trade(me.across_y, lambda slot: g_sum, lambda slot: ggot.at[me.c], over_sum, 6)

    swap = lambda src, dst, index: send(src, dst, (sib0, sib1), index, me.sibling())
    att_swap = swap(atts.at[own], atts.at[other], 0)
    datt_swap = swap(datts.at[own], datts.at[other], 1)
    a1_swap = swap(a1s.at[own], a1s.at[other], 2)
    queries = pl.ds(0, 2048)
    dq_swap = swap(dqkvs.at[own, queries], dqkvs.at[other, queries], 3)
    rest = pl.ds(2048, 512)
    dkv_swap = swap(dqkvs.at[own, rest], dqkvs.at[other, rest], 4)
    gain_swap = swap(gown, gsib, 5)

    for i in range(16):
        grow[0, :, 128 * i : 128 * i + 128] = gains[i, 0:1, :]
        grow[1, :, 128 * i : 128 * i + 128] = gains[i, 8:9, :]
    grow[2] = jnp.zeros((1, 2048), F32)
    grow[3] = jnp.zeros((1, 2048), F32)
    kept = []

    def norm_two_back():
        @pl.loop(0, 8)
        def _(i):
            at = pl.ds(pl.multiple_of(16 * i, 16), 16)
            values, grad = h1[at], da2[at]
            scale = lax.rsqrt(jnp.mean(values * values, axis=1, keepdims=True) + EPS)
            grow[3] += jnp.sum(grad * values * scale, axis=0, keepdims=True)
            grad = grad * grow[1]
            level = jnp.mean(grad * values, axis=1, keepdims=True) * scale * scale * scale
            total = dy[at].astype(F32) + scale * grad - values * level
            dh1[at] = total
            datts[at] = total.astype(BF)

        datt_swap.start()

    def heads_back():
        for n in range(4):
            wo_load(n).wait()
            part = dot_back(datts[own], stream[n % 2, :, 0:2048]).astype(BF)
            for half in (0, 1):
                pile(dost.at[n, half], part, half)
            if n < 2:
                wo_load(n + 2).start()
        for n in range(2):
            for copy in qkv_load(n):
                copy.start()

    def terms(left, right, out, job):
        @pl.loop(0, 8)
        def _(i):
            at = pl.multiple_of((chip_of(me, 7 - i) * 2 + me.co) * 128, 128)
            out[7 - i] = dot_rows(left[:, pl.ds(at, 128)], right[...]).astype(BF)

            @pl.when(i == 1)
            def _():
                job.start()

    def output_terms():
        att_swap.wait_recv()
        datt_swap.wait_recv()
        terms(atts, datts, op, o_job)

    def query_terms():
        a1_swap.wait_recv()
        dq_swap.wait_recv()
        terms(a1s, dqkvs.at[:, pl.ds(0, 2048)], qp, q_job)

    def kv_terms():
        dkv_swap.wait_recv()
        terms(a1s, dqkvs.at[:, pl.ds(2048, 512)], kp, k_job)

    def kv_blocks():
        mate = partner[0]
        for out, base in ((kgrad, 0), (vgrad, 256)):
            for n in range(4):
                first = base + 64 * n
                for slot in range(8):
                    kvp[slot, 0:64, first : first + 64] = out[n, 64 * slot : 64 * slot + 64, :]
                    if slot == 0:
                        late = out[n, 576:640, :]
                    else:
                        late = jnp.where(mate == slot, out[n, 512:576, :], jnp.zeros((64, 64), BF))
                    kvp[slot, 64:128, first : first + 64] = late

    def kv_back():
        for i in range(2):
            at = slice(128 * i, 128 * i + 128)
            block = dkv[:, at]
            dqkvs[own, 2048 + 128 * i : 2176 + 128 * i] = (block * cosine[...] - turned(block) * sine[...]).astype(BF)
        dqkvs[own, 2304:2560] = dkv[:, 256:512].astype(BF)
        dkv_swap.start()

    def inputs_back():
        for n in range(4):
            for copy in qkv_load(n):
                copy.wait()
            da1[:, 512 * n : 512 * n + 512] = dot_back(dqkvs[own], stream[n % 2])
            if n < 2:
                for copy in qkv_load(n + 2):
                    copy.start()

    def norm_one_back():
        @pl.loop(0, 8)
        def _(i):
            at = pl.ds(pl.multiple_of(16 * i, 16), 16)
            values, grad = x[at].astype(F32), da1[at]
            scale = lax.rsqrt(jnp.mean(values * values, axis=1, keepdims=True) + EPS)
            grow[2] += jnp.sum(grad * values * scale, axis=0, keepdims=True)
            grad = grad * grow[0]
            level = jnp.mean(grad * values, axis=1, keepdims=True) * scale * scale * scale
            tokens_grad[at] = (dh1[at] + scale * grad - values * level).astype(BF)

        gown[...] = jnp.zeros((16, 16, 128), F32)
        for i in range(16):
            gown[i, 0:1, :] = grow[2, :, 128 * i : 128 * i + 128]
            gown[i, 8:9, :] = grow[3, :, 128 * i : 128 * i + 128]
        gain_swap.start()

    def gain_terms():
        gain_swap.wait_recv()
        for slot in range(8):
            block = me.fsdp_at(STEPS[slot], PAIRS[slot])
            gp[slot] = gown[block] + gsib[block]

    def dn_begin():
        dn_swap.wait()
        dn_task.start()
        kept.append(load(dnp, dn_at(0, 0, 0, 0, None), local.at[7]))

    def gu_begin():
        guload.wait()
        kept.append(load(gu_own, gu_all.at[me.c], local.at[6]))
        gu_task.start()

    def e_begin():
        e_task.start()
        ggot[me.c] = g_sum[...]

    def attend(n, half):
        count = 512 if half == 0 else 640
        keys = pl.ds(0, count)
        key, query, out = kst[n, keys, :], qst[n, half], dost[n, half]
        sT[keys] = dot_back(key, query)
        dT[keys] = dot_back(vst[n, keys, :], out)
        for i in range(4):
            at = pl.ds(128 * i, 128)
            parts = []
            for first, size in ((0, 512), (512, 128))[: 1 + half]:
                scores = sT[first : first + size, at]
                if half == 0:
                    scores = scores + bias_p[...]
                elif first:
                    scores = scores + bias_c[...]
                probs = jnp.exp(scores - lse[2 * n + half, :, at])
                grad = dT[first : first + size, at]
                parts.append((first, size, probs, grad))
            level = sum(jnp.sum(probs * grad, axis=0, keepdims=True) for _, _, probs, grad in parts)
            for first, size, probs, grad in parts:
                pT[first : first + size, at] = probs.astype(BF)
                dsT[first : first + size, at] = (probs * (grad - level)).astype(BF)
        rows = slice(64 * half, 64 * half + 64)
        for i, block in enumerate(unpile(dot_rows(key, dsT[keys]) * SCALE)):
            block = block * cosine[rows] - turned(block) * sine[rows]
            first = pl.multiple_of(512 * n + 128 * i, 128)
            dqkvs[rows, pl.ds(first, 128)] = block.astype(BF)
        return dot_in(dsT[keys], query), dot_in(pT[keys], out)

    nload.wait()
    n_job.start()
    gu_begin()
    a1load.wait()
    a1_swap.start()
    norm_two_back()
    n_job.turn(1)
    attload.wait()
    att_swap.start()
    n_job.turn(0)
    mload.wait()
    m_job.start()
    output_terms()
    heads_back()
    n_job.pair()

    @pl.loop(0, 4)
    def _(n):
        key_one, value_one = attend(n, 0)
        key_two, value_two = attend(n, 1)
        for out, one, two in ((kgrad, key_one, key_two), (vgrad, value_one, value_two)):
            out[n, 0:512] = (one + two[0:512]).astype(BF)
            out[n, 512:640] = two[512:640].astype(BF)

        @pl.when(n == 0)
        def _():
            m_job.turn(1)
            o_job.turn(1)

        @pl.when(n == 2)
        def _():
            n_job.finish(dn_sum)

    kv_blocks()
    d_job.start()
    o_job.turn(0)
    gu_task.turn(0)
    m_job.pair()
    dq_swap.start()
    d_job.turn(1)
    dn_swap.start()
    d_job.turn(0)
    query_terms()
    o_job.pair()
    gu_task.pair()
    m_job.turn(0)
    d_job.pair()
    q_job.turn(1)
    gu_task.turn(1)
    dn_begin()
    o_job.finish(o_sum)
    o_sums.start()
    gu_task.last(0)
    d_job.finish(dkv)
    kv_back()
    kv_terms()
    q_job.turn(0)
    q_job.pair()
    dn_task.pair()
    gu_task.last(1)
    inputs_back()
    k_job.turn(1)
    norm_one_back()
    o_sums.got()
    sum_up(o_sum, o_got, o_out)
    o_spread.start()
    m_job.finish(mixed, (h1,))
    k_job.turn(0)
    gain_terms()
    dn_task.turn(0)
    q_job.finish(q_sum)
    k_job.pair()
    q_sums.start()
    e_job.start()
    o_spread.got()
    k_job.finish(kv_sum)
    dn_task.turn(1)
    e_job.turn(1)
    e_job.pair()
    k_sums.start()
    q_sums.got()
    sum_up(q_sum, q_got, q_out)
    q_spread.start()
    e_job.turn(0)
    e_job.finish(g_sum)
    e_begin()
    dn_task.last(0)
    dn_task.last(1)
    k_sums.got()
    sum_up(kv_sum, k_got, kv_out)
    k_spread.start()
    q_spread.got()
    e_task.got()
    k_spread.got()
    total = ggot[0]
    for index in range(1, 8):
        total = total + ggot[index]
    gains_out[...] = total
    jobs = (o_job, q_job, k_job, e_job, m_job, d_job, n_job, o_sums, q_sums, k_sums)
    for job in (*jobs, gu_task, dn_task, e_task, o_spread, q_spread, k_spread):
        job.end()
    for copy in (att_swap, datt_swap, a1_swap, dq_swap, dkv_swap, gain_swap):
        copy.wait_send()
    for copy in kept:
        copy.wait()


def back(da2, h1, dy, x, gains, wo, q, kw, qst, kst, vst, lse, cosine, sine, bias_p, bias_c, partner, a1, att, mpart, gu, gdown):
    scratch = [
        pltpu.VMEM((256, 2048), BF),
        pltpu.VMEM((256, 2048), BF),
        pltpu.VMEM((256, 2560), BF),
        pltpu.VMEM((256, 2048), BF),
        pltpu.VMEM((4, 1, 2048), F32),
        pltpu.VMEM((128, 2048), F32),
        pltpu.VMEM((16, 16, 128), F32),
        pltpu.VMEM((16, 16, 128), F32),
        pltpu.VMEM((8, 128, 2048), BF),
        pltpu.VMEM((2, 512, 2560), BF),
        pltpu.VMEM((4, 2, 512, 64), BF),
        pltpu.VMEM((640, 512), F32),
        pltpu.VMEM((640, 512), F32),
        pltpu.VMEM((640, 512), BF),
        pltpu.VMEM((640, 512), BF),
        pltpu.VMEM((4, 640, 64), BF),
        pltpu.VMEM((4, 640, 64), BF),
        pltpu.VMEM((8, 128, 512), BF),
        pltpu.VMEM((128, 512), F32),
        pltpu.VMEM((128, 2048), F32),
        pltpu.VMEM((8, 352, 256), BF),
        pltpu.VMEM((352, 256), BF),
        pltpu.VMEM((352, 256), BF),
        pltpu.VMEM((128, 1536), BF),
        pltpu.VMEM((8, 128, 2048), BF),
        pltpu.VMEM((8, 128, 2048), BF),
        pltpu.VMEM((8, 128, 512), BF),
        pltpu.VMEM((8, 16, 128), F32),
        pltpu.VMEM((8, 16, 128), F32),
        pltpu.VMEM((128, 2048), BF),
        pltpu.VMEM((128, 2048), BF),
        pltpu.VMEM((128, 512), BF),
        pltpu.VMEM((16, 128), F32),
        *scatter_buffers(128, 2048),
        *scatter_buffers(128, 2048),
        *scatter_buffers(128, 512),
        *scatter_buffers(16, 128, F32),
        *scatter_buffers(128, 2048),
        *scatter_buffers(128, 512),
        *scatter_buffers(352, 256),
        pltpu.VMEM((8, 16, 2048), BF),
        pltpu.VMEM((8, 16, 2048), BF),
        pltpu.VMEM((8, 16, 512), BF),
        pltpu.SemaphoreType.DMA((6,)),
        pltpu.SemaphoreType.DMA((6,)),
        *dma_sems(5, 9),
        *dma_sems(2, 9),
        *dma_sems(2, 9),
        *dma_sems(7, 8),
        pltpu.SemaphoreType.DMA,
        pltpu.SemaphoreType.DMA,
        pltpu.SemaphoreType.DMA((11,)),
    ]
    return pl.pallas_call(
        back_kernel,
        out_shape=(
            jax.ShapeDtypeStruct((128, 2048), BF),
            jax.ShapeDtypeStruct((128, 2048), BF),
            jax.ShapeDtypeStruct((128, 2048), BF),
            jax.ShapeDtypeStruct((128, 512), BF),
            jax.ShapeDtypeStruct((128, 2048), BF),
            jax.ShapeDtypeStruct((16, 128), F32),
            jax.ShapeDtypeStruct((8, 128, 1536), BF),
            jax.ShapeDtypeStruct((352, 2048), BF),
        ),
        in_specs=[VMEM] * 5 + [ANY] * 3 + [VMEM] * 8 + [pl.BlockSpec(memory_space=pltpu.SMEM)] + [ANY] * 5,
        out_specs=[VMEM] * 6 + [ANY] * 2,
        scratch_shapes=scratch,
        compiler_params=params(5, 62),
        name="back",
    )(da2, h1, dy, x, gains, wo, q, kw, qst, kst, vst, lse, cosine, sine, bias_p, bias_c, partner, a1, att, mpart, gu, gdown)


def widen_kernel(parts, gate, up):
    for out, base in ((gate, 0), (up, 768)):
        for pair in range(4):
            even = parts[2 * pair, :, base : base + 768].astype(F32)
            odd = pltpu.roll(parts[2 * pair + 1, :, base : base + 768].astype(F32), 64, 1)
            first = 1408 * pair
            out[:, first : first + 640] = even[:, 0:640]
            out[:, first + 640 : first + 768] = even[:, 640:768] + odd[:, 0:128]
            out[:, first + 768 : first + 1408] = odd[:, 128:768]


def widen(parts):
    out = jax.ShapeDtypeStruct((128, 5632), F32)
    block = pl.BlockSpec((16, 5632), lambda i: (i, 0))
    return pl.pallas_call(
        widen_kernel,
        grid=(8,),
        out_shape=(out, out),
        in_specs=[pl.BlockSpec((8, 16, 1536), lambda i: (0, i, 0))],
        out_specs=[block, block],
        name="widen",
    )(parts)


def tables(position):
    freq = BASE ** (-(jnp.arange(HEAD_DIM // 2, dtype=jnp.float32) * 2.0) / HEAD_DIM)
    angle = position.astype(jnp.float32)[:, None] * freq[None, :]
    angle = jnp.concatenate([angle, angle], axis=-1)
    return (jnp.cos(angle), jnp.sin(angle))


def timeline(table_flat, total_len, row_count):
    everywhere = jnp.arange(total_len, dtype=jnp.int32)
    half_len = row_count // 2
    moment = jnp.repeat(table_flat, half_len) * half_len + everywhere % half_len
    prompt_len = total_len // 2
    cont_len = total_len // 8
    later = moment >= prompt_len
    segment = jnp.where(later, 1 + (moment - prompt_len) // cont_len, 0)
    position = jnp.where(later, prompt_len + (moment - prompt_len) % cont_len, moment)
    return (segment, position)


def on_device(
    tokens,
    block_deal,
    attn_gain,
    query_weight,
    key_weight,
    value_weight,
    output_weight,
    mlp_gain,
    gate_weight,
    up_weight,
    down_weight,
    cotangent,
):
    row_count = tokens.shape[1]
    c = lax.axis_index("ctx")
    f = lax.axis_index("fsdp")
    full_len = row_count * 8

    def sliced(weight):
        return jnp.pad(lax.dynamic_slice_in_dim(weight, c * 704, 704, 1), ((0, 0), (0, 64)))

    none = jnp.zeros((7, 128), F32)
    gains = jnp.concatenate([attn_gain.astype(F32)[None], none, mlp_gain.astype(F32)[None], none])
    kv_weight = jnp.concatenate([key_weight, value_weight], axis=1)
    gu = jnp.concatenate([sliced(gate_weight), sliced(up_weight)], axis=1)

    y, zl = c // 2, c % 2
    order = jnp.stack([((y + STEPS[s]) % 4) * 2 + (zl + PAIRS[s]) % 2 for s in range(8)])
    deal = jnp.take(lax.dynamic_index_in_dim(block_deal, f, 0, keepdims=False), order, axis=0)
    mate_block = 8 + (deal[0, 1] - 8 + 1 - 2 * ((deal[0, 1] - 8) % 2))
    mate = jnp.argmax((deal[:, 1] == mate_block).astype(jnp.int32)).astype(jnp.int32)
    segment, position = timeline(deal.reshape(-1), full_len, row_count)
    own_segment, own_position = segment[:row_count], position[:row_count]
    cosine, sine = tables(own_position)
    sign = jnp.where(jnp.arange(HEAD_DIM) < 32, -1.0, 1.0)
    cosine_two = jnp.concatenate([cosine, cosine], axis=1)
    sine_two = jnp.concatenate([sine * sign, sine * sign], axis=1)
    prompt_position = position.reshape(8, 2, 64)[:, 0].reshape(512)
    bias_p = jnp.where(prompt_position[:, None] <= own_position[None, :64], 0.0, -1e30)
    mate_seen = deal[0, 1] > mate_block
    step = jnp.arange(64)
    bias_c = jnp.concatenate(
        [
            jnp.broadcast_to(jnp.where(mate_seen, 0.0, -1e30), (64, 64)),
            jnp.where(step[:, None] <= step[None, :], 0.0, -1e30),
        ]
    )
    bias_p = jnp.concatenate([bias_p, bias_p], axis=1).astype(F32)
    bias_c = jnp.concatenate([bias_c, bias_c], axis=1).astype(F32)

    gains_all, q_all, kv_all, wo_all, gu_all, dn_all, dy_all, normed, qst, kst, vst, attended, lse, hidden_state, normed_two = front(
        tokens[0], gains, query_weight, kv_weight, output_weight, gu, down_weight, cotangent[0], cosine_two, sine_two, bias_p, bias_c, mate[None]
    )
    wo_all = wo_all.reshape(2048, 2048)
    q_all = q_all.reshape(2048, 2048)
    kv_all = kv_all.reshape(2048, 512)

    grad_normed_two, mixed_parts, gu_sum, dn_parts = feed_forward(normed_two, gu_all, dn_all, dy_all, cotangent[0])

    mixed, tokens_grad, query_grad, kv_grad, o_grad, gain_grads, gu_grads, dn_grad = back(
        grad_normed_two, hidden_state, cotangent[0], tokens[0], gains_all, wo_all, q_all, kv_all, qst, kst, vst, lse,
        cosine_two, sine_two, bias_p, bias_c, mate[None], normed, attended, mixed_parts, gu_sum, dn_parts,
    )

    gate_grad, up_grad = widen(gu_grads)
    return (
        mixed[None],
        tokens_grad[None],
        gain_grads[0],
        query_grad.astype(F32),
        kv_grad[:, :256].astype(F32),
        kv_grad[:, 256:].astype(F32),
        o_grad.astype(F32),
        gain_grads[8],
        gate_grad,
        up_grad,
        dn_grad.astype(F32),
    )


def solution(mesh):
    held = P("fsdp", "ctx", None)
    rows = P("fsdp", None)
    return jax.shard_map(
        on_device,
        mesh=mesh,
        in_specs=(held, P(), P("fsdp"), rows, rows, rows, rows, P("fsdp"), rows, rows, rows, held),
        out_specs=(held, held, P("fsdp"), rows, rows, rows, rows, P("fsdp"), rows, rows, rows),
        check_vma=False,
    )
```

```python
import functools

import jax
import jax.numpy as jnp
from jax import lax
from jax.experimental import pallas as pl
from jax.experimental.pallas import tpu as pltpu
from jax.sharding import PartitionSpec as P

MESH = pl.DeviceIdType.MESH
BF = jnp.bfloat16
F32 = jnp.float32
ANY = pl.BlockSpec(memory_space=pl.ANY)
VMEM = pl.BlockSpec(memory_space=pltpu.VMEM)

HEAD_DIM = 64
EPS = 1e-05
SCALE = 0.125
BASE = 10000.0

SLOT = {(0, 0): 0, (0, 1): 1, (1, 0): 2, (3, 0): 3, (1, 1): 4, (3, 1): 5, (2, 0): 6, (2, 1): 7}
STEPS = (0, 0, 1, 3, 1, 3, 2, 2)
PAIRS = (0, 1, 0, 0, 1, 1, 0, 1)


def slot_of(dr, dp):
    return SLOT[(dr % 4, dp % 2)]


class Place:
    def __init__(self):
        self.c = lax.axis_index("ctx")
        self.f = lax.axis_index("fsdp")
        self.y, self.zl = lax.div(self.c, 2), lax.rem(self.c, 2)
        self.j, self.co = lax.div(self.f, 2), lax.rem(self.f, 2)
        self.x, self.zh = lax.div(self.j, 2), lax.rem(self.j, 2)

    def ctx_at(self, dr, dp):
        return lax.rem(self.y + dr % 4, 4) * 2 + lax.rem(self.zl + dp, 2)

    def chip_at(self, dr, dp):
        return lax.rem(self.x + dr % 4, 4) * 2 + lax.rem(self.zh + dp, 2)

    def fsdp_at(self, dr, dp):
        return self.chip_at(dr, dp) * 2 + self.co

    def across_y(self, dr, dp):
        return {"ctx": self.ctx_at(dr, dp), "fsdp": self.f}

    def across_x(self, dr, dp):
        return {"ctx": self.c, "fsdp": self.fsdp_at(dr, dp)}

    def sibling(self):
        return {"ctx": self.c, "fsdp": self.f + 1 - 2 * self.co}


def chip_of(me, t):
    dr = jnp.where(t < 2, 0, jnp.where(t >= 6, 2, 1 + 2 * lax.rem(t, 2)))
    dp = jnp.where(t < 2, t, jnp.where(t >= 6, t - 6, lax.div(t, 4)))
    return lax.rem(me.x + dr, 4) * 2 + lax.rem(me.zh + dp, 2)


def greet(devices):
    barrier = pltpu.get_barrier_semaphore()
    for device in devices:
        pl.semaphore_signal(barrier, 1, device_id=device, device_id_type=MESH)
    pl.semaphore_wait(barrier, len(devices))


class Swap:
    def __init__(self, me, src, dst, sems, local):
        self.moved = me.c != me.j
        self.to = {"ctx": me.j, "fsdp": 2 * me.c + me.co}
        self.copy = pltpu.make_async_remote_copy(
            src, dst, sems[0], sems[1], device_id=self.to, device_id_type=MESH
        )
        self.keep = pltpu.make_async_copy(src, dst, local)

    def start(self):
        pl.when(self.moved)(self.copy.start)
        pl.when(jnp.logical_not(self.moved))(self.keep.start)

    def wait(self):
        pl.when(self.moved)(self.copy.wait)
        pl.when(jnp.logical_not(self.moved))(self.keep.wait)


def greet_all(me, plane=False):
    barrier = pltpu.get_barrier_semaphore()
    others = near(me.across_x) + [me.sibling()]
    others += [me.across_y(STEPS[s], PAIRS[s]) for s in range(1, 8)] if plane else near(me.across_y)
    for device in others:
        pl.semaphore_signal(barrier, 1, device_id=device, device_id_type=MESH)
    moved = me.c != me.j

    @pl.when(moved)
    def _():
        to = {"ctx": me.j, "fsdp": 2 * me.c + me.co}
        pl.semaphore_signal(barrier, 1, device_id=to, device_id_type=MESH)

    pl.semaphore_wait(barrier, len(others) + jnp.where(moved, 1, 0))


def near(dev):
    return [dev(1, 0), dev(-1, 0), dev(0, 1)]


def send(src, dst, sems, index, device):
    return pltpu.make_async_remote_copy(
        src, dst, sems[0].at[index], sems[1].at[index], device_id=device, device_id_type=MESH
    )


class Gather:
    MOVES = (
        ((0, 0), (0, 1), None),
        ((0, 0), (1, 0), None),
        ((0, 0), (-1, 0), None),
        ((0, 1), (1, 0), None),
        ((0, 1), (-1, 0), None),
        ((-1, 0), (1, 0), 0),
        ((-1, 1), (1, 0), 0),
        ((1, 0), (-1, 0), 1),
        ((1, 1), (-1, 0), 1),
    )

    def __init__(self, dev, own, loc, sems, row, sibling=None, sibling_sems=None):
        self.loc = loc
        self.copies = []
        for index, (block, to, half) in enumerate(self.MOVES):
            src = own if block == (0, 0) else loc(*block, 0, 0, half)
            dst = loc(*block, *to, half)
            self.copies.append(send(src, dst, sems, (row, index), dev(*to)))
        self.passed = {}
        if sibling is not None:
            self.passed[9] = send(own, loc(0, 0, 0, 0, None), sibling_sems, (row, 9), sibling)
            for index, ((dr, dp), (er, ep), half) in enumerate(self.MOVES):
                ref = loc(dr - er, dp + ep, 0, 0, half)
                self.passed[index] = send(ref, ref, sibling_sems, (row, index), sibling)
        self.own = own

    def _pass(self, index):
        if self.passed:
            self.passed[index].start()

    def _got(self, index):
        self.copies[index].wait_recv()
        self._pass(index)

    def start(self):
        for index in (0, 1, 2):
            self.copies[index].start()
        self._pass(9)

    def pair(self):
        self._got(0)
        self.copies[3].start()
        self.copies[4].start()

    def turn(self, dp):
        for got, on in (((1, 5), (2, 7)) if dp == 0 else ((3, 6), (4, 8))):
            self._got(got)
            self.copies[on].start()

    def last(self, dp):
        for got in ((5, 7) if dp == 0 else (6, 8)):
            self._got(got)

    def sync(self):
        for copy in self.passed.values():
            copy.wait()

    def end(self):
        for copy in self.copies:
            copy.wait_send()


def row_half(half, rows):
    return pl.ds(0, rows) if half is None else pl.ds(half * (rows // 2), rows // 2)


def add_into(ref, rows, others, step=16):
    step = min(step, rows)

    @pl.loop(0, rows // step)
    def _(i):
        at = pl.ds(pl.multiple_of(i * step, step), step)
        total = ref[at].astype(F32)
        for other in others:
            total = total + other[at].astype(F32)
        ref[at] = total.astype(ref.dtype)


class Scatter:
    def __init__(self, dev, part, rows, halves, fulls, paired, sems, row, cut=None):
        self.part, self.rows, self.cut = part, rows, cut
        self.halves, self.fulls, self.paired = halves, fulls, paired
        self.first, self.second = {}, {}
        for dp in (0, 1):
            for way, sign in ((0, 1), (1, -1)):
                self.first[way, dp] = send(
                    self._half(part(slot_of(2, dp)), way), halves.at[way, dp], sems, (row, way * 2 + dp), dev(sign, 0)
                )
                self.second[way, dp] = send(
                    part(slot_of(sign, dp)), fulls.at[way, dp], sems, (row, 4 + way * 2 + dp), dev(sign, 0)
                )
        self.third = send(part(slot_of(0, 1)), paired, sems, (row, 8), dev(0, 1))

    def _half(self, ref, way):
        if self.cut is None:
            return ref.at[pl.ds(way * (self.rows // 2), self.rows // 2)]
        return ref.at[:, pl.ds(way * (self.cut // 2), self.cut // 2)]

    def start(self):
        for dp in (1, 0):
            for way in (0, 1):
                self.first[way, dp].start()

    def turn(self, dp):
        for way, sign in ((0, 1), (1, -1)):
            self.first[way, dp].wait_recv()
            block = self._half(self.part(slot_of(sign, dp)), way)
            add_into(block, block.shape[0], [self.halves.at[way, dp]])
            self.second[way, dp].start()

    def pair(self):
        for way in (0, 1):
            self.second[way, 1].wait_recv()
        add_into(self.part(slot_of(0, 1)), self.rows, [self.fulls.at[0, 1], self.fulls.at[1, 1]])
        self.third.start()

    def finish(self, out, extra=()):
        for way in (0, 1):
            self.second[way, 0].wait_recv()
        self.third.wait_recv()
        own = self.part(0)
        terms = [own, self.fulls.at[0, 0], self.fulls.at[1, 0], self.paired, *extra]

        @pl.loop(0, self.rows // 16)
        def _(i):
            at = pl.ds(pl.multiple_of(i * 16, 16), 16)
            total = terms[0][at].astype(F32)
            for term in terms[1:]:
                total = total + term[at].astype(F32)
            out[at] = total.astype(out.dtype)

    def end(self):
        for copy in (*self.first.values(), *self.second.values(), self.third):
            copy.wait_send()


def mirror(slot):
    return slot_of(-STEPS[slot], PAIRS[slot])


class Trade:
    def __init__(self, dev, what, where, sems, row):
        self.copies = [
            pltpu.make_async_remote_copy(
                what(slot), where(slot), sems[0].at[row, slot], sems[1].at[row, mirror(slot)],
                device_id=dev(STEPS[slot], PAIRS[slot]), device_id_type=MESH,
            )
            for slot in range(1, 8)
        ]

    def start(self):
        for copy in self.copies:
            copy.start()

    def got(self):
        for copy in self.copies:
            copy.wait_recv()

    def end(self):
        for copy in self.copies:
            copy.wait_send()


def scatter_buffers(rows, columns, dtype=BF, cut=False):
    half = (rows, columns // 2) if cut else (rows // 2, columns)
    return [
        pltpu.VMEM((2, 2, *half), dtype),
        pltpu.VMEM((2, 2, rows, columns), dtype),
        pltpu.VMEM((rows, columns), dtype),
    ]


def dma_sems(rows, count):
    return [pltpu.SemaphoreType.DMA((rows, count)), pltpu.SemaphoreType.DMA((rows, count))]


def params(collective_id, vmem=56):
    return pltpu.CompilerParams(
        collective_id=collective_id, has_side_effects=True, vmem_limit_bytes=vmem << 20
    )


def dot_in(left, right):
    return jnp.dot(left, right, preferred_element_type=F32)


def dot_back(left, right):
    return lax.dot_general(left, right, (((1,), (1,)), ((), ())), preferred_element_type=F32)


def dot_rows(left, right):
    return lax.dot_general(left, right, (((0,), (0,)), ((), ())), preferred_element_type=F32)


def load(src, dst, sem):
    copy = pltpu.make_async_copy(src, dst, sem)
    copy.start()
    return copy


def turned(values):
    lane = lax.broadcasted_iota(jnp.int32, values.shape, 1)
    low = lax.rem(lane, 64) < 32
    return jnp.where(low, pltpu.roll(values, 96, 1), pltpu.roll(values, 32, 1))


def pile(out, values, half):
    for h in range(8):
        out[pl.ds(64 * h, 64), :] = values[64 * half : 64 * half + 64, 64 * h : 64 * h + 64]


def unpile(values):
    flat = values.T
    return [
        jnp.concatenate([flat[128 * m : 128 * m + 64], flat[128 * m + 64 : 128 * m + 128]], axis=1)
        for m in range(4)
    ]


def norm_scale(ref, out):
    values = ref[...].astype(F32)
    out[...] = lax.rsqrt(jnp.mean(values * values, axis=1, keepdims=True) + EPS)


def place_tables(me, deal, freq, cosine, sine, bias_p, bias_c):
    def block(slot, part):
        return deal[(me.f * 8 + me.ctx_at(STEPS[slot], PAIRS[slot])) * 2 + part]

    first, second = block(0, 0), block(0, 1)
    odd = lax.rem(second, 2)
    row = lax.broadcasted_iota(jnp.int32, (128, 128), 0)
    lane = lax.broadcasted_iota(jnp.int32, (128, 128), 1)
    position = jnp.where(row < 64, first * 64 + row, 448 + odd * 64 + row)
    angle = position.astype(F32) * freq[...]
    cosine[...] = jnp.cos(angle)
    sine[...] = jnp.where(lax.rem(lane, 64) < 32, -jnp.sin(angle), jnp.sin(angle))
    row, lane = row[:64], lax.rem(lane[:64], 64)
    mate = jnp.int32(0)
    for slot in range(8):
        seen = block(slot, 0) * 64 + row <= first * 64 + lane
        bias_p[pl.ds(64 * slot, 64), :] = jnp.where(seen, 0.0, -1e30)
        if slot:
            mate = mate + jnp.where(block(slot, 1) == second + 1 - 2 * odd, slot, 0)
    bias_c[pl.ds(0, 64), :] = jnp.where(odd + 0 * row == 1, 0.0, -1e30)
    bias_c[pl.ds(64, 64), :] = jnp.where(row <= lane, 0.0, -1e30)
    return mate


def find_mate(me, deal):
    def block(slot):
        return deal[(me.f * 8 + me.ctx_at(STEPS[slot], PAIRS[slot])) * 2 + 1]

    second = block(0)
    mate = jnp.int32(0)
    for slot in range(1, 8):
        mate = mate + jnp.where(block(slot) == second + 1 - 2 * lax.rem(second, 2), slot, 0)
    return mate


def fore_kernel(
    x, attn_gain, mlp_gain, deal, freq, q_in, key_in, value_in, wo_in, gate_in, up_in, dn_in, dy_in,
    gains, q_out, kw_out, wo_out, a1, qst, kst, vst, att, lse, h1, cosine, sine, bias_p, bias_c,
    da2_out, mpart, gu_out, gdown,
    qw, kw, wo, kv_own, kv, sT, pT, scale, gu_win, dnp, acts, gu, wd, dy, hid, mstage,
    d_half, d_full, d_pair, grecv, gdrecv, g_half, g_full, g_pair,
    s0, s1, t0, t1, y0, y1, u0, u1, w0, w1, rs0, rs1, sib0, sib1, local, msem,
):
    me = Place()
    greet_all(me)
    def gains_at(dr, dp, er, ep, half):
        return gains.at[me.fsdp_at(dr, dp), row_half(half, 16)]

    def slot_at(ref, rows):
        def loc(dr, dp, er, ep, half):
            return ref.at[slot_of(dr - er, dp + ep), row_half(half, rows)]

        return loc

    def columns(first, index):
        return pl.ds(pl.multiple_of(first + index * 128, 128), 128)

    def plain(ref, count):
        def loc(dr, dp, er, ep, half):
            return ref.at[me.chip_at(dr, dp), me.co, row_half(half, 128), pl.ds(0, count)]

        return loc

    def strip_x(ref, first):
        def loc(dr, dp, er, ep, half):
            return ref.at[me.chip_at(dr, dp), me.co, row_half(half, 128), columns(first, me.c)]

        return loc

    def strip_y(ref, first):
        def loc(dr, dp, er, ep, half):
            chips = pl.ds(0, 8) if half is None else pl.ds(4 * half, 4)
            return ref.at[chips, me.co, :, columns(first, me.ctx_at(dr, dp))]

        return loc

    def wd_at(dr, dp, er, ep, half):
        size = 352 if half is None else 176
        first = me.co * 352 + (0 if half is None else half * size)
        return wd.at[
            pl.ds(pl.multiple_of(first, 16), size),
            pl.ds(pl.multiple_of(me.chip_at(dr, dp) * 256, 256), 256),
        ]

    def gu_at(dr, dp, er, ep, half):
        size = 128 if half is None else 64
        first = me.fsdp_at(dr, dp) * 128 + (0 if half is None else half * size)
        return gu.at[pl.ds(pl.multiple_of(first, size), size)]

    def over_x(own, loc, row, both=True):
        own = loc(0, 0, 0, 0, None) if own is None else own
        return Gather(me.across_x, own, loc, (s0, s1), row, me.sibling() if both else None, (t0, t1))

    def over_y(own, loc, row, both=True):
        own = loc(0, 0, 0, 0, None) if own is None else own
        return Gather(me.across_y, own, loc, (y0, y1), row, me.sibling() if both else None, (u0, u1))

    g = over_x(None, gains_at, 0)
    k = over_x(None, plain(kw, 512), 1)
    q = over_x(q_in.at[:, pl.ds(0, 1024)], plain(qw, 1024), 2)
    qx = over_x(q_in.at[:, columns(1024, me.c)], strip_x(qw, 1024), 3, both=False)
    o = over_x(wo_in.at[:, pl.ds(0, 1024)], plain(wo, 1024), 4)
    ox = over_x(wo_in.at[:, columns(1024, me.c)], strip_x(wo, 1024), 5, both=False)
    m = over_x(None, gu_at, 6)
    dn = over_x(dnp, wd_at, 7)
    qy = over_y(None, strip_y(qw, 1024), 0)
    oy = over_y(None, strip_y(wo, 1024), 1)
    dy_task = over_y(dy_in, slot_at(dy, 128), 2, both=False)
    kv_task = over_y(kv_own, slot_at(kv, 128), 3, both=False)
    a = over_y(None, slot_at(acts, 128), 4, both=False)
    swap = Swap(me, dn_in.at[:, pl.ds(pl.multiple_of(me.c * 256, 256), 256)], dnp, (w0, w1), local.at[0])

    own_kw = plain(kw, 512)(0, 0, 0, 0, None)
    loads = [
        load(key_in, own_kw.at[:, pl.ds(0, 256)], local.at[1]),
        load(value_in, own_kw.at[:, pl.ds(256, 256)], local.at[2]),
    ]
    kept = {task: load(task.own, task.loc(0, 0, 0, 0, None), local.at[3 + i]) for i, task in enumerate((q, qx, o, ox, dy_task))}
    window = pl.ds(pl.multiple_of(me.y * 1408 + me.zl * 640, 128), 768)
    loads.append(load(gate_in.at[:, window], gu_win.at[0], local.at[8]))
    loads.append(load(up_in.at[:, window], gu_win.at[1], local.at[9]))
    gains[me.f] = jnp.zeros((16, 128), F32)
    gains[me.f, pl.ds(0, 1), :] = attn_gain[...].astype(F32)
    gains[me.f, pl.ds(8, 1), :] = mlp_gain[...].astype(F32)

    dpart = wo.at[:, 0]
    dgu = wo.at[:, 1, :, pl.ds(0, 1536)]
    gsib = qw.at[:, 0, :, pl.ds(0, 1536)]
    gown = qw.at[:, 1, :, pl.ds(0, 1536)]

    def gd(t):
        rows = pl.ds(pl.multiple_of(lax.div(t, 6) * 768, 768), 768)
        return gu.at[rows, pl.ds(pl.multiple_of(lax.rem(t, 6) * 256, 256), 256)]

    saved = []

    def put_gate_up():
        loads[2].wait()
        loads[3].wait()

        @pl.loop(0, 8)
        def _(i):
            rows = pl.ds(pl.multiple_of(16 * i, 16), 16)
            out = pl.ds(pl.multiple_of(me.f * 128 + 16 * i, 16), 16)
            for w in (0, 1):
                values = gu_win[w, rows].astype(F32)
                values = jnp.where(me.zl == 1, pltpu.roll(values, 704, 1), values)
                lane = lax.broadcasted_iota(jnp.int32, values.shape, 1)
                gu[out, 768 * w : 768 * w + 768] = jnp.where(lane < 704, values, 0.0).astype(BF)

        wd[pl.ds(704, 64)] = jnp.zeros((64, 2048), BF)

    def normed():
        norm_scale(x, scale)

        @pl.loop(0, 16)
        def _(i):
            at = pl.ds(pl.multiple_of(i * 128, 128), 128)
            a1[:, at] = (x[:, at].astype(F32) * scale[...] * gains[i, pl.ds(0, 1), :]).astype(BF)

    def project_kv():
        raw = dot_in(a1[...], kw[...].reshape(2048, 512))
        for i in range(2):
            part = raw[:, 128 * i : 128 * i + 128]
            kv_own[:, 128 * i : 128 * i + 128] = (part * cosine[...] + turned(part) * sine[...]).astype(BF)
        kv_own[:, 256:] = raw[:, 256:].astype(BF)
        kv[0] = kv_own[...]

    def project_q():
        @pl.loop(0, 4)
        def _(n):
            raw = dot_in(a1[...], qw[:, :, :, pl.ds(pl.multiple_of(512 * n, 512), 512)].reshape(2048, 512))
            for i in range(4):
                part = raw[:, 128 * i : 128 * i + 128]
                part = ((part * cosine[...] + turned(part) * sine[...]).astype(BF).astype(F32) * SCALE).astype(BF)
                for half in (0, 1):
                    for e in (0, 1):
                        rows = pl.ds(64 * (2 * i + e), 64)
                        qst[n, half, rows, :] = part[64 * half : 64 * half + 64, 64 * e : 64 * e + 64]

    def collect_kv(mate):
        beside = kv[mate]
        for out, base in ((kst, 0), (vst, 256)):
            for n in range(4):
                first = base + 64 * n
                for slot in range(8):
                    out[n, pl.ds(64 * slot, 64), :] = kv[slot, 0:64, first : first + 64]
                out[n, pl.ds(512, 64), :] = beside[64:128, first : first + 64]
                out[n, pl.ds(576, 64), :] = kv_own[64:128, first : first + 64]

    def attend(n, half):
        count = 512 if half == 0 else 640
        keys = pl.ds(0, count)
        sT[keys] = dot_back(kst[n, keys, :], qst[n, half])
        for i in range(4):
            at = pl.ds(128 * i, 128)
            if half == 0:
                scores = sT[keys, at] + bias_p[...]
                peak = jnp.max(scores, axis=0, keepdims=True)
                raised = jnp.exp(scores - peak)
                total = jnp.sum(raised, axis=0, keepdims=True)
                pT[keys, at] = (raised * (1.0 / total)).astype(BF)
            else:
                first = sT[0:512, at]
                rest = sT[512:640, at] + bias_c[...]
                peak = jnp.maximum(
                    jnp.max(first, axis=0, keepdims=True), jnp.max(rest, axis=0, keepdims=True)
                )
                first = jnp.exp(first - peak)
                rest = jnp.exp(rest - peak)
                total = jnp.sum(first, axis=0, keepdims=True) + jnp.sum(rest, axis=0, keepdims=True)
                pT[0:512, at] = (first * (1.0 / total)).astype(BF)
                pT[512:640, at] = (rest * (1.0 / total)).astype(BF)
            lse[2 * n + half, :, at] = peak + jnp.log(total)
        for i, block in enumerate(unpile(dot_rows(vst[n, keys, :], pT[keys]))):
            first = pl.multiple_of(512 * n + 128 * i, 128)
            att[pl.ds(64 * half, 64), pl.ds(first, 128)] = block.astype(BF)

    def project_o():
        @pl.loop(0, 4)
        def _(n):
            at = pl.ds(pl.multiple_of(512 * n, 512), 512)
            h1[:, at] = x[:, at].astype(F32) + dot_in(att[...], wo[:, :, :, at].reshape(2048, 512))

    def normed_two():
        norm_scale(h1, scale)

        @pl.loop(0, 16)
        def _(i):
            at = pl.ds(pl.multiple_of(i * 128, 128), 128)
            acts[0, :, at] = (h1[:, at] * scale[...] * gains[i, pl.ds(8, 1), :]).astype(BF)

    def mpart_copy(n):
        return pltpu.make_async_copy(mstage, mpart.at[pl.ds(2 * n, 2)], msem)

    def group(n):
        at = pl.ds(2 * n, 2)
        rows = pl.ds(pl.multiple_of(256 * n, 256), 256)
        for h in range(3):
            first, second = pl.ds(256 * h, 256), pl.ds(768 + 256 * h, 256)
            here = acts[at].reshape(256, 2048)
            gate = dot_in(here, gu[:, first])
            up = dot_in(here, gu[:, second])
            back = dot_back(dy[at].reshape(256, 2048), wd[first, :])
            curve = 1.0 / (1.0 + jnp.exp(-gate))
            silu = gate * curve
            hid[rows, first] = (silu * up).astype(BF)
            dgu[at, :, first] = (back * up * (curve + silu * (1.0 - curve))).astype(BF).reshape(2, 128, 256)
            dgu[at, :, second] = (back * silu).astype(BF).reshape(2, 128, 256)

        @pl.when(n > 0)
        def _():
            mpart_copy(n - 1).wait()

        for i in range(4):
            wide = pl.ds(512 * i, 512)
            grads = dgu[at].reshape(256, 1536)
            dpart[at, :, wide] = dot_back(grads, gu[wide, :]).astype(BF).reshape(2, 128, 512)
            mstage[:, :, wide] = dot_in(hid[rows, :], wd[:, wide]).astype(BF).reshape(2, 128, 512)
        mpart_copy(n).start()

    d = Scatter(me.across_y, lambda slot: dpart.at[slot], 128, d_half, d_full, d_pair, (rs0, rs1), 0)
    gjob = Scatter(me.across_x, lambda slot: gown.at[slot], 128, g_half, g_full, g_pair, (rs0, rs1), 1)

    def weight_terms(t, core):
        at = pl.multiple_of((chip_of(me, t) * 2 + core) * 128, 128)
        left = acts[:, :, pl.ds(at, 128)].reshape(1024, 128)
        return dot_rows(left, dgu[...].reshape(1024, 1536))

    def gu_to(t):
        return send(gsib.at[t], grecv.at[t], (sib0, sib1), 8 + t, me.sibling())

    def down_to(t):
        mine = pl.ds(pl.multiple_of((1 - me.co) * 352, 16), 352)
        return send(gd(t).at[mine], gdrecv.at[t], (sib0, sib1), t, me.sibling())

    def terms_for_sibling():
        @pl.loop(0, 8)
        def _(i):
            gsib[7 - i] = weight_terms(7 - i, 1 - me.co).astype(BF)
            gu_to(7 - i).start()

    def own_terms(start, stop):
        @pl.loop(start, stop)
        def _(i):
            gu_to(7 - i).wait_recv()
            gown[7 - i] = (weight_terms(7 - i, me.co) + grecv[7 - i].astype(F32)).astype(BF)

    def down_terms():
        @pl.loop(0, 8)
        def _(t):
            at = pl.multiple_of(chip_of(me, t) * 256, 256)
            gd(t)[...] = dot_rows(hid[...], dy[:, :, pl.ds(at, 256)].reshape(1024, 256)).astype(BF)
            down_to(t).start()

    def down_sums():
        @pl.loop(0, 8)
        def _(t):
            down_to(t).wait_recv()

            @pl.loop(0, 22)
            def _(i):
                mine = gd(t)[pl.ds(pl.multiple_of(me.co * 352 + i * 16, 16), 16)].astype(F32)
                at = pl.ds(pl.multiple_of(i * 16, 16), 16)
                gdown[t, at] = (mine + gdrecv[t, at].astype(F32)).astype(BF)

    qx.start()
    g.start()
    dy_task.start()
    ox.start()
    qx.pair()
    g.turn(0)
    qx.turn(0)
    loads[0].wait()
    loads[1].wait()
    k.start()
    qx.turn(1)
    qx.last(0)
    g.pair()
    q.start()
    mate = place_tables(me, deal, freq, cosine, sine, bias_p, bias_c)
    qx.last(1)
    g.turn(1)
    g.last(0)
    kept[qx].wait()
    qy.start()
    o.start()
    k.turn(0)
    swap.start()
    dy_task.pair()
    ox.turn(0)
    k.pair()
    qy.turn(0)
    q.turn(0)
    g.last(1)
    k.turn(1)
    o.turn(0)
    ox.last(0)
    qy.pair()
    k.last(0)
    g.sync()
    normed()
    ox.pair()
    swap.wait()
    kept[dn] = load(dnp, wd_at(0, 0, 0, 0, None), local.at[13])
    dn.start()
    k.last(1)
    ox.turn(1)
    q.pair()
    k.sync()
    project_kv()
    kv_task.start()
    o.pair()
    qy.turn(1)
    kv_task.pair()
    ox.last(1)
    qy.last(0)
    q.turn(1)
    qy.last(1)
    kv_task.turn(0)
    kept[ox].wait()
    oy.start()
    q.last(0)
    put_gate_up()
    dn.turn(0)
    kv_task.last(0)
    kv_task.turn(1)
    o.turn(1)
    o.last(0)
    q.last(1)
    dn.pair()
    oy.pair()
    qy.sync()
    m.start()
    q.sync()
    kept[q].wait()
    saved.append(load(qw, q_out, local.at[10]))
    saved.append(load(kw, kw_out, local.at[11]))
    project_q()
    kv_task.last(1)
    oy.turn(0)
    collect_kv(mate)

    @pl.loop(0, 4)
    def _(n):
        attend(n, 0)
        attend(n, 1)

        @pl.when(n == 0)
        def _():
            o.last(1)
            oy.turn(1)
            dn.turn(1)

        @pl.when(n == 1)
        def _():
            dy_task.turn(0)
            oy.last(0)
            dy_task.turn(1)
            dn.last(0)

        @pl.when(n == 2)
        def _():
            oy.last(1)

    o.sync()
    m.turn(0)
    oy.sync()
    kept[o].wait()
    saved.append(load(wo, wo_out, local.at[12]))
    project_o()
    normed_two()
    a.start()
    m.pair()
    m.turn(1)
    m.last(0)
    dn.last(1)
    dy_task.last(0)
    a.pair()
    dy_task.last(1)
    m.last(1)
    a.turn(0)
    m.sync()
    dn.sync()

    for task in (o, ox, oy):
        task.end()
    saved[2].wait()
    kept[dn].wait()
    kept[dy_task].wait()

    @pl.loop(0, 4)
    def _(n):
        group(n)

        @pl.when(n == 0)
        def _():
            a.turn(1)

        @pl.when(n == 1)
        def _():
            a.last(0)

        @pl.when(n == 2)
        def _():
            a.last(1)

    d.start()
    for task in (q, qx, qy):
        task.end()
    saved[0].wait()
    terms_for_sibling()
    d.turn(1)
    own_terms(0, 2)
    gjob.start()
    d.turn(0)
    own_terms(2, 4)
    gjob.turn(1)
    d.pair()
    own_terms(4, 8)
    m.end()
    down_terms()
    gjob.turn(0)
    gjob.pair()
    d.finish(da2_out)
    down_sums()
    gjob.finish(gu_out)
    for task in (g, k, dn, dy_task, kv_task, a, d, gjob):
        task.end()
    saved[1].wait()
    mpart_copy(3).wait()

    @pl.loop(0, 8)
    def _(t):
        gu_to(t).wait_send()
        down_to(t).wait_send()


def fore(x, attn_gain, mlp_gain, deal, freq, q, key, value, wo, gate, up, dn, dy):
    shape = jax.ShapeDtypeStruct
    smem = pl.BlockSpec(memory_space=pltpu.SMEM)
    return pl.pallas_call(
        fore_kernel,
        out_shape=(
            shape((16, 16, 128), F32),
            shape((8, 2, 128, 2048), BF),
            shape((8, 2, 128, 512), BF),
            shape((8, 2, 128, 2048), BF),
            shape((128, 2048), BF),
            shape((4, 2, 512, 64), BF),
            shape((4, 640, 64), BF),
            shape((4, 640, 64), BF),
            shape((128, 2048), BF),
            shape((8, 1, 512), F32),
            shape((128, 2048), F32),
            shape((128, 128), F32),
            shape((128, 128), F32),
            shape((512, 128), F32),
            shape((128, 128), F32),
            shape((128, 2048), F32),
            shape((8, 128, 2048), BF),
            shape((128, 1536), BF),
            shape((8, 352, 256), BF),
        ),
        in_specs=[VMEM] * 3 + [smem, VMEM] + [ANY] * 8,
        out_specs=[VMEM] + [ANY] * 3 + [VMEM] * 12 + [ANY] + [VMEM] * 2,
        scratch_shapes=[
            pltpu.VMEM((8, 2, 128, 2048), BF),
            pltpu.VMEM((8, 2, 128, 512), BF),
            pltpu.VMEM((8, 2, 128, 2048), BF),
            pltpu.VMEM((128, 512), BF),
            pltpu.VMEM((8, 128, 512), BF),
            pltpu.VMEM((640, 512), F32),
            pltpu.VMEM((640, 512), BF),
            pltpu.VMEM((128, 1), F32),
            pltpu.VMEM((2, 128, 768), BF),
            pltpu.VMEM((352, 256), BF),
            pltpu.VMEM((8, 128, 2048), BF),
            pltpu.VMEM((2048, 1536), BF),
            pltpu.VMEM((768, 2048), BF),
            pltpu.VMEM((8, 128, 2048), BF),
            pltpu.VMEM((1024, 768), BF),
            pltpu.VMEM((2, 128, 2048), BF),
            *scatter_buffers(128, 2048),
            pltpu.VMEM((8, 128, 1536), BF),
            pltpu.VMEM((8, 352, 256), BF),
            *scatter_buffers(128, 1536),
            *dma_sems(8, 9),
            *dma_sems(8, 10),
            *dma_sems(5, 9),
            *dma_sems(2, 10),
            pltpu.SemaphoreType.DMA,
            pltpu.SemaphoreType.DMA,
            *dma_sems(2, 9),
            pltpu.SemaphoreType.DMA((16,)),
            pltpu.SemaphoreType.DMA((16,)),
            pltpu.SemaphoreType.DMA((14,)),
            pltpu.SemaphoreType.DMA,
        ],
        compiler_params=params(1, 63),
        name="fore",
    )(x, attn_gain, mlp_gain, deal, freq, q, key, value, wo, gate, up, dn, dy)


def back_kernel(
    da2, h1, dy, x, gains, wo_in, q_in, kw_in, qst, kst, vst, lse, cosine, sine, bias_p, bias_c, deal,
    a1_in, att_in, mpart_in, gu, gdown_in,
    mixed, tokens_grad, q_out, kv_out, o_out, gains_out, gu_all, dn_all,
    a1s, atts, dqkvs, datts, grow, dh1, gown, gsib, mpart, stream, dost, sT, dT, pT, dsT,
    kgrad, vgrad, kvp, dkv, da1, gdown, dn_sum, dnp, gu_own,
    qp, op, kp, gp, ggot, q_sum, o_sum, kv_sum, g_sum,
    q_half, q_full, q_pair, o_half, o_full, o_pair, k_half, k_full, k_pair, e_half, e_full, e_pair,
    m_half, m_full, m_pair, d_half, d_full, d_pair, n_half, n_full, n_pair,
    o_got, q_got, k_got,
    sib0, sib1, x0, x1, y0, y1, ag0, ag1, z0, z1, swap0, swap1, local,
):
    me = Place()
    greet_all(me, plane=True)
    nload = load(gdown_in, gdown, local.at[0])
    own, other = pl.ds(0, 128), pl.ds(128, 128)
    mload = load(mpart_in, mpart, local.at[1])
    guload = load(gu, gu_own, local.at[6])
    a1load = load(a1_in, a1s.at[own], local.at[2])
    attload = load(att_in, atts.at[own], local.at[3])

    def wo_load(n):
        return pltpu.make_async_copy(
            wo_in.at[pl.ds(512 * n, 512)], stream.at[n % 2, :, pl.ds(0, 2048)], local.at[4 + n % 2]
        )

    def qkv_load(n):
        rows = pl.ds(512 * n, 512)
        return (
            pltpu.make_async_copy(q_in.at[rows], stream.at[n % 2, :, pl.ds(0, 2048)], local.at[4 + n % 2]),
            pltpu.make_async_copy(kw_in.at[rows], stream.at[n % 2, :, pl.ds(2048, 512)], local.at[9 + n % 2]),
        )

    wo_load(0).start()
    wo_load(1).start()

    over_x, over_y, over_ag, over_sum = (x0, x1), (y0, y1), (ag0, ag1), (z0, z1)
    o_job = Scatter(me.across_x, lambda slot: op.at[slot], 128, o_half, o_full, o_pair, over_x, 0)
    q_job = Scatter(me.across_x, lambda slot: qp.at[slot], 128, q_half, q_full, q_pair, over_x, 1)
    k_job = Scatter(me.across_x, lambda slot: kp.at[slot], 128, k_half, k_full, k_pair, over_x, 2)
    e_job = Scatter(me.across_x, lambda slot: gp.at[slot], 16, e_half, e_full, e_pair, over_x, 3)
    n_job = Scatter(me.across_x, lambda slot: gdown.at[slot], 352, n_half, n_full, n_pair, over_x, 4)
    dn_swap = Swap(me, dn_sum, dnp, (swap0, swap1), local.at[8])
    m_job = Scatter(me.across_y, lambda slot: mpart.at[slot], 128, m_half, m_full, m_pair, over_y, 0)
    d_job = Scatter(me.across_y, lambda slot: kvp.at[slot], 128, d_half, d_full, d_pair, over_y, 1)

    def at_ctx(ref):
        def loc(dr, dp, er, ep, half):
            return ref.at[me.ctx_at(dr, dp), row_half(half, ref.shape[1])]

        return loc

    def dn_at(dr, dp, er, ep, half):
        first = pl.multiple_of(me.ctx_at(dr, dp) * 256, 256)
        return dn_all.at[row_half(half, 352), pl.ds(first, 256)]

    gu_task = Gather(me.across_y, gu_own, at_ctx(gu_all), over_ag, 0)
    dn_task = Gather(me.across_y, dnp, dn_at, over_ag, 1)
    def block_at(ref, slot):
        first = pl.multiple_of(me.ctx_at(STEPS[slot], PAIRS[slot]) * 16, 16)
        return ref.at[pl.ds(first, 16)]

    def sum_over_ctx(total, got, row):
        return Trade(
            me.across_y, lambda slot: block_at(total, slot), lambda slot: got.at[mirror(slot)], over_sum, row
        )

    def spread(out, row):
        return Trade(me.across_y, lambda slot: block_at(out, 0), lambda slot: block_at(out, 0), over_sum, row)

    def sum_up(total, got, out):
        value = block_at(total, 0)[...].astype(F32)
        for slot in range(1, 8):
            value = value + got[slot].astype(F32)
        block_at(out, 0)[...] = value.astype(BF)

    o_sums = sum_over_ctx(o_sum, o_got, 0)
    q_sums = sum_over_ctx(q_sum, q_got, 1)
    k_sums = sum_over_ctx(kv_sum, k_got, 2)
    o_spread = spread(o_out, 3)
    q_spread = spread(q_out, 4)
    k_spread = spread(kv_out, 5)
    e_task = Trade(me.across_y, lambda slot: g_sum, lambda slot: ggot.at[me.c], over_sum, 6)

    swap = lambda src, dst, index: send(src, dst, (sib0, sib1), index, me.sibling())
    att_swap = swap(atts.at[own], atts.at[other], 0)
    datt_swap = swap(datts.at[own], datts.at[other], 1)
    a1_swap = swap(a1s.at[own], a1s.at[other], 2)
    queries = pl.ds(0, 2048)
    dq_swap = swap(dqkvs.at[own, queries], dqkvs.at[other, queries], 3)
    rest = pl.ds(2048, 512)
    dkv_swap = swap(dqkvs.at[own, rest], dqkvs.at[other, rest], 4)
    gain_swap = swap(gown, gsib, 5)

    for i in range(16):
        grow[0, :, 128 * i : 128 * i + 128] = gains[i, 0:1, :]
        grow[1, :, 128 * i : 128 * i + 128] = gains[i, 8:9, :]
    grow[2] = jnp.zeros((1, 2048), F32)
    grow[3] = jnp.zeros((1, 2048), F32)
    kept = []

    def norm_two_back():
        @pl.loop(0, 8)
        def _(i):
            at = pl.ds(pl.multiple_of(16 * i, 16), 16)
            values, grad = h1[at], da2[at]
            scale = lax.rsqrt(jnp.mean(values * values, axis=1, keepdims=True) + EPS)
            grow[3] += jnp.sum(grad * values * scale, axis=0, keepdims=True)
            grad = grad * grow[1]
            level = jnp.mean(grad * values, axis=1, keepdims=True) * scale * scale * scale
            total = dy[at].astype(F32) + scale * grad - values * level
            dh1[at] = total
            datts[at] = total.astype(BF)

        datt_swap.start()

    def heads_back():
        for n in range(4):
            wo_load(n).wait()
            part = dot_back(datts[own], stream[n % 2, :, 0:2048]).astype(BF)
            for half in (0, 1):
                pile(dost.at[n, half], part, half)
            if n < 2:
                wo_load(n + 2).start()
        for n in range(2):
            for copy in qkv_load(n):
                copy.start()

    def terms(left, right, out, job):
        @pl.loop(0, 8)
        def _(i):
            at = pl.multiple_of((chip_of(me, 7 - i) * 2 + me.co) * 128, 128)
            out[7 - i] = dot_rows(left[:, pl.ds(at, 128)], right[...]).astype(BF)

            @pl.when(i == 1)
            def _():
                job.start()

    def output_terms():
        att_swap.wait_recv()
        datt_swap.wait_recv()
        terms(atts, datts, op, o_job)

    def query_terms():
        a1_swap.wait_recv()
        dq_swap.wait_recv()
        terms(a1s, dqkvs.at[:, pl.ds(0, 2048)], qp, q_job)

    def kv_terms():
        dkv_swap.wait_recv()
        terms(a1s, dqkvs.at[:, pl.ds(2048, 512)], kp, k_job)

    def kv_blocks():
        mate = find_mate(me, deal)
        for out, base in ((kgrad, 0), (vgrad, 256)):
            for n in range(4):
                first = base + 64 * n
                for slot in range(8):
                    kvp[slot, 0:64, first : first + 64] = out[n, 64 * slot : 64 * slot + 64, :]
                    if slot == 0:
                        late = out[n, 576:640, :]
                    else:
                        late = jnp.where(mate == slot, out[n, 512:576, :], jnp.zeros((64, 64), BF))
                    kvp[slot, 64:128, first : first + 64] = late

    def kv_back():
        for i in range(2):
            at = slice(128 * i, 128 * i + 128)
            block = dkv[:, at]
            dqkvs[own, 2048 + 128 * i : 2176 + 128 * i] = (block * cosine[...] - turned(block) * sine[...]).astype(BF)
        dqkvs[own, 2304:2560] = dkv[:, 256:512].astype(BF)
        dkv_swap.start()

    def inputs_back():
        for n in range(4):
            for copy in qkv_load(n):
                copy.wait()
            da1[:, 512 * n : 512 * n + 512] = dot_back(dqkvs[own], stream[n % 2])
            if n < 2:
                for copy in qkv_load(n + 2):
                    copy.start()

    def norm_one_back():
        @pl.loop(0, 8)
        def _(i):
            at = pl.ds(pl.multiple_of(16 * i, 16), 16)
            values, grad = x[at].astype(F32), da1[at]
            scale = lax.rsqrt(jnp.mean(values * values, axis=1, keepdims=True) + EPS)
            grow[2] += jnp.sum(grad * values * scale, axis=0, keepdims=True)
            grad = grad * grow[0]
            level = jnp.mean(grad * values, axis=1, keepdims=True) * scale * scale * scale
            tokens_grad[at] = (dh1[at] + scale * grad - values * level).astype(BF)

        gown[...] = jnp.zeros((16, 16, 128), F32)
        for i in range(16):
            gown[i, 0:1, :] = grow[2, :, 128 * i : 128 * i + 128]
            gown[i, 8:9, :] = grow[3, :, 128 * i : 128 * i + 128]
        gain_swap.start()

    def gain_terms():
        gain_swap.wait_recv()
        for slot in range(8):
            block = me.fsdp_at(STEPS[slot], PAIRS[slot])
            gp[slot] = gown[block] + gsib[block]

    def dn_begin():
        dn_swap.wait()
        dn_task.start()
        kept.append(load(dnp, dn_at(0, 0, 0, 0, None), local.at[7]))

    def gu_begin():
        guload.wait()
        kept.append(load(gu_own, gu_all.at[me.c], local.at[6]))
        gu_task.start()

    def e_begin():
        e_task.start()
        ggot[me.c] = g_sum[...]

    def attend(n, half):
        count = 512 if half == 0 else 640
        keys = pl.ds(0, count)
        key, query, out = kst[n, keys, :], qst[n, half], dost[n, half]
        sT[keys] = dot_back(key, query)
        dT[keys] = dot_back(vst[n, keys, :], out)
        for i in range(4):
            at = pl.ds(128 * i, 128)
            parts = []
            for first, size in ((0, 512), (512, 128))[: 1 + half]:
                scores = sT[first : first + size, at]
                if half == 0:
                    scores = scores + bias_p[...]
                elif first:
                    scores = scores + bias_c[...]
                probs = jnp.exp(scores - lse[2 * n + half, :, at])
                grad = dT[first : first + size, at]
                parts.append((first, size, probs, grad))
            level = sum(jnp.sum(probs * grad, axis=0, keepdims=True) for _, _, probs, grad in parts)
            for first, size, probs, grad in parts:
                pT[first : first + size, at] = probs.astype(BF)
                dsT[first : first + size, at] = (probs * (grad - level)).astype(BF)
        rows = slice(64 * half, 64 * half + 64)
        for i, block in enumerate(unpile(dot_rows(key, dsT[keys]) * SCALE)):
            block = block * cosine[rows] - turned(block) * sine[rows]
            first = pl.multiple_of(512 * n + 128 * i, 128)
            dqkvs[rows, pl.ds(first, 128)] = block.astype(BF)
        return dot_in(dsT[keys], query), dot_in(pT[keys], out)

    nload.wait()
    n_job.start()
    gu_begin()
    a1load.wait()
    a1_swap.start()
    norm_two_back()
    n_job.turn(1)
    attload.wait()
    att_swap.start()
    n_job.turn(0)
    mload.wait()
    m_job.start()
    output_terms()
    heads_back()
    n_job.pair()

    @pl.loop(0, 4)
    def _(n):
        key_one, value_one = attend(n, 0)
        key_two, value_two = attend(n, 1)
        for out, one, two in ((kgrad, key_one, key_two), (vgrad, value_one, value_two)):
            out[n, 0:512] = (one + two[0:512]).astype(BF)
            out[n, 512:640] = two[512:640].astype(BF)

        @pl.when(n == 0)
        def _():
            m_job.turn(1)
            o_job.turn(1)

        @pl.when(n == 2)
        def _():
            n_job.finish(dn_sum)

    kv_blocks()
    d_job.start()
    o_job.turn(0)
    gu_task.turn(0)
    m_job.pair()
    dq_swap.start()
    d_job.turn(1)
    dn_swap.start()
    d_job.turn(0)
    query_terms()
    o_job.pair()
    gu_task.pair()
    m_job.turn(0)
    d_job.pair()
    q_job.turn(1)
    gu_task.turn(1)
    dn_begin()
    o_job.finish(o_sum)
    o_sums.start()
    gu_task.last(0)
    d_job.finish(dkv)
    kv_back()
    kv_terms()
    q_job.turn(0)
    q_job.pair()
    dn_task.pair()
    gu_task.last(1)
    inputs_back()
    k_job.turn(1)
    norm_one_back()
    o_sums.got()
    sum_up(o_sum, o_got, o_out)
    o_spread.start()
    m_job.finish(mixed, (h1,))
    k_job.turn(0)
    gain_terms()
    dn_task.turn(0)
    q_job.finish(q_sum)
    k_job.pair()
    q_sums.start()
    e_job.start()
    o_spread.got()
    k_job.finish(kv_sum)
    dn_task.turn(1)
    e_job.turn(1)
    e_job.pair()
    k_sums.start()
    q_sums.got()
    sum_up(q_sum, q_got, q_out)
    q_spread.start()
    e_job.turn(0)
    e_job.finish(g_sum)
    e_begin()
    dn_task.last(0)
    dn_task.last(1)
    k_sums.got()
    sum_up(kv_sum, k_got, kv_out)
    k_spread.start()
    q_spread.got()
    e_task.got()
    k_spread.got()
    total = ggot[0]
    for index in range(1, 8):
        total = total + ggot[index]
    gains_out[...] = total
    jobs = (o_job, q_job, k_job, e_job, m_job, d_job, n_job, o_sums, q_sums, k_sums)
    for job in (*jobs, gu_task, dn_task, e_task, o_spread, q_spread, k_spread):
        job.end()
    for copy in (att_swap, datt_swap, a1_swap, dq_swap, dkv_swap, gain_swap):
        copy.wait_send()
    for copy in kept:
        copy.wait()


def back(da2, h1, dy, x, gains, wo, q, kw, qst, kst, vst, lse, cosine, sine, bias_p, bias_c, deal, a1, att, mpart, gu, gdown):
    scratch = [
        pltpu.VMEM((256, 2048), BF),
        pltpu.VMEM((256, 2048), BF),
        pltpu.VMEM((256, 2560), BF),
        pltpu.VMEM((256, 2048), BF),
        pltpu.VMEM((4, 1, 2048), F32),
        pltpu.VMEM((128, 2048), F32),
        pltpu.VMEM((16, 16, 128), F32),
        pltpu.VMEM((16, 16, 128), F32),
        pltpu.VMEM((8, 128, 2048), BF),
        pltpu.VMEM((2, 512, 2560), BF),
        pltpu.VMEM((4, 2, 512, 64), BF),
        pltpu.VMEM((640, 512), F32),
        pltpu.VMEM((640, 512), F32),
        pltpu.VMEM((640, 512), BF),
        pltpu.VMEM((640, 512), BF),
        pltpu.VMEM((4, 640, 64), BF),
        pltpu.VMEM((4, 640, 64), BF),
        pltpu.VMEM((8, 128, 512), BF),
        pltpu.VMEM((128, 512), F32),
        pltpu.VMEM((128, 2048), F32),
        pltpu.VMEM((8, 352, 256), BF),
        pltpu.VMEM((352, 256), BF),
        pltpu.VMEM((352, 256), BF),
        pltpu.VMEM((128, 1536), BF),
        pltpu.VMEM((8, 128, 2048), BF),
        pltpu.VMEM((8, 128, 2048), BF),
        pltpu.VMEM((8, 128, 512), BF),
        pltpu.VMEM((8, 16, 128), F32),
        pltpu.VMEM((8, 16, 128), F32),
        pltpu.VMEM((128, 2048), BF),
        pltpu.VMEM((128, 2048), BF),
        pltpu.VMEM((128, 512), BF),
        pltpu.VMEM((16, 128), F32),
        *scatter_buffers(128, 2048),
        *scatter_buffers(128, 2048),
        *scatter_buffers(128, 512),
        *scatter_buffers(16, 128, F32),
        *scatter_buffers(128, 2048),
        *scatter_buffers(128, 512),
        *scatter_buffers(352, 256),
        pltpu.VMEM((8, 16, 2048), BF),
        pltpu.VMEM((8, 16, 2048), BF),
        pltpu.VMEM((8, 16, 512), BF),
        pltpu.SemaphoreType.DMA((6,)),
        pltpu.SemaphoreType.DMA((6,)),
        *dma_sems(5, 9),
        *dma_sems(2, 9),
        *dma_sems(2, 9),
        *dma_sems(7, 8),
        pltpu.SemaphoreType.DMA,
        pltpu.SemaphoreType.DMA,
        pltpu.SemaphoreType.DMA((11,)),
    ]
    return pl.pallas_call(
        back_kernel,
        out_shape=(
            jax.ShapeDtypeStruct((128, 2048), BF),
            jax.ShapeDtypeStruct((128, 2048), BF),
            jax.ShapeDtypeStruct((128, 2048), BF),
            jax.ShapeDtypeStruct((128, 512), BF),
            jax.ShapeDtypeStruct((128, 2048), BF),
            jax.ShapeDtypeStruct((16, 128), F32),
            jax.ShapeDtypeStruct((8, 128, 1536), BF),
            jax.ShapeDtypeStruct((352, 2048), BF),
        ),
        in_specs=[VMEM] * 5 + [ANY] * 3 + [VMEM] * 8 + [pl.BlockSpec(memory_space=pltpu.SMEM)] + [ANY] * 5,
        out_specs=[VMEM] * 6 + [ANY] * 2,
        scratch_shapes=scratch,
        compiler_params=params(5, 62),
        name="back",
    )(da2, h1, dy, x, gains, wo, q, kw, qst, kst, vst, lse, cosine, sine, bias_p, bias_c, deal, a1, att, mpart, gu, gdown)


def widen_kernel(parts, gate, up):
    for out, base in ((gate, 0), (up, 768)):
        for pair in range(4):
            even = parts[2 * pair, :, base : base + 768].astype(F32)
            odd = pltpu.roll(parts[2 * pair + 1, :, base : base + 768].astype(F32), 64, 1)
            first = 1408 * pair
            out[:, first : first + 640] = even[:, 0:640]
            out[:, first + 640 : first + 768] = even[:, 640:768] + odd[:, 0:128]
            out[:, first + 768 : first + 1408] = odd[:, 128:768]


def widen(parts):
    out = jax.ShapeDtypeStruct((128, 5632), F32)
    block = pl.BlockSpec((16, 5632), lambda i: (i, 0))
    return pl.pallas_call(
        widen_kernel,
        grid=(8,),
        out_shape=(out, out),
        in_specs=[pl.BlockSpec((8, 16, 1536), lambda i: (0, i, 0))],
        out_specs=[block, block],
        name="widen",
    )(parts)


def on_device(
    tokens,
    block_deal,
    attn_gain,
    query_weight,
    key_weight,
    value_weight,
    output_weight,
    mlp_gain,
    gate_weight,
    up_weight,
    down_weight,
    cotangent,
):
    freq = BASE ** (-(jnp.arange(HEAD_DIM // 2, dtype=F32) * 2.0) / HEAD_DIM)
    freq = jnp.concatenate([freq] * 4)[None]
    deal = block_deal.reshape(256)
    (
        gains, q_all, kv_all, wo_all, a1, qst, kst, vst, att, lse, h1, cosine, sine, bias_p, bias_c,
        da2, mixed_parts, gu_sum, dn_parts,
    ) = fore(
        tokens[0], attn_gain[None], mlp_gain[None], deal, freq, query_weight, key_weight, value_weight, output_weight,
        gate_weight, up_weight, down_weight, cotangent[0],
    )
    mixed, tokens_grad, query_grad, kv_grad, o_grad, gain_grads, gu_grads, dn_grad = back(
        da2, h1, cotangent[0], tokens[0], gains, wo_all.reshape(2048, 2048), q_all.reshape(2048, 2048),
        kv_all.reshape(2048, 512), qst, kst, vst, lse, cosine, sine, bias_p, bias_c, deal, a1, att, mixed_parts,
        gu_sum, dn_parts,
    )
    gate_grad, up_grad = widen(gu_grads)
    return (
        mixed[None],
        tokens_grad[None],
        gain_grads[0],
        query_grad.astype(F32),
        kv_grad[:, :256].astype(F32),
        kv_grad[:, 256:].astype(F32),
        o_grad.astype(F32),
        gain_grads[8],
        gate_grad,
        up_grad,
        dn_grad.astype(F32),
    )


def solution(mesh):
    held = P("fsdp", "ctx", None)
    rows = P("fsdp", None)
    return jax.shard_map(
        on_device,
        mesh=mesh,
        in_specs=(held, P(), P("fsdp"), rows, rows, rows, rows, P("fsdp"), rows, rows, rows, held),
        out_specs=(held, held, P("fsdp"), rows, rows, rows, rows, P("fsdp"), rows, rows, rows),
        check_vma=False,
    )
```

```python
import functools

import jax
import jax.numpy as jnp
from jax import lax
from jax.experimental import pallas as pl
from jax.experimental.pallas import tpu as pltpu
from jax.sharding import PartitionSpec as P

MESH = pl.DeviceIdType.MESH
BF = jnp.bfloat16
F32 = jnp.float32
ANY = pl.BlockSpec(memory_space=pl.ANY)
VMEM = pl.BlockSpec(memory_space=pltpu.VMEM)

HEAD_DIM = 64
EPS = 1e-05
SCALE = 0.125
BASE = 10000.0

SLOT = {(0, 0): 0, (0, 1): 1, (1, 0): 2, (3, 0): 3, (1, 1): 4, (3, 1): 5, (2, 0): 6, (2, 1): 7}
STEPS = (0, 0, 1, 3, 1, 3, 2, 2)
PAIRS = (0, 1, 0, 0, 1, 1, 0, 1)


def slot_of(dr, dp):
    return SLOT[(dr % 4, dp % 2)]


class Place:
    def __init__(self):
        self.c = lax.axis_index("ctx")
        self.f = lax.axis_index("fsdp")
        self.y, self.zl = lax.div(self.c, 2), lax.rem(self.c, 2)
        self.j, self.co = lax.div(self.f, 2), lax.rem(self.f, 2)
        self.x, self.zh = lax.div(self.j, 2), lax.rem(self.j, 2)

    def ctx_at(self, dr, dp):
        return lax.rem(self.y + dr % 4, 4) * 2 + lax.rem(self.zl + dp, 2)

    def chip_at(self, dr, dp):
        return lax.rem(self.x + dr % 4, 4) * 2 + lax.rem(self.zh + dp, 2)

    def fsdp_at(self, dr, dp):
        return self.chip_at(dr, dp) * 2 + self.co

    def across_y(self, dr, dp):
        return {"ctx": self.ctx_at(dr, dp), "fsdp": self.f}

    def across_x(self, dr, dp):
        return {"ctx": self.c, "fsdp": self.fsdp_at(dr, dp)}

    def sibling(self):
        return {"ctx": self.c, "fsdp": self.f + 1 - 2 * self.co}


def chip_of(me, t):
    dr = jnp.where(t < 2, 0, jnp.where(t >= 6, 2, 1 + 2 * lax.rem(t, 2)))
    dp = jnp.where(t < 2, t, jnp.where(t >= 6, t - 6, lax.div(t, 4)))
    return lax.rem(me.x + dr, 4) * 2 + lax.rem(me.zh + dp, 2)


def greet(devices):
    barrier = pltpu.get_barrier_semaphore()
    for device in devices:
        pl.semaphore_signal(barrier, 1, device_id=device, device_id_type=MESH)
    pl.semaphore_wait(barrier, len(devices))


class Swap:
    def __init__(self, me, src, dst, sems, local):
        self.moved = me.c != me.j
        self.to = {"ctx": me.j, "fsdp": 2 * me.c + me.co}
        self.copy = pltpu.make_async_remote_copy(
            src, dst, sems[0], sems[1], device_id=self.to, device_id_type=MESH
        )
        self.keep = pltpu.make_async_copy(src, dst, local)

    def start(self):
        pl.when(self.moved)(self.copy.start)
        pl.when(jnp.logical_not(self.moved))(self.keep.start)

    def wait(self):
        pl.when(self.moved)(self.copy.wait)
        pl.when(jnp.logical_not(self.moved))(self.keep.wait)


def greet_all(me, plane=False):
    barrier = pltpu.get_barrier_semaphore()
    others = near(me.across_x) + [me.sibling()]
    others += [me.across_y(STEPS[s], PAIRS[s]) for s in range(1, 8)] if plane else near(me.across_y)
    for device in others:
        pl.semaphore_signal(barrier, 1, device_id=device, device_id_type=MESH)
    moved = me.c != me.j

    @pl.when(moved)
    def _():
        to = {"ctx": me.j, "fsdp": 2 * me.c + me.co}
        pl.semaphore_signal(barrier, 1, device_id=to, device_id_type=MESH)

    pl.semaphore_wait(barrier, len(others) + jnp.where(moved, 1, 0))


def near(dev):
    return [dev(1, 0), dev(-1, 0), dev(0, 1)]


def send(src, dst, sems, index, device):
    return pltpu.make_async_remote_copy(
        src, dst, sems[0].at[index], sems[1].at[index], device_id=device, device_id_type=MESH
    )


class Gather:
    MOVES = (
        ((0, 0), (0, 1), None),
        ((0, 0), (1, 0), None),
        ((0, 0), (-1, 0), None),
        ((0, 1), (1, 0), None),
        ((0, 1), (-1, 0), None),
        ((-1, 0), (1, 0), 0),
        ((-1, 1), (1, 0), 0),
        ((1, 0), (-1, 0), 1),
        ((1, 1), (-1, 0), 1),
    )

    def __init__(self, dev, own, loc, sems, row, sibling=None, sibling_sems=None):
        self.loc = loc
        self.copies = []
        for index, (block, to, half) in enumerate(self.MOVES):
            src = own if block == (0, 0) else loc(*block, 0, 0, half)
            dst = loc(*block, *to, half)
            self.copies.append(send(src, dst, sems, (row, index), dev(*to)))
        self.passed = {}
        if sibling is not None:
            self.passed[9] = send(own, loc(0, 0, 0, 0, None), sibling_sems, (row, 9), sibling)
            for index, ((dr, dp), (er, ep), half) in enumerate(self.MOVES):
                ref = loc(dr - er, dp + ep, 0, 0, half)
                self.passed[index] = send(ref, ref, sibling_sems, (row, index), sibling)
        self.own = own

    def _pass(self, index):
        if self.passed:
            self.passed[index].start()

    def _got(self, index):
        self.copies[index].wait_recv()
        self._pass(index)

    def start(self):
        for index in (0, 1, 2):
            self.copies[index].start()
        self._pass(9)

    def pair(self):
        self._got(0)
        self.copies[3].start()
        self.copies[4].start()

    def turn(self, dp):
        for got, on in (((1, 5), (2, 7)) if dp == 0 else ((3, 6), (4, 8))):
            self._got(got)
            self.copies[on].start()

    def last(self, dp):
        for got in ((5, 7) if dp == 0 else (6, 8)):
            self._got(got)

    def sync(self):
        for copy in self.passed.values():
            copy.wait()

    def end(self):
        for copy in self.copies:
            copy.wait_send()


def row_half(half, rows):
    return pl.ds(0, rows) if half is None else pl.ds(half * (rows // 2), rows // 2)


def add_into(ref, rows, others, step=16):
    step = min(step, rows)

    @pl.loop(0, rows // step)
    def _(i):
        at = pl.ds(pl.multiple_of(i * step, step), step)
        total = ref[at].astype(F32)
        for other in others:
            total = total + other[at].astype(F32)
        ref[at] = total.astype(ref.dtype)


class Scatter:
    def __init__(self, dev, part, rows, halves, fulls, paired, sems, row, cut=None):
        self.part, self.rows, self.cut = part, rows, cut
        self.halves, self.fulls, self.paired = halves, fulls, paired
        self.first, self.second = {}, {}
        for dp in (0, 1):
            for way, sign in ((0, 1), (1, -1)):
                self.first[way, dp] = send(
                    self._half(part(slot_of(2, dp)), way), halves.at[way, dp], sems, (row, way * 2 + dp), dev(sign, 0)
                )
                self.second[way, dp] = send(
                    part(slot_of(sign, dp)), fulls.at[way, dp], sems, (row, 4 + way * 2 + dp), dev(sign, 0)
                )
        self.third = send(part(slot_of(0, 1)), paired, sems, (row, 8), dev(0, 1))

    def _half(self, ref, way):
        if self.cut is None:
            return ref.at[pl.ds(way * (self.rows // 2), self.rows // 2)]
        return ref.at[:, pl.ds(way * (self.cut // 2), self.cut // 2)]

    def start(self):
        for dp in (1, 0):
            for way in (0, 1):
                self.first[way, dp].start()

    def turn(self, dp):
        for way, sign in ((0, 1), (1, -1)):
            self.first[way, dp].wait_recv()
            block = self._half(self.part(slot_of(sign, dp)), way)
            add_into(block, block.shape[0], [self.halves.at[way, dp]])
            self.second[way, dp].start()

    def pair(self):
        for way in (0, 1):
            self.second[way, 1].wait_recv()
        add_into(self.part(slot_of(0, 1)), self.rows, [self.fulls.at[0, 1], self.fulls.at[1, 1]])
        self.third.start()

    def finish(self, out, extra=()):
        for way in (0, 1):
            self.second[way, 0].wait_recv()
        self.third.wait_recv()
        own = self.part(0)
        terms = [own, self.fulls.at[0, 0], self.fulls.at[1, 0], self.paired, *extra]

        @pl.loop(0, self.rows // 16)
        def _(i):
            at = pl.ds(pl.multiple_of(i * 16, 16), 16)
            total = terms[0][at].astype(F32)
            for term in terms[1:]:
                total = total + term[at].astype(F32)
            out[at] = total.astype(out.dtype)

    def end(self):
        for copy in (*self.first.values(), *self.second.values(), self.third):
            copy.wait_send()


def mirror(slot):
    return slot_of(-STEPS[slot], PAIRS[slot])


class Trade:
    def __init__(self, dev, what, where, sems, row):
        self.copies = [
            pltpu.make_async_remote_copy(
                what(slot), where(slot), sems[0].at[row, slot], sems[1].at[row, mirror(slot)],
                device_id=dev(STEPS[slot], PAIRS[slot]), device_id_type=MESH,
            )
            for slot in range(1, 8)
        ]

    def start(self):
        for copy in self.copies:
            copy.start()

    def got(self):
        for copy in self.copies:
            copy.wait_recv()

    def end(self):
        for copy in self.copies:
            copy.wait_send()


def scatter_buffers(rows, columns, dtype=BF, cut=False):
    half = (rows, columns // 2) if cut else (rows // 2, columns)
    return [
        pltpu.VMEM((2, 2, *half), dtype),
        pltpu.VMEM((2, 2, rows, columns), dtype),
        pltpu.VMEM((rows, columns), dtype),
    ]


def dma_sems(rows, count):
    return [pltpu.SemaphoreType.DMA((rows, count)), pltpu.SemaphoreType.DMA((rows, count))]


def params(collective_id, vmem=56):
    return pltpu.CompilerParams(
        collective_id=collective_id, has_side_effects=True, vmem_limit_bytes=vmem << 20
    )


def dot_in(left, right):
    return jnp.dot(left, right, preferred_element_type=F32)


def dot_back(left, right):
    return lax.dot_general(left, right, (((1,), (1,)), ((), ())), preferred_element_type=F32)


def dot_rows(left, right):
    return lax.dot_general(left, right, (((0,), (0,)), ((), ())), preferred_element_type=F32)


def load(src, dst, sem):
    copy = pltpu.make_async_copy(src, dst, sem)
    copy.start()
    return copy


def turned(values):
    lane = lax.broadcasted_iota(jnp.int32, values.shape, 1)
    low = lax.rem(lane, 64) < 32
    return jnp.where(low, pltpu.roll(values, 96, 1), pltpu.roll(values, 32, 1))


def pile(out, values, half):
    for h in range(8):
        out[pl.ds(64 * h, 64), :] = values[64 * half : 64 * half + 64, 64 * h : 64 * h + 64]


def unpile(values):
    flat = values.T
    return [
        jnp.concatenate([flat[128 * m : 128 * m + 64], flat[128 * m + 64 : 128 * m + 128]], axis=1)
        for m in range(4)
    ]


def norm_scale(ref, out):
    values = ref[...].astype(F32)
    out[...] = lax.rsqrt(jnp.mean(values * values, axis=1, keepdims=True) + EPS)


def place_tables(me, deal, freq, cosine, sine, bias_p, bias_c):
    def block(slot, part):
        return deal[(me.f * 8 + me.ctx_at(STEPS[slot], PAIRS[slot])) * 2 + part]

    first, second = block(0, 0), block(0, 1)
    odd = lax.rem(second, 2)
    row = lax.broadcasted_iota(jnp.int32, (128, 128), 0)
    lane = lax.broadcasted_iota(jnp.int32, (128, 128), 1)
    position = jnp.where(row < 64, first * 64 + row, 448 + odd * 64 + row)
    angle = position.astype(F32) * freq[...]
    cosine[...] = jnp.cos(angle)
    sine[...] = jnp.where(lax.rem(lane, 64) < 32, -jnp.sin(angle), jnp.sin(angle))
    row, lane = row[:64], lax.rem(lane[:64], 64)
    mate = jnp.int32(0)
    for slot in range(8):
        seen = block(slot, 0) * 64 + row <= first * 64 + lane
        bias_p[pl.ds(64 * slot, 64), :] = jnp.where(seen, 0.0, -1e30)
        if slot:
            mate = mate + jnp.where(block(slot, 1) == second + 1 - 2 * odd, slot, 0)
    bias_c[pl.ds(0, 64), :] = jnp.where(odd + 0 * row == 1, 0.0, -1e30)
    bias_c[pl.ds(64, 64), :] = jnp.where(row <= lane, 0.0, -1e30)
    return mate


def find_mate(me, deal):
    def block(slot):
        return deal[(me.f * 8 + me.ctx_at(STEPS[slot], PAIRS[slot])) * 2 + 1]

    second = block(0)
    mate = jnp.int32(0)
    for slot in range(1, 8):
        mate = mate + jnp.where(block(slot) == second + 1 - 2 * lax.rem(second, 2), slot, 0)
    return mate


def layer_kernel(
    x, attn_gain, mlp_gain, deal, freq, q_in, key_in, value_in, wo_in, gate_in, up_in, dn_in, dy_in,
    mixed, tokens_grad, q_grad, kv_grad, o_grad, gains_out, gu_all, dn_all,
    q_saved, kw_saved, wo_saved, mpart, m_half, m_full, m_pair,
    gains, a1s, atts, qst, kst, vst, lse, h1, cosine, sine, bias_p, bias_c,
    qw, kw, wo, kv_own, kv, sT, pT, dT, dsT, scale, gu_win, dnp, acts, gu, wd, dy, hid,
    grecv, gdrecv, g_pair, da2, datts, dqkvs, grow, gown_rows, gsib_rows, dn_moved,
    n_half, n_full, n_pair, e_half, e_full, e_pair, gp, ggot, g_sum, o_got, q_got, k_got,
    s0, s1, t0, t1, y0, y1, u0, u1, r0, r1, z0, z1, c0, c1, w0, w1, v0, v1, credit, local,
):
    me = Place()
    greet_all(me, plane=True)
    own, other = pl.ds(0, 128), pl.ds(128, 128)
    slots = iter(range(64))

    def load(src, dst):
        copy = pltpu.make_async_copy(src, dst, local.at[next(slots)])
        copy.start()
        return copy

    def later(src, dst):
        return pltpu.make_async_copy(src, dst, local.at[next(slots)])

    def aligned(index, step):
        return index if isinstance(index, int) else pl.multiple_of(index, step)

    def gains_at(dr, dp, er, ep, half):
        return gains.at[me.fsdp_at(dr, dp), row_half(half, 16)]

    def slot_at(ref, rows):
        def loc(dr, dp, er, ep, half):
            return ref.at[slot_of(dr - er, dp + ep), row_half(half, rows)]

        return loc

    def acts_at(dr, dp, er, ep, half):
        slot = slot_of(dr - er, dp + ep)
        return acts.at[slot // 2, slot % 2, row_half(half, 128)]

    def columns(first, index):
        return pl.ds(pl.multiple_of(first + index * 128, 128), 128)

    def plain(ref, count):
        def loc(dr, dp, er, ep, half):
            return ref.at[me.chip_at(dr, dp), me.co, row_half(half, 128), pl.ds(0, count)]

        return loc

    def strip_x(ref, first):
        def loc(dr, dp, er, ep, half):
            return ref.at[me.chip_at(dr, dp), me.co, row_half(half, 128), columns(first, me.c)]

        return loc

    def strip_y(ref, first):
        def loc(dr, dp, er, ep, half):
            chips = pl.ds(0, 8) if half is None else pl.ds(4 * half, 4)
            return ref.at[chips, me.co, :, columns(first, me.ctx_at(dr, dp))]

        return loc

    def wd_at(dr, dp, er, ep, half):
        size = 352 if half is None else 176
        first = me.co * 352 + (0 if half is None else half * size)
        return wd.at[
            pl.ds(pl.multiple_of(first, 16), size),
            pl.ds(pl.multiple_of(me.chip_at(dr, dp) * 256, 256), 256),
        ]

    def gu_at(dr, dp, er, ep, half):
        size = 128 if half is None else 64
        first = me.fsdp_at(dr, dp) * 128 + (0 if half is None else half * size)
        return gu.at[pl.ds(pl.multiple_of(first, size), size)]

    def over_x(own, loc, row, both=True):
        own = loc(0, 0, 0, 0, None) if own is None else own
        return Gather(me.across_x, own, loc, (s0, s1), row, me.sibling() if both else None, (t0, t1))

    def over_y(own, loc, row, both=True):
        own = loc(0, 0, 0, 0, None) if own is None else own
        return Gather(me.across_y, own, loc, (y0, y1), row, me.sibling() if both else None, (u0, u1))

    g = over_x(None, gains_at, 0)
    k = over_x(None, plain(kw, 512), 1)
    q = over_x(q_in.at[:, pl.ds(0, 1024)], plain(qw, 1024), 2)
    qx = over_x(q_in.at[:, columns(1024, me.c)], strip_x(qw, 1024), 3, both=False)
    o = over_x(wo_in.at[:, pl.ds(0, 1024)], plain(wo, 1024), 4)
    ox = over_x(wo_in.at[:, columns(1024, me.c)], strip_x(wo, 1024), 5, both=False)
    m = over_x(None, gu_at, 6)
    dn = over_x(dnp, wd_at, 7)
    qy = over_y(None, strip_y(qw, 1024), 0)
    oy = over_y(None, strip_y(wo, 1024), 1)
    dy_task = over_y(dy_in, slot_at(dy, 128), 2, both=False)
    kv_task = over_y(kv_own, slot_at(kv, 128), 3, both=False)
    a = over_y(None, acts_at, 4, both=False)
    swap = Swap(me, dn_in.at[:, pl.ds(pl.multiple_of(me.c * 256, 256), 256)], dnp, (w0, w1), local.at[next(slots)])

    own_kw = plain(kw, 512)(0, 0, 0, 0, None)
    loads = [load(key_in, own_kw.at[:, pl.ds(0, 256)]), load(value_in, own_kw.at[:, pl.ds(256, 256)])]
    kept = {task: load(task.own, task.loc(0, 0, 0, 0, None)) for task in (q, qx, o, ox, dy_task)}
    window = pl.ds(pl.multiple_of(me.y * 1408 + me.zl * 640, 128), 768)
    loads.append(load(gate_in.at[:, window], gu_win.at[0]))
    loads.append(load(up_in.at[:, window], gu_win.at[1]))
    gains[me.f] = jnp.zeros((16, 128), F32)
    gains[me.f, pl.ds(0, 1), :] = attn_gain[...].astype(F32)
    gains[me.f, pl.ds(8, 1), :] = mlp_gain[...].astype(F32)

    dpart = op = wo.at[:, 0]
    qp = wo.at[:, 1]
    dgu = wo.at[:, 1, :, pl.ds(0, 1536)]
    kvp = kv

    def gsib(t):
        return gu.at[pl.ds(aligned(128 * t, 128), 128)]

    def gown(t):
        return gu.at[pl.ds(aligned(1024 + 128 * t, 128), 128)]

    def kp(t):
        return gu.at[pl.ds(aligned(128 * t, 128), 128), pl.ds(0, 512)]

    def gd(t):
        return wd.at[:, pl.ds(aligned(256 * t, 256), 256)]

    def gd_own(t):
        return gd(t).at[pl.ds(pl.multiple_of(me.co * 352, 16), 352)]

    def dost(n, half):
        return grecv.at[pl.ds(0, 4), :, pl.ds(pl.multiple_of(512 + 128 * (2 * n + half), 128), 128)]

    saved = []

    def put_gate_up():
        loads[2].wait()
        loads[3].wait()

        @pl.loop(0, 8)
        def _(i):
            rows = pl.ds(pl.multiple_of(16 * i, 16), 16)
            out = pl.ds(pl.multiple_of(me.f * 128 + 16 * i, 16), 16)
            for w in (0, 1):
                values = gu_win[w, rows].astype(F32)
                values = jnp.where(me.zl == 1, pltpu.roll(values, 704, 1), values)
                lane = lax.broadcasted_iota(jnp.int32, values.shape, 1)
                gu[out, 768 * w : 768 * w + 768] = jnp.where(lane < 704, values, 0.0).astype(BF)

        wd[pl.ds(704, 64)] = jnp.zeros((64, 2048), BF)

    def normed():
        norm_scale(x, scale)

        @pl.loop(0, 16)
        def _(i):
            at = pl.ds(pl.multiple_of(i * 128, 128), 128)
            a1s[own, at] = (x[:, at].astype(F32) * scale[...] * gains[i, pl.ds(0, 1), :]).astype(BF)

    def project_kv():
        raw = dot_in(a1s[own], kw[...].reshape(2048, 512))
        for i in range(2):
            part = raw[:, 128 * i : 128 * i + 128]
            kv_own[:, 128 * i : 128 * i + 128] = (part * cosine[...] + turned(part) * sine[...]).astype(BF)
        kv_own[:, 256:] = raw[:, 256:].astype(BF)
        kv[0] = kv_own[...]

    def project_q():
        @pl.loop(0, 4)
        def _(n):
            raw = dot_in(a1s[own], qw[:, :, :, pl.ds(pl.multiple_of(512 * n, 512), 512)].reshape(2048, 512))
            for i in range(4):
                part = raw[:, 128 * i : 128 * i + 128]
                part = ((part * cosine[...] + turned(part) * sine[...]).astype(BF).astype(F32) * SCALE).astype(BF)
                for half in (0, 1):
                    for e in (0, 1):
                        rows = pl.ds(64 * (2 * i + e), 64)
                        qst[n, half, rows, :] = part[64 * half : 64 * half + 64, 64 * e : 64 * e + 64]

    def collect_kv(mate):
        beside = kv[mate]
        for out, base in ((kst, 0), (vst, 256)):
            for n in range(4):
                first = base + 64 * n
                for slot in range(8):
                    out[n, pl.ds(64 * slot, 64), :] = kv[slot, 0:64, first : first + 64]
                out[n, pl.ds(512, 64), :] = beside[64:128, first : first + 64]
                out[n, pl.ds(576, 64), :] = kv_own[64:128, first : first + 64]

    def attend(n, half):
        count = 512 if half == 0 else 640
        keys = pl.ds(0, count)
        sT[keys] = dot_back(kst[n, keys, :], qst[n, half])
        for i in range(4):
            at = pl.ds(128 * i, 128)
            if half == 0:
                scores = sT[keys, at] + bias_p[...]
                peak = jnp.max(scores, axis=0, keepdims=True)
                raised = jnp.exp(scores - peak)
                total = jnp.sum(raised, axis=0, keepdims=True)
                pT[keys, at] = (raised * (1.0 / total)).astype(BF)
            else:
                first = sT[0:512, at]
                rest = sT[512:640, at] + bias_c[...]
                peak = jnp.maximum(
                    jnp.max(first, axis=0, keepdims=True), jnp.max(rest, axis=0, keepdims=True)
                )
                first = jnp.exp(first - peak)
                rest = jnp.exp(rest - peak)
                total = jnp.sum(first, axis=0, keepdims=True) + jnp.sum(rest, axis=0, keepdims=True)
                pT[0:512, at] = (first * (1.0 / total)).astype(BF)
                pT[512:640, at] = (rest * (1.0 / total)).astype(BF)
            lse[2 * n + half, :, at] = peak + jnp.log(total)
        for i, block in enumerate(unpile(dot_rows(vst[n, keys, :], pT[keys]))):
            first = pl.multiple_of(512 * n + 128 * i, 128)
            atts[pl.ds(64 * half, 64), pl.ds(first, 128)] = block.astype(BF)

    def project_o():
        @pl.loop(0, 4)
        def _(n):
            at = pl.ds(pl.multiple_of(512 * n, 512), 512)
            h1[:, at] = x[:, at].astype(F32) + dot_in(atts[own], wo[:, :, :, at].reshape(2048, 512))

    def normed_two():
        norm_scale(h1, scale)

        @pl.loop(0, 16)
        def _(i):
            at = pl.ds(pl.multiple_of(i * 128, 128), 128)
            acts[0, 0, :, at] = (h1[:, at] * scale[...] * gains[i, pl.ds(8, 1), :]).astype(BF)

    def mpart_copy(n):
        return [
            pltpu.make_async_copy(
                kv.at[pl.ds(2 * i, 2)], mpart.at[pl.ds(2 * n, 2), :, pl.ds(512 * i, 512)], local.at[60 + i]
            )
            for i in range(4)
        ]

    def group(n):
        at = pl.ds(2 * n, 2)
        rows = pl.ds(pl.multiple_of(256 * n, 256), 256)
        for h in range(3):
            first, second = pl.ds(256 * h, 256), pl.ds(768 + 256 * h, 256)
            here = acts[n].reshape(256, 2048)
            gate = dot_in(here, gu[:, first])
            up = dot_in(here, gu[:, second])
            back = dot_back(dy[at].reshape(256, 2048), wd[first, :])
            curve = 1.0 / (1.0 + jnp.exp(-gate))
            silu = gate * curve
            hid[rows, first] = (silu * up).astype(BF)
            dgu[at, :, first] = (back * up * (curve + silu * (1.0 - curve))).astype(BF).reshape(2, 128, 256)
            dgu[at, :, second] = (back * silu).astype(BF).reshape(2, 128, 256)

        @pl.when(n > 0)
        def _():
            for copy in mpart_copy(n - 1):
                copy.wait()

        for i in range(4):
            wide = pl.ds(512 * i, 512)
            grads = dgu[at].reshape(256, 1536)
            dpart[at, :, wide] = dot_back(grads, gu[wide, :]).astype(BF).reshape(2, 128, 512)
            kv[pl.ds(2 * i, 2)] = dot_in(hid[rows, :], wd[:, wide]).astype(BF).reshape(2, 128, 512)
        for copy in mpart_copy(n):
            copy.start()

    class Views:
        def __init__(self, pick):
            self.pick = pick

        @property
        def at(self):
            return self

        def __getitem__(self, index):
            return self.pick(index)

    def scatter(dev, part, place, columns, row, pair=None):
        wide = pl.ds(0, columns)
        halves = Views(lambda index: place.at[4 + index[0], pl.ds(64 * index[1], 64), wide])
        fulls = Views(lambda index: place.at[2 * index[0] + index[1], :, wide])
        paired = place.at[6, :, wide] if pair is None else pair
        return Scatter(dev, part, 128, halves, fulls, paired, (r0, r1), row)

    first_bay, second_bay = qw.at[:, 0], qw.at[:, 1]
    d = scatter(me.across_y, lambda slot: dpart.at[slot], second_bay, 2048, 0)
    gjob = scatter(me.across_x, gown, first_bay, 1536, 1, g_pair)
    n_job = Scatter(me.across_x, gd_own, 352, n_half, n_full, n_pair, (r0, r1), 2)
    o_job = scatter(me.across_x, lambda slot: op.at[slot], first_bay, 2048, 3)
    q_job = scatter(me.across_x, lambda slot: qp.at[slot], second_bay, 2048, 4)
    k_job = scatter(me.across_x, kp, kw.at[:, 0], 512, 5)
    e_job = Scatter(me.across_x, lambda slot: gp.at[slot], 16, e_half, e_full, e_pair, (r0, r1), 6)
    d_job = scatter(me.across_y, lambda slot: kvp.at[slot], kw.at[:, 1], 512, 7)

    def weight_terms(t, core):
        at = pl.multiple_of((chip_of(me, t) * 2 + core) * 128, 128)
        left = acts[:, :, :, pl.ds(at, 128)].reshape(1024, 128)
        return dot_rows(left, dgu[...].reshape(1024, 1536))

    def gu_to(t):
        return send(gsib(t), grecv.at[t], (c0, c1), 8 + t, me.sibling())

    def down_to(t):
        mine = pl.ds(pl.multiple_of((1 - me.co) * 352, 16), 352)
        return send(gd(t).at[mine], gdrecv.at[t], (c0, c1), t, me.sibling())

    def terms_for_sibling(start):
        @pl.loop(start, start + 2)
        def _(i):
            gsib(7 - i)[...] = weight_terms(7 - i, 1 - me.co).astype(BF)
            gu_to(7 - i).start()

    def sibling_has_terms():
        @pl.loop(0, 8)
        def _(t):
            gu_to(t).wait_send()

    def own_terms(start):
        @pl.loop(start, start + 2)
        def _(i):
            gu_to(7 - i).wait_recv()
            gown(7 - i)[...] = (weight_terms(7 - i, me.co) + grecv[7 - i].astype(F32)).astype(BF)

    def down_terms():
        @pl.loop(0, 8)
        def _(t):
            at = pl.multiple_of(chip_of(me, t) * 256, 256)
            gd(t)[...] = dot_rows(hid[...], dy[:, :, pl.ds(at, 256)].reshape(1024, 256)).astype(BF)
            down_to(t).start()

    def down_sums():
        @pl.loop(0, 8)
        def _(t):
            down_to(t).wait_recv()

            @pl.loop(0, 22)
            def _(i):
                at = pl.ds(pl.multiple_of(i * 16, 16), 16)
                mine = gd(t).at[pl.ds(pl.multiple_of(me.co * 352 + i * 16, 16), 16)]
                mine[...] = (mine[...].astype(F32) + gdrecv[t, at].astype(F32)).astype(BF)

    m_first, m_second = {}, {}
    for dp in (0, 1):
        for way, sign in ((0, 1), (1, -1)):
            m_first[way, dp] = send(
                mpart.at[slot_of(2, dp), pl.ds(64 * way, 64)], m_half.at[way, dp], (r0, r1), (8, way * 2 + dp),
                me.across_y(sign, 0),
            )
            m_second[way, dp] = send(
                dy.at[1 + 2 * way + dp], m_full.at[way, dp], (r0, r1), (8, 4 + way * 2 + dp), me.across_y(sign, 0)
            )
    m_third = send(dy.at[5], m_pair, (r0, r1), (8, 8), me.across_y(0, 1))

    def m_start():
        dy_task.end()
        for copy in mpart_copy(3):
            copy.wait()
        for dp in (1, 0):
            for way in (0, 1):
                m_first[way, dp].start()

    m_parts = {(way, dp): later(mpart.at[slot_of(1 - 2 * way, dp)], dy.at[1 + 2 * way + dp]) for way in (0, 1) for dp in (0, 1)}
    m_halves = {(way, dp): later(m_half.at[way, dp], dy.at[6 + way, pl.ds(0, 64)]) for way in (0, 1) for dp in (0, 1)}
    m_fulls = {(way, dp): later(m_full.at[way, dp], dy.at[6 + way]) for way in (0, 1) for dp in (0, 1)}
    m_mine, m_near, m_last = later(mpart.at[0], dy.at[1]), later(mpart.at[1], dy.at[5]), later(m_pair, dy.at[2])
    m_out = later(dy.at[1], mixed)

    def m_turn(dp):
        for way in (0, 1):
            m_parts[way, dp].start()
        for way in (0, 1):
            m_first[way, dp].wait_recv()
            m_halves[way, dp].start()
        for way in (0, 1):
            m_parts[way, dp].wait()
            m_halves[way, dp].wait()
            add_into(dy.at[1 + 2 * way + dp, pl.ds(64 * way, 64)], 64, [dy.at[6 + way, pl.ds(0, 64)]])
            m_second[way, dp].start()

    def m_pair_up():
        m_near.start()
        for way in (0, 1):
            m_second[way, 1].wait_recv()
            m_fulls[way, 1].start()
        m_near.wait()
        for way in (0, 1):
            m_fulls[way, 1].wait()
        add_into(dy.at[5], 128, [dy.at[6], dy.at[7]])
        m_third.start()

    def m_finish():
        for dp in (0, 1):
            m_second[0, dp].wait_send()
        m_mine.start()
        for way in (0, 1):
            m_second[way, 0].wait_recv()
            m_fulls[way, 0].start()
        m_third.wait_recv()
        m_last.start()
        m_mine.wait()
        for way in (0, 1):
            m_fulls[way, 0].wait()
        m_last.wait()

        @pl.loop(0, 8)
        def _(i):
            at = pl.ds(pl.multiple_of(i * 16, 16), 16)
            total = h1[at]
            for slot in (1, 2, 6, 7):
                total = total + dy[slot, at].astype(F32)
            dy[1, at] = total.astype(BF)

        m_out.start()

    def wo_load(n):
        return pltpu.make_async_copy(
            wo_saved.at[pl.ds(2 * n, 2)], acts.at[pl.ds(2 * (n % 2), 2)], local.at[56 + n % 2]
        )

    def q_load(n):
        return pltpu.make_async_copy(q_saved.at[pl.ds(2 * n, 2)], acts.at[pl.ds(2 * (n % 2), 2)], local.at[58 + n % 2])

    def kw_load():
        return [
            load(kw_saved.at[chip], grecv.at[pl.ds(2 * (chip % 4), 2), :, pl.ds(512 * (chip // 4), 512)])
            for chip in range(8)
        ]

    def at_ctx(ref):
        def loc(dr, dp, er, ep, half):
            return ref.at[me.ctx_at(dr, dp), row_half(half, ref.shape[1])]

        return loc

    def dn_at(dr, dp, er, ep, half):
        first = pl.multiple_of(me.ctx_at(dr, dp) * 256, 256)
        return dn_all.at[row_half(half, 352), pl.ds(first, 256)]

    gu_task = over_y(gown(0), at_ctx(gu_all), 5, both=False)
    dn_task = over_y(dn_moved, dn_at, 6, both=False)
    dn_swap = Swap(me, gd_own(0), dn_moved, (v0, v1), local.at[next(slots)])
    gu_keep = later(gown(0), gu_all.at[me.c])
    dn_keep = later(dn_moved, dn_at(0, 0, 0, 0, None))
    dn_local = later(dnp, wd_at(0, 0, 0, 0, None))
    tokens_out = later(datts.at[own], tokens_grad)

    def block_at(ref, slot):
        first = pl.multiple_of(me.ctx_at(STEPS[slot], PAIRS[slot]) * 16, 16)
        return ref.at[pl.ds(first, 16)]

    def sum_over_ctx(total, got, row):
        return Trade(
            me.across_y, lambda slot: block_at(total, slot), lambda slot: got.at[mirror(slot)], (z0, z1), row
        )

    def spread(out, row):
        return Trade(me.across_y, lambda slot: block_at(out, 0), lambda slot: block_at(out, 0), (z0, z1), row)

    def sum_up(total, got, out):
        value = block_at(total, 0)[...].astype(F32)
        for slot in range(1, 8):
            value = value + got[slot].astype(F32)
        block_at(out, 0)[...] = value.astype(BF)

    o_sum, q_sum, kv_sum = op.at[0], qp.at[0], kp(0)
    o_sums = sum_over_ctx(o_sum, o_got, 0)
    q_sums = sum_over_ctx(q_sum, q_got, 1)
    k_sums = sum_over_ctx(kv_sum, k_got, 2)
    o_spread = spread(o_grad, 3)
    q_spread = spread(q_grad, 4)
    k_spread = spread(kv_grad, 5)
    e_task = Trade(me.across_y, lambda slot: g_sum, lambda slot: ggot.at[me.c], (z0, z1), 6)

    def to_sibling(src, dst, index):
        return send(src, dst, (c0, c1), 16 + index, me.sibling())

    att_swap = to_sibling(atts.at[own], atts.at[other], 0)
    datt_swap = to_sibling(datts.at[own], datts.at[other], 1)
    a1_swap = to_sibling(a1s.at[own], a1s.at[other], 2)
    queries, rest = pl.ds(0, 2048), pl.ds(2048, 512)
    dq_swap = to_sibling(dqkvs.at[own, queries], dqkvs.at[other, queries], 3)
    dkv_swap = to_sibling(dqkvs.at[own, rest], dqkvs.at[other, rest], 4)
    gain_swap = to_sibling(gown_rows, gsib_rows, 5)

    def norm_two_back():
        for i in range(16):
            grow[0, :, 128 * i : 128 * i + 128] = gains[i, 0:1, :]
            grow[1, :, 128 * i : 128 * i + 128] = gains[i, 8:9, :]
        grow[2] = jnp.zeros((1, 2048), F32)
        grow[3] = jnp.zeros((1, 2048), F32)

        @pl.loop(0, 8)
        def _(i):
            at = pl.ds(pl.multiple_of(16 * i, 16), 16)
            values, grad = h1[at], da2[at]
            scale = lax.rsqrt(jnp.mean(values * values, axis=1, keepdims=True) + EPS)
            grow[3] += jnp.sum(grad * values * scale, axis=0, keepdims=True)
            grad = grad * grow[1]
            level = jnp.mean(grad * values, axis=1, keepdims=True) * scale * scale * scale
            total = dy[0, at].astype(F32) + scale * grad - values * level
            da2[at] = total
            datts[at] = total.astype(BF)

        datt_swap.start()

    def heads_back():
        for n in range(4):
            wo_load(n).wait()
            part = dot_back(datts[own], acts[2 * (n % 2) : 2 * (n % 2) + 2].reshape(512, 2048)).astype(BF)
            for half in (0, 1):
                place = dost(n, half)
                for h in range(8):
                    place[h // 2, pl.ds(64 * (h % 2), 64), pl.ds(0, 64)] = part[
                        64 * half : 64 * half + 64, 64 * h : 64 * h + 64
                    ]
            if n < 2:
                wo_load(n + 2).start()
        for n in range(2):
            q_load(n).start()

    def terms(left, right, out, job):
        @pl.loop(0, 8)
        def _(i):
            at = pl.multiple_of((chip_of(me, 7 - i) * 2 + me.co) * 128, 128)
            out(7 - i)[...] = dot_rows(left[:, pl.ds(at, 128)], right[...]).astype(BF)

            @pl.when(i == 1)
            def _():
                job.start()

    def output_terms():
        att_swap.wait_recv()
        datt_swap.wait_recv()
        pl.semaphore_wait(credit, 3)
        terms(atts, datts, lambda t: op.at[t], o_job)

    def query_terms():
        a1_swap.wait_recv()
        dq_swap.wait_recv()
        terms(a1s, dqkvs.at[:, pl.ds(0, 2048)], lambda t: qp.at[t], q_job)

    def kv_terms():
        dkv_swap.wait_recv()
        terms(a1s, dqkvs.at[:, pl.ds(2048, 512)], kp, k_job)

    def kv_blocks(mate):
        for part, base in ((0, 0), (64, 256)):
            for n in range(4):
                first = base + 64 * n
                block = grecv[0:5, :, 128 * n : 128 * n + 128].reshape(640, 128)[:, part : part + 64]
                for slot in range(8):
                    kvp[slot, 0:64, first : first + 64] = block[64 * slot : 64 * slot + 64]
                    if slot == 0:
                        late = block[576:640]
                    else:
                        late = jnp.where(mate == slot, block[512:576], jnp.zeros((64, 64), BF))
                    kvp[slot, 64:128, first : first + 64] = late

    def kv_back():
        for i in range(2):
            at = slice(128 * i, 128 * i + 128)
            block = sT[512:640, at]
            dqkvs[own, 2048 + 128 * i : 2176 + 128 * i] = (block * cosine[...] - turned(block) * sine[...]).astype(BF)
        dqkvs[own, 2304:2560] = sT[512:640, 256:512].astype(BF)
        dkv_swap.start()

    def inputs_back():
        for copy in kw_back:
            copy.wait()
        for n in range(4):
            q_load(n).wait()
            block = dot_back(dqkvs[own, queries], acts[2 * (n % 2) : 2 * (n % 2) + 2].reshape(512, 2048))
            four, wide = pl.ds(4 * (n % 2), 4), pl.ds(512 * (n // 2), 512)
            block = block + dot_back(dqkvs[own, rest], grecv[four, :, wide].reshape(512, 512))
            sT[pl.ds(128 * n, 128)] = block
            if n < 2:
                q_load(n + 2).start()

    def norm_one_back():
        datt_swap.wait_send()

        @pl.loop(0, 8)
        def _(i):
            at = pl.ds(pl.multiple_of(16 * i, 16), 16)
            values = x[at].astype(F32)
            grad = jnp.concatenate([sT[pl.ds(pl.multiple_of(128 * n + 16 * i, 16), 16)] for n in range(4)], axis=1)
            scale = lax.rsqrt(jnp.mean(values * values, axis=1, keepdims=True) + EPS)
            grow[2] += jnp.sum(grad * values * scale, axis=0, keepdims=True)
            grad = grad * grow[0]
            level = jnp.mean(grad * values, axis=1, keepdims=True) * scale * scale * scale
            datts[at] = (da2[at] + scale * grad - values * level).astype(BF)

        tokens_out.start()

        gown_rows[...] = jnp.zeros((16, 16, 128), F32)
        for i in range(16):
            gown_rows[i, 0:1, :] = grow[2, :, 128 * i : 128 * i + 128]
            gown_rows[i, 8:9, :] = grow[3, :, 128 * i : 128 * i + 128]
        gain_swap.start()

    def gain_terms():
        gain_swap.wait_recv()
        for slot in range(8):
            block = me.fsdp_at(STEPS[slot], PAIRS[slot])
            gp[slot] = gown_rows[block] + gsib_rows[block]

    def dn_begin():
        dn_swap.wait()
        dn_task.start()
        dn_keep.start()

    def gu_begin():
        gu_keep.start()
        gu_task.start()

    def e_begin():
        e_task.start()
        ggot[me.c] = g_sum[...]

    def attend_back(n, half):
        count = 512 if half == 0 else 640
        keys = pl.ds(0, count)
        key, query, out = kst[n, keys, :], qst[n, half], dost(n, half)[...].reshape(512, 128)[:, 0:64]
        sT[keys] = dot_back(key, query)
        dT[keys] = dot_back(vst[n, keys, :], out)
        for i in range(4):
            at = pl.ds(128 * i, 128)
            parts = []
            for first, size in ((0, 512), (512, 128))[: 1 + half]:
                scores = sT[first : first + size, at]
                if half == 0:
                    scores = scores + bias_p[...]
                elif first:
                    scores = scores + bias_c[...]
                probs = jnp.exp(scores - lse[2 * n + half, :, at])
                grad = dT[first : first + size, at]
                parts.append((first, size, probs, grad))
            level = sum(jnp.sum(probs * grad, axis=0, keepdims=True) for _, _, probs, grad in parts)
            for first, size, probs, grad in parts:
                pT[first : first + size, at] = probs.astype(BF)
                dsT[first : first + size, at] = (probs * (grad - level)).astype(BF)
        rows = slice(64 * half, 64 * half + 64)
        for i, block in enumerate(unpile(dot_rows(key, dsT[keys]) * SCALE)):
            block = block * cosine[rows] - turned(block) * sine[rows]
            first = pl.multiple_of(512 * n + 128 * i, 128)
            dqkvs[rows, pl.ds(first, 128)] = block.astype(BF)
        return dot_in(dsT[keys], query), dot_in(pT[keys], out)

    def keep_kv_grads(n, one, two):
        keys = jnp.concatenate([one[0] + two[0][0:512], two[0][512:640]], axis=0)
        values = jnp.concatenate([one[1] + two[1][0:512], two[1][512:640]], axis=0)
        both = jnp.concatenate([keys, values], axis=1).astype(BF)
        grecv[pl.ds(0, 5), :, pl.ds(pl.multiple_of(128 * n, 128), 128)] = both.reshape(5, 128, 128)

    qx.start()
    dy_task.start()
    ox.start()
    g.start()
    loads[0].wait()
    loads[1].wait()
    k.start()
    mate = place_tables(me, deal, freq, cosine, sine, bias_p, bias_c)
    qx.turn(0)
    ox.turn(0)
    qx.pair()
    k.turn(0)
    qx.turn(1)
    q.start()
    g.turn(0)
    qx.last(1)
    qx.last(0)
    kept[qx].wait()
    qy.start()
    g.pair()
    dy_task.pair()
    q.turn(0)
    g.turn(1)
    k.pair()
    ox.pair()
    k.turn(1)
    o.start()
    q.last(0)
    ox.turn(1)
    ox.last(0)
    swap.start()
    g.last(0)
    qy.turn(0)
    qy.pair()
    g.last(1)
    k.last(0)
    put_gate_up()
    k.last(1)
    q.pair()
    g.sync()
    normed()
    k.sync()
    ox.last(1)
    o.pair()
    project_kv()
    kv_task.start()
    o.turn(0)
    qy.last(0)
    qy.turn(1)
    kv_task.pair()
    kept[ox].wait()
    oy.start()
    q.turn(1)
    swap.wait()
    dn_local.start()
    dn.start()
    qy.last(1)
    m.start()
    kv_task.turn(0)
    q.last(1)
    qy.sync()
    kv_task.turn(1)
    oy.pair()
    kv_task.last(0)
    q.sync()
    kept[q].wait()
    saved.append(load(qw, q_saved))
    saved.append(load(kw, kw_saved))
    project_q()
    o.turn(1)
    kv_task.last(1)
    oy.turn(0)
    collect_kv(mate)
    a1_swap.start()

    @pl.loop(0, 4)
    def _(n):
        attend(n, 0)
        attend(n, 1)

        @pl.when(n == 0)
        def _():
            o.last(0)
            dn.turn(0)
            oy.turn(1)
            dn.pair()

        @pl.when(n == 1)
        def _():
            dy_task.turn(0)
            oy.last(0)

        @pl.when(n == 2)
        def _():
            o.last(1)
            oy.last(1)
            m.pair()

    dy_task.turn(1)
    o.sync()
    oy.sync()
    kept[o].wait()
    saved.append(load(wo, wo_saved))
    project_o()
    normed_two()
    for task in (k, q, qx, qy):
        task.end()
    saved[0].wait()
    saved[1].wait()
    a.start()
    m.turn(0)
    dy_task.last(1)
    dy_task.last(0)
    m.turn(1)
    dn.last(0)
    dn.turn(1)
    a.pair()
    a.turn(0)
    dn.last(1)
    m.last(1)
    m.last(0)
    m.sync()
    dn.sync()

    for task in (o, ox, oy, kv_task):
        task.end()
    saved[2].wait()
    dn_local.wait()
    kept[dy_task].wait()

    @pl.loop(0, 4)
    def _(n):
        group(n)

        @pl.when(n == 0)
        def _():
            a.turn(1)

        @pl.when(n == 2)
        def _():
            a.last(0)
            att_swap.start()
            a.last(1)

    d.start()
    m.end()
    terms_for_sibling(0)
    dn.end()
    down_terms()
    d.turn(1)
    own_terms(0)
    gjob.start()
    terms_for_sibling(2)
    terms_for_sibling(4)
    own_terms(2)
    terms_for_sibling(6)
    down_sums()
    n_job.start()
    d.turn(0)
    own_terms(4)
    gjob.turn(1)
    m_start()
    own_terms(6)
    a.end()
    wo_load(0).start()
    wo_load(1).start()
    d.pair()
    n_job.turn(1)
    gjob.pair()
    gjob.turn(0)
    d.finish(da2)
    n_job.turn(0)
    norm_two_back()
    m_turn(1)
    gjob.finish(gown(0))
    for device in near(me.across_x):
        pl.semaphore_signal(credit, 1, device_id=device, device_id_type=MESH)
    gu_begin()
    d.end()
    output_terms()
    m_turn(0)
    heads_back()

    @pl.loop(0, 4)
    def _(n):
        one, two = attend_back(n, 0), attend_back(n, 1)
        keep_kv_grads(n, one, two)

        @pl.when(n == 0)
        def _():
            o_job.turn(1)
            n_job.pair()

        @pl.when(n == 1)
        def _():
            m_pair_up()

    dq_swap.start()
    o_job.turn(0)
    kv_blocks(mate)
    kw_back = kw_load()
    d_job.start()
    n_job.finish(gd_own(0))
    dn_swap.start()
    o_job.pair()
    gu_task.turn(0)
    d_job.turn(1)
    d_job.turn(0)
    query_terms()
    gu_task.pair()
    d_job.pair()
    o_job.finish(o_sum)
    d_job.finish(sT.at[pl.ds(512, 128)])
    o_sums.start()
    q_job.turn(1)
    m_finish()
    dn_begin()
    kv_back()
    o_sums.got()
    gu_task.turn(1)
    sum_up(o_sum, o_got, o_grad)
    sibling_has_terms()
    kv_terms()
    o_spread.start()
    k_job.turn(1)
    q_job.turn(0)
    dn_task.pair()
    q_job.pair()
    dn_task.turn(0)
    gu_task.last(0)
    k_job.turn(0)
    inputs_back()
    norm_one_back()
    k_job.pair()
    gain_terms()
    dn_task.turn(1)
    q_job.finish(q_sum)
    q_sums.start()
    k_job.finish(kv_sum)
    e_job.start()
    dn_task.last(0)
    e_job.turn(1)
    dn_task.last(1)
    e_job.pair()
    k_sums.start()
    e_job.turn(0)
    q_sums.got()
    sum_up(q_sum, q_got, q_grad)
    q_spread.start()
    e_job.finish(g_sum)
    k_sums.got()
    sum_up(kv_sum, k_got, kv_grad)
    gu_task.last(1)
    k_spread.start()
    o_spread.got()
    e_begin()
    k_spread.got()
    q_spread.got()
    e_task.got()
    total = ggot[0]
    for index in range(1, 8):
        total = total + ggot[index]
    gains_out[...] = total
    for job in (g, gjob, n_job, o_job, q_job, k_job, e_job, d_job, gu_task, dn_task):
        job.end()
    for job in (o_sums, q_sums, k_sums, o_spread, q_spread, k_spread, e_task):
        job.end()
    for copy in (*m_first.values(), m_second[1, 0], m_second[1, 1], m_third):
        copy.wait_send()
    m_out.wait()
    tokens_out.wait()
    gu_keep.wait()
    dn_keep.wait()
    for copy in (att_swap, a1_swap, dq_swap, dkv_swap, gain_swap):
        copy.wait_send()

    @pl.loop(0, 8)
    def _(t):
        down_to(t).wait_send()


def layer(x, attn_gain, mlp_gain, deal, freq, q, key, value, wo, gate, up, dn, dy):
    shape = jax.ShapeDtypeStruct
    smem = pl.BlockSpec(memory_space=pltpu.SMEM)
    vmem = pltpu.VMEM
    outs = pl.pallas_call(
        layer_kernel,
        out_shape=(
            shape((128, 2048), BF),
            shape((128, 2048), BF),
            shape((128, 2048), BF),
            shape((128, 512), BF),
            shape((128, 2048), BF),
            shape((16, 128), F32),
            shape((8, 128, 1536), BF),
            shape((352, 2048), BF),
            shape((8, 2, 128, 2048), BF),
            shape((8, 2, 128, 512), BF),
            shape((8, 2, 128, 2048), BF),
            shape((8, 128, 2048), BF),
            shape((2, 2, 64, 2048), BF),
            shape((2, 2, 128, 2048), BF),
            shape((128, 2048), BF),
        ),
        in_specs=[VMEM] * 3 + [smem, VMEM] + [ANY] * 8,
        out_specs=[ANY] * 2 + [VMEM] * 4 + [ANY] * 9,
        scratch_shapes=[
            vmem((16, 16, 128), F32),
            vmem((256, 2048), BF),
            vmem((256, 2048), BF),
            vmem((4, 2, 512, 64), BF),
            vmem((4, 640, 64), BF),
            vmem((4, 640, 64), BF),
            vmem((8, 1, 512), F32),
            vmem((128, 2048), F32),
            vmem((128, 128), F32),
            vmem((128, 128), F32),
            vmem((512, 128), F32),
            vmem((128, 128), F32),
            vmem((8, 2, 128, 2048), BF),
            vmem((8, 2, 128, 512), BF),
            vmem((8, 2, 128, 2048), BF),
            vmem((128, 512), BF),
            vmem((8, 128, 512), BF),
            vmem((640, 512), F32),
            vmem((640, 512), BF),
            vmem((640, 512), F32),
            vmem((640, 512), BF),
            vmem((128, 1), F32),
            vmem((2, 128, 768), BF),
            vmem((352, 256), BF),
            vmem((4, 2, 128, 2048), BF),
            vmem((2048, 1536), BF),
            vmem((768, 2048), BF),
            vmem((8, 128, 2048), BF),
            vmem((1024, 768), BF),
            vmem((8, 128, 1536), BF),
            vmem((8, 352, 256), BF),
            vmem((128, 1536), BF),
            vmem((128, 2048), F32),
            vmem((256, 2048), BF),
            vmem((256, 2560), BF),
            vmem((4, 1, 2048), F32),
            vmem((16, 16, 128), F32),
            vmem((16, 16, 128), F32),
            vmem((352, 256), BF),
            *scatter_buffers(352, 256),
            *scatter_buffers(16, 128, F32),
            vmem((8, 16, 128), F32),
            vmem((8, 16, 128), F32),
            vmem((16, 128), F32),
            vmem((8, 16, 2048), BF),
            vmem((8, 16, 2048), BF),
            vmem((8, 16, 512), BF),
            *dma_sems(8, 9),
            *dma_sems(8, 10),
            *dma_sems(7, 9),
            *dma_sems(2, 10),
            *dma_sems(9, 9),
            *dma_sems(7, 8),
            pltpu.SemaphoreType.DMA((22,)),
            pltpu.SemaphoreType.DMA((22,)),
            pltpu.SemaphoreType.DMA,
            pltpu.SemaphoreType.DMA,
            pltpu.SemaphoreType.DMA,
            pltpu.SemaphoreType.DMA,
            pltpu.SemaphoreType.REGULAR,
            pltpu.SemaphoreType.DMA((64,)),
        ],
        compiler_params=params(1, 63),
        name="layer",
    )(x, attn_gain, mlp_gain, deal, freq, q, key, value, wo, gate, up, dn, dy)
    return outs[:8]


def widen_kernel(parts, gate, up):
    for out, base in ((gate, 0), (up, 768)):
        for pair in range(4):
            even = parts[2 * pair, :, base : base + 768].astype(F32)
            odd = pltpu.roll(parts[2 * pair + 1, :, base : base + 768].astype(F32), 64, 1)
            first = 1408 * pair
            out[:, first : first + 640] = even[:, 0:640]
            out[:, first + 640 : first + 768] = even[:, 640:768] + odd[:, 0:128]
            out[:, first + 768 : first + 1408] = odd[:, 128:768]


def widen(parts):
    out = jax.ShapeDtypeStruct((128, 5632), F32)
    block = pl.BlockSpec((16, 5632), lambda i: (i, 0))
    return pl.pallas_call(
        widen_kernel,
        grid=(8,),
        out_shape=(out, out),
        in_specs=[pl.BlockSpec((8, 16, 1536), lambda i: (0, i, 0))],
        out_specs=[block, block],
        name="widen",
    )(parts)


def on_device(
    tokens,
    block_deal,
    attn_gain,
    query_weight,
    key_weight,
    value_weight,
    output_weight,
    mlp_gain,
    gate_weight,
    up_weight,
    down_weight,
    cotangent,
):
    freq = BASE ** (-(jnp.arange(HEAD_DIM // 2, dtype=F32) * 2.0) / HEAD_DIM)
    freq = jnp.concatenate([freq] * 4)[None]
    deal = block_deal.reshape(256)
    mixed, tokens_grad, query_grad, kv_grad, o_grad, gain_grads, gu_grads, dn_grad = layer(
        tokens[0], attn_gain[None], mlp_gain[None], deal, freq, query_weight, key_weight, value_weight, output_weight,
        gate_weight, up_weight, down_weight, cotangent[0],
    )
    gate_grad, up_grad = widen(gu_grads)
    return (
        mixed[None],
        tokens_grad[None],
        gain_grads[0],
        query_grad.astype(F32),
        kv_grad[:, :256].astype(F32),
        kv_grad[:, 256:].astype(F32),
        o_grad.astype(F32),
        gain_grads[8],
        gate_grad,
        up_grad,
        dn_grad.astype(F32),
    )


def solution(mesh):
    held = P("fsdp", "ctx", None)
    rows = P("fsdp", None)
    return jax.shard_map(
        on_device,
        mesh=mesh,
        in_specs=(held, P(), P("fsdp"), rows, rows, rows, rows, P("fsdp"), rows, rows, rows, held),
        out_specs=(held, held, P("fsdp"), rows, rows, rows, rows, P("fsdp"), rows, rows, rows),
        check_vma=False,
    )
```

```python
import functools

import jax
import jax.numpy as jnp
from jax import lax
from jax.experimental import pallas as pl
from jax.experimental.pallas import tpu as pltpu
from jax.sharding import PartitionSpec as P
import numpy as np

MESH = pl.DeviceIdType.MESH
BF = jnp.bfloat16
F32 = jnp.float32
ANY = pl.BlockSpec(memory_space=pl.ANY)
VMEM = pl.BlockSpec(memory_space=pltpu.VMEM)

HEAD_DIM = 64
EPS = 1e-05
SCALE = 0.125
BASE = 10000.0

SLOT = {(0, 0): 0, (0, 1): 1, (1, 0): 2, (3, 0): 3, (1, 1): 4, (3, 1): 5, (2, 0): 6, (2, 1): 7}
STEPS = (0, 0, 1, 3, 1, 3, 2, 2)
PAIRS = (0, 1, 0, 0, 1, 1, 0, 1)


def slot_of(dr, dp):
    return SLOT[(dr % 4, dp % 2)]


class Place:
    def __init__(self):
        self.c = lax.axis_index("ctx")
        self.f = lax.axis_index("fsdp")
        self.y, self.zl = lax.div(self.c, 2), lax.rem(self.c, 2)
        self.j, self.co = lax.div(self.f, 2), lax.rem(self.f, 2)
        self.x, self.zh = lax.div(self.j, 2), lax.rem(self.j, 2)

    def ctx_at(self, dr, dp):
        return lax.rem(self.y + dr % 4, 4) * 2 + lax.rem(self.zl + dp, 2)

    def chip_at(self, dr, dp):
        return lax.rem(self.x + dr % 4, 4) * 2 + lax.rem(self.zh + dp, 2)

    def fsdp_at(self, dr, dp):
        return self.chip_at(dr, dp) * 2 + self.co

    def across_y(self, dr, dp):
        return {"ctx": self.ctx_at(dr, dp), "fsdp": self.f}

    def across_x(self, dr, dp):
        return {"ctx": self.c, "fsdp": self.fsdp_at(dr, dp)}

    def sibling(self):
        return {"ctx": self.c, "fsdp": self.f + 1 - 2 * self.co}


def chip_of(me, t):
    dr = jnp.where(t < 2, 0, jnp.where(t >= 6, 2, 1 + 2 * lax.rem(t, 2)))
    dp = jnp.where(t < 2, t, jnp.where(t >= 6, t - 6, lax.div(t, 4)))
    return lax.rem(me.x + dr, 4) * 2 + lax.rem(me.zh + dp, 2)


def greet(devices):
    barrier = pltpu.get_barrier_semaphore()
    for device in devices:
        pl.semaphore_signal(barrier, 1, device_id=device, device_id_type=MESH)
    pl.semaphore_wait(barrier, len(devices))


class Swap:
    def __init__(self, me, src, dst, sems, local):
        self.moved = me.c != me.j
        self.to = {"ctx": me.j, "fsdp": 2 * me.c + me.co}
        self.copy = pltpu.make_async_remote_copy(
            src, dst, sems[0], sems[1], device_id=self.to, device_id_type=MESH
        )
        self.keep = pltpu.make_async_copy(src, dst, local)

    def start(self):
        pl.when(self.moved)(self.copy.start)
        pl.when(jnp.logical_not(self.moved))(self.keep.start)

    def wait(self):
        pl.when(self.moved)(self.copy.wait)
        pl.when(jnp.logical_not(self.moved))(self.keep.wait)


def greet_all(me, plane=False):
    barrier = pltpu.get_barrier_semaphore()
    others = near(me.across_x) + [me.sibling()]
    others += [me.across_y(STEPS[s], PAIRS[s]) for s in range(1, 8)] if plane else near(me.across_y)
    for device in others:
        pl.semaphore_signal(barrier, 1, device_id=device, device_id_type=MESH)
    moved = me.c != me.j

    @pl.when(moved)
    def _():
        to = {"ctx": me.j, "fsdp": 2 * me.c + me.co}
        pl.semaphore_signal(barrier, 1, device_id=to, device_id_type=MESH)

    pl.semaphore_wait(barrier, len(others) + jnp.where(moved, 1, 0))


def near(dev):
    return [dev(1, 0), dev(-1, 0), dev(0, 1)]


def send(src, dst, sems, index, device):
    return pltpu.make_async_remote_copy(
        src, dst, sems[0].at[index], sems[1].at[index], device_id=device, device_id_type=MESH
    )


class Gather:
    MOVES = (
        ((0, 0), (0, 1), None),
        ((0, 0), (1, 0), None),
        ((0, 0), (-1, 0), None),
        ((0, 1), (1, 0), None),
        ((0, 1), (-1, 0), None),
        ((-1, 0), (1, 0), 0),
        ((-1, 1), (1, 0), 0),
        ((1, 0), (-1, 0), 1),
        ((1, 1), (-1, 0), 1),
    )

    def __init__(self, dev, own, loc, sems, row, sibling=None, sibling_sems=None):
        self.loc = loc
        self.copies = []
        for index, (block, to, half) in enumerate(self.MOVES):
            src = own if block == (0, 0) else loc(*block, 0, 0, half)
            dst = loc(*block, *to, half)
            self.copies.append(send(src, dst, sems, (row, index), dev(*to)))
        self.passed = {}
        if sibling is not None:
            self.passed[9] = send(own, loc(0, 0, 0, 0, None), sibling_sems, (row, 9), sibling)
            for index, ((dr, dp), (er, ep), half) in enumerate(self.MOVES):
                ref = loc(dr - er, dp + ep, 0, 0, half)
                self.passed[index] = send(ref, ref, sibling_sems, (row, index), sibling)
        self.own = own

    def _pass(self, index):
        if self.passed:
            self.passed[index].start()

    def _got(self, index):
        self.copies[index].wait_recv()
        self._pass(index)

    def start(self):
        for index in (0, 1, 2):
            self.copies[index].start()
        self._pass(9)

    def pair(self):
        self._got(0)
        self.copies[3].start()
        self.copies[4].start()

    def turn(self, dp):
        for got, on in (((1, 5), (2, 7)) if dp == 0 else ((3, 6), (4, 8))):
            self._got(got)
            self.copies[on].start()

    def last(self, dp):
        for got in ((5, 7) if dp == 0 else (6, 8)):
            self._got(got)

    def sync(self):
        for copy in self.passed.values():
            copy.wait()

    def end(self):
        for copy in self.copies:
            copy.wait_send()


class RingFirst:
    MOVES = (
        ((0, 0), (0, 1), None),
        ((0, 0), (1, 0), None),
        ((0, 0), (-1, 0), None),
        ((-1, 0), (1, 0), 0),
        ((1, 0), (-1, 0), 1),
        ((-1, 0), (0, 1), None),
        ((1, 0), (0, 1), None),
        ((2, 0), (0, 1), 0),
        ((2, 0), (0, 1), 1),
    )

    def __init__(self, dev, own, loc, sems, row):
        self.own, self.loc = own, loc
        self.copies = []
        for index, (block, to, half) in enumerate(self.MOVES):
            src = own if block == (0, 0) else loc(*block, 0, 0, half)
            self.copies.append(send(src, loc(*block, *to, half), sems, (row, index), dev(*to)))

    def go(self, *indices):
        for index in indices:
            self.copies[index].start()

    def got(self, *indices):
        for index in indices:
            self.copies[index].wait_recv()

    def end(self):
        for copy in self.copies:
            copy.wait_send()


def row_half(half, rows):
    return pl.ds(0, rows) if half is None else pl.ds(half * (rows // 2), rows // 2)


def add_into(ref, rows, others, step=16):
    step = min(step, rows)

    @pl.loop(0, rows // step)
    def _(i):
        at = pl.ds(pl.multiple_of(i * step, step), step)
        total = ref[at].astype(F32)
        for other in others:
            total = total + other[at].astype(F32)
        ref[at] = total.astype(ref.dtype)


class Scatter:
    def __init__(self, dev, part, rows, halves, fulls, paired, sems, row, cut=None):
        self.part, self.rows, self.cut = part, rows, cut
        self.halves, self.fulls, self.paired = halves, fulls, paired
        self.first, self.second = {}, {}
        for dp in (0, 1):
            for way, sign in ((0, 1), (1, -1)):
                self.first[way, dp] = send(
                    self._half(part(slot_of(2, dp)), way), halves.at[way, dp], sems, (row, way * 2 + dp), dev(sign, 0)
                )
                self.second[way, dp] = send(
                    part(slot_of(sign, dp)), fulls.at[way, dp], sems, (row, 4 + way * 2 + dp), dev(sign, 0)
                )
        self.third = send(part(slot_of(0, 1)), paired, sems, (row, 8), dev(0, 1))

    def _half(self, ref, way):
        if self.cut is None:
            return ref.at[pl.ds(way * (self.rows // 2), self.rows // 2)]
        return ref.at[:, pl.ds(way * (self.cut // 2), self.cut // 2)]

    def start(self):
        for dp in (1, 0):
            for way in (0, 1):
                self.first[way, dp].start()

    def turn(self, dp):
        for way, sign in ((0, 1), (1, -1)):
            self.first[way, dp].wait_recv()
            block = self._half(self.part(slot_of(sign, dp)), way)
            add_into(block, block.shape[0], [self.halves.at[way, dp]])
            self.second[way, dp].start()

    def pair(self):
        for way in (0, 1):
            self.second[way, 1].wait_recv()
        add_into(self.part(slot_of(0, 1)), self.rows, [self.fulls.at[0, 1], self.fulls.at[1, 1]])
        self.third.start()

    def finish(self, out, extra=()):
        for way in (0, 1):
            self.second[way, 0].wait_recv()
        self.third.wait_recv()
        own = self.part(0)
        terms = [own, self.fulls.at[0, 0], self.fulls.at[1, 0], self.paired, *extra]

        @pl.loop(0, self.rows // 16)
        def _(i):
            at = pl.ds(pl.multiple_of(i * 16, 16), 16)
            total = terms[0][at].astype(F32)
            for term in terms[1:]:
                total = total + term[at].astype(F32)
            out[at] = total.astype(out.dtype)

    def end(self):
        for copy in (*self.first.values(), *self.second.values(), self.third):
            copy.wait_send()


def mirror(slot):
    return slot_of(-STEPS[slot], PAIRS[slot])


class Trade:
    def __init__(self, dev, what, where, sems, row):
        self.copies = [
            pltpu.make_async_remote_copy(
                what(slot), where(slot), sems[0].at[row, slot], sems[1].at[row, mirror(slot)],
                device_id=dev(STEPS[slot], PAIRS[slot]), device_id_type=MESH,
            )
            for slot in range(1, 8)
        ]

    def start(self):
        for copy in self.copies:
            copy.start()

    def got(self):
        for copy in self.copies:
            copy.wait_recv()

    def end(self):
        for copy in self.copies:
            copy.wait_send()


def scatter_buffers(rows, columns, dtype=BF, cut=False):
    half = (rows, columns // 2) if cut else (rows // 2, columns)
    return [
        pltpu.VMEM((2, 2, *half), dtype),
        pltpu.VMEM((2, 2, rows, columns), dtype),
        pltpu.VMEM((rows, columns), dtype),
    ]


def dma_sems(rows, count):
    return [pltpu.SemaphoreType.DMA((rows, count)), pltpu.SemaphoreType.DMA((rows, count))]


def params(collective_id, vmem=56):
    return pltpu.CompilerParams(
        collective_id=collective_id, has_side_effects=True, vmem_limit_bytes=vmem << 20
    )


def dot_in(left, right):
    return jnp.dot(left, right, preferred_element_type=F32)


def dot_back(left, right):
    return lax.dot_general(left, right, (((1,), (1,)), ((), ())), preferred_element_type=F32)


def dot_rows(left, right):
    return lax.dot_general(left, right, (((0,), (0,)), ((), ())), preferred_element_type=F32)


def load(src, dst, sem):
    copy = pltpu.make_async_copy(src, dst, sem)
    copy.start()
    return copy


def turned(values):
    lane = lax.broadcasted_iota(jnp.int32, values.shape, 1)
    low = lax.rem(lane, 64) < 32
    return jnp.where(low, pltpu.roll(values, 96, 1), pltpu.roll(values, 32, 1))


def pile(out, values, half):
    for h in range(8):
        out[pl.ds(64 * h, 64), :] = values[64 * half : 64 * half + 64, 64 * h : 64 * h + 64]


def unpile(values):
    flat = values.T
    return [
        jnp.concatenate([flat[128 * m : 128 * m + 64], flat[128 * m + 64 : 128 * m + 128]], axis=1)
        for m in range(4)
    ]


def norm_scale(ref, out):
    values = ref[...].astype(F32)
    out[...] = lax.rsqrt(jnp.mean(values * values, axis=1, keepdims=True) + EPS)


def place_tables(me, deal, freq, cosine, sine, bias_p, bias_c):
    def block(slot, part):
        return deal[(me.f * 8 + me.ctx_at(STEPS[slot], PAIRS[slot])) * 2 + part]

    first, second = block(0, 0), block(0, 1)
    odd = lax.rem(second, 2)
    row = lax.broadcasted_iota(jnp.int32, (128, 128), 0)
    lane = lax.broadcasted_iota(jnp.int32, (128, 128), 1)
    position = jnp.where(row < 64, first * 64 + row, 448 + odd * 64 + row)
    angle = position.astype(F32) * freq[...]
    cosine[...] = jnp.cos(angle)
    sine[...] = jnp.where(lax.rem(lane, 64) < 32, -jnp.sin(angle), jnp.sin(angle))
    row, lane = row[:64], lax.rem(lane[:64], 64)
    mate = jnp.int32(0)
    for slot in range(8):
        seen = block(slot, 0) * 64 + row <= first * 64 + lane
        bias_p[pl.ds(64 * slot, 64), :] = jnp.where(seen, 0.0, -1e30)
        if slot:
            mate = mate + jnp.where(block(slot, 1) == second + 1 - 2 * odd, slot, 0)
    bias_c[pl.ds(0, 64), :] = jnp.where(odd + 0 * row == 1, 0.0, -1e30)
    bias_c[pl.ds(64, 64), :] = jnp.where(row <= lane, 0.0, -1e30)
    return mate


def find_mate(me, deal):
    def block(slot):
        return deal[(me.f * 8 + me.ctx_at(STEPS[slot], PAIRS[slot])) * 2 + 1]

    second = block(0)
    mate = jnp.int32(0)
    for slot in range(1, 8):
        mate = mate + jnp.where(block(slot) == second + 1 - 2 * lax.rem(second, 2), slot, 0)
    return mate


def layer_kernel(
    x, attn_gain, mlp_gain, deal, freq, q_in, key_in, value_in, wo_in, gate_in, up_in, dn_in, dy_in,
    mixed, tokens_grad, q_grad, kv_grad, o_grad, gains_out, gu_all, dn_all,
    q_saved, kw_saved, wo_saved, mpart, m_half, m_full, m_pair,
    gains, a1s, atts, qst, kst, vst, lse, h1, cosine, sine, bias_p, bias_c,
    qw, kw, wo, kv_own, kv, sT, pT, dT, dsT, scale, gu_win, dnp, acts, gu, wd, dy, hid,
    grecv, gdrecv, g_pair, da2, datts, dqkvs, grow, gown_rows, gsib_rows, dn_moved,
    n_half, n_full, n_pair, e_half, e_full, e_pair, gp, ggot, g_sum, o_got, q_got, k_got,
    s0, s1, t0, t1, y0, y1, u0, u1, r0, r1, z0, z1, c0, c1, w0, w1, v0, v1, credit, local,
):
    me = Place()
    greet_all(me, plane=True)
    own, other = pl.ds(0, 128), pl.ds(128, 128)
    slots = iter(range(64))

    def load(src, dst):
        copy = pltpu.make_async_copy(src, dst, local.at[next(slots)])
        copy.start()
        return copy

    def later(src, dst):
        return pltpu.make_async_copy(src, dst, local.at[next(slots)])

    def aligned(index, step):
        return index if isinstance(index, int) else pl.multiple_of(index, step)

    def gains_at(dr, dp, er, ep, half):
        return gains.at[me.fsdp_at(dr, dp), row_half(half, 16)]

    def slot_at(ref, rows):
        def loc(dr, dp, er, ep, half):
            return ref.at[slot_of(dr - er, dp + ep), row_half(half, rows)]

        return loc

    def acts_at(dr, dp, er, ep, half):
        slot = slot_of(dr - er, dp + ep)
        return acts.at[slot // 2, slot % 2, row_half(half, 128)]

    def columns(first, index):
        return pl.ds(pl.multiple_of(first + index * 128, 128), 128)

    def plain(ref, count):
        def loc(dr, dp, er, ep, half):
            return ref.at[me.chip_at(dr, dp), me.co, row_half(half, 128), pl.ds(0, count)]

        return loc

    def strip_x(ref, first):
        def loc(dr, dp, er, ep, half):
            return ref.at[me.chip_at(dr, dp), me.co, row_half(half, 128), columns(first, me.c)]

        return loc

    def strip_y(ref, first):
        def loc(dr, dp, er, ep, half):
            chips = pl.ds(0, 8) if half is None else pl.ds(4 * half, 4)
            return ref.at[chips, me.co, :, columns(first, me.ctx_at(dr, dp))]

        return loc

    def wd_at(dr, dp, er, ep, half):
        size = 352 if half is None else 176
        first = me.co * 352 + (0 if half is None else half * size)
        return wd.at[
            pl.ds(pl.multiple_of(first, 16), size),
            pl.ds(pl.multiple_of(me.chip_at(dr, dp) * 256, 256), 256),
        ]

    def gu_at(dr, dp, er, ep, half):
        size = 128 if half is None else 64
        first = me.fsdp_at(dr, dp) * 128 + (0 if half is None else half * size)
        return gu.at[pl.ds(pl.multiple_of(first, size), size)]

    def over_x(own, loc, row, both=True):
        own = loc(0, 0, 0, 0, None) if own is None else own
        return Gather(me.across_x, own, loc, (s0, s1), row, me.sibling() if both else None, (t0, t1))

    def over_y(own, loc, row, both=True):
        own = loc(0, 0, 0, 0, None) if own is None else own
        return Gather(me.across_y, own, loc, (y0, y1), row, me.sibling() if both else None, (u0, u1))

    g = over_x(None, gains_at, 0)
    k = over_x(None, plain(kw, 512), 1)
    q = over_x(q_in.at[:, pl.ds(0, 1024)], plain(qw, 1024), 2)
    qx = over_x(q_in.at[:, columns(1024, me.c)], strip_x(qw, 1024), 3, both=False)
    o = over_x(wo_in.at[:, pl.ds(0, 1024)], plain(wo, 1024), 4)
    ox = over_x(wo_in.at[:, columns(1024, me.c)], strip_x(wo, 1024), 5, both=False)
    m = over_x(None, gu_at, 6)
    dn = over_x(dnp, wd_at, 7)
    qy = over_y(None, strip_y(qw, 1024), 0)
    oy = over_y(None, strip_y(wo, 1024), 1)
    dy_task = RingFirst(me.across_y, dy_in, slot_at(dy, 128), (y0, y1), 2)
    kv_task = over_y(kv_own, slot_at(kv, 128), 3, both=False)
    a = over_y(None, acts_at, 4, both=False)
    swap = Swap(me, dn_in.at[:, pl.ds(pl.multiple_of(me.c * 256, 256), 256)], dnp, (w0, w1), local.at[next(slots)])

    own_kw = plain(kw, 512)(0, 0, 0, 0, None)
    loads = [load(key_in, own_kw.at[:, pl.ds(0, 256)]), load(value_in, own_kw.at[:, pl.ds(256, 256)])]
    kept = {task: load(task.own, task.loc(0, 0, 0, 0, None)) for task in (q, qx, o, ox, dy_task)}
    window = pl.ds(pl.multiple_of(me.y * 1408 + me.zl * 640, 128), 768)
    loads.append(load(gate_in.at[:, window], gu_win.at[0]))
    loads.append(load(up_in.at[:, window], gu_win.at[1]))
    gains[me.f] = jnp.zeros((16, 128), F32)
    gains[me.f, pl.ds(0, 1), :] = attn_gain[...].astype(F32)
    gains[me.f, pl.ds(8, 1), :] = mlp_gain[...].astype(F32)

    dpart = op = wo.at[:, 0]
    qp = wo.at[:, 1]
    dgu = wo.at[:, 1, :, pl.ds(0, 1536)]
    kvp = kv

    def gsib(t):
        return gu.at[pl.ds(aligned(128 * t, 128), 128)]

    def gown(t):
        return gu.at[pl.ds(aligned(1024 + 128 * t, 128), 128)]

    def kp(t):
        return gu.at[pl.ds(aligned(128 * t, 128), 128), pl.ds(0, 512)]

    def gd(t):
        return wd.at[:, pl.ds(aligned(256 * t, 256), 256)]

    def gd_own(t):
        return gd(t).at[pl.ds(pl.multiple_of(me.co * 352, 16), 352)]

    def dost(n, half):
        return grecv.at[pl.ds(0, 4), :, pl.ds(pl.multiple_of(512 + 128 * (2 * n + half), 128), 128)]

    saved = []

    def put_gate_up():
        loads[2].wait()
        loads[3].wait()

        @pl.loop(0, 8)
        def _(i):
            rows = pl.ds(pl.multiple_of(16 * i, 16), 16)
            out = pl.ds(pl.multiple_of(me.f * 128 + 16 * i, 16), 16)
            for w in (0, 1):
                values = gu_win[w, rows].astype(F32)
                values = jnp.where(me.zl == 1, pltpu.roll(values, 704, 1), values)
                lane = lax.broadcasted_iota(jnp.int32, values.shape, 1)
                gu[out, 768 * w : 768 * w + 768] = jnp.where(lane < 704, values, 0.0).astype(BF)

        wd[pl.ds(704, 64)] = jnp.zeros((64, 2048), BF)

    def normed():
        norm_scale(x, scale)

        @pl.loop(0, 16)
        def _(i):
            at = pl.ds(pl.multiple_of(i * 128, 128), 128)
            a1s[own, at] = (x[:, at].astype(F32) * scale[...] * gains[i, pl.ds(0, 1), :]).astype(BF)

    def project_kv():
        raw = dot_in(a1s[own], kw[...].reshape(2048, 512))
        for i in range(2):
            part = raw[:, 128 * i : 128 * i + 128]
            kv_own[:, 128 * i : 128 * i + 128] = (part * cosine[...] + turned(part) * sine[...]).astype(BF)
        kv_own[:, 256:] = raw[:, 256:].astype(BF)
        kv[0] = kv_own[...]

    def project_q():
        @pl.loop(0, 4)
        def _(n):
            raw = dot_in(a1s[own], qw[:, :, :, pl.ds(pl.multiple_of(512 * n, 512), 512)].reshape(2048, 512))
            for i in range(4):
                part = raw[:, 128 * i : 128 * i + 128]
                part = ((part * cosine[...] + turned(part) * sine[...]).astype(BF).astype(F32) * SCALE).astype(BF)
                for half in (0, 1):
                    for e in (0, 1):
                        rows = pl.ds(64 * (2 * i + e), 64)
                        qst[n, half, rows, :] = part[64 * half : 64 * half + 64, 64 * e : 64 * e + 64]

    def collect_kv(mate):
        beside = kv[mate]
        for out, base in ((kst, 0), (vst, 256)):
            for n in range(4):
                first = base + 64 * n
                for slot in range(8):
                    out[n, pl.ds(64 * slot, 64), :] = kv[slot, 0:64, first : first + 64]
                out[n, pl.ds(512, 64), :] = beside[64:128, first : first + 64]
                out[n, pl.ds(576, 64), :] = kv_own[64:128, first : first + 64]

    def attend(n, half):
        count = 512 if half == 0 else 640
        keys = pl.ds(0, count)
        sT[keys] = dot_back(kst[n, keys, :], qst[n, half])
        for i in range(4):
            at = pl.ds(128 * i, 128)
            if half == 0:
                scores = sT[keys, at] + bias_p[...]
                peak = jnp.max(scores, axis=0, keepdims=True)
                raised = jnp.exp(scores - peak)
                total = jnp.sum(raised, axis=0, keepdims=True)
                pT[keys, at] = (raised * (1.0 / total)).astype(BF)
            else:
                first = sT[0:512, at]
                rest = sT[512:640, at] + bias_c[...]
                peak = jnp.maximum(
                    jnp.max(first, axis=0, keepdims=True), jnp.max(rest, axis=0, keepdims=True)
                )
                first = jnp.exp(first - peak)
                rest = jnp.exp(rest - peak)
                total = jnp.sum(first, axis=0, keepdims=True) + jnp.sum(rest, axis=0, keepdims=True)
                pT[0:512, at] = (first * (1.0 / total)).astype(BF)
                pT[512:640, at] = (rest * (1.0 / total)).astype(BF)
            lse[2 * n + half, :, at] = peak + jnp.log(total)
        for i, block in enumerate(unpile(dot_rows(vst[n, keys, :], pT[keys]))):
            first = pl.multiple_of(512 * n + 128 * i, 128)
            atts[pl.ds(64 * half, 64), pl.ds(first, 128)] = block.astype(BF)

    def project_o():
        @pl.loop(0, 4)
        def _(n):
            at = pl.ds(pl.multiple_of(512 * n, 512), 512)
            h1[:, at] = x[:, at].astype(F32) + dot_in(atts[own], wo[:, :, :, at].reshape(2048, 512))

    def normed_two():
        norm_scale(h1, scale)

        @pl.loop(0, 16)
        def _(i):
            at = pl.ds(pl.multiple_of(i * 128, 128), 128)
            acts[0, 0, :, at] = (h1[:, at] * scale[...] * gains[i, pl.ds(8, 1), :]).astype(BF)

    def mpart_copy(n):
        return [
            pltpu.make_async_copy(
                kv.at[pl.ds(2 * i, 2)], mpart.at[pl.ds(2 * n, 2), :, pl.ds(512 * i, 512)], local.at[60 + i]
            )
            for i in range(4)
        ]

    def group(n):
        at = pl.ds(2 * n, 2)
        rows = pl.ds(pl.multiple_of(256 * n, 256), 256)
        for h in range(3):
            first, second = pl.ds(256 * h, 256), pl.ds(768 + 256 * h, 256)
            here = acts[n].reshape(256, 2048)
            gate = dot_in(here, gu[:, first])
            up = dot_in(here, gu[:, second])
            back = dot_back(dy[at].reshape(256, 2048), wd[first, :])
            curve = 1.0 / (1.0 + jnp.exp(-gate))
            silu = gate * curve
            hid[rows, first] = (silu * up).astype(BF)
            dgu[at, :, first] = (back * up * (curve + silu * (1.0 - curve))).astype(BF).reshape(2, 128, 256)
            dgu[at, :, second] = (back * silu).astype(BF).reshape(2, 128, 256)

        @pl.when(n > 0)
        def _():
            for copy in mpart_copy(n - 1):
                copy.wait()

        for i in range(4):
            wide = pl.ds(512 * i, 512)
            grads = dgu[at].reshape(256, 1536)
            dpart[at, :, wide] = dot_back(grads, gu[wide, :]).astype(BF).reshape(2, 128, 512)
            kv[pl.ds(2 * i, 2)] = dot_in(hid[rows, :], wd[:, wide]).astype(BF).reshape(2, 128, 512)
        for copy in mpart_copy(n):
            copy.start()

    def group_half(slot):
        rows = pl.ds(128 * slot, 128)
        here = acts[slot // 2, slot % 2]
        for h in range(3):
            first, second = pl.ds(256 * h, 256), pl.ds(768 + 256 * h, 256)
            gate = dot_in(here, gu[:, first])
            up = dot_in(here, gu[:, second])
            back = dot_back(dy[slot], wd[first, :])
            curve = 1.0 / (1.0 + jnp.exp(-gate))
            silu = gate * curve
            hid[rows, first] = (silu * up).astype(BF)
            dgu[slot, :, first] = (back * up * (curve + silu * (1.0 - curve))).astype(BF)
            dgu[slot, :, second] = (back * silu).astype(BF)
        for i in range(4):
            wide = pl.ds(512 * i, 512)
            dpart[slot, :, wide] = dot_back(dgu[slot], gu[wide, :]).astype(BF)

    def group_out():
        for copy in mpart_copy(2):
            copy.wait()
        for i in range(4):
            wide = pl.ds(512 * i, 512)
            kv[pl.ds(2 * i, 2)] = dot_in(hid[pl.ds(768, 256), :], wd[:, wide]).astype(BF).reshape(2, 128, 512)
        for copy in mpart_copy(3):
            copy.start()

    class Views:
        def __init__(self, pick):
            self.pick = pick

        @property
        def at(self):
            return self

        def __getitem__(self, index):
            return self.pick(index)

    def scatter(dev, part, place, columns, row, pair=None):
        wide = pl.ds(0, columns)
        halves = Views(lambda index: place.at[4 + index[0], pl.ds(64 * index[1], 64), wide])
        fulls = Views(lambda index: place.at[2 * index[0] + index[1], :, wide])
        paired = place.at[6, :, wide] if pair is None else pair
        return Scatter(dev, part, 128, halves, fulls, paired, (r0, r1), row)

    first_bay, second_bay = qw.at[:, 0], qw.at[:, 1]
    d = scatter(me.across_y, lambda slot: dpart.at[slot], second_bay, 2048, 0)
    gjob = scatter(me.across_x, gown, first_bay, 1536, 1, g_pair)
    n_job = Scatter(me.across_x, gd_own, 352, n_half, n_full, n_pair, (r0, r1), 2)
    o_job = scatter(me.across_x, lambda slot: op.at[slot], first_bay, 2048, 3)
    q_job = scatter(me.across_x, lambda slot: qp.at[slot], second_bay, 2048, 4)
    k_job = scatter(me.across_x, kp, kw.at[:, 0], 512, 5)
    e_job = Scatter(me.across_x, lambda slot: gp.at[slot], 16, e_half, e_full, e_pair, (r0, r1), 6)
    d_job = scatter(me.across_y, lambda slot: kvp.at[slot], kw.at[:, 1], 512, 7)

    def weight_terms(t, core):
        at = pl.multiple_of((chip_of(me, t) * 2 + core) * 128, 128)
        left = acts[:, :, :, pl.ds(at, 128)].reshape(1024, 128)
        return dot_rows(left, dgu[...].reshape(1024, 1536))

    def gu_to(t):
        return send(gsib(t), grecv.at[t], (c0, c1), 8 + t, me.sibling())

    def down_to(t):
        mine = pl.ds(pl.multiple_of((1 - me.co) * 352, 16), 352)
        return send(gd(t).at[mine], gdrecv.at[t], (c0, c1), t, me.sibling())

    def terms_for_sibling(start):
        @pl.loop(start, start + 2)
        def _(i):
            gsib(7 - i)[...] = weight_terms(7 - i, 1 - me.co).astype(BF)
            gu_to(7 - i).start()

    def sibling_has_terms():
        @pl.loop(0, 8)
        def _(t):
            gu_to(t).wait_send()

    def own_terms(start):
        @pl.loop(start, start + 2)
        def _(i):
            gu_to(7 - i).wait_recv()
            gown(7 - i)[...] = (weight_terms(7 - i, me.co) + grecv[7 - i].astype(F32)).astype(BF)

    def down_terms():
        @pl.loop(0, 8)
        def _(t):
            at = pl.multiple_of(chip_of(me, t) * 256, 256)
            gd(t)[...] = dot_rows(hid[...], dy[:, :, pl.ds(at, 256)].reshape(1024, 256)).astype(BF)
            down_to(t).start()

    def down_sums():
        @pl.loop(0, 8)
        def _(t):
            down_to(t).wait_recv()

            @pl.loop(0, 22)
            def _(i):
                at = pl.ds(pl.multiple_of(i * 16, 16), 16)
                mine = gd(t).at[pl.ds(pl.multiple_of(me.co * 352 + i * 16, 16), 16)]
                mine[...] = (mine[...].astype(F32) + gdrecv[t, at].astype(F32)).astype(BF)

    m_first, m_second = {}, {}
    for dp in (0, 1):
        for way, sign in ((0, 1), (1, -1)):
            m_first[way, dp] = send(
                mpart.at[slot_of(2, dp), pl.ds(64 * way, 64)], m_half.at[way, dp], (r0, r1), (8, way * 2 + dp),
                me.across_y(sign, 0),
            )
            m_second[way, dp] = send(
                dy.at[1 + 2 * way + dp], m_full.at[way, dp], (r0, r1), (8, 4 + way * 2 + dp), me.across_y(sign, 0)
            )
    m_third = send(dy.at[5], m_pair, (r0, r1), (8, 8), me.across_y(0, 1))

    def m_start():
        dy_task.end()
        for copy in mpart_copy(3):
            copy.wait()
        for dp in (1, 0):
            for way in (0, 1):
                m_first[way, dp].start()

    m_parts = {(way, dp): later(mpart.at[slot_of(1 - 2 * way, dp)], dy.at[1 + 2 * way + dp]) for way in (0, 1) for dp in (0, 1)}
    m_halves = {(way, dp): later(m_half.at[way, dp], dy.at[6 + way, pl.ds(0, 64)]) for way in (0, 1) for dp in (0, 1)}
    m_fulls = {(way, dp): later(m_full.at[way, dp], dy.at[6 + way]) for way in (0, 1) for dp in (0, 1)}
    m_mine, m_near, m_last = later(mpart.at[0], dy.at[1]), later(mpart.at[1], dy.at[5]), later(m_pair, dy.at[2])
    m_out = later(dy.at[1], mixed)

    def m_turn(dp):
        for way in (0, 1):
            m_parts[way, dp].start()
        for way in (0, 1):
            m_first[way, dp].wait_recv()
            m_halves[way, dp].start()
        for way in (0, 1):
            m_parts[way, dp].wait()
            m_halves[way, dp].wait()
            add_into(dy.at[1 + 2 * way + dp, pl.ds(64 * way, 64)], 64, [dy.at[6 + way, pl.ds(0, 64)]])
            m_second[way, dp].start()

    def m_pair_up():
        m_near.start()
        for way in (0, 1):
            m_second[way, 1].wait_recv()
            m_fulls[way, 1].start()
        m_near.wait()
        for way in (0, 1):
            m_fulls[way, 1].wait()
        add_into(dy.at[5], 128, [dy.at[6], dy.at[7]])
        m_third.start()

    def m_finish():
        for dp in (0, 1):
            m_second[0, dp].wait_send()
        m_mine.start()
        for way in (0, 1):
            m_second[way, 0].wait_recv()
            m_fulls[way, 0].start()
        m_third.wait_recv()
        m_last.start()
        m_mine.wait()
        for way in (0, 1):
            m_fulls[way, 0].wait()
        m_last.wait()

        @pl.loop(0, 8)
        def _(i):
            at = pl.ds(pl.multiple_of(i * 16, 16), 16)
            total = h1[at]
            for slot in (1, 2, 6, 7):
                total = total + dy[slot, at].astype(F32)
            dy[1, at] = total.astype(BF)

        m_out.start()

    def wo_load(n):
        return pltpu.make_async_copy(
            wo_saved.at[pl.ds(2 * n, 2)], acts.at[pl.ds(2 * (n % 2), 2)], local.at[56 + n % 2]
        )

    def q_load(n):
        return pltpu.make_async_copy(q_saved.at[pl.ds(2 * n, 2)], acts.at[pl.ds(2 * (n % 2), 2)], local.at[58 + n % 2])

    def kw_load():
        return [
            load(kw_saved.at[chip], grecv.at[pl.ds(2 * (chip % 4), 2), :, pl.ds(512 * (chip // 4), 512)])
            for chip in range(8)
        ]

    def at_ctx(ref):
        def loc(dr, dp, er, ep, half):
            return ref.at[me.ctx_at(dr, dp), row_half(half, ref.shape[1])]

        return loc

    def dn_at(dr, dp, er, ep, half):
        first = pl.multiple_of(me.ctx_at(dr, dp) * 256, 256)
        return dn_all.at[row_half(half, 352), pl.ds(first, 256)]

    gu_task = over_y(gown(0), at_ctx(gu_all), 5, both=False)
    dn_task = over_y(dn_moved, dn_at, 6, both=False)
    dn_swap = Swap(me, gd_own(0), dn_moved, (v0, v1), local.at[next(slots)])
    gu_keep = later(gown(0), gu_all.at[me.c])
    dn_keep = later(dn_moved, dn_at(0, 0, 0, 0, None))
    dn_local = later(dnp, wd_at(0, 0, 0, 0, None))
    tokens_out = later(datts.at[own], tokens_grad)

    def block_at(ref, slot):
        first = pl.multiple_of(me.ctx_at(STEPS[slot], PAIRS[slot]) * 16, 16)
        return ref.at[pl.ds(first, 16)]

    def sum_over_ctx(total, got, row):
        return Trade(
            me.across_y, lambda slot: block_at(total, slot), lambda slot: got.at[mirror(slot)], (z0, z1), row
        )

    def spread(out, row):
        return Trade(me.across_y, lambda slot: block_at(out, 0), lambda slot: block_at(out, 0), (z0, z1), row)

    def sum_up(total, got, out):
        value = block_at(total, 0)[...].astype(F32)
        for slot in range(1, 8):
            value = value + got[slot].astype(F32)
        block_at(out, 0)[...] = value.astype(BF)

    o_sum, q_sum, kv_sum = op.at[0], qp.at[0], kp(0)
    o_sums = sum_over_ctx(o_sum, o_got, 0)
    q_sums = sum_over_ctx(q_sum, q_got, 1)
    k_sums = sum_over_ctx(kv_sum, k_got, 2)
    o_spread = spread(o_grad, 3)
    q_spread = spread(q_grad, 4)
    k_spread = spread(kv_grad, 5)
    e_task = Trade(me.across_y, lambda slot: g_sum, lambda slot: ggot.at[me.c], (z0, z1), 6)

    def to_sibling(src, dst, index):
        return send(src, dst, (c0, c1), 16 + index, me.sibling())

    att_swap = to_sibling(atts.at[own], atts.at[other], 0)
    datt_swap = to_sibling(datts.at[own], datts.at[other], 1)
    a1_swap = to_sibling(a1s.at[own], a1s.at[other], 2)
    queries, rest = pl.ds(0, 2048), pl.ds(2048, 512)
    dq_swap = to_sibling(dqkvs.at[own, queries], dqkvs.at[other, queries], 3)
    dkv_swap = to_sibling(dqkvs.at[own, rest], dqkvs.at[other, rest], 4)
    gain_swap = to_sibling(gown_rows, gsib_rows, 5)

    def norm_two_back():
        for i in range(16):
            grow[0, :, 128 * i : 128 * i + 128] = gains[i, 0:1, :]
            grow[1, :, 128 * i : 128 * i + 128] = gains[i, 8:9, :]
        grow[2] = jnp.zeros((1, 2048), F32)
        grow[3] = jnp.zeros((1, 2048), F32)

        @pl.loop(0, 8)
        def _(i):
            at = pl.ds(pl.multiple_of(16 * i, 16), 16)
            values, grad = h1[at], da2[at]
            scale = lax.rsqrt(jnp.mean(values * values, axis=1, keepdims=True) + EPS)
            grow[3] += jnp.sum(grad * values * scale, axis=0, keepdims=True)
            grad = grad * grow[1]
            level = jnp.mean(grad * values, axis=1, keepdims=True) * scale * scale * scale
            total = dy[0, at].astype(F32) + scale * grad - values * level
            da2[at] = total
            datts[at] = total.astype(BF)

        datt_swap.start()

    def heads_back():
        for n in range(4):
            wo_load(n).wait()
            part = dot_back(datts[own], acts[2 * (n % 2) : 2 * (n % 2) + 2].reshape(512, 2048)).astype(BF)
            for half in (0, 1):
                place = dost(n, half)
                for h in range(8):
                    place[h // 2, pl.ds(64 * (h % 2), 64), pl.ds(0, 64)] = part[
                        64 * half : 64 * half + 64, 64 * h : 64 * h + 64
                    ]
            if n < 2:
                wo_load(n + 2).start()
        for n in range(2):
            q_load(n).start()

    def terms(left, right, out, job):
        @pl.loop(0, 8)
        def _(i):
            at = pl.multiple_of((chip_of(me, 7 - i) * 2 + me.co) * 128, 128)
            out(7 - i)[...] = dot_rows(left[:, pl.ds(at, 128)], right[...]).astype(BF)

            @pl.when(i == 1)
            def _():
                job.start()

    def output_terms():
        att_swap.wait_recv()
        datt_swap.wait_recv()
        pl.semaphore_wait(credit, 3)
        terms(atts, datts, lambda t: op.at[t], o_job)

    def query_terms():
        a1_swap.wait_recv()
        dq_swap.wait_recv()
        terms(a1s, dqkvs.at[:, pl.ds(0, 2048)], lambda t: qp.at[t], q_job)

    def kv_terms():
        dkv_swap.wait_recv()
        terms(a1s, dqkvs.at[:, pl.ds(2048, 512)], kp, k_job)

    def kv_blocks(mate):
        for part, base in ((0, 0), (64, 256)):
            for n in range(4):
                first = base + 64 * n
                block = grecv[0:5, :, 128 * n : 128 * n + 128].reshape(640, 128)[:, part : part + 64]
                for slot in range(8):
                    kvp[slot, 0:64, first : first + 64] = block[64 * slot : 64 * slot + 64]
                    if slot == 0:
                        late = block[576:640]
                    else:
                        late = jnp.where(mate == slot, block[512:576], jnp.zeros((64, 64), BF))
                    kvp[slot, 64:128, first : first + 64] = late

    def kv_back():
        for i in range(2):
            at = slice(128 * i, 128 * i + 128)
            block = sT[512:640, at]
            dqkvs[own, 2048 + 128 * i : 2176 + 128 * i] = (block * cosine[...] - turned(block) * sine[...]).astype(BF)
        dqkvs[own, 2304:2560] = sT[512:640, 256:512].astype(BF)
        dkv_swap.start()

    def inputs_back():
        for copy in kw_back:
            copy.wait()
        for n in range(4):
            q_load(n).wait()
            block = dot_back(dqkvs[own, queries], acts[2 * (n % 2) : 2 * (n % 2) + 2].reshape(512, 2048))
            four, wide = pl.ds(4 * (n % 2), 4), pl.ds(512 * (n // 2), 512)
            block = block + dot_back(dqkvs[own, rest], grecv[four, :, wide].reshape(512, 512))
            sT[pl.ds(128 * n, 128)] = block
            if n < 2:
                q_load(n + 2).start()

    def norm_one_back():
        datt_swap.wait_send()

        @pl.loop(0, 8)
        def _(i):
            at = pl.ds(pl.multiple_of(16 * i, 16), 16)
            values = x[at].astype(F32)
            grad = jnp.concatenate([sT[pl.ds(pl.multiple_of(128 * n + 16 * i, 16), 16)] for n in range(4)], axis=1)
            scale = lax.rsqrt(jnp.mean(values * values, axis=1, keepdims=True) + EPS)
            grow[2] += jnp.sum(grad * values * scale, axis=0, keepdims=True)
            grad = grad * grow[0]
            level = jnp.mean(grad * values, axis=1, keepdims=True) * scale * scale * scale
            datts[at] = (da2[at] + scale * grad - values * level).astype(BF)

        tokens_out.start()

        gown_rows[...] = jnp.zeros((16, 16, 128), F32)
        for i in range(16):
            gown_rows[i, 0:1, :] = grow[2, :, 128 * i : 128 * i + 128]
            gown_rows[i, 8:9, :] = grow[3, :, 128 * i : 128 * i + 128]
        gain_swap.start()

    def gain_terms():
        gain_swap.wait_recv()
        for slot in range(8):
            block = me.fsdp_at(STEPS[slot], PAIRS[slot])
            gp[slot] = gown_rows[block] + gsib_rows[block]

    def dn_begin():
        dn_swap.wait()
        dn_task.start()
        dn_keep.start()

    def gu_begin():
        gu_keep.start()
        gu_task.start()

    def e_begin():
        e_task.start()
        ggot[me.c] = g_sum[...]

    def attend_back(n, half):
        count = 512 if half == 0 else 640
        keys = pl.ds(0, count)
        key, query, out = kst[n, keys, :], qst[n, half], dost(n, half)[...].reshape(512, 128)[:, 0:64]
        sT[keys] = dot_back(key, query)
        dT[keys] = dot_back(vst[n, keys, :], out)
        for i in range(4):
            at = pl.ds(128 * i, 128)
            parts = []
            for first, size in ((0, 512), (512, 128))[: 1 + half]:
                scores = sT[first : first + size, at]
                if half == 0:
                    scores = scores + bias_p[...]
                elif first:
                    scores = scores + bias_c[...]
                probs = jnp.exp(scores - lse[2 * n + half, :, at])
                grad = dT[first : first + size, at]
                parts.append((first, size, probs, grad))
            level = sum(jnp.sum(probs * grad, axis=0, keepdims=True) for _, _, probs, grad in parts)
            for first, size, probs, grad in parts:
                pT[first : first + size, at] = probs.astype(BF)
                dsT[first : first + size, at] = (probs * (grad - level)).astype(BF)
        rows = slice(64 * half, 64 * half + 64)
        for i, block in enumerate(unpile(dot_rows(key, dsT[keys]) * SCALE)):
            block = block * cosine[rows] - turned(block) * sine[rows]
            first = pl.multiple_of(512 * n + 128 * i, 128)
            dqkvs[rows, pl.ds(first, 128)] = block.astype(BF)
        return dot_in(dsT[keys], query), dot_in(pT[keys], out)

    def keep_kv_grads(n, one, two):
        keys = jnp.concatenate([one[0] + two[0][0:512], two[0][512:640]], axis=0)
        values = jnp.concatenate([one[1] + two[1][0:512], two[1][512:640]], axis=0)
        both = jnp.concatenate([keys, values], axis=1).astype(BF)
        grecv[pl.ds(0, 5), :, pl.ds(pl.multiple_of(128 * n, 128), 128)] = both.reshape(5, 128, 128)

    qx.start()
    g.start()
    loads[0].wait()
    loads[1].wait()
    k.start()
    dy_task.go(1, 2)
    ox.start()
    qx.pair()
    qx.turn(0)
    q.start()
    qx.turn(1)
    qx.last(0)
    put_gate_up()
    g.pair()
    ox.pair()
    swap.start()
    k.pair()
    k.turn(0)
    ox.turn(0)
    qx.last(1)
    kept[qx].wait()
    qy.start()
    q.turn(0)
    g.turn(0)
    k.turn(1)
    g.turn(1)
    ox.turn(1)
    o.start()
    ox.last(0)
    mate = place_tables(me, deal, freq, cosine, sine, bias_p, bias_c)
    q.pair()
    qy.pair()
    k.last(0)
    g.last(1)
    g.last(0)
    ox.last(1)
    swap.wait()
    dn_local.start()
    dn.start()
    k.last(1)
    qy.turn(0)
    o.pair()
    kept[ox].wait()
    oy.start()
    qy.turn(1)
    g.sync()
    q.last(0)
    normed()
    qy.last(0)
    k.sync()
    project_kv()
    q.turn(1)
    kv_task.start()
    dy_task.go(0)
    kv_task.pair()
    o.turn(0)
    kv_task.turn(0)
    qy.last(1)
    oy.pair()
    o.turn(1)
    q.last(1)
    m.start()
    kv_task.turn(1)
    dn.pair()
    oy.turn(0)
    o.last(0)
    qy.sync()
    q.sync()
    kept[q].wait()
    saved.append(load(qw, q_saved))
    saved.append(load(kw, kw_saved))
    project_q()
    o.last(1)
    dn.turn(0)
    oy.turn(1)
    dy_task.got(1, 2)
    dy_task.go(3, 4)
    dy_task.go(5)
    kv_task.last(0)
    kv_task.last(1)
    dy_task.got(0)
    collect_kv(mate)

    @pl.loop(0, 4)
    def _(n):
        attend(n, 0)
        attend(n, 1)

        @pl.when(n == 0)
        def _():
            o.sync()
            oy.last(0)

        @pl.when(n == 1)
        def _():
            oy.last(1)
            m.pair()

    oy.sync()
    kept[o].wait()
    saved.append(load(wo, wo_saved))
    project_o()
    normed_two()
    for task in (k, q, qx, qy):
        task.end()
    saved[0].wait()
    saved[1].wait()
    a.start()
    dy_task.go(6)
    m.turn(0)
    m.turn(1)
    dy_task.got(3, 4)
    dy_task.go(7, 8)
    m.last(0)
    dn.turn(1)
    dn.last(0)
    a.pair()
    m.last(1)
    a.turn(0)
    dn.last(1)
    m.sync()
    dn.sync()

    for task in (o, ox, oy, kv_task):
        task.end()
    saved[2].wait()
    dn_local.wait()
    kept[dy_task].wait()

    @pl.loop(0, 3)
    def _(n):
        group(n)

        @pl.when(n == 1)
        def _():
            a.turn(1)
            dy_task.got(5, 6)

    a.last(0)
    group_half(6)
    dy_task.got(7, 8)
    a.last(1)
    group_half(7)
    d.start()
    m.end()
    terms_for_sibling(0)
    terms_for_sibling(2)
    own_terms(0)
    terms_for_sibling(4)
    d.turn(1)
    group_out()
    gjob.start()
    dn.end()
    down_terms()
    d.turn(0)
    own_terms(2)
    own_terms(4)
    down_sums()
    att_swap.start()
    n_job.start()
    gjob.turn(1)
    terms_for_sibling(6)
    d.pair()
    gjob.turn(0)
    n_job.turn(0)
    n_job.turn(1)
    m_start()
    own_terms(6)
    a.end()
    wo_load(0).start()
    wo_load(1).start()
    gjob.pair()
    d.finish(da2)
    m_turn(1)
    norm_two_back()
    gjob.finish(gown(0))
    for device in near(me.across_x):
        pl.semaphore_signal(credit, 1, device_id=device, device_id_type=MESH)
    gu_begin()
    d.end()
    output_terms()
    heads_back()
    m_pair_up()

    @pl.loop(0, 4)
    def _(n):
        one, two = attend_back(n, 0), attend_back(n, 1)
        keep_kv_grads(n, one, two)

        @pl.when(n == 0)
        def _():
            gu_task.pair()
            a1_swap.start()
            o_job.turn(1)

        @pl.when(n == 1)
        def _():
            o_job.turn(0)

    kv_blocks(mate)
    kw_back = kw_load()
    gu_task.turn(0)
    d_job.start()
    n_job.pair()
    dq_swap.start()
    gu_task.turn(1)
    o_job.pair()
    d_job.turn(1)
    query_terms()
    n_job.finish(gd_own(0))
    dn_swap.start()
    d_job.turn(0)
    d_job.pair()
    o_job.finish(o_sum)
    dn_begin()
    gu_task.last(0)
    q_job.turn(1)
    d_job.finish(sT.at[pl.ds(512, 128)])
    o_sums.start()
    kv_back()
    inputs_back()
    dn_task.pair()
    norm_one_back()
    sibling_has_terms()
    kv_terms()
    o_sums.got()
    sum_up(o_sum, o_got, o_grad)
    o_spread.start()
    dn_task.turn(0)
    m_turn(0)
    gain_terms()
    e_job.start()
    k_job.turn(1)
    q_job.pair()
    e_job.turn(1)
    q_job.turn(0)
    e_job.pair()
    k_job.pair()
    k_job.turn(0)
    e_job.turn(0)
    dn_task.turn(1)
    q_job.finish(q_sum)
    q_sums.start()
    e_job.finish(g_sum)
    k_job.finish(kv_sum)
    m_finish()
    k_sums.start()
    e_begin()
    q_sums.got()
    sum_up(q_sum, q_got, q_grad)
    q_spread.start()
    dn_task.last(0)
    o_spread.got()
    k_sums.got()
    dn_task.last(1)
    sum_up(kv_sum, k_got, kv_grad)
    k_spread.start()
    e_task.got()
    q_spread.got()
    gu_task.last(1)
    k_spread.got()
    total = ggot[0]
    for index in range(1, 8):
        total = total + ggot[index]
    gains_out[...] = total
    for job in (g, gjob, n_job, o_job, q_job, k_job, e_job, d_job, gu_task, dn_task):
        job.end()
    for job in (o_sums, q_sums, k_sums, o_spread, q_spread, k_spread, e_task):
        job.end()
    for copy in (*m_first.values(), m_second[1, 0], m_second[1, 1], m_third):
        copy.wait_send()
    m_out.wait()
    tokens_out.wait()
    gu_keep.wait()
    dn_keep.wait()
    for copy in (att_swap, a1_swap, dq_swap, dkv_swap, gain_swap):
        copy.wait_send()

    @pl.loop(0, 8)
    def _(t):
        down_to(t).wait_send()


def layer(x, attn_gain, mlp_gain, deal, freq, q, key, value, wo, gate, up, dn, dy):
    shape = jax.ShapeDtypeStruct
    smem = pl.BlockSpec(memory_space=pltpu.SMEM)
    vmem = pltpu.VMEM
    outs = pl.pallas_call(
        layer_kernel,
        out_shape=(
            shape((128, 2048), BF),
            shape((128, 2048), BF),
            shape((128, 2048), BF),
            shape((128, 512), BF),
            shape((128, 2048), BF),
            shape((16, 128), F32),
            shape((8, 128, 1536), BF),
            shape((352, 2048), BF),
            shape((8, 2, 128, 2048), BF),
            shape((8, 2, 128, 512), BF),
            shape((8, 2, 128, 2048), BF),
            shape((8, 128, 2048), BF),
            shape((2, 2, 64, 2048), BF),
            shape((2, 2, 128, 2048), BF),
            shape((128, 2048), BF),
        ),
        in_specs=[VMEM] * 3 + [smem, VMEM] + [ANY] * 8,
        out_specs=[ANY] * 2 + [VMEM] * 4 + [ANY] * 9,
        scratch_shapes=[
            vmem((16, 16, 128), F32),
            vmem((256, 2048), BF),
            vmem((256, 2048), BF),
            vmem((4, 2, 512, 64), BF),
            vmem((4, 640, 64), BF),
            vmem((4, 640, 64), BF),
            vmem((8, 1, 512), F32),
            vmem((128, 2048), F32),
            vmem((128, 128), F32),
            vmem((128, 128), F32),
            vmem((512, 128), F32),
            vmem((128, 128), F32),
            vmem((8, 2, 128, 2048), BF),
            vmem((8, 2, 128, 512), BF),
            vmem((8, 2, 128, 2048), BF),
            vmem((128, 512), BF),
            vmem((8, 128, 512), BF),
            vmem((640, 512), F32),
            vmem((640, 512), BF),
            vmem((640, 512), F32),
            vmem((640, 512), BF),
            vmem((128, 1), F32),
            vmem((2, 128, 768), BF),
            vmem((352, 256), BF),
            vmem((4, 2, 128, 2048), BF),
            vmem((2048, 1536), BF),
            vmem((768, 2048), BF),
            vmem((8, 128, 2048), BF),
            vmem((1024, 768), BF),
            vmem((8, 128, 1536), BF),
            vmem((8, 352, 256), BF),
            vmem((128, 1536), BF),
            vmem((128, 2048), F32),
            vmem((256, 2048), BF),
            vmem((256, 2560), BF),
            vmem((4, 1, 2048), F32),
            vmem((16, 16, 128), F32),
            vmem((16, 16, 128), F32),
            vmem((352, 256), BF),
            *scatter_buffers(352, 256),
            *scatter_buffers(16, 128, F32),
            vmem((8, 16, 128), F32),
            vmem((8, 16, 128), F32),
            vmem((16, 128), F32),
            vmem((8, 16, 2048), BF),
            vmem((8, 16, 2048), BF),
            vmem((8, 16, 512), BF),
            *dma_sems(8, 9),
            *dma_sems(8, 10),
            *dma_sems(7, 9),
            *dma_sems(2, 10),
            *dma_sems(9, 9),
            *dma_sems(7, 8),
            pltpu.SemaphoreType.DMA((22,)),
            pltpu.SemaphoreType.DMA((22,)),
            pltpu.SemaphoreType.DMA,
            pltpu.SemaphoreType.DMA,
            pltpu.SemaphoreType.DMA,
            pltpu.SemaphoreType.DMA,
            pltpu.SemaphoreType.REGULAR,
            pltpu.SemaphoreType.DMA((64,)),
        ],
        compiler_params=params(1, 63),
        name="layer",
    )(x, attn_gain, mlp_gain, deal, freq, q, key, value, wo, gate, up, dn, dy)
    return outs[:8]


def finish_kernel(
    mixed_in, tokens_in, q_in, kv_in, o_in, gu_in, dn_in,
    mixed, tokens_grad, q_out, key_out, value_out, o_out, gate_out, up_out, dn_out,
    b_mixed, b_tokens, b_q, b_kv, b_o, b_gu, b_dn, f_q, f_key, f_value, f_o, f_gate, f_up, f_dn, sems,
):
    slots = iter(range(24))

    def move(src, dst):
        return pltpu.make_async_copy(src, dst, sems.at[next(slots)])

    loads = [
        move(src, dst)
        for src, dst in (
            (gu_in.at[pl.ds(0, 4)], b_gu.at[pl.ds(0, 4)]), (gu_in.at[pl.ds(4, 4)], b_gu.at[pl.ds(4, 4)]), (dn_in, b_dn),
            (q_in, b_q), (o_in, b_o), (kv_in, b_kv), (mixed_in, b_mixed), (tokens_in, b_tokens),
        )
    ]
    for copy in loads:
        copy.start()
    stores = []

    def store(src, dst):
        copy = move(src, dst)
        copy.start()
        stores.append(copy)

    def widen(pair):
        first = 1408 * pair

        @pl.loop(0, 8)
        def _(i):
            rows = pl.ds(pl.multiple_of(16 * i, 16), 16)
            for out, base in ((f_gate, 0), (f_up, 768)):
                even = b_gu[2 * pair, rows, base : base + 768].astype(F32)
                odd = pltpu.roll(b_gu[2 * pair + 1, rows, base : base + 768].astype(F32), 64, 1)
                out[rows, first : first + 640] = even[:, 0:640]
                out[rows, first + 640 : first + 768] = even[:, 640:768] + odd[:, 0:128]
                out[rows, first + 768 : first + 1408] = odd[:, 128:768]

    for half in (0, 1):
        loads[half].wait()
        widen(2 * half)
        widen(2 * half + 1)
        wide = pl.ds(2816 * half, 2816)
        store(f_gate.at[:, wide], gate_out.at[:, wide])
        store(f_up.at[:, wide], up_out.at[:, wide])

    def cast(src, dst, rows):
        @pl.loop(0, rows // 32)
        def _(i):
            at = pl.ds(pl.multiple_of(32 * i, 32), 32)
            dst[at] = src[at].astype(F32)

    loads[2].wait()
    cast(b_dn, f_dn, 352)
    store(f_dn, dn_out)
    loads[3].wait()
    cast(b_q, f_q, 128)
    store(f_q, q_out)
    loads[4].wait()
    cast(b_o, f_o, 128)
    store(f_o, o_out)
    loads[5].wait()
    f_key[...] = b_kv[:, 0:256].astype(F32)
    f_value[...] = b_kv[:, 256:512].astype(F32)
    store(f_key, key_out)
    store(f_value, value_out)
    loads[6].wait()
    store(b_mixed, mixed)
    loads[7].wait()
    store(b_tokens, tokens_grad)
    for copy in stores:
        copy.wait()


def finish(mixed, tokens_grad, q, kv, o, gu, dn):
    shape, vmem = jax.ShapeDtypeStruct, pltpu.VMEM
    wholes = [(128, 2048), (128, 256), (128, 256), (128, 2048), (128, 5632), (128, 5632), (352, 2048)]
    return pl.pallas_call(
        finish_kernel,
        out_shape=(shape((128, 2048), BF), shape((128, 2048), BF), *[shape(dims, F32) for dims in wholes]),
        in_specs=[ANY] * 7,
        out_specs=[ANY] * 9,
        scratch_shapes=[
            vmem((128, 2048), BF),
            vmem((128, 2048), BF),
            vmem((128, 2048), BF),
            vmem((128, 512), BF),
            vmem((128, 2048), BF),
            vmem((8, 128, 1536), BF),
            vmem((352, 2048), BF),
            *[vmem(dims, F32) for dims in wholes],
            pltpu.SemaphoreType.DMA((24,)),
        ],
        compiler_params=pltpu.CompilerParams(vmem_limit_bytes=62 << 20),
        name="finish",
    )(mixed, tokens_grad, q, kv, o, gu, dn)


def on_device(
    tokens,
    block_deal,
    attn_gain,
    query_weight,
    key_weight,
    value_weight,
    output_weight,
    mlp_gain,
    gate_weight,
    up_weight,
    down_weight,
    cotangent,
):
    freq = BASE ** (-(np.arange(HEAD_DIM // 2, dtype=np.float32) * 2.0) / HEAD_DIM)
    freq = np.concatenate([freq] * 4)[None].astype(np.float32)
    deal = block_deal.reshape(256)
    mixed, tokens_grad, query_grad, kv_grad, o_grad, gain_grads, gu_grads, dn_grad = layer(
        tokens[0], attn_gain[None], mlp_gain[None], deal, freq, query_weight, key_weight, value_weight, output_weight,
        gate_weight, up_weight, down_weight, cotangent[0],
    )
    mixed, tokens_grad, *grads = finish(mixed, tokens_grad, query_grad, kv_grad, o_grad, gu_grads, dn_grad)
    return (mixed[None], tokens_grad[None], gain_grads[0], *grads[:4], gain_grads[8], *grads[4:])


def solution(mesh):
    held = P("fsdp", "ctx", None)
    rows = P("fsdp", None)
    return jax.shard_map(
        on_device,
        mesh=mesh,
        in_specs=(held, P(), P("fsdp"), rows, rows, rows, rows, P("fsdp"), rows, rows, rows, held),
        out_specs=(held, held, P("fsdp"), rows, rows, rows, rows, P("fsdp"), rows, rows, rows),
        check_vma=False,
    )
```

```python
import functools

import jax
import jax.numpy as jnp
from jax import lax
from jax.experimental import pallas as pl
from jax.experimental.pallas import tpu as pltpu
from jax.sharding import PartitionSpec as P
import numpy as np

MESH = pl.DeviceIdType.MESH
BF = jnp.bfloat16
F32 = jnp.float32
ANY = pl.BlockSpec(memory_space=pl.ANY)
VMEM = pl.BlockSpec(memory_space=pltpu.VMEM)

HEAD_DIM = 64
EPS = 1e-05
SCALE = 0.125
BASE = 10000.0

SLOT = {(0, 0): 0, (0, 1): 1, (1, 0): 2, (3, 0): 3, (1, 1): 4, (3, 1): 5, (2, 0): 6, (2, 1): 7}
STEPS = (0, 0, 1, 3, 1, 3, 2, 2)
PAIRS = (0, 1, 0, 0, 1, 1, 0, 1)


def slot_of(dr, dp):
    return SLOT[(dr % 4, dp % 2)]


class Place:
    def __init__(self):
        self.c = lax.axis_index("ctx")
        self.f = lax.axis_index("fsdp")
        self.y, self.zl = lax.div(self.c, 2), lax.rem(self.c, 2)
        self.j, self.co = lax.div(self.f, 2), lax.rem(self.f, 2)
        self.x, self.zh = lax.div(self.j, 2), lax.rem(self.j, 2)

    def ctx_at(self, dr, dp):
        return lax.rem(self.y + dr % 4, 4) * 2 + lax.rem(self.zl + dp, 2)

    def chip_at(self, dr, dp):
        return lax.rem(self.x + dr % 4, 4) * 2 + lax.rem(self.zh + dp, 2)

    def fsdp_at(self, dr, dp):
        return self.chip_at(dr, dp) * 2 + self.co

    def across_y(self, dr, dp):
        return {"ctx": self.ctx_at(dr, dp), "fsdp": self.f}

    def across_x(self, dr, dp):
        return {"ctx": self.c, "fsdp": self.fsdp_at(dr, dp)}

    def sibling(self):
        return {"ctx": self.c, "fsdp": self.f + 1 - 2 * self.co}


def chip_of(me, t):
    dr = jnp.where(t < 2, 0, jnp.where(t >= 6, 2, 1 + 2 * lax.rem(t, 2)))
    dp = jnp.where(t < 2, t, jnp.where(t >= 6, t - 6, lax.div(t, 4)))
    return lax.rem(me.x + dr, 4) * 2 + lax.rem(me.zh + dp, 2)


def greet(devices):
    barrier = pltpu.get_barrier_semaphore()
    for device in devices:
        pl.semaphore_signal(barrier, 1, device_id=device, device_id_type=MESH)
    pl.semaphore_wait(barrier, len(devices))


class Swap:
    def __init__(self, me, src, dst, sems, local):
        self.moved = me.c != me.j
        self.to = {"ctx": me.j, "fsdp": 2 * me.c + me.co}
        self.copy = pltpu.make_async_remote_copy(
            src, dst, sems[0], sems[1], device_id=self.to, device_id_type=MESH
        )
        self.keep = pltpu.make_async_copy(src, dst, local)

    def start(self):
        pl.when(self.moved)(self.copy.start)
        pl.when(jnp.logical_not(self.moved))(self.keep.start)

    def wait(self):
        pl.when(self.moved)(self.copy.wait)
        pl.when(jnp.logical_not(self.moved))(self.keep.wait)


def greet_all(me, plane=False):
    barrier = pltpu.get_barrier_semaphore()
    others = near(me.across_x) + [me.sibling()]
    others += [me.across_y(STEPS[s], PAIRS[s]) for s in range(1, 8)] if plane else near(me.across_y)
    for device in others:
        pl.semaphore_signal(barrier, 1, device_id=device, device_id_type=MESH)
    moved = me.c != me.j

    @pl.when(moved)
    def _():
        to = {"ctx": me.j, "fsdp": 2 * me.c + me.co}
        pl.semaphore_signal(barrier, 1, device_id=to, device_id_type=MESH)

    pl.semaphore_wait(barrier, len(others) + jnp.where(moved, 1, 0))


def near(dev):
    return [dev(1, 0), dev(-1, 0), dev(0, 1)]


def send(src, dst, sems, index, device):
    return pltpu.make_async_remote_copy(
        src, dst, sems[0].at[index], sems[1].at[index], device_id=device, device_id_type=MESH
    )


class Gather:
    MOVES = (
        ((0, 0), (0, 1), None),
        ((0, 0), (1, 0), None),
        ((0, 0), (-1, 0), None),
        ((0, 1), (1, 0), None),
        ((0, 1), (-1, 0), None),
        ((-1, 0), (1, 0), 0),
        ((-1, 1), (1, 0), 0),
        ((1, 0), (-1, 0), 1),
        ((1, 1), (-1, 0), 1),
    )

    def __init__(self, dev, own, loc, sems, row, sibling=None, sibling_sems=None):
        self.loc = loc
        self.copies = []
        for index, (block, to, half) in enumerate(self.MOVES):
            src = own if block == (0, 0) else loc(*block, 0, 0, half)
            dst = loc(*block, *to, half)
            self.copies.append(send(src, dst, sems, (row, index), dev(*to)))
        self.passed = {}
        if sibling is not None:
            self.passed[9] = send(own, loc(0, 0, 0, 0, None), sibling_sems, (row, 9), sibling)
            for index, ((dr, dp), (er, ep), half) in enumerate(self.MOVES):
                ref = loc(dr - er, dp + ep, 0, 0, half)
                self.passed[index] = send(ref, ref, sibling_sems, (row, index), sibling)
        self.own = own

    def _pass(self, index):
        if self.passed:
            self.passed[index].start()

    def _got(self, index):
        self.copies[index].wait_recv()
        self._pass(index)

    def start(self):
        for index in (0, 1, 2):
            self.copies[index].start()
        self._pass(9)

    def pair(self):
        self._got(0)
        self.copies[3].start()
        self.copies[4].start()

    def turn(self, dp):
        for got, on in (((1, 5), (2, 7)) if dp == 0 else ((3, 6), (4, 8))):
            self._got(got)
            self.copies[on].start()

    def last(self, dp):
        for got in ((5, 7) if dp == 0 else (6, 8)):
            self._got(got)

    def sync(self):
        for copy in self.passed.values():
            copy.wait()

    def end(self):
        for copy in self.copies:
            copy.wait_send()


class RingFirst:
    MOVES = (
        ((0, 0), (0, 1), None),
        ((0, 0), (1, 0), None),
        ((0, 0), (-1, 0), None),
        ((-1, 0), (1, 0), 0),
        ((1, 0), (-1, 0), 1),
        ((-1, 0), (0, 1), None),
        ((1, 0), (0, 1), None),
        ((2, 0), (0, 1), 0),
        ((2, 0), (0, 1), 1),
    )

    def __init__(self, dev, own, loc, sems, row):
        self.own, self.loc = own, loc
        self.copies = []
        for index, (block, to, half) in enumerate(self.MOVES):
            src = own if block == (0, 0) else loc(*block, 0, 0, half)
            self.copies.append(send(src, loc(*block, *to, half), sems, (row, index), dev(*to)))

    def go(self, *indices):
        for index in indices:
            self.copies[index].start()

    def got(self, *indices):
        for index in indices:
            self.copies[index].wait_recv()

    def end(self):
        for copy in self.copies:
            copy.wait_send()


def row_half(half, rows):
    return pl.ds(0, rows) if half is None else pl.ds(half * (rows // 2), rows // 2)


def add_into(ref, rows, others, step=16):
    step = min(step, rows)

    @pl.loop(0, rows // step)
    def _(i):
        at = pl.ds(pl.multiple_of(i * step, step), step)
        total = ref[at].astype(F32)
        for other in others:
            total = total + other[at].astype(F32)
        ref[at] = total.astype(ref.dtype)


class Scatter:
    def __init__(self, dev, part, rows, halves, fulls, paired, sems, row, cut=None):
        self.part, self.rows, self.cut = part, rows, cut
        self.halves, self.fulls, self.paired = halves, fulls, paired
        self.first, self.second = {}, {}
        for dp in (0, 1):
            for way, sign in ((0, 1), (1, -1)):
                self.first[way, dp] = send(
                    self._half(part(slot_of(2, dp)), way), halves.at[way, dp], sems, (row, way * 2 + dp), dev(sign, 0)
                )
                self.second[way, dp] = send(
                    part(slot_of(sign, dp)), fulls.at[way, dp], sems, (row, 4 + way * 2 + dp), dev(sign, 0)
                )
        self.third = send(part(slot_of(0, 1)), paired, sems, (row, 8), dev(0, 1))

    def _half(self, ref, way):
        if self.cut is None:
            return ref.at[pl.ds(way * (self.rows // 2), self.rows // 2)]
        return ref.at[:, pl.ds(way * (self.cut // 2), self.cut // 2)]

    def start(self):
        for dp in (1, 0):
            for way in (0, 1):
                self.first[way, dp].start()

    def turn(self, dp):
        for way, sign in ((0, 1), (1, -1)):
            self.first[way, dp].wait_recv()
            block = self._half(self.part(slot_of(sign, dp)), way)
            add_into(block, block.shape[0], [self.halves.at[way, dp]])
            self.second[way, dp].start()

    def pair(self):
        for way in (0, 1):
            self.second[way, 1].wait_recv()
        add_into(self.part(slot_of(0, 1)), self.rows, [self.fulls.at[0, 1], self.fulls.at[1, 1]])
        self.third.start()

    def finish(self, out, extra=()):
        for way in (0, 1):
            self.second[way, 0].wait_recv()
        self.third.wait_recv()
        own = self.part(0)
        terms = [own, self.fulls.at[0, 0], self.fulls.at[1, 0], self.paired, *extra]

        @pl.loop(0, self.rows // 16)
        def _(i):
            at = pl.ds(pl.multiple_of(i * 16, 16), 16)
            total = terms[0][at].astype(F32)
            for term in terms[1:]:
                total = total + term[at].astype(F32)
            out[at] = total.astype(out.dtype)

    def end(self):
        for copy in (*self.first.values(), *self.second.values(), self.third):
            copy.wait_send()


def mirror(slot):
    return slot_of(-STEPS[slot], PAIRS[slot])


class Trade:
    def __init__(self, dev, what, where, sems, row):
        self.copies = [
            pltpu.make_async_remote_copy(
                what(slot), where(slot), sems[0].at[row, slot], sems[1].at[row, mirror(slot)],
                device_id=dev(STEPS[slot], PAIRS[slot]), device_id_type=MESH,
            )
            for slot in range(1, 8)
        ]

    def start(self):
        for copy in self.copies:
            copy.start()

    def got(self):
        for copy in self.copies:
            copy.wait_recv()

    def end(self):
        for copy in self.copies:
            copy.wait_send()


def scatter_buffers(rows, columns, dtype=BF, cut=False):
    half = (rows, columns // 2) if cut else (rows // 2, columns)
    return [
        pltpu.VMEM((2, 2, *half), dtype),
        pltpu.VMEM((2, 2, rows, columns), dtype),
        pltpu.VMEM((rows, columns), dtype),
    ]


def dma_sems(rows, count):
    return [pltpu.SemaphoreType.DMA((rows, count)), pltpu.SemaphoreType.DMA((rows, count))]


def params(collective_id, vmem=56):
    return pltpu.CompilerParams(
        collective_id=collective_id, has_side_effects=True, vmem_limit_bytes=vmem << 20
    )


def dot_in(left, right):
    return jnp.dot(left, right, preferred_element_type=F32)


def dot_back(left, right):
    return lax.dot_general(left, right, (((1,), (1,)), ((), ())), preferred_element_type=F32)


def dot_rows(left, right):
    return lax.dot_general(left, right, (((0,), (0,)), ((), ())), preferred_element_type=F32)


def load(src, dst, sem):
    copy = pltpu.make_async_copy(src, dst, sem)
    copy.start()
    return copy


def turned(values):
    lane = lax.broadcasted_iota(jnp.int32, values.shape, 1)
    low = lax.rem(lane, 64) < 32
    return jnp.where(low, pltpu.roll(values, 96, 1), pltpu.roll(values, 32, 1))


def pile(out, values, half):
    for h in range(8):
        out[pl.ds(64 * h, 64), :] = values[64 * half : 64 * half + 64, 64 * h : 64 * h + 64]


def unpile(values):
    flat = values.T
    return [
        jnp.concatenate([flat[128 * m : 128 * m + 64], flat[128 * m + 64 : 128 * m + 128]], axis=1)
        for m in range(4)
    ]


def norm_scale(ref, out):
    values = ref[...].astype(F32)
    out[...] = lax.rsqrt(jnp.mean(values * values, axis=1, keepdims=True) + EPS)


def place_tables(me, deal, freq, cosine, sine, bias_p, bias_c):
    def block(slot, part):
        return deal[me.f, me.ctx_at(STEPS[slot], PAIRS[slot]), part]

    first, second = block(0, 0), block(0, 1)
    odd = lax.rem(second, 2)
    row = lax.broadcasted_iota(jnp.int32, (128, 128), 0)
    lane = lax.broadcasted_iota(jnp.int32, (128, 128), 1)
    position = jnp.where(row < 64, first * 64 + row, 448 + odd * 64 + row)
    angle = position.astype(F32) * freq[...]
    cosine[...] = jnp.cos(angle)
    sine[...] = jnp.where(lax.rem(lane, 64) < 32, -jnp.sin(angle), jnp.sin(angle))
    row, lane = row[:64], lax.rem(lane[:64], 64)
    mate = jnp.int32(0)
    for slot in range(8):
        seen = block(slot, 0) * 64 + row <= first * 64 + lane
        bias_p[pl.ds(64 * slot, 64), :] = jnp.where(seen, 0.0, -1e30)
        if slot:
            mate = mate + jnp.where(block(slot, 1) == second + 1 - 2 * odd, slot, 0)
    bias_c[pl.ds(0, 64), :] = jnp.where(odd + 0 * row == 1, 0.0, -1e30)
    bias_c[pl.ds(64, 64), :] = jnp.where(row <= lane, 0.0, -1e30)
    return mate


def layer_kernel(
    x_in, attn_gain, mlp_gain, deal, freq, q_in, key_in, value_in, wo_in, gate_in, up_in, dn_in, dy_in,
    mixed, tokens_grad, q_grad, kv_grad, o_grad, gains_out, gu_all, dn_all,
    q_saved, kw_saved, wo_saved, mpart, m_half, m_full, m_pair,
    x, gains, a1s, atts, qst, kst, vst, lse, h1, cosine, sine, bias_p, bias_c,
    qw, kw, wo, kv_own, kv, sT, pT, dT, dsT, scale, gu_win, dnp, acts, gu, wd, dy, hid,
    grecv, gdrecv, g_pair, da2, datts, dqkvs, grow, gown_rows, gsib_rows, dn_moved,
    n_half, n_full, n_pair, e_half, e_full, e_pair, gp, ggot, g_sum, o_got, q_got, k_got,
    s0, s1, t0, t1, y0, y1, u0, u1, r0, r1, z0, z1, c0, c1, w0, w1, v0, v1, credit, local,
):
    me = Place()
    greet_all(me, plane=True)
    own, other = pl.ds(0, 128), pl.ds(128, 128)
    slots = iter(range(64))

    def load(src, dst):
        copy = pltpu.make_async_copy(src, dst, local.at[next(slots)])
        copy.start()
        return copy

    def later(src, dst):
        return pltpu.make_async_copy(src, dst, local.at[next(slots)])

    def aligned(index, step):
        return index if isinstance(index, int) else pl.multiple_of(index, step)

    def gains_at(dr, dp, er, ep, half):
        return gains.at[me.fsdp_at(dr, dp), row_half(half, 16)]

    def slot_at(ref, rows):
        def loc(dr, dp, er, ep, half):
            return ref.at[slot_of(dr - er, dp + ep), row_half(half, rows)]

        return loc

    def acts_at(dr, dp, er, ep, half):
        slot = slot_of(dr - er, dp + ep)
        return acts.at[slot // 2, slot % 2, row_half(half, 128)]

    def columns(first, index):
        return pl.ds(pl.multiple_of(first + index * 128, 128), 128)

    def plain(ref, count):
        def loc(dr, dp, er, ep, half):
            return ref.at[me.chip_at(dr, dp), me.co, row_half(half, 128), pl.ds(0, count)]

        return loc

    def strip_x(ref, first):
        def loc(dr, dp, er, ep, half):
            return ref.at[me.chip_at(dr, dp), me.co, row_half(half, 128), columns(first, me.c)]

        return loc

    def strip_y(ref, first):
        def loc(dr, dp, er, ep, half):
            chips = pl.ds(0, 8) if half is None else pl.ds(4 * half, 4)
            return ref.at[chips, me.co, :, columns(first, me.ctx_at(dr, dp))]

        return loc

    def wd_at(dr, dp, er, ep, half):
        size = 352 if half is None else 176
        first = me.co * 352 + (0 if half is None else half * size)
        return wd.at[
            pl.ds(pl.multiple_of(first, 16), size),
            pl.ds(pl.multiple_of(me.chip_at(dr, dp) * 256, 256), 256),
        ]

    def gu_at(dr, dp, er, ep, half):
        size = 128 if half is None else 64
        first = me.fsdp_at(dr, dp) * 128 + (0 if half is None else half * size)
        return gu.at[pl.ds(pl.multiple_of(first, size), size)]

    def over_x(own, loc, row, both=True):
        own = loc(0, 0, 0, 0, None) if own is None else own
        return Gather(me.across_x, own, loc, (s0, s1), row, me.sibling() if both else None, (t0, t1))

    def over_y(own, loc, row, both=True):
        own = loc(0, 0, 0, 0, None) if own is None else own
        return Gather(me.across_y, own, loc, (y0, y1), row, me.sibling() if both else None, (u0, u1))

    g = over_x(None, gains_at, 0)
    k = over_x(None, plain(kw, 512), 1)
    q = over_x(q_in.at[:, pl.ds(0, 1024)], plain(qw, 1024), 2)
    qx = over_x(q_in.at[:, columns(1024, me.c)], strip_x(qw, 1024), 3, both=False)
    o = over_x(wo_in.at[:, pl.ds(0, 1024)], plain(wo, 1024), 4)
    ox = over_x(wo_in.at[:, columns(1024, me.c)], strip_x(wo, 1024), 5, both=False)
    m = over_x(None, gu_at, 6)
    dn = over_x(dnp, wd_at, 7)
    qy = over_y(None, strip_y(qw, 1024), 0)
    oy = over_y(None, strip_y(wo, 1024), 1)
    dy_task = over_y(dy_in, slot_at(dy, 128), 2, both=False)
    kv_task = over_y(kv_own, slot_at(kv, 128), 3, both=False)
    a = over_y(None, acts_at, 4, both=False)
    swap = Swap(me, dn_in.at[:, pl.ds(pl.multiple_of(me.c * 256, 256), 256)], dnp, (w0, w1), local.at[next(slots)])

    own_kw = plain(kw, 512)(0, 0, 0, 0, None)
    x_load = load(x_in, x)
    loads = [load(key_in, own_kw.at[:, pl.ds(0, 256)]), load(value_in, own_kw.at[:, pl.ds(256, 256)])]
    kept = {task: load(task.own, task.loc(0, 0, 0, 0, None)) for task in (q, qx, o, ox, dy_task)}
    window = pl.ds(pl.multiple_of(me.y * 1408 + me.zl * 640, 128), 768)
    loads.append(load(gate_in.at[:, window], gu_win.at[0]))
    loads.append(load(up_in.at[:, window], gu_win.at[1]))
    gains[me.f] = jnp.zeros((16, 128), F32)
    gains[me.f, pl.ds(0, 1), :] = attn_gain[...].astype(F32)
    gains[me.f, pl.ds(8, 1), :] = mlp_gain[...].astype(F32)

    dpart = op = wo.at[:, 0]
    qp = wo.at[:, 1]
    dgu = wo.at[:, 1, :, pl.ds(0, 1536)]
    kvp = kv

    def gsib(t):
        return gu.at[pl.ds(aligned(128 * t, 128), 128)]

    def gown(t):
        return gu.at[pl.ds(aligned(1024 + 128 * t, 128), 128)]

    def kp(t):
        return gu.at[pl.ds(aligned(128 * t, 128), 128), pl.ds(0, 512)]

    def gd(t):
        return wd.at[:, pl.ds(aligned(256 * t, 256), 256)]

    def gd_own(t):
        return gd(t).at[pl.ds(pl.multiple_of(me.co * 352, 16), 352)]

    def dost(n, half):
        return grecv.at[pl.ds(0, 4), :, pl.ds(pl.multiple_of(512 + 128 * (2 * n + half), 128), 128)]

    saved = []

    def put_gate_up():
        loads[2].wait()
        loads[3].wait()

        @pl.loop(0, 8)
        def _(i):
            rows = pl.ds(pl.multiple_of(16 * i, 16), 16)
            out = pl.ds(pl.multiple_of(me.f * 128 + 16 * i, 16), 16)
            for w in (0, 1):
                values = gu_win[w, rows].astype(F32)
                values = jnp.where(me.zl == 1, pltpu.roll(values, 704, 1), values)
                lane = lax.broadcasted_iota(jnp.int32, values.shape, 1)
                gu[out, 768 * w : 768 * w + 768] = jnp.where(lane < 704, values, 0.0).astype(BF)

        wd[pl.ds(704, 64)] = jnp.zeros((64, 2048), BF)

    def normed():
        norm_scale(x, scale)

        @pl.loop(0, 16)
        def _(i):
            at = pl.ds(pl.multiple_of(i * 128, 128), 128)
            a1s[own, at] = (x[:, at].astype(F32) * scale[...] * gains[i, pl.ds(0, 1), :]).astype(BF)

    def project_kv():
        raw = dot_in(a1s[own], kw[...].reshape(2048, 512))
        for i in range(2):
            part = raw[:, 128 * i : 128 * i + 128]
            kv_own[:, 128 * i : 128 * i + 128] = (part * cosine[...] + turned(part) * sine[...]).astype(BF)
        kv_own[:, 256:] = raw[:, 256:].astype(BF)
        kv[0] = kv_own[...]

    def project_q():
        @pl.loop(0, 4)
        def _(n):
            raw = dot_in(a1s[own], qw[:, :, :, pl.ds(pl.multiple_of(512 * n, 512), 512)].reshape(2048, 512))
            for i in range(4):
                part = raw[:, 128 * i : 128 * i + 128]
                part = ((part * cosine[...] + turned(part) * sine[...]).astype(BF).astype(F32) * SCALE).astype(BF)
                for half in (0, 1):
                    for e in (0, 1):
                        rows = pl.ds(64 * (2 * i + e), 64)
                        qst[n, half, rows, :] = part[64 * half : 64 * half + 64, 64 * e : 64 * e + 64]

    def collect_kv(mate):
        beside = kv[mate]
        for out, base in ((kst, 0), (vst, 256)):
            for n in range(4):
                first = base + 64 * n
                for slot in range(8):
                    out[n, pl.ds(64 * slot, 64), :] = kv[slot, 0:64, first : first + 64]
                out[n, pl.ds(512, 64), :] = beside[64:128, first : first + 64]
                out[n, pl.ds(576, 64), :] = kv_own[64:128, first : first + 64]

    def attend(n, half):
        count = 512 if half == 0 else 640
        keys = pl.ds(0, count)
        sT[keys] = dot_back(kst[n, keys, :], qst[n, half])
        for i in range(4):
            at = pl.ds(128 * i, 128)
            if half == 0:
                scores = sT[keys, at] + bias_p[...]
                peak = jnp.max(scores, axis=0, keepdims=True)
                raised = jnp.exp(scores - peak)
                total = jnp.sum(raised, axis=0, keepdims=True)
                pT[keys, at] = (raised * (1.0 / total)).astype(BF)
            else:
                first = sT[0:512, at]
                rest = sT[512:640, at] + bias_c[...]
                peak = jnp.maximum(
                    jnp.max(first, axis=0, keepdims=True), jnp.max(rest, axis=0, keepdims=True)
                )
                first = jnp.exp(first - peak)
                rest = jnp.exp(rest - peak)
                total = jnp.sum(first, axis=0, keepdims=True) + jnp.sum(rest, axis=0, keepdims=True)
                pT[0:512, at] = (first * (1.0 / total)).astype(BF)
                pT[512:640, at] = (rest * (1.0 / total)).astype(BF)
            lse[2 * n + half, :, at] = peak + jnp.log(total)
        for i, block in enumerate(unpile(dot_rows(vst[n, keys, :], pT[keys]))):
            first = pl.multiple_of(512 * n + 128 * i, 128)
            atts[pl.ds(64 * half, 64), pl.ds(first, 128)] = block.astype(BF)

    def project_o():
        @pl.loop(0, 4)
        def _(n):
            at = pl.ds(pl.multiple_of(512 * n, 512), 512)
            h1[:, at] = x[:, at].astype(F32) + dot_in(atts[own], wo[:, :, :, at].reshape(2048, 512))

    def normed_two():
        norm_scale(h1, scale)

        @pl.loop(0, 16)
        def _(i):
            at = pl.ds(pl.multiple_of(i * 128, 128), 128)
            acts[0, 0, :, at] = (h1[:, at] * scale[...] * gains[i, pl.ds(8, 1), :]).astype(BF)

    def mpart_copy(n):
        return [
            pltpu.make_async_copy(
                kv.at[pl.ds(2 * i, 2)], mpart.at[pl.ds(2 * n, 2), :, pl.ds(512 * i, 512)], local.at[60 + i]
            )
            for i in range(4)
        ]

    def group(n):
        at = pl.ds(2 * n, 2)
        rows = pl.ds(pl.multiple_of(256 * n, 256), 256)
        for h in range(3):
            first, second = pl.ds(256 * h, 256), pl.ds(768 + 256 * h, 256)
            here = acts[n].reshape(256, 2048)
            gate = dot_in(here, gu[:, first])
            up = dot_in(here, gu[:, second])
            back = dot_back(dy[at].reshape(256, 2048), wd[first, :])
            curve = 1.0 / (1.0 + jnp.exp(-gate))
            silu = gate * curve
            hid[rows, first] = (silu * up).astype(BF)
            dgu[at, :, first] = (back * up * (curve + silu * (1.0 - curve))).astype(BF).reshape(2, 128, 256)
            dgu[at, :, second] = (back * silu).astype(BF).reshape(2, 128, 256)

        @pl.when(n > 0)
        def _():
            for copy in mpart_copy(n - 1):
                copy.wait()

        for i in range(4):
            wide = pl.ds(512 * i, 512)
            grads = dgu[at].reshape(256, 1536)
            dpart[at, :, wide] = dot_back(grads, gu[wide, :]).astype(BF).reshape(2, 128, 512)
            kv[pl.ds(2 * i, 2)] = dot_in(hid[rows, :], wd[:, wide]).astype(BF).reshape(2, 128, 512)
        for copy in mpart_copy(n):
            copy.start()

    def group_half(slot):
        rows = pl.ds(128 * slot, 128)
        here = acts[slot // 2, slot % 2]
        for h in range(3):
            first, second = pl.ds(256 * h, 256), pl.ds(768 + 256 * h, 256)
            gate = dot_in(here, gu[:, first])
            up = dot_in(here, gu[:, second])
            back = dot_back(dy[slot], wd[first, :])
            curve = 1.0 / (1.0 + jnp.exp(-gate))
            silu = gate * curve
            hid[rows, first] = (silu * up).astype(BF)
            dgu[slot, :, first] = (back * up * (curve + silu * (1.0 - curve))).astype(BF)
            dgu[slot, :, second] = (back * silu).astype(BF)
        for i in range(4):
            wide = pl.ds(512 * i, 512)
            dpart[slot, :, wide] = dot_back(dgu[slot], gu[wide, :]).astype(BF)

    def group_out():
        for copy in mpart_copy(2):
            copy.wait()
        for i in range(4):
            wide = pl.ds(512 * i, 512)
            kv[pl.ds(2 * i, 2)] = dot_in(hid[pl.ds(768, 256), :], wd[:, wide]).astype(BF).reshape(2, 128, 512)
        for copy in mpart_copy(3):
            copy.start()

    class Views:
        def __init__(self, pick):
            self.pick = pick

        @property
        def at(self):
            return self

        def __getitem__(self, index):
            return self.pick(index)

    def scatter(dev, part, place, columns, row, pair=None):
        wide = pl.ds(0, columns)
        halves = Views(lambda index: place.at[4 + index[0], pl.ds(64 * index[1], 64), wide])
        fulls = Views(lambda index: place.at[2 * index[0] + index[1], :, wide])
        paired = place.at[6, :, wide] if pair is None else pair
        return Scatter(dev, part, 128, halves, fulls, paired, (r0, r1), row)

    first_bay, second_bay = qw.at[:, 0], qw.at[:, 1]
    d = scatter(me.across_y, lambda slot: dpart.at[slot], second_bay, 2048, 0)
    gjob = scatter(me.across_x, gown, first_bay, 1536, 1, g_pair)
    n_job = Scatter(me.across_x, gd_own, 352, n_half, n_full, n_pair, (r0, r1), 2)
    o_job = scatter(me.across_x, lambda slot: op.at[slot], second_bay, 2048, 3)
    q_job = scatter(me.across_x, lambda slot: qp.at[slot], first_bay, 2048, 4)
    k_job = scatter(me.across_x, kp, kw.at[:, 0], 512, 5)
    e_job = Scatter(me.across_x, lambda slot: gp.at[slot], 16, e_half, e_full, e_pair, (r0, r1), 6)
    d_job = scatter(me.across_y, lambda slot: kvp.at[slot], kw.at[:, 1], 512, 7)

    def weight_terms(t, core):
        at = pl.multiple_of((chip_of(me, t) * 2 + core) * 128, 128)
        left = acts[:, :, :, pl.ds(at, 128)].reshape(1024, 128)
        return dot_rows(left, dgu[...].reshape(1024, 1536))

    def gu_to(t):
        return send(gsib(t), grecv.at[t], (c0, c1), 8 + t, me.sibling())

    def down_to(t):
        mine = pl.ds(pl.multiple_of((1 - me.co) * 352, 16), 352)
        return send(gd(t).at[mine], gdrecv.at[t], (c0, c1), t, me.sibling())

    def terms_for_sibling(start):
        @pl.loop(start, start + 2)
        def _(i):
            gsib(7 - i)[...] = weight_terms(7 - i, 1 - me.co).astype(BF)
            gu_to(7 - i).start()

    def sibling_has_terms():
        @pl.loop(0, 8)
        def _(t):
            gu_to(t).wait_send()

    def own_terms(start):
        @pl.loop(start, start + 2)
        def _(i):
            gu_to(7 - i).wait_recv()
            gown(7 - i)[...] = (weight_terms(7 - i, me.co) + grecv[7 - i].astype(F32)).astype(BF)

    def down_terms():
        @pl.loop(0, 8)
        def _(t):
            at = pl.multiple_of(chip_of(me, t) * 256, 256)
            gd(t)[...] = dot_rows(hid[...], dy[:, :, pl.ds(at, 256)].reshape(1024, 256)).astype(BF)
            down_to(t).start()

    def down_sums():
        @pl.loop(0, 8)
        def _(t):
            down_to(t).wait_recv()

            @pl.loop(0, 22)
            def _(i):
                at = pl.ds(pl.multiple_of(i * 16, 16), 16)
                mine = gd(t).at[pl.ds(pl.multiple_of(me.co * 352 + i * 16, 16), 16)]
                mine[...] = (mine[...].astype(F32) + gdrecv[t, at].astype(F32)).astype(BF)

    m_first, m_second = {}, {}
    for dp in (0, 1):
        for way, sign in ((0, 1), (1, -1)):
            m_first[way, dp] = send(
                mpart.at[slot_of(2, dp), pl.ds(64 * way, 64)], m_half.at[way, dp], (r0, r1), (8, way * 2 + dp),
                me.across_y(sign, 0),
            )
            m_second[way, dp] = send(
                dy.at[1 + 2 * way + dp], m_full.at[way, dp], (r0, r1), (8, 4 + way * 2 + dp), me.across_y(sign, 0)
            )
    m_third = send(dy.at[5], m_pair, (r0, r1), (8, 8), me.across_y(0, 1))

    def m_start():
        dy_task.end()
        for copy in mpart_copy(3):
            copy.wait()
        for dp in (1, 0):
            for way in (0, 1):
                m_first[way, dp].start()

    m_parts = {(way, dp): later(mpart.at[slot_of(1 - 2 * way, dp)], dy.at[1 + 2 * way + dp]) for way in (0, 1) for dp in (0, 1)}
    m_halves = {(way, dp): later(m_half.at[way, dp], dy.at[6 + way, pl.ds(0, 64)]) for way in (0, 1) for dp in (0, 1)}
    m_fulls = {(way, dp): later(m_full.at[way, dp], dy.at[6 + way]) for way in (0, 1) for dp in (0, 1)}
    m_mine, m_near, m_last = later(mpart.at[0], dy.at[1]), later(mpart.at[1], dy.at[5]), later(m_pair, dy.at[2])
    m_out = later(dy.at[1], mixed)

    def m_turn(dp):
        for way in (0, 1):
            m_parts[way, dp].start()
        for way in (0, 1):
            m_first[way, dp].wait_recv()
            m_halves[way, dp].start()
        for way in (0, 1):
            m_parts[way, dp].wait()
            m_halves[way, dp].wait()
            add_into(dy.at[1 + 2 * way + dp, pl.ds(64 * way, 64)], 64, [dy.at[6 + way, pl.ds(0, 64)]])
            m_second[way, dp].start()

    def m_pair_up():
        m_near.start()
        for way in (0, 1):
            m_second[way, 1].wait_recv()
            m_fulls[way, 1].start()
        m_near.wait()
        for way in (0, 1):
            m_fulls[way, 1].wait()
        add_into(dy.at[5], 128, [dy.at[6], dy.at[7]])
        m_third.start()

    def m_finish():
        for dp in (0, 1):
            m_second[0, dp].wait_send()
        m_mine.start()
        for way in (0, 1):
            m_second[way, 0].wait_recv()
            m_fulls[way, 0].start()
        m_third.wait_recv()
        m_last.start()
        m_mine.wait()
        for way in (0, 1):
            m_fulls[way, 0].wait()
        m_last.wait()

        @pl.loop(0, 8)
        def _(i):
            at = pl.ds(pl.multiple_of(i * 16, 16), 16)
            total = h1[at]
            for slot in (1, 2, 6, 7):
                total = total + dy[slot, at].astype(F32)
            dy[1, at] = total.astype(BF)

        m_out.start()

    def wo_load(n):
        return pltpu.make_async_copy(
            wo_saved.at[pl.ds(2 * n, 2)], acts.at[pl.ds(2 * (n % 2), 2)], local.at[56 + n % 2]
        )

    def q_load(n):
        return pltpu.make_async_copy(q_saved.at[pl.ds(2 * n, 2)], acts.at[pl.ds(2 * (n % 2), 2)], local.at[58 + n % 2])

    def kw_load():
        return [
            load(kw_saved.at[chip], grecv.at[pl.ds(2 * (chip % 4), 2), :, pl.ds(512 * (chip // 4), 512)])
            for chip in range(8)
        ]

    def at_ctx(ref):
        def loc(dr, dp, er, ep, half):
            return ref.at[me.ctx_at(dr, dp), row_half(half, ref.shape[1])]

        return loc

    def dn_at(dr, dp, er, ep, half):
        first = pl.multiple_of(me.ctx_at(dr, dp) * 256, 256)
        return dn_all.at[row_half(half, 352), pl.ds(first, 256)]

    gu_task = over_y(gown(0), at_ctx(gu_all), 5, both=False)
    dn_task = over_y(dn_moved, dn_at, 6, both=False)
    dn_swap = Swap(me, gd_own(0), dn_moved, (v0, v1), local.at[next(slots)])
    gu_keep = later(gown(0), gu_all.at[me.c])
    dn_keep = later(dn_moved, dn_at(0, 0, 0, 0, None))
    dn_local = later(dnp, wd_at(0, 0, 0, 0, None))
    tokens_out = later(datts.at[own], tokens_grad)

    def block_at(ref, slot):
        first = pl.multiple_of(me.ctx_at(STEPS[slot], PAIRS[slot]) * 16, 16)
        return ref.at[pl.ds(first, 16)]

    def sum_over_ctx(total, got, row):
        return Trade(
            me.across_y, lambda slot: block_at(total, slot), lambda slot: got.at[mirror(slot)], (z0, z1), row
        )

    def spread(out, row):
        return Trade(me.across_y, lambda slot: block_at(out, 0), lambda slot: block_at(out, 0), (z0, z1), row)

    def sum_up(total, got, out):
        value = block_at(total, 0)[...].astype(F32)
        for slot in range(1, 8):
            value = value + got[slot].astype(F32)
        block_at(out, 0)[...] = value.astype(BF)

    o_sum, q_sum, kv_sum = op.at[0], qp.at[0], kp(0)
    o_sums = sum_over_ctx(o_sum, o_got, 0)
    q_sums = sum_over_ctx(q_sum, q_got, 1)
    k_sums = sum_over_ctx(kv_sum, k_got, 2)
    o_spread = spread(o_grad, 3)
    q_spread = spread(q_grad, 4)
    k_spread = spread(kv_grad, 5)
    e_task = Trade(me.across_y, lambda slot: g_sum, lambda slot: ggot.at[me.c], (z0, z1), 6)

    def to_sibling(src, dst, index):
        return send(src, dst, (c0, c1), 16 + index, me.sibling())

    att_swap = to_sibling(atts.at[own], atts.at[other], 0)
    datt_swap = to_sibling(datts.at[own], datts.at[other], 1)
    a1_swap = to_sibling(a1s.at[own], a1s.at[other], 2)
    queries, rest = pl.ds(0, 2048), pl.ds(2048, 512)
    dq_swap = to_sibling(dqkvs.at[own, queries], dqkvs.at[other, queries], 3)
    dkv_swap = to_sibling(dqkvs.at[own, rest], dqkvs.at[other, rest], 4)
    gain_swap = to_sibling(gown_rows, gsib_rows, 5)

    def norm_two_back():
        for i in range(16):
            grow[0, :, 128 * i : 128 * i + 128] = gains[i, 0:1, :]
            grow[1, :, 128 * i : 128 * i + 128] = gains[i, 8:9, :]
        grow[2] = jnp.zeros((1, 2048), F32)
        grow[3] = jnp.zeros((1, 2048), F32)

        @pl.loop(0, 8)
        def _(i):
            at = pl.ds(pl.multiple_of(16 * i, 16), 16)
            values, grad = h1[at], da2[at]
            scale = lax.rsqrt(jnp.mean(values * values, axis=1, keepdims=True) + EPS)
            grow[3] += jnp.sum(grad * values * scale, axis=0, keepdims=True)
            grad = grad * grow[1]
            level = jnp.mean(grad * values, axis=1, keepdims=True) * scale * scale * scale
            total = dy[0, at].astype(F32) + scale * grad - values * level
            da2[at] = total
            datts[at] = total.astype(BF)

        datt_swap.start()

    def heads_back():
        for n in range(4):
            wo_load(n).wait()
            part = dot_back(datts[own], acts[2 * (n % 2) : 2 * (n % 2) + 2].reshape(512, 2048)).astype(BF)
            for half in (0, 1):
                place = dost(n, half)
                for h in range(8):
                    place[h // 2, pl.ds(64 * (h % 2), 64), pl.ds(0, 64)] = part[
                        64 * half : 64 * half + 64, 64 * h : 64 * h + 64
                    ]
            if n < 2:
                wo_load(n + 2).start()
        for n in range(2):
            q_load(n).start()

    def terms(left, right, out, job):
        @pl.loop(0, 8)
        def _(i):
            at = pl.multiple_of((chip_of(me, 7 - i) * 2 + me.co) * 128, 128)
            out(7 - i)[...] = dot_rows(left[:, pl.ds(at, 128)], right[...]).astype(BF)

            @pl.when(i == 1)
            def _():
                job.start()

    def output_terms():
        att_swap.wait_recv()
        datt_swap.wait_recv()
        pl.semaphore_wait(credit, 3)
        terms(atts, datts, lambda t: op.at[t], o_job)

    def query_terms():
        a1_swap.wait_recv()
        dq_swap.wait_recv()
        terms(a1s, dqkvs.at[:, pl.ds(0, 2048)], lambda t: qp.at[t], q_job)

    def kv_terms():
        dkv_swap.wait_recv()
        terms(a1s, dqkvs.at[:, pl.ds(2048, 512)], kp, k_job)

    def kv_blocks(mate):
        for part, base in ((0, 0), (64, 256)):
            for n in range(4):
                first = base + 64 * n
                block = grecv[0:5, :, 128 * n : 128 * n + 128].reshape(640, 128)[:, part : part + 64]
                for slot in range(8):
                    kvp[slot, 0:64, first : first + 64] = block[64 * slot : 64 * slot + 64]
                    if slot == 0:
                        late = block[576:640]
                    else:
                        late = jnp.where(mate == slot, block[512:576], jnp.zeros((64, 64), BF))
                    kvp[slot, 64:128, first : first + 64] = late

    def kv_back():
        for i in range(2):
            at = slice(128 * i, 128 * i + 128)
            block = sT[512:640, at]
            dqkvs[own, 2048 + 128 * i : 2176 + 128 * i] = (block * cosine[...] - turned(block) * sine[...]).astype(BF)
        dqkvs[own, 2304:2560] = sT[512:640, 256:512].astype(BF)
        dkv_swap.start()

    def inputs_back():
        for copy in kw_back:
            copy.wait()
        for n in range(4):
            q_load(n).wait()
            block = dot_back(dqkvs[own, queries], acts[2 * (n % 2) : 2 * (n % 2) + 2].reshape(512, 2048))
            four, wide = pl.ds(4 * (n % 2), 4), pl.ds(512 * (n // 2), 512)
            block = block + dot_back(dqkvs[own, rest], grecv[four, :, wide].reshape(512, 512))
            sT[pl.ds(128 * n, 128)] = block
            if n < 2:
                q_load(n + 2).start()

    def norm_one_back():
        datt_swap.wait_send()

        @pl.loop(0, 8)
        def _(i):
            at = pl.ds(pl.multiple_of(16 * i, 16), 16)
            values = x[at].astype(F32)
            grad = jnp.concatenate([sT[pl.ds(pl.multiple_of(128 * n + 16 * i, 16), 16)] for n in range(4)], axis=1)
            scale = lax.rsqrt(jnp.mean(values * values, axis=1, keepdims=True) + EPS)
            grow[2] += jnp.sum(grad * values * scale, axis=0, keepdims=True)
            grad = grad * grow[0]
            level = jnp.mean(grad * values, axis=1, keepdims=True) * scale * scale * scale
            datts[at] = (da2[at] + scale * grad - values * level).astype(BF)

        tokens_out.start()

        gown_rows[...] = jnp.zeros((16, 16, 128), F32)
        for i in range(16):
            gown_rows[i, 0:1, :] = grow[2, :, 128 * i : 128 * i + 128]
            gown_rows[i, 8:9, :] = grow[3, :, 128 * i : 128 * i + 128]
        gain_swap.start()

    def gain_terms():
        gain_swap.wait_recv()
        for slot in range(8):
            block = me.fsdp_at(STEPS[slot], PAIRS[slot])
            gp[slot] = gown_rows[block] + gsib_rows[block]

    def dn_begin():
        dn_swap.wait()
        dn_task.start()
        dn_keep.start()

    def gu_begin():
        gu_keep.start()
        gu_task.start()

    def e_begin():
        e_task.start()
        ggot[me.c] = g_sum[...]

    def attend_back(n, half):
        count = 512 if half == 0 else 640
        keys = pl.ds(0, count)
        key, query, out = kst[n, keys, :], qst[n, half], dost(n, half)[...].reshape(512, 128)[:, 0:64]
        sT[keys] = dot_back(key, query)
        dT[keys] = dot_back(vst[n, keys, :], out)
        for i in range(4):
            at = pl.ds(128 * i, 128)
            parts = []
            for first, size in ((0, 512), (512, 128))[: 1 + half]:
                scores = sT[first : first + size, at]
                if half == 0:
                    scores = scores + bias_p[...]
                elif first:
                    scores = scores + bias_c[...]
                probs = jnp.exp(scores - lse[2 * n + half, :, at])
                grad = dT[first : first + size, at]
                parts.append((first, size, probs, grad))
            level = sum(jnp.sum(probs * grad, axis=0, keepdims=True) for _, _, probs, grad in parts)
            for first, size, probs, grad in parts:
                pT[first : first + size, at] = probs.astype(BF)
                dsT[first : first + size, at] = (probs * (grad - level)).astype(BF)
        rows = slice(64 * half, 64 * half + 64)
        for i, block in enumerate(unpile(dot_rows(key, dsT[keys]) * SCALE)):
            block = block * cosine[rows] - turned(block) * sine[rows]
            first = pl.multiple_of(512 * n + 128 * i, 128)
            dqkvs[rows, pl.ds(first, 128)] = block.astype(BF)
        return dot_in(dsT[keys], query), dot_in(pT[keys], out)

    def keep_kv_grads(n, one, two):
        keys = jnp.concatenate([one[0] + two[0][0:512], two[0][512:640]], axis=0)
        values = jnp.concatenate([one[1] + two[1][0:512], two[1][512:640]], axis=0)
        both = jnp.concatenate([keys, values], axis=1).astype(BF)
        grecv[pl.ds(0, 5), :, pl.ds(pl.multiple_of(128 * n, 128), 128)] = both.reshape(5, 128, 128)

    qx.start()
    ox.start()
    dy_task.start()
    loads[0].wait()
    loads[1].wait()
    k.start()
    qx.turn(0)
    ox.pair()
    ox.turn(0)
    ox.turn(1)
    g.start()
    qx.pair()
    qx.last(0)
    ox.last(1)
    ox.last(0)
    g.turn(0)
    k.turn(0)
    kept[ox].wait()
    oy.start()
    qx.turn(1)
    q.start()
    k.last(0)
    qx.last(1)
    swap.start()
    kept[qx].wait()
    qy.start()
    g.pair()
    k.pair()
    oy.turn(0)
    q.turn(0)
    oy.pair()
    k.turn(1)
    g.turn(1)
    g.last(0)
    o.start()
    g.last(1)
    qy.turn(0)
    mate = place_tables(me, deal, freq, cosine, sine, bias_p, bias_c)
    q.pair()
    k.last(1)
    g.sync()
    k.sync()
    x_load.wait()
    normed()
    oy.turn(1)
    q.last(0)
    project_kv()
    kv_task.start()
    oy.last(0)
    o.turn(0)
    qy.pair()
    put_gate_up()
    q.turn(1)
    o.pair()
    kv_task.pair()
    oy.last(1)
    swap.wait()
    dn_local.start()
    dn.start()
    kv_task.turn(0)
    qy.turn(1)
    q.last(1)
    kv_task.turn(1)
    qy.last(0)
    o.turn(1)
    m.start()
    dy_task.pair()
    o.last(0)
    oy.sync()
    dy_task.turn(0)
    kv_task.last(1)
    qy.last(1)
    dn.turn(0)
    kv_task.last(0)
    q.sync()
    dn.pair()
    collect_kv(mate)
    qy.sync()
    kept[q].wait()
    saved.append(load(qw, q_saved))
    saved.append(load(kw, kw_saved))
    project_q()

    @pl.loop(0, 4)
    def _(n):
        attend(n, 0)
        attend(n, 1)

        @pl.when(n == 0)
        def _():
            o.last(1)

        @pl.when(n == 2)
        def _():
            dy_task.turn(1)

    m.pair()
    o.sync()
    kept[o].wait()
    saved.append(load(wo, wo_saved))
    project_o()
    a1_swap.start()
    normed_two()
    for task in (k, q, qx, qy):
        task.end()
    saved[0].wait()
    saved[1].wait()
    m.turn(0)
    a.start()
    dy_task.last(0)
    m.turn(1)
    dy_task.last(1)
    m.last(0)
    dn.turn(1)
    dn.last(0)
    a.pair()
    att_swap.start()
    m.last(1)
    dn.last(1)
    m.sync()
    a.turn(0)
    dn.sync()

    for task in (o, ox, oy, kv_task):
        task.end()
    saved[2].wait()
    dn_local.wait()
    kept[dy_task].wait()

    @pl.loop(0, 3)
    def _(n):
        group(n)

        @pl.when(n == 1)
        def _():
            a.turn(1)

    a.last(0)
    group_half(6)
    a.last(1)
    group_half(7)
    d.start()
    m.end()
    terms_for_sibling(0)
    terms_for_sibling(2)
    own_terms(0)
    gjob.start()
    terms_for_sibling(4)
    own_terms(2)
    d.turn(1)
    terms_for_sibling(6)
    own_terms(4)
    gjob.turn(1)
    group_out()
    dn.end()
    down_terms()
    own_terms(6)
    a.end()
    wo_load(0).start()
    wo_load(1).start()
    d.turn(0)
    down_sums()
    n_job.start()
    d.pair()
    n_job.turn(1)
    gjob.turn(0)
    n_job.turn(0)
    m_start()
    n_job.pair()
    d.finish(da2)
    norm_two_back()
    for device in near(me.across_x):
        pl.semaphore_signal(credit, 1, device_id=device, device_id_type=MESH)
    m_turn(1)
    gjob.pair()
    d.end()
    output_terms()
    n_job.finish(gd_own(0))
    dn_swap.start()
    heads_back()

    @pl.loop(0, 4)
    def _(n):
        one, two = attend_back(n, 0), attend_back(n, 1)
        keep_kv_grads(n, one, two)

        @pl.when(n == 0)
        def _():
            dn_begin()
            gjob.finish(gown(0))
            o_job.turn(1)
            gu_begin()

        @pl.when(n == 1)
        def _():
            o_job.turn(0)

    kv_blocks(mate)
    kw_back = kw_load()
    d_job.start()
    dn_task.pair()
    d_job.turn(1)
    o_job.pair()
    d_job.turn(0)
    gu_task.turn(0)
    dq_swap.start()
    query_terms()
    d_job.pair()
    gu_task.pair()
    m_pair_up()
    m_turn(0)
    o_job.finish(o_sum)
    d_job.finish(sT.at[pl.ds(512, 128)])
    kv_back()
    o_sums.start()
    q_job.turn(1)
    inputs_back()
    norm_one_back()
    sibling_has_terms()
    kv_terms()
    gain_terms()
    gu_task.last(0)
    e_job.start()
    q_job.turn(0)
    q_job.pair()
    gu_task.turn(1)
    m_finish()
    e_job.turn(1)
    k_job.turn(1)
    o_sums.got()
    sum_up(o_sum, o_got, o_grad)
    dn_task.turn(0)
    o_spread.start()
    dn_task.turn(1)
    q_job.finish(q_sum)
    k_job.turn(0)
    gu_task.last(1)
    e_job.pair()
    k_job.pair()
    q_sums.start()
    e_job.turn(0)
    dn_task.last(1)
    e_job.finish(g_sum)
    k_job.finish(kv_sum)
    dn_task.last(0)
    e_begin()
    k_sums.start()
    q_sums.got()
    sum_up(q_sum, q_got, q_grad)
    q_spread.start()
    o_spread.got()
    k_sums.got()
    sum_up(kv_sum, k_got, kv_grad)
    k_spread.start()
    e_task.got()
    q_spread.got()
    k_spread.got()
    total = ggot[0]
    for index in range(1, 8):
        total = total + ggot[index]
    gains_out[...] = total
    for job in (g, gjob, n_job, o_job, q_job, k_job, e_job, d_job, gu_task, dn_task):
        job.end()
    for job in (o_sums, q_sums, k_sums, o_spread, q_spread, k_spread, e_task):
        job.end()
    for copy in (*m_first.values(), m_second[1, 0], m_second[1, 1], m_third):
        copy.wait_send()
    m_out.wait()
    tokens_out.wait()
    gu_keep.wait()
    dn_keep.wait()
    for copy in (att_swap, a1_swap, dq_swap, dkv_swap, gain_swap):
        copy.wait_send()

    @pl.loop(0, 8)
    def _(t):
        down_to(t).wait_send()


def layer(x, attn_gain, mlp_gain, deal, freq, q, key, value, wo, gate, up, dn, dy):
    shape = jax.ShapeDtypeStruct
    smem = pl.BlockSpec(memory_space=pltpu.SMEM)
    vmem = pltpu.VMEM
    outs = pl.pallas_call(
        layer_kernel,
        out_shape=(
            shape((128, 2048), BF),
            shape((128, 2048), BF),
            shape((128, 2048), BF),
            shape((128, 512), BF),
            shape((128, 2048), BF),
            shape((16, 128), F32),
            shape((8, 128, 1536), BF),
            shape((352, 2048), BF),
            shape((8, 2, 128, 2048), BF),
            shape((8, 2, 128, 512), BF),
            shape((8, 2, 128, 2048), BF),
            shape((8, 128, 2048), BF),
            shape((2, 2, 64, 2048), BF),
            shape((2, 2, 128, 2048), BF),
            shape((128, 2048), BF),
        ),
        in_specs=[ANY] + [VMEM] * 2 + [smem, VMEM] + [ANY] * 8,
        out_specs=[ANY] * 2 + [VMEM] * 4 + [ANY] * 9,
        scratch_shapes=[
            vmem((128, 2048), BF),
            vmem((16, 16, 128), F32),
            vmem((256, 2048), BF),
            vmem((256, 2048), BF),
            vmem((4, 2, 512, 64), BF),
            vmem((4, 640, 64), BF),
            vmem((4, 640, 64), BF),
            vmem((8, 1, 512), F32),
            vmem((128, 2048), F32),
            vmem((128, 128), F32),
            vmem((128, 128), F32),
            vmem((512, 128), F32),
            vmem((128, 128), F32),
            vmem((8, 2, 128, 2048), BF),
            vmem((8, 2, 128, 512), BF),
            vmem((8, 2, 128, 2048), BF),
            vmem((128, 512), BF),
            vmem((8, 128, 512), BF),
            vmem((640, 512), F32),
            vmem((640, 512), BF),
            vmem((640, 512), F32),
            vmem((640, 512), BF),
            vmem((128, 1), F32),
            vmem((2, 128, 768), BF),
            vmem((352, 256), BF),
            vmem((4, 2, 128, 2048), BF),
            vmem((2048, 1536), BF),
            vmem((768, 2048), BF),
            vmem((8, 128, 2048), BF),
            vmem((1024, 768), BF),
            vmem((8, 128, 1536), BF),
            vmem((8, 352, 256), BF),
            vmem((128, 1536), BF),
            vmem((128, 2048), F32),
            vmem((256, 2048), BF),
            vmem((256, 2560), BF),
            vmem((4, 1, 2048), F32),
            vmem((16, 16, 128), F32),
            vmem((16, 16, 128), F32),
            vmem((352, 256), BF),
            *scatter_buffers(352, 256),
            *scatter_buffers(16, 128, F32),
            vmem((8, 16, 128), F32),
            vmem((8, 16, 128), F32),
            vmem((16, 128), F32),
            vmem((8, 16, 2048), BF),
            vmem((8, 16, 2048), BF),
            vmem((8, 16, 512), BF),
            *dma_sems(8, 9),
            *dma_sems(8, 10),
            *dma_sems(7, 9),
            *dma_sems(2, 10),
            *dma_sems(9, 9),
            *dma_sems(7, 8),
            pltpu.SemaphoreType.DMA((22,)),
            pltpu.SemaphoreType.DMA((22,)),
            pltpu.SemaphoreType.DMA,
            pltpu.SemaphoreType.DMA,
            pltpu.SemaphoreType.DMA,
            pltpu.SemaphoreType.DMA,
            pltpu.SemaphoreType.REGULAR,
            pltpu.SemaphoreType.DMA((64,)),
        ],
        compiler_params=params(1, 63),
        name="layer",
    )(x, attn_gain, mlp_gain, deal, freq, q, key, value, wo, gate, up, dn, dy)
    return outs[:8]


def finish_kernel(
    mixed_in, tokens_in, q_in, kv_in, o_in, gu_in, dn_in, gains,
    mixed, tokens_grad, q_out, key_out, value_out, o_out, gate_out, up_out, dn_out, first_gain, second_gain,
    b_mixed, b_tokens, b_q, b_kv, b_o, b_gu, b_dn, f_q, f_key, f_value, f_o, f_gate, f_up, f_dn, sems,
):
    slots = iter(range(24))

    def move(src, dst):
        return pltpu.make_async_copy(src, dst, sems.at[next(slots)])

    loads = [
        move(src, dst)
        for src, dst in (
            (q_in, b_q), (o_in, b_o), (dn_in, b_dn), (gu_in.at[pl.ds(0, 4)], b_gu.at[pl.ds(0, 4)]),
            (gu_in.at[pl.ds(4, 4)], b_gu.at[pl.ds(4, 4)]), (kv_in, b_kv), (mixed_in, b_mixed), (tokens_in, b_tokens),
        )
    ]
    for copy in loads:
        copy.start()
    stores = []

    def store(src, dst):
        copy = move(src, dst)
        copy.start()
        stores.append(copy)

    def widen(pair):
        first = 1408 * pair

        @pl.loop(0, 8)
        def _(i):
            rows = pl.ds(pl.multiple_of(16 * i, 16), 16)
            for out, base in ((f_gate, 0), (f_up, 768)):
                even = b_gu[2 * pair, rows, base : base + 768].astype(F32)
                odd = pltpu.roll(b_gu[2 * pair + 1, rows, base : base + 768].astype(F32), 64, 1)
                out[rows, first : first + 640] = even[:, 0:640]
                out[rows, first + 640 : first + 768] = even[:, 640:768] + odd[:, 0:128]
                out[rows, first + 768 : first + 1408] = odd[:, 128:768]

    def cast(src, dst, rows):
        @pl.loop(0, rows // 32)
        def _(i):
            at = pl.ds(pl.multiple_of(32 * i, 32), 32)
            dst[at] = src[at].astype(F32)

    for index, src, dst, out, rows in (
        (0, b_q, f_q, q_out, 128), (1, b_o, f_o, o_out, 128), (2, b_dn, f_dn, dn_out, 352)
    ):
        loads[index].wait()
        cast(src, dst, rows)
        store(dst, out)
    for half in (0, 1):
        loads[3 + half].wait()
        for pair in (2 * half, 2 * half + 1):
            widen(pair)
            wide = pl.ds(1408 * pair, 1408)
            store(f_gate.at[:, wide], gate_out.at[:, wide])
            store(f_up.at[:, wide], up_out.at[:, wide])
    first_gain[...] = gains[0:1, :]
    second_gain[...] = gains[8:9, :]
    loads[5].wait()
    f_key[...] = b_kv[:, 0:256].astype(F32)
    f_value[...] = b_kv[:, 256:512].astype(F32)
    store(f_key, key_out)
    store(f_value, value_out)
    loads[6].wait()
    store(b_mixed, mixed)
    loads[7].wait()
    store(b_tokens, tokens_grad)
    for copy in stores:
        copy.wait()


def finish(mixed, tokens_grad, q, kv, o, gu, dn, gains):
    shape, vmem = jax.ShapeDtypeStruct, pltpu.VMEM
    wholes = [(128, 2048), (128, 256), (128, 256), (128, 2048), (128, 5632), (128, 5632), (352, 2048)]
    return pl.pallas_call(
        finish_kernel,
        out_shape=(shape((128, 2048), BF), shape((128, 2048), BF), *[shape(dims, F32) for dims in (*wholes, (1, 128), (1, 128))]),
        in_specs=[ANY] * 7 + [VMEM],
        out_specs=[ANY] * 9 + [VMEM] * 2,
        scratch_shapes=[
            vmem((128, 2048), BF),
            vmem((128, 2048), BF),
            vmem((128, 2048), BF),
            vmem((128, 512), BF),
            vmem((128, 2048), BF),
            vmem((8, 128, 1536), BF),
            vmem((352, 2048), BF),
            *[vmem(dims, F32) for dims in wholes],
            pltpu.SemaphoreType.DMA((24,)),
        ],
        compiler_params=pltpu.CompilerParams(vmem_limit_bytes=62 << 20),
        name="finish",
    )(mixed, tokens_grad, q, kv, o, gu, dn, gains)


def on_device(
    tokens,
    block_deal,
    attn_gain,
    query_weight,
    key_weight,
    value_weight,
    output_weight,
    mlp_gain,
    gate_weight,
    up_weight,
    down_weight,
    cotangent,
):
    freq = BASE ** (-(np.arange(HEAD_DIM // 2, dtype=np.float32) * 2.0) / HEAD_DIM)
    freq = np.concatenate([freq] * 4)[None].astype(np.float32)
    mixed, tokens_grad, query_grad, kv_grad, o_grad, gain_grads, gu_grads, dn_grad = layer(
        tokens[0], attn_gain[None], mlp_gain[None], block_deal, freq, query_weight, key_weight, value_weight, output_weight,
        gate_weight, up_weight, down_weight, cotangent[0],
    )
    mixed, tokens_grad, *grads, first_gain, second_gain = finish(
        mixed, tokens_grad, query_grad, kv_grad, o_grad, gu_grads, dn_grad, gain_grads
    )
    return (mixed[None], tokens_grad[None], first_gain[0], *grads[:4], second_gain[0], *grads[4:])


def solution(mesh):
    held = P("fsdp", "ctx", None)
    rows = P("fsdp", None)
    return jax.shard_map(
        on_device,
        mesh=mesh,
        in_specs=(held, P(), P("fsdp"), rows, rows, rows, rows, P("fsdp"), rows, rows, rows, held),
        out_specs=(held, held, P("fsdp"), rows, rows, rows, rows, P("fsdp"), rows, rows, rows),
        check_vma=False,
    )
```

```python
import functools

import jax
import jax.numpy as jnp
from jax import lax
from jax.experimental import pallas as pl
from jax.experimental.pallas import tpu as pltpu
from jax.sharding import PartitionSpec as P
import numpy as np

MESH = pl.DeviceIdType.MESH
BF = jnp.bfloat16
F32 = jnp.float32
ANY = pl.BlockSpec(memory_space=pl.ANY)
VMEM = pl.BlockSpec(memory_space=pltpu.VMEM)

HEAD_DIM = 64
EPS = 1e-05
SCALE = 0.125
BASE = 10000.0

SLOT = {(0, 0): 0, (0, 1): 1, (1, 0): 2, (3, 0): 3, (1, 1): 4, (3, 1): 5, (2, 0): 6, (2, 1): 7}
STEPS = (0, 0, 1, 3, 1, 3, 2, 2)
PAIRS = (0, 1, 0, 0, 1, 1, 0, 1)


def slot_of(dr, dp):
    return SLOT[(dr % 4, dp % 2)]


class Place:
    def __init__(self):
        self.c = lax.axis_index("ctx")
        self.f = lax.axis_index("fsdp")
        self.y, self.zl = lax.div(self.c, 2), lax.rem(self.c, 2)
        self.j, self.co = lax.div(self.f, 2), lax.rem(self.f, 2)
        self.x, self.zh = lax.div(self.j, 2), lax.rem(self.j, 2)

    def ctx_at(self, dr, dp):
        return lax.rem(self.y + dr % 4, 4) * 2 + lax.rem(self.zl + dp, 2)

    def chip_at(self, dr, dp):
        return lax.rem(self.x + dr % 4, 4) * 2 + lax.rem(self.zh + dp, 2)

    def fsdp_at(self, dr, dp):
        return self.chip_at(dr, dp) * 2 + self.co

    def across_y(self, dr, dp):
        return {"ctx": self.ctx_at(dr, dp), "fsdp": self.f}

    def across_x(self, dr, dp):
        return {"ctx": self.c, "fsdp": self.fsdp_at(dr, dp)}

    def sibling(self):
        return {"ctx": self.c, "fsdp": self.f + 1 - 2 * self.co}


def chip_of(me, t):
    dr = jnp.where(t < 2, 0, jnp.where(t >= 6, 2, 1 + 2 * lax.rem(t, 2)))
    dp = jnp.where(t < 2, t, jnp.where(t >= 6, t - 6, lax.div(t, 4)))
    return lax.rem(me.x + dr, 4) * 2 + lax.rem(me.zh + dp, 2)


def greet(devices):
    barrier = pltpu.get_barrier_semaphore()
    for device in devices:
        pl.semaphore_signal(barrier, 1, device_id=device, device_id_type=MESH)
    pl.semaphore_wait(barrier, len(devices))


class Swap:
    def __init__(self, me, src, dst, sems, local):
        self.moved = me.c != me.j
        self.to = {"ctx": me.j, "fsdp": 2 * me.c + me.co}
        self.copy = pltpu.make_async_remote_copy(
            src, dst, sems[0], sems[1], device_id=self.to, device_id_type=MESH
        )
        self.keep = pltpu.make_async_copy(src, dst, local)

    def start(self):
        pl.when(self.moved)(self.copy.start)
        pl.when(jnp.logical_not(self.moved))(self.keep.start)

    def wait(self):
        pl.when(self.moved)(self.copy.wait)
        pl.when(jnp.logical_not(self.moved))(self.keep.wait)


def greet_all(me, plane=False):
    barrier = pltpu.get_barrier_semaphore()
    others = near(me.across_x) + [me.sibling()]
    others += [me.across_y(STEPS[s], PAIRS[s]) for s in range(1, 8)] if plane else near(me.across_y)
    for device in others:
        pl.semaphore_signal(barrier, 1, device_id=device, device_id_type=MESH)
    moved = me.c != me.j

    @pl.when(moved)
    def _():
        to = {"ctx": me.j, "fsdp": 2 * me.c + me.co}
        pl.semaphore_signal(barrier, 1, device_id=to, device_id_type=MESH)

    pl.semaphore_wait(barrier, len(others) + jnp.where(moved, 1, 0))


def near(dev):
    return [dev(1, 0), dev(-1, 0), dev(0, 1)]


def send(src, dst, sems, index, device):
    return pltpu.make_async_remote_copy(
        src, dst, sems[0].at[index], sems[1].at[index], device_id=device, device_id_type=MESH
    )


class Gather:
    MOVES = (
        ((0, 0), (0, 1), None),
        ((0, 0), (1, 0), None),
        ((0, 0), (-1, 0), None),
        ((0, 1), (1, 0), None),
        ((0, 1), (-1, 0), None),
        ((-1, 0), (1, 0), 0),
        ((-1, 1), (1, 0), 0),
        ((1, 0), (-1, 0), 1),
        ((1, 1), (-1, 0), 1),
    )

    def __init__(self, dev, own, loc, sems, row, sibling=None, sibling_sems=None):
        self.loc = loc
        self.copies = []
        for index, (block, to, half) in enumerate(self.MOVES):
            src = own if block == (0, 0) else loc(*block, 0, 0, half)
            dst = loc(*block, *to, half)
            self.copies.append(send(src, dst, sems, (row, index), dev(*to)))
        self.passed = {}
        if sibling is not None:
            self.passed[9] = send(own, loc(0, 0, 0, 0, None), sibling_sems, (row, 9), sibling)
            for index, ((dr, dp), (er, ep), half) in enumerate(self.MOVES):
                ref = loc(dr - er, dp + ep, 0, 0, half)
                self.passed[index] = send(ref, ref, sibling_sems, (row, index), sibling)
        self.own = own

    def _pass(self, index):
        if self.passed:
            self.passed[index].start()

    def _got(self, index):
        self.copies[index].wait_recv()
        self._pass(index)

    def start(self):
        for index in (0, 1, 2):
            self.copies[index].start()
        self._pass(9)

    def pair(self):
        self._got(0)
        self.copies[3].start()
        self.copies[4].start()

    def turn(self, dp):
        for got, on in (((1, 5), (2, 7)) if dp == 0 else ((3, 6), (4, 8))):
            self._got(got)
            self.copies[on].start()

    def last(self, dp):
        for got in ((5, 7) if dp == 0 else (6, 8)):
            self._got(got)

    def sync(self):
        for copy in self.passed.values():
            copy.wait()

    def end(self):
        for copy in self.copies:
            copy.wait_send()


class RingFirst:
    MOVES = (
        ((0, 0), (0, 1), None),
        ((0, 0), (1, 0), None),
        ((0, 0), (-1, 0), None),
        ((-1, 0), (1, 0), 0),
        ((1, 0), (-1, 0), 1),
        ((-1, 0), (0, 1), None),
        ((1, 0), (0, 1), None),
        ((2, 0), (0, 1), 0),
        ((2, 0), (0, 1), 1),
    )

    def __init__(self, dev, own, loc, sems, row):
        self.own, self.loc = own, loc
        self.copies = []
        for index, (block, to, half) in enumerate(self.MOVES):
            src = own if block == (0, 0) else loc(*block, 0, 0, half)
            self.copies.append(send(src, loc(*block, *to, half), sems, (row, index), dev(*to)))

    def go(self, *indices):
        for index in indices:
            self.copies[index].start()

    def got(self, *indices):
        for index in indices:
            self.copies[index].wait_recv()

    def end(self):
        for copy in self.copies:
            copy.wait_send()


def row_half(half, rows):
    return pl.ds(0, rows) if half is None else pl.ds(half * (rows // 2), rows // 2)


def add_into(ref, rows, others, step=16):
    step = min(step, rows)

    @pl.loop(0, rows // step)
    def _(i):
        at = pl.ds(pl.multiple_of(i * step, step), step)
        total = ref[at].astype(F32)
        for other in others:
            total = total + other[at].astype(F32)
        ref[at] = total.astype(ref.dtype)


class Scatter:
    def __init__(self, dev, part, rows, halves, fulls, paired, sems, row, cut=None):
        self.part, self.rows, self.cut = part, rows, cut
        self.halves, self.fulls, self.paired = halves, fulls, paired
        self.first, self.second = {}, {}
        for dp in (0, 1):
            for way, sign in ((0, 1), (1, -1)):
                self.first[way, dp] = send(
                    self._half(part(slot_of(2, dp)), way), halves.at[way, dp], sems, (row, way * 2 + dp), dev(sign, 0)
                )
                self.second[way, dp] = send(
                    part(slot_of(sign, dp)), fulls.at[way, dp], sems, (row, 4 + way * 2 + dp), dev(sign, 0)
                )
        self.third = send(part(slot_of(0, 1)), paired, sems, (row, 8), dev(0, 1))

    def _half(self, ref, way):
        if self.cut is None:
            return ref.at[pl.ds(way * (self.rows // 2), self.rows // 2)]
        return ref.at[:, pl.ds(way * (self.cut // 2), self.cut // 2)]

    def start(self):
        for dp in (1, 0):
            for way in (0, 1):
                self.first[way, dp].start()

    def turn(self, dp):
        for way, sign in ((0, 1), (1, -1)):
            self.first[way, dp].wait_recv()
            block = self._half(self.part(slot_of(sign, dp)), way)
            add_into(block, block.shape[0], [self.halves.at[way, dp]])
            self.second[way, dp].start()

    def pair(self):
        for way in (0, 1):
            self.second[way, 1].wait_recv()
        add_into(self.part(slot_of(0, 1)), self.rows, [self.fulls.at[0, 1], self.fulls.at[1, 1]])
        self.third.start()

    def finish(self, out, extra=()):
        for way in (0, 1):
            self.second[way, 0].wait_recv()
        self.third.wait_recv()
        own = self.part(0)
        terms = [own, self.fulls.at[0, 0], self.fulls.at[1, 0], self.paired, *extra]

        @pl.loop(0, self.rows // 16)
        def _(i):
            at = pl.ds(pl.multiple_of(i * 16, 16), 16)
            total = terms[0][at].astype(F32)
            for term in terms[1:]:
                total = total + term[at].astype(F32)
            out[at] = total.astype(out.dtype)

    def end(self):
        for copy in (*self.first.values(), *self.second.values(), self.third):
            copy.wait_send()


def mirror(slot):
    return slot_of(-STEPS[slot], PAIRS[slot])


class Trade:
    def __init__(self, dev, what, where, sems, row):
        self.copies = [
            pltpu.make_async_remote_copy(
                what(slot), where(slot), sems[0].at[row, slot], sems[1].at[row, mirror(slot)],
                device_id=dev(STEPS[slot], PAIRS[slot]), device_id_type=MESH,
            )
            for slot in range(1, 8)
        ]

    def start(self):
        for copy in self.copies:
            copy.start()

    def got(self):
        for copy in self.copies:
            copy.wait_recv()

    def end(self):
        for copy in self.copies:
            copy.wait_send()


def scatter_buffers(rows, columns, dtype=BF, cut=False):
    half = (rows, columns // 2) if cut else (rows // 2, columns)
    return [
        pltpu.VMEM((2, 2, *half), dtype),
        pltpu.VMEM((2, 2, rows, columns), dtype),
        pltpu.VMEM((rows, columns), dtype),
    ]


def dma_sems(rows, count):
    return [pltpu.SemaphoreType.DMA((rows, count)), pltpu.SemaphoreType.DMA((rows, count))]


def params(collective_id, vmem=56):
    return pltpu.CompilerParams(
        collective_id=collective_id, has_side_effects=True, vmem_limit_bytes=vmem << 20
    )


def dot_in(left, right):
    return jnp.dot(left, right, preferred_element_type=F32)


def dot_back(left, right):
    return lax.dot_general(left, right, (((1,), (1,)), ((), ())), preferred_element_type=F32)


def dot_rows(left, right):
    return lax.dot_general(left, right, (((0,), (0,)), ((), ())), preferred_element_type=F32)


def load(src, dst, sem):
    copy = pltpu.make_async_copy(src, dst, sem)
    copy.start()
    return copy


def turned(values):
    lane = lax.broadcasted_iota(jnp.int32, values.shape, 1)
    low = lax.rem(lane, 64) < 32
    return jnp.where(low, pltpu.roll(values, 96, 1), pltpu.roll(values, 32, 1))


def pile(out, values, half):
    for h in range(8):
        out[pl.ds(64 * h, 64), :] = values[64 * half : 64 * half + 64, 64 * h : 64 * h + 64]


def unpile(values):
    flat = values.T
    return [
        jnp.concatenate([flat[128 * m : 128 * m + 64], flat[128 * m + 64 : 128 * m + 128]], axis=1)
        for m in range(4)
    ]


def norm_scale(ref, out):
    values = ref[...].astype(F32)
    out[...] = lax.rsqrt(jnp.mean(values * values, axis=1, keepdims=True) + EPS)


def place_tables(me, deal, freq, cosine, sine, bias_p, bias_c):
    def block(slot, part):
        return deal[me.f, me.ctx_at(STEPS[slot], PAIRS[slot]), part]

    first, second = block(0, 0), block(0, 1)
    odd = lax.rem(second, 2)
    row = lax.broadcasted_iota(jnp.int32, (128, 128), 0)
    lane = lax.broadcasted_iota(jnp.int32, (128, 128), 1)
    position = jnp.where(row < 64, first * 64 + row, 448 + odd * 64 + row)
    angle = position.astype(F32) * freq[...]
    cosine[...] = jnp.cos(angle)
    sine[...] = jnp.where(lax.rem(lane, 64) < 32, -jnp.sin(angle), jnp.sin(angle))
    row, lane = row[:64], lax.rem(lane[:64], 64)
    mate = jnp.int32(0)
    for slot in range(8):
        seen = block(slot, 0) * 64 + row <= first * 64 + lane
        bias_p[pl.ds(64 * slot, 64), :] = jnp.where(seen, 0.0, -1e30)
        if slot:
            mate = mate + jnp.where(block(slot, 1) == second + 1 - 2 * odd, slot, 0)
    bias_c[pl.ds(0, 64), :] = jnp.where(odd + 0 * row == 1, 0.0, -1e30)
    bias_c[pl.ds(64, 64), :] = jnp.where(row <= lane, 0.0, -1e30)
    return mate


def layer_kernel(
    x_in, attn_gain, mlp_gain, deal, freq, q_in, key_in, value_in, wo_in, gate_in, up_in, dn_in, dy_in,
    mixed, tokens_grad, q_grad, kv_grad, o_grad, gains_out, gu_all, dn_all,
    q_saved, kw_saved, wo_saved, mpart, m_half, m_full, m_pair,
    x, gains, a1s, atts, qst, kst, vst, lse, h1, cosine, sine, bias_p, bias_c,
    qw, kw, wo, kv_own, kv, sT, pT, dT, dsT, scale, gu_win, dnp, acts, gu, wd, dy, hid,
    grecv, gdrecv, g_pair, da2, datts, dqkvs, grow, gown_rows, gsib_rows, dn_moved,
    n_half, n_full, n_pair, e_half, e_full, e_pair, gp, ggot, g_sum, o_got, q_got, k_got,
    s0, s1, t0, t1, y0, y1, u0, u1, r0, r1, z0, z1, c0, c1, w0, w1, v0, v1, credit, local,
):
    me = Place()
    greet_all(me, plane=True)
    own, other = pl.ds(0, 128), pl.ds(128, 128)
    slots = iter(range(64))

    def load(src, dst):
        copy = pltpu.make_async_copy(src, dst, local.at[next(slots)])
        copy.start()
        return copy

    def later(src, dst):
        return pltpu.make_async_copy(src, dst, local.at[next(slots)])

    def aligned(index, step):
        return index if isinstance(index, int) else pl.multiple_of(index, step)

    def gains_at(dr, dp, er, ep, half):
        return gains.at[me.fsdp_at(dr, dp), row_half(half, 16)]

    def slot_at(ref, rows):
        def loc(dr, dp, er, ep, half):
            return ref.at[slot_of(dr - er, dp + ep), row_half(half, rows)]

        return loc

    def acts_at(dr, dp, er, ep, half):
        slot = slot_of(dr - er, dp + ep)
        return acts.at[slot // 2, slot % 2, row_half(half, 128)]

    def columns(first, index):
        return pl.ds(pl.multiple_of(first + index * 128, 128), 128)

    def plain(ref, count):
        def loc(dr, dp, er, ep, half):
            return ref.at[me.chip_at(dr, dp), me.co, row_half(half, 128), pl.ds(0, count)]

        return loc

    def strip_x(ref, first):
        def loc(dr, dp, er, ep, half):
            return ref.at[me.chip_at(dr, dp), me.co, row_half(half, 128), columns(first, me.c)]

        return loc

    def strip_y(ref, first):
        def loc(dr, dp, er, ep, half):
            chips = pl.ds(0, 8) if half is None else pl.ds(4 * half, 4)
            return ref.at[chips, me.co, :, columns(first, me.ctx_at(dr, dp))]

        return loc

    def wd_at(dr, dp, er, ep, half):
        size = 352 if half is None else 176
        first = me.co * 352 + (0 if half is None else half * size)
        return wd.at[
            pl.ds(pl.multiple_of(first, 16), size),
            pl.ds(pl.multiple_of(me.chip_at(dr, dp) * 256, 256), 256),
        ]

    def gu_at(dr, dp, er, ep, half):
        size = 128 if half is None else 64
        first = me.fsdp_at(dr, dp) * 128 + (0 if half is None else half * size)
        return gu.at[pl.ds(pl.multiple_of(first, size), size)]

    def over_x(own, loc, row, both=True):
        own = loc(0, 0, 0, 0, None) if own is None else own
        return Gather(me.across_x, own, loc, (s0, s1), row, me.sibling() if both else None, (t0, t1))

    def over_y(own, loc, row, both=True):
        own = loc(0, 0, 0, 0, None) if own is None else own
        return Gather(me.across_y, own, loc, (y0, y1), row, me.sibling() if both else None, (u0, u1))

    g = over_x(None, gains_at, 0)
    k = over_x(None, plain(kw, 512), 1)
    q = over_x(q_in.at[:, pl.ds(0, 1024)], plain(qw, 1024), 2)
    qx = over_x(q_in.at[:, columns(1024, me.c)], strip_x(qw, 1024), 3, both=False)
    o = over_x(wo_in.at[:, pl.ds(0, 1024)], plain(wo, 1024), 4)
    ox = over_x(wo_in.at[:, columns(1024, me.c)], strip_x(wo, 1024), 5, both=False)
    m = over_x(None, gu_at, 6)
    dn = over_x(dnp, wd_at, 7)
    qy = over_y(None, strip_y(qw, 1024), 0)
    oy = over_y(None, strip_y(wo, 1024), 1)
    dy_task = over_y(dy_in, slot_at(dy, 128), 2, both=False)
    kv_task = over_y(kv_own, slot_at(kv, 128), 3, both=False)
    a = over_y(None, acts_at, 4, both=False)
    swap = Swap(me, dn_in.at[:, pl.ds(pl.multiple_of(me.c * 256, 256), 256)], dnp, (w0, w1), local.at[next(slots)])

    own_kw = plain(kw, 512)(0, 0, 0, 0, None)
    x_load = load(x_in, x)
    loads = [load(key_in, own_kw.at[:, pl.ds(0, 256)]), load(value_in, own_kw.at[:, pl.ds(256, 256)])]
    kept = {task: load(task.own, task.loc(0, 0, 0, 0, None)) for task in (q, qx, o, ox, dy_task)}
    window = pl.ds(pl.multiple_of(me.y * 1408 + me.zl * 640, 128), 768)
    loads.append(load(gate_in.at[:, window], gu_win.at[0]))
    loads.append(load(up_in.at[:, window], gu_win.at[1]))
    gains[me.f] = jnp.zeros((16, 128), F32)
    gains[me.f, pl.ds(0, 1), :] = attn_gain[...].astype(F32)
    gains[me.f, pl.ds(8, 1), :] = mlp_gain[...].astype(F32)

    dpart = op = wo.at[:, 0]
    qp = wo.at[:, 1]
    dgu = wo.at[:, 1, :, pl.ds(0, 1536)]
    kvp = kv

    def gsib(t):
        return gu.at[pl.ds(aligned(128 * t, 128), 128)]

    def gown(t):
        return gu.at[pl.ds(aligned(1024 + 128 * t, 128), 128)]

    def kp(t):
        return gu.at[pl.ds(aligned(128 * t, 128), 128), pl.ds(0, 512)]

    def gd(t):
        return wd.at[:, pl.ds(aligned(256 * t, 256), 256)]

    def gd_own(t):
        return gd(t).at[pl.ds(pl.multiple_of(me.co * 352, 16), 352)]

    def dost(n, half):
        return grecv.at[pl.ds(0, 4), :, pl.ds(pl.multiple_of(512 + 128 * (2 * n + half), 128), 128)]

    saved = []

    def put_gate_up():
        loads[2].wait()
        loads[3].wait()

        @pl.loop(0, 8)
        def _(i):
            rows = pl.ds(pl.multiple_of(16 * i, 16), 16)
            out = pl.ds(pl.multiple_of(me.f * 128 + 16 * i, 16), 16)
            for w in (0, 1):
                values = gu_win[w, rows].astype(F32)
                values = jnp.where(me.zl == 1, pltpu.roll(values, 704, 1), values)
                lane = lax.broadcasted_iota(jnp.int32, values.shape, 1)
                gu[out, 768 * w : 768 * w + 768] = jnp.where(lane < 704, values, 0.0).astype(BF)

        wd[pl.ds(704, 64)] = jnp.zeros((64, 2048), BF)

    def normed():
        norm_scale(x, scale)

        @pl.loop(0, 16)
        def _(i):
            at = pl.ds(pl.multiple_of(i * 128, 128), 128)
            a1s[own, at] = (x[:, at].astype(F32) * scale[...] * gains[i, pl.ds(0, 1), :]).astype(BF)

    def project_kv():
        raw = dot_in(a1s[own], kw[...].reshape(2048, 512))
        for i in range(2):
            part = raw[:, 128 * i : 128 * i + 128]
            kv_own[:, 128 * i : 128 * i + 128] = (part * cosine[...] + turned(part) * sine[...]).astype(BF)
        kv_own[:, 256:] = raw[:, 256:].astype(BF)
        kv[0] = kv_own[...]

    def project_q():
        @pl.loop(0, 4)
        def _(n):
            raw = dot_in(a1s[own], qw[:, :, :, pl.ds(pl.multiple_of(512 * n, 512), 512)].reshape(2048, 512))
            for i in range(4):
                part = raw[:, 128 * i : 128 * i + 128]
                part = ((part * cosine[...] + turned(part) * sine[...]).astype(BF).astype(F32) * SCALE).astype(BF)
                for half in (0, 1):
                    for e in (0, 1):
                        rows = pl.ds(64 * (2 * i + e), 64)
                        qst[n, half, rows, :] = part[64 * half : 64 * half + 64, 64 * e : 64 * e + 64]

    def collect_kv(mate):
        beside = kv[mate]
        for out, base in ((kst, 0), (vst, 256)):
            for n in range(4):
                first = base + 64 * n
                for slot in range(8):
                    out[n, pl.ds(64 * slot, 64), :] = kv[slot, 0:64, first : first + 64]
                out[n, pl.ds(512, 64), :] = beside[64:128, first : first + 64]
                out[n, pl.ds(576, 64), :] = kv_own[64:128, first : first + 64]

    def attend(n, half):
        count = 512 if half == 0 else 640
        keys = pl.ds(0, count)
        sT[keys] = dot_back(kst[n, keys, :], qst[n, half])
        for i in range(4):
            at = pl.ds(128 * i, 128)
            if half == 0:
                scores = sT[keys, at] + bias_p[...]
                peak = jnp.max(scores, axis=0, keepdims=True)
                raised = jnp.exp(scores - peak)
                total = jnp.sum(raised, axis=0, keepdims=True)
                pT[keys, at] = (raised * (1.0 / total)).astype(BF)
            else:
                first = sT[0:512, at]
                rest = sT[512:640, at] + bias_c[...]
                peak = jnp.maximum(
                    jnp.max(first, axis=0, keepdims=True), jnp.max(rest, axis=0, keepdims=True)
                )
                first = jnp.exp(first - peak)
                rest = jnp.exp(rest - peak)
                total = jnp.sum(first, axis=0, keepdims=True) + jnp.sum(rest, axis=0, keepdims=True)
                pT[0:512, at] = (first * (1.0 / total)).astype(BF)
                pT[512:640, at] = (rest * (1.0 / total)).astype(BF)
            lse[2 * n + half, :, at] = peak + jnp.log(total)
        for i, block in enumerate(unpile(dot_rows(vst[n, keys, :], pT[keys]))):
            first = pl.multiple_of(512 * n + 128 * i, 128)
            atts[pl.ds(64 * half, 64), pl.ds(first, 128)] = block.astype(BF)

    def project_o():
        @pl.loop(0, 4)
        def _(n):
            at = pl.ds(pl.multiple_of(512 * n, 512), 512)
            h1[:, at] = x[:, at].astype(F32) + dot_in(atts[own], wo[:, :, :, at].reshape(2048, 512))

    def normed_two():
        norm_scale(h1, scale)

        @pl.loop(0, 16)
        def _(i):
            at = pl.ds(pl.multiple_of(i * 128, 128), 128)
            acts[0, 0, :, at] = (h1[:, at] * scale[...] * gains[i, pl.ds(8, 1), :]).astype(BF)

    def mpart_copy(n):
        return [
            pltpu.make_async_copy(
                kv.at[pl.ds(2 * i, 2)], mpart.at[pl.ds(2 * n, 2), :, pl.ds(512 * i, 512)], local.at[60 + i]
            )
            for i in range(4)
        ]

    def group(n):
        at = pl.ds(2 * n, 2)
        rows = pl.ds(pl.multiple_of(256 * n, 256), 256)
        for h in range(3):
            first, second = pl.ds(256 * h, 256), pl.ds(768 + 256 * h, 256)
            here = acts[n].reshape(256, 2048)
            gate = dot_in(here, gu[:, first])
            up = dot_in(here, gu[:, second])
            back = dot_back(dy[at].reshape(256, 2048), wd[first, :])
            curve = 1.0 / (1.0 + jnp.exp(-gate))
            silu = gate * curve
            hid[rows, first] = (silu * up).astype(BF)
            dgu[at, :, first] = (back * up * (curve + silu * (1.0 - curve))).astype(BF).reshape(2, 128, 256)
            dgu[at, :, second] = (back * silu).astype(BF).reshape(2, 128, 256)

        @pl.when(n > 0)
        def _():
            for copy in mpart_copy(n - 1):
                copy.wait()

        for i in range(4):
            wide = pl.ds(512 * i, 512)
            grads = dgu[at].reshape(256, 1536)
            dpart[at, :, wide] = dot_back(grads, gu[wide, :]).astype(BF).reshape(2, 128, 512)
            kv[pl.ds(2 * i, 2)] = dot_in(hid[rows, :], wd[:, wide]).astype(BF).reshape(2, 128, 512)
        for copy in mpart_copy(n):
            copy.start()

    def group_half(slot):
        rows = pl.ds(128 * slot, 128)
        here = acts[slot // 2, slot % 2]
        for h in range(3):
            first, second = pl.ds(256 * h, 256), pl.ds(768 + 256 * h, 256)
            gate = dot_in(here, gu[:, first])
            up = dot_in(here, gu[:, second])
            back = dot_back(dy[slot], wd[first, :])
            curve = 1.0 / (1.0 + jnp.exp(-gate))
            silu = gate * curve
            hid[rows, first] = (silu * up).astype(BF)
            dgu[slot, :, first] = (back * up * (curve + silu * (1.0 - curve))).astype(BF)
            dgu[slot, :, second] = (back * silu).astype(BF)
        for i in range(4):
            wide = pl.ds(512 * i, 512)
            dpart[slot, :, wide] = dot_back(dgu[slot], gu[wide, :]).astype(BF)

    def group_out():
        for copy in mpart_copy(2):
            copy.wait()
        for i in range(4):
            wide = pl.ds(512 * i, 512)
            kv[pl.ds(2 * i, 2)] = dot_in(hid[pl.ds(768, 256), :], wd[:, wide]).astype(BF).reshape(2, 128, 512)
        for copy in mpart_copy(3):
            copy.start()

    class Views:
        def __init__(self, pick):
            self.pick = pick

        @property
        def at(self):
            return self

        def __getitem__(self, index):
            return self.pick(index)

    def scatter(dev, part, place, columns, row, pair=None):
        wide = pl.ds(0, columns)
        halves = Views(lambda index: place.at[4 + index[0], pl.ds(64 * index[1], 64), wide])
        fulls = Views(lambda index: place.at[2 * index[0] + index[1], :, wide])
        paired = place.at[6, :, wide] if pair is None else pair
        return Scatter(dev, part, 128, halves, fulls, paired, (r0, r1), row)

    first_bay, second_bay = qw.at[:, 0], qw.at[:, 1]
    d = scatter(me.across_y, lambda slot: dpart.at[slot], second_bay, 2048, 0)
    gjob = scatter(me.across_x, gown, first_bay, 1536, 1, g_pair)
    n_job = Scatter(me.across_x, gd_own, 352, n_half, n_full, n_pair, (r0, r1), 2)
    o_job = scatter(me.across_x, lambda slot: op.at[slot], second_bay, 2048, 3)
    q_job = scatter(me.across_x, lambda slot: qp.at[slot], first_bay, 2048, 4)
    k_job = scatter(me.across_x, kp, kw.at[:, 0], 512, 5)
    e_job = Scatter(me.across_x, lambda slot: gp.at[slot], 16, e_half, e_full, e_pair, (r0, r1), 6)
    d_job = scatter(me.across_y, lambda slot: kvp.at[slot], kw.at[:, 1], 512, 7)

    def weight_terms(t, core):
        at = pl.multiple_of((chip_of(me, t) * 2 + core) * 128, 128)
        left = acts[:, :, :, pl.ds(at, 128)].reshape(1024, 128)
        return dot_rows(left, dgu[...].reshape(1024, 1536))

    def gu_to(t):
        return send(gsib(t), grecv.at[t], (c0, c1), 8 + t, me.sibling())

    def down_to(t):
        mine = pl.ds(pl.multiple_of((1 - me.co) * 352, 16), 352)
        return send(gd(t).at[mine], gdrecv.at[t], (c0, c1), t, me.sibling())

    def terms_for_sibling(start):
        @pl.loop(start, start + 2)
        def _(i):
            gsib(7 - i)[...] = weight_terms(7 - i, 1 - me.co).astype(BF)
            gu_to(7 - i).start()

    def sibling_has_terms():
        @pl.loop(0, 8)
        def _(t):
            gu_to(t).wait_send()

    def own_terms(start):
        @pl.loop(start, start + 2)
        def _(i):
            gu_to(7 - i).wait_recv()
            gown(7 - i)[...] = (weight_terms(7 - i, me.co) + grecv[7 - i].astype(F32)).astype(BF)

    def down_terms():
        @pl.loop(0, 8)
        def _(t):
            at = pl.multiple_of(chip_of(me, t) * 256, 256)
            gd(t)[...] = dot_rows(hid[...], dy[:, :, pl.ds(at, 256)].reshape(1024, 256)).astype(BF)
            down_to(t).start()

    def down_sums():
        @pl.loop(0, 8)
        def _(t):
            down_to(t).wait_recv()

            @pl.loop(0, 22)
            def _(i):
                at = pl.ds(pl.multiple_of(i * 16, 16), 16)
                mine = gd(t).at[pl.ds(pl.multiple_of(me.co * 352 + i * 16, 16), 16)]
                mine[...] = (mine[...].astype(F32) + gdrecv[t, at].astype(F32)).astype(BF)

    m_first, m_second = {}, {}
    for dp in (0, 1):
        for way, sign in ((0, 1), (1, -1)):
            m_first[way, dp] = send(
                mpart.at[slot_of(2, dp), pl.ds(64 * way, 64)], m_half.at[way, dp], (r0, r1), (8, way * 2 + dp),
                me.across_y(sign, 0),
            )
            m_second[way, dp] = send(
                dy.at[1 + 2 * way + dp], m_full.at[way, dp], (r0, r1), (8, 4 + way * 2 + dp), me.across_y(sign, 0)
            )
    m_third = send(dy.at[5], m_pair, (r0, r1), (8, 8), me.across_y(0, 1))

    def m_start():
        dy_task.end()
        for copy in mpart_copy(3):
            copy.wait()
        for dp in (1, 0):
            for way in (0, 1):
                m_first[way, dp].start()

    m_parts = {(way, dp): later(mpart.at[slot_of(1 - 2 * way, dp)], dy.at[1 + 2 * way + dp]) for way in (0, 1) for dp in (0, 1)}
    m_halves = {(way, dp): later(m_half.at[way, dp], dy.at[6 + way, pl.ds(0, 64)]) for way in (0, 1) for dp in (0, 1)}
    m_fulls = {(way, dp): later(m_full.at[way, dp], dy.at[6 + way]) for way in (0, 1) for dp in (0, 1)}
    m_mine, m_near, m_last = later(mpart.at[0], dy.at[1]), later(mpart.at[1], dy.at[5]), later(m_pair, dy.at[2])
    m_out = later(dy.at[1], mixed)

    def m_turn(dp):
        for way in (0, 1):
            m_parts[way, dp].start()
        for way in (0, 1):
            m_first[way, dp].wait_recv()
            m_halves[way, dp].start()
        for way in (0, 1):
            m_parts[way, dp].wait()
            m_halves[way, dp].wait()
            add_into(dy.at[1 + 2 * way + dp, pl.ds(64 * way, 64)], 64, [dy.at[6 + way, pl.ds(0, 64)]])
            m_second[way, dp].start()

    def m_pair_up():
        m_near.start()
        for way in (0, 1):
            m_second[way, 1].wait_recv()
            m_fulls[way, 1].start()
        m_near.wait()
        for way in (0, 1):
            m_fulls[way, 1].wait()
        add_into(dy.at[5], 128, [dy.at[6], dy.at[7]])
        m_third.start()

    def m_finish():
        for dp in (0, 1):
            m_second[0, dp].wait_send()
        m_mine.start()
        for way in (0, 1):
            m_second[way, 0].wait_recv()
            m_fulls[way, 0].start()
        m_third.wait_recv()
        m_last.start()
        m_mine.wait()
        for way in (0, 1):
            m_fulls[way, 0].wait()
        m_last.wait()

        @pl.loop(0, 8)
        def _(i):
            at = pl.ds(pl.multiple_of(i * 16, 16), 16)
            total = h1[at]
            for slot in (1, 2, 6, 7):
                total = total + dy[slot, at].astype(F32)
            dy[1, at] = total.astype(BF)

        m_out.start()

    def wo_load(n):
        return pltpu.make_async_copy(
            wo_saved.at[pl.ds(2 * n, 2)], acts.at[pl.ds(2 * (n % 2), 2)], local.at[56 + n % 2]
        )

    def q_load(n):
        return pltpu.make_async_copy(q_saved.at[pl.ds(2 * n, 2)], acts.at[pl.ds(2 * (n % 2), 2)], local.at[58 + n % 2])

    def kw_load():
        return [
            load(kw_saved.at[chip], grecv.at[pl.ds(2 * (chip % 4), 2), :, pl.ds(512 * (chip // 4), 512)])
            for chip in range(8)
        ]

    def at_ctx(ref):
        def loc(dr, dp, er, ep, half):
            return ref.at[me.ctx_at(dr, dp), row_half(half, ref.shape[1])]

        return loc

    def dn_at(dr, dp, er, ep, half):
        first = pl.multiple_of(me.ctx_at(dr, dp) * 256, 256)
        return dn_all.at[row_half(half, 352), pl.ds(first, 256)]

    gu_task = over_y(gown(0), at_ctx(gu_all), 5, both=False)
    dn_task = over_y(dn_moved, dn_at, 6, both=False)
    dn_swap = Swap(me, gd_own(0), dn_moved, (v0, v1), local.at[next(slots)])
    gu_keep = later(gown(0), gu_all.at[me.c])
    dn_keep = later(dn_moved, dn_at(0, 0, 0, 0, None))
    dn_local = later(dnp, wd_at(0, 0, 0, 0, None))
    tokens_out = later(datts.at[own], tokens_grad)

    def block_at(ref, slot):
        first = pl.multiple_of(me.ctx_at(STEPS[slot], PAIRS[slot]) * 16, 16)
        return ref.at[pl.ds(first, 16)]

    def sum_over_ctx(total, got, row):
        return Trade(
            me.across_y, lambda slot: block_at(total, slot), lambda slot: got.at[mirror(slot)], (z0, z1), row
        )

    def spread(out, row):
        return Trade(me.across_y, lambda slot: block_at(out, 0), lambda slot: block_at(out, 0), (z0, z1), row)

    def sum_up(total, got, out):
        value = block_at(total, 0)[...].astype(F32)
        for slot in range(1, 8):
            value = value + got[slot].astype(F32)
        block_at(out, 0)[...] = value.astype(BF)

    o_sum, q_sum, kv_sum = op.at[0], qp.at[0], kp(0)
    o_sums = sum_over_ctx(o_sum, o_got, 0)
    q_sums = sum_over_ctx(q_sum, q_got, 1)
    k_sums = sum_over_ctx(kv_sum, k_got, 2)
    o_spread = spread(o_grad, 3)
    q_spread = spread(q_grad, 4)
    k_spread = spread(kv_grad, 5)
    e_task = Trade(me.across_y, lambda slot: g_sum, lambda slot: ggot.at[me.c], (z0, z1), 6)

    def to_sibling(src, dst, index):
        return send(src, dst, (c0, c1), 16 + index, me.sibling())

    att_swap = to_sibling(atts.at[own], atts.at[other], 0)
    datt_swap = to_sibling(datts.at[own], datts.at[other], 1)
    a1_swap = to_sibling(a1s.at[own], a1s.at[other], 2)
    queries, rest = pl.ds(0, 2048), pl.ds(2048, 512)
    dq_swap = to_sibling(dqkvs.at[own, queries], dqkvs.at[other, queries], 3)
    dkv_swap = to_sibling(dqkvs.at[own, rest], dqkvs.at[other, rest], 4)
    gain_swap = to_sibling(gown_rows, gsib_rows, 5)

    def norm_two_back():
        for i in range(16):
            grow[0, :, 128 * i : 128 * i + 128] = gains[i, 0:1, :]
            grow[1, :, 128 * i : 128 * i + 128] = gains[i, 8:9, :]
        grow[2] = jnp.zeros((1, 2048), F32)
        grow[3] = jnp.zeros((1, 2048), F32)

        @pl.loop(0, 8)
        def _(i):
            at = pl.ds(pl.multiple_of(16 * i, 16), 16)
            values, grad = h1[at], da2[at]
            scale = lax.rsqrt(jnp.mean(values * values, axis=1, keepdims=True) + EPS)
            grow[3] += jnp.sum(grad * values * scale, axis=0, keepdims=True)
            grad = grad * grow[1]
            level = jnp.mean(grad * values, axis=1, keepdims=True) * scale * scale * scale
            total = dy[0, at].astype(F32) + scale * grad - values * level
            da2[at] = total
            datts[at] = total.astype(BF)

        datt_swap.start()

    def heads_back():
        for n in range(4):
            wo_load(n).wait()
            part = dot_back(datts[own], acts[2 * (n % 2) : 2 * (n % 2) + 2].reshape(512, 2048)).astype(BF)
            for half in (0, 1):
                place = dost(n, half)
                for h in range(8):
                    place[h // 2, pl.ds(64 * (h % 2), 64), pl.ds(0, 64)] = part[
                        64 * half : 64 * half + 64, 64 * h : 64 * h + 64
                    ]
            if n < 2:
                wo_load(n + 2).start()
        for n in range(2):
            q_load(n).start()

    def terms(left, right, out, job):
        @pl.loop(0, 8)
        def _(i):
            at = pl.multiple_of((chip_of(me, 7 - i) * 2 + me.co) * 128, 128)
            out(7 - i)[...] = dot_rows(left[:, pl.ds(at, 128)], right[...]).astype(BF)

            @pl.when(i == 1)
            def _():
                job.start()

    def output_terms():
        att_swap.wait_recv()
        datt_swap.wait_recv()
        pl.semaphore_wait(credit, 3)
        terms(atts, datts, lambda t: op.at[t], o_job)

    def query_terms():
        a1_swap.wait_recv()
        dq_swap.wait_recv()
        terms(a1s, dqkvs.at[:, pl.ds(0, 2048)], lambda t: qp.at[t], q_job)

    def kv_terms():
        dkv_swap.wait_recv()
        terms(a1s, dqkvs.at[:, pl.ds(2048, 512)], kp, k_job)

    def kv_blocks(mate):
        for part, base in ((0, 0), (64, 256)):
            for n in range(4):
                first = base + 64 * n
                block = grecv[0:5, :, 128 * n : 128 * n + 128].reshape(640, 128)[:, part : part + 64]
                for slot in range(8):
                    kvp[slot, 0:64, first : first + 64] = block[64 * slot : 64 * slot + 64]
                    if slot == 0:
                        late = block[576:640]
                    else:
                        late = jnp.where(mate == slot, block[512:576], jnp.zeros((64, 64), BF))
                    kvp[slot, 64:128, first : first + 64] = late

    def kv_back():
        for i in range(2):
            at = slice(128 * i, 128 * i + 128)
            block = sT[512:640, at]
            dqkvs[own, 2048 + 128 * i : 2176 + 128 * i] = (block * cosine[...] - turned(block) * sine[...]).astype(BF)
        dqkvs[own, 2304:2560] = sT[512:640, 256:512].astype(BF)
        dkv_swap.start()

    def inputs_back():
        for copy in kw_back:
            copy.wait()
        for n in range(4):
            q_load(n).wait()
            block = dot_back(dqkvs[own, queries], acts[2 * (n % 2) : 2 * (n % 2) + 2].reshape(512, 2048))
            four, wide = pl.ds(4 * (n % 2), 4), pl.ds(512 * (n // 2), 512)
            block = block + dot_back(dqkvs[own, rest], grecv[four, :, wide].reshape(512, 512))
            sT[pl.ds(128 * n, 128)] = block
            if n < 2:
                q_load(n + 2).start()

    def norm_one_back():
        datt_swap.wait_send()

        @pl.loop(0, 8)
        def _(i):
            at = pl.ds(pl.multiple_of(16 * i, 16), 16)
            values = x[at].astype(F32)
            grad = jnp.concatenate([sT[pl.ds(pl.multiple_of(128 * n + 16 * i, 16), 16)] for n in range(4)], axis=1)
            scale = lax.rsqrt(jnp.mean(values * values, axis=1, keepdims=True) + EPS)
            grow[2] += jnp.sum(grad * values * scale, axis=0, keepdims=True)
            grad = grad * grow[0]
            level = jnp.mean(grad * values, axis=1, keepdims=True) * scale * scale * scale
            datts[at] = (da2[at] + scale * grad - values * level).astype(BF)

        tokens_out.start()

        gown_rows[...] = jnp.zeros((16, 16, 128), F32)
        for i in range(16):
            gown_rows[i, 0:1, :] = grow[2, :, 128 * i : 128 * i + 128]
            gown_rows[i, 8:9, :] = grow[3, :, 128 * i : 128 * i + 128]
        gain_swap.start()

    def gain_terms():
        gain_swap.wait_recv()
        for slot in range(8):
            block = me.fsdp_at(STEPS[slot], PAIRS[slot])
            gp[slot] = gown_rows[block] + gsib_rows[block]

    def dn_begin():
        dn_swap.wait()
        dn_task.start()
        dn_keep.start()

    def gu_begin():
        gu_keep.start()
        gu_task.start()

    def e_begin():
        e_task.start()
        ggot[me.c] = g_sum[...]

    def attend_back(n, half):
        count = 512 if half == 0 else 640
        keys = pl.ds(0, count)
        key, query, out = kst[n, keys, :], qst[n, half], dost(n, half)[...].reshape(512, 128)[:, 0:64]
        sT[keys] = dot_back(key, query)
        dT[keys] = dot_back(vst[n, keys, :], out)
        for i in range(4):
            at = pl.ds(128 * i, 128)
            parts = []
            for first, size in ((0, 512), (512, 128))[: 1 + half]:
                scores = sT[first : first + size, at]
                if half == 0:
                    scores = scores + bias_p[...]
                elif first:
                    scores = scores + bias_c[...]
                probs = jnp.exp(scores - lse[2 * n + half, :, at])
                grad = dT[first : first + size, at]
                parts.append((first, size, probs, grad))
            level = sum(jnp.sum(probs * grad, axis=0, keepdims=True) for _, _, probs, grad in parts)
            for first, size, probs, grad in parts:
                pT[first : first + size, at] = probs.astype(BF)
                dsT[first : first + size, at] = (probs * (grad - level)).astype(BF)
        rows = slice(64 * half, 64 * half + 64)
        for i, block in enumerate(unpile(dot_rows(key, dsT[keys]) * SCALE)):
            block = block * cosine[rows] - turned(block) * sine[rows]
            first = pl.multiple_of(512 * n + 128 * i, 128)
            dqkvs[rows, pl.ds(first, 128)] = block.astype(BF)
        return dot_in(dsT[keys], query), dot_in(pT[keys], out)

    def keep_kv_grads(n, one, two):
        keys = jnp.concatenate([one[0] + two[0][0:512], two[0][512:640]], axis=0)
        values = jnp.concatenate([one[1] + two[1][0:512], two[1][512:640]], axis=0)
        both = jnp.concatenate([keys, values], axis=1).astype(BF)
        grecv[pl.ds(0, 5), :, pl.ds(pl.multiple_of(128 * n, 128), 128)] = both.reshape(5, 128, 128)

    qx.start()
    dy_task.start()
    g.start()
    loads[0].wait()
    loads[1].wait()
    k.start()
    g.turn(0)
    qx.turn(0)
    qx.pair()
    ox.start()
    qx.last(0)
    qx.turn(1)
    o.start()
    swap.start()
    qx.last(1)
    kept[qx].wait()
    qy.start()
    mate = place_tables(me, deal, freq, cosine, sine, bias_p, bias_c)
    q.start()
    g.pair()
    dy_task.pair()
    k.pair()
    qy.turn(0)
    g.turn(1)
    g.last(0)
    k.turn(0)
    ox.turn(0)
    k.turn(1)
    q.turn(0)
    ox.pair()
    g.last(1)
    k.last(0)
    qy.pair()
    k.last(1)
    o.pair()
    ox.turn(1)
    g.sync()
    k.sync()
    x_load.wait()
    normed()
    project_kv()
    qy.last(0)
    ox.last(0)
    kv_task.start()
    q.pair()
    ox.last(1)
    qy.turn(1)
    swap.wait()
    dn_local.start()
    dn.start()
    kv_task.pair()
    kept[ox].wait()
    oy.start()
    kv_task.turn(0)
    q.turn(1)
    o.turn(0)
    qy.last(1)
    kv_task.turn(1)
    o.turn(1)
    put_gate_up()
    qy.sync()
    m.start()
    q.last(1)
    q.last(0)
    oy.pair()
    q.sync()
    oy.turn(0)
    kv_task.last(0)
    kept[q].wait()
    saved.append(load(qw, q_saved))
    saved.append(load(kw, kw_saved))
    project_q()
    kv_task.last(1)
    collect_kv(mate)
    a1_swap.start()
    o.last(1)

    @pl.loop(0, 4)
    def _(n):
        attend(n, 0)
        attend(n, 1)

        @pl.when(n == 0)
        def _():
            oy.turn(1)
            dn.turn(0)
            dn.pair()
            o.last(0)

        @pl.when(n == 1)
        def _():
            dy_task.turn(0)
            oy.last(0)

        @pl.when(n == 2)
        def _():
            dy_task.turn(1)
            oy.last(1)
            m.pair()

    o.sync()
    oy.sync()
    kept[o].wait()
    saved.append(load(wo, wo_saved))
    project_o()
    normed_two()
    for task in (k, q, qx, qy):
        task.end()
    saved[0].wait()
    saved[1].wait()
    a.start()
    m.turn(0)
    dn.last(0)
    m.turn(1)
    dn.turn(1)
    m.last(1)
    m.last(0)
    a.pair()
    dn.last(1)
    m.sync()
    att_swap.start()
    dy_task.last(1)
    dy_task.last(0)
    dn.sync()

    for task in (o, ox, oy, kv_task):
        task.end()
    saved[2].wait()
    dn_local.wait()
    kept[dy_task].wait()

    @pl.loop(0, 3)
    def _(n):
        group(n)

        @pl.when(n == 0)
        def _():
            a.turn(0)

        @pl.when(n == 1)
        def _():
            a.turn(1)

    a.last(0)
    group_half(6)
    a.last(1)
    group_half(7)
    d.start()
    m.end()
    terms_for_sibling(0)
    terms_for_sibling(2)
    own_terms(0)
    gjob.start()
    terms_for_sibling(4)
    terms_for_sibling(6)
    d.turn(1)
    own_terms(2)
    own_terms(4)
    group_out()
    gjob.turn(1)
    dn.end()
    down_terms()
    down_sums()
    n_job.start()
    d.turn(0)
    d.pair()
    n_job.turn(1)
    gjob.turn(0)
    n_job.turn(0)
    m_start()
    own_terms(6)
    a.end()
    wo_load(0).start()
    wo_load(1).start()
    n_job.pair()
    d.finish(da2)
    norm_two_back()
    for device in near(me.across_x):
        pl.semaphore_signal(credit, 1, device_id=device, device_id_type=MESH)
    gjob.pair()
    m_turn(1)
    d.end()
    output_terms()
    heads_back()
    gjob.finish(gown(0))
    gu_begin()

    @pl.loop(0, 4)
    def _(n):
        one, two = attend_back(n, 0), attend_back(n, 1)
        keep_kv_grads(n, one, two)

        @pl.when(n == 0)
        def _():
            o_job.turn(1)
            m_pair_up()

        @pl.when(n == 2)
        def _():
            gu_task.pair()
            o_job.turn(0)

    kv_blocks(mate)
    kw_back = kw_load()
    dq_swap.start()
    d_job.start()
    n_job.finish(gd_own(0))
    dn_swap.start()
    o_job.pair()
    query_terms()
    gu_task.turn(0)
    d_job.turn(1)
    d_job.turn(0)
    gu_task.last(0)
    gu_task.turn(1)
    d_job.pair()
    o_job.finish(o_sum)
    o_sums.start()
    q_job.turn(1)
    d_job.finish(sT.at[pl.ds(512, 128)])
    kv_back()
    m_turn(0)
    dn_begin()
    inputs_back()
    o_sums.got()
    sum_up(o_sum, o_got, o_grad)
    sibling_has_terms()
    kv_terms()
    o_spread.start()
    q_job.pair()
    dn_task.pair()
    gu_task.last(1)
    k_job.turn(1)
    q_job.turn(0)
    m_finish()
    norm_one_back()
    gain_terms()
    dn_task.turn(0)
    k_job.turn(0)
    k_job.pair()
    e_job.start()
    dn_task.turn(1)
    q_job.finish(q_sum)
    q_sums.start()
    e_job.turn(0)
    e_job.turn(1)
    k_job.finish(kv_sum)
    e_job.pair()
    k_sums.start()
    dn_task.last(0)
    q_sums.got()
    sum_up(q_sum, q_got, q_grad)
    q_spread.start()
    e_job.finish(g_sum)
    e_begin()
    k_sums.got()
    sum_up(kv_sum, k_got, kv_grad)
    k_spread.start()
    o_spread.got()
    q_spread.got()
    e_task.got()
    dn_task.last(1)
    k_spread.got()
    total = ggot[0]
    for index in range(1, 8):
        total = total + ggot[index]
    gains_out[...] = total
    for job in (g, gjob, n_job, o_job, q_job, k_job, e_job, d_job, gu_task, dn_task):
        job.end()
    for job in (o_sums, q_sums, k_sums, o_spread, q_spread, k_spread, e_task):
        job.end()
    for copy in (*m_first.values(), m_second[1, 0], m_second[1, 1], m_third):
        copy.wait_send()
    m_out.wait()
    tokens_out.wait()
    gu_keep.wait()
    dn_keep.wait()
    for copy in (att_swap, a1_swap, dq_swap, dkv_swap, gain_swap):
        copy.wait_send()

    @pl.loop(0, 8)
    def _(t):
        down_to(t).wait_send()


def layer(x, attn_gain, mlp_gain, deal, freq, q, key, value, wo, gate, up, dn, dy):
    shape = jax.ShapeDtypeStruct
    smem = pl.BlockSpec(memory_space=pltpu.SMEM)
    vmem = pltpu.VMEM
    outs = pl.pallas_call(
        layer_kernel,
        out_shape=(
            shape((128, 2048), BF),
            shape((128, 2048), BF),
            shape((128, 2048), BF),
            shape((128, 512), BF),
            shape((128, 2048), BF),
            shape((16, 128), F32),
            shape((8, 128, 1536), BF),
            shape((352, 2048), BF),
            shape((8, 2, 128, 2048), BF),
            shape((8, 2, 128, 512), BF),
            shape((8, 2, 128, 2048), BF),
            shape((8, 128, 2048), BF),
            shape((2, 2, 64, 2048), BF),
            shape((2, 2, 128, 2048), BF),
            shape((128, 2048), BF),
        ),
        in_specs=[ANY] + [VMEM] * 2 + [smem, VMEM] + [ANY] * 8,
        out_specs=[ANY] * 2 + [VMEM] * 4 + [ANY] * 9,
        scratch_shapes=[
            vmem((128, 2048), BF),
            vmem((16, 16, 128), F32),
            vmem((256, 2048), BF),
            vmem((256, 2048), BF),
            vmem((4, 2, 512, 64), BF),
            vmem((4, 640, 64), BF),
            vmem((4, 640, 64), BF),
            vmem((8, 1, 512), F32),
            vmem((128, 2048), F32),
            vmem((128, 128), F32),
            vmem((128, 128), F32),
            vmem((512, 128), F32),
            vmem((128, 128), F32),
            vmem((8, 2, 128, 2048), BF),
            vmem((8, 2, 128, 512), BF),
            vmem((8, 2, 128, 2048), BF),
            vmem((128, 512), BF),
            vmem((8, 128, 512), BF),
            vmem((640, 512), F32),
            vmem((640, 512), BF),
            vmem((640, 512), F32),
            vmem((640, 512), BF),
            vmem((128, 1), F32),
            vmem((2, 128, 768), BF),
            vmem((352, 256), BF),
            vmem((4, 2, 128, 2048), BF),
            vmem((2048, 1536), BF),
            vmem((768, 2048), BF),
            vmem((8, 128, 2048), BF),
            vmem((1024, 768), BF),
            vmem((8, 128, 1536), BF),
            vmem((8, 352, 256), BF),
            vmem((128, 1536), BF),
            vmem((128, 2048), F32),
            vmem((256, 2048), BF),
            vmem((256, 2560), BF),
            vmem((4, 1, 2048), F32),
            vmem((16, 16, 128), F32),
            vmem((16, 16, 128), F32),
            vmem((352, 256), BF),
            *scatter_buffers(352, 256),
            *scatter_buffers(16, 128, F32),
            vmem((8, 16, 128), F32),
            vmem((8, 16, 128), F32),
            vmem((16, 128), F32),
            vmem((8, 16, 2048), BF),
            vmem((8, 16, 2048), BF),
            vmem((8, 16, 512), BF),
            *dma_sems(8, 9),
            *dma_sems(8, 10),
            *dma_sems(7, 9),
            *dma_sems(2, 10),
            *dma_sems(9, 9),
            *dma_sems(7, 8),
            pltpu.SemaphoreType.DMA((22,)),
            pltpu.SemaphoreType.DMA((22,)),
            pltpu.SemaphoreType.DMA,
            pltpu.SemaphoreType.DMA,
            pltpu.SemaphoreType.DMA,
            pltpu.SemaphoreType.DMA,
            pltpu.SemaphoreType.REGULAR,
            pltpu.SemaphoreType.DMA((64,)),
        ],
        compiler_params=params(1, 63),
        name="layer",
    )(x, attn_gain, mlp_gain, deal, freq, q, key, value, wo, gate, up, dn, dy)
    return outs[:8]


def finish_kernel(
    mixed_in, tokens_in, q_in, kv_in, o_in, gu_in, dn_in, gains,
    mixed, tokens_grad, q_out, key_out, value_out, o_out, gate_out, up_out, dn_out, first_gain, second_gain,
    b_mixed, b_tokens, b_q, b_kv, b_o, b_gu, b_dn, f_q, f_key, f_value, f_o, f_gate, f_up, f_dn, sems,
):
    slots = iter(range(24))

    def move(src, dst):
        return pltpu.make_async_copy(src, dst, sems.at[next(slots)])

    loads = [
        move(src, dst)
        for src, dst in (
            (q_in, b_q), (o_in, b_o), (dn_in, b_dn), (gu_in.at[pl.ds(0, 4)], b_gu.at[pl.ds(0, 4)]),
            (gu_in.at[pl.ds(4, 4)], b_gu.at[pl.ds(4, 4)]), (kv_in, b_kv), (mixed_in, b_mixed), (tokens_in, b_tokens),
        )
    ]
    for copy in loads:
        copy.start()
    stores = []

    def store(src, dst):
        copy = move(src, dst)
        copy.start()
        stores.append(copy)

    def widen(pair):
        first = 1408 * pair

        @pl.loop(0, 8)
        def _(i):
            rows = pl.ds(pl.multiple_of(16 * i, 16), 16)
            for out, base in ((f_gate, 0), (f_up, 768)):
                even = b_gu[2 * pair, rows, base : base + 768].astype(F32)
                odd = pltpu.roll(b_gu[2 * pair + 1, rows, base : base + 768].astype(F32), 64, 1)
                out[rows, first : first + 640] = even[:, 0:640]
                out[rows, first + 640 : first + 768] = even[:, 640:768] + odd[:, 0:128]
                out[rows, first + 768 : first + 1408] = odd[:, 128:768]

    def cast(src, dst, rows):
        @pl.loop(0, rows // 32)
        def _(i):
            at = pl.ds(pl.multiple_of(32 * i, 32), 32)
            dst[at] = src[at].astype(F32)

    for index, src, dst, out, rows in (
        (0, b_q, f_q, q_out, 128), (1, b_o, f_o, o_out, 128), (2, b_dn, f_dn, dn_out, 352)
    ):
        loads[index].wait()
        cast(src, dst, rows)
        store(dst, out)
    for half in (0, 1):
        loads[3 + half].wait()
        for pair in (2 * half, 2 * half + 1):
            widen(pair)
            wide = pl.ds(1408 * pair, 1408)
            store(f_gate.at[:, wide], gate_out.at[:, wide])
            store(f_up.at[:, wide], up_out.at[:, wide])
    first_gain[...] = gains[0:1, :]
    second_gain[...] = gains[8:9, :]
    loads[5].wait()
    f_key[...] = b_kv[:, 0:256].astype(F32)
    f_value[...] = b_kv[:, 256:512].astype(F32)
    store(f_key, key_out)
    store(f_value, value_out)
    loads[6].wait()
    store(b_mixed, mixed)
    loads[7].wait()
    store(b_tokens, tokens_grad)
    for copy in stores:
        copy.wait()


def finish(mixed, tokens_grad, q, kv, o, gu, dn, gains):
    shape, vmem = jax.ShapeDtypeStruct, pltpu.VMEM
    wholes = [(128, 2048), (128, 256), (128, 256), (128, 2048), (128, 5632), (128, 5632), (352, 2048)]
    return pl.pallas_call(
        finish_kernel,
        out_shape=(shape((128, 2048), BF), shape((128, 2048), BF), *[shape(dims, F32) for dims in (*wholes, (1, 128), (1, 128))]),
        in_specs=[ANY] * 7 + [VMEM],
        out_specs=[ANY] * 9 + [VMEM] * 2,
        scratch_shapes=[
            vmem((128, 2048), BF),
            vmem((128, 2048), BF),
            vmem((128, 2048), BF),
            vmem((128, 512), BF),
            vmem((128, 2048), BF),
            vmem((8, 128, 1536), BF),
            vmem((352, 2048), BF),
            *[vmem(dims, F32) for dims in wholes],
            pltpu.SemaphoreType.DMA((24,)),
        ],
        compiler_params=pltpu.CompilerParams(vmem_limit_bytes=62 << 20),
        name="finish",
    )(mixed, tokens_grad, q, kv, o, gu, dn, gains)


def on_device(
    tokens,
    block_deal,
    attn_gain,
    query_weight,
    key_weight,
    value_weight,
    output_weight,
    mlp_gain,
    gate_weight,
    up_weight,
    down_weight,
    cotangent,
):
    freq = BASE ** (-(np.arange(HEAD_DIM // 2, dtype=np.float32) * 2.0) / HEAD_DIM)
    freq = np.concatenate([freq] * 4)[None].astype(np.float32)
    mixed, tokens_grad, query_grad, kv_grad, o_grad, gain_grads, gu_grads, dn_grad = layer(
        tokens[0], attn_gain[None], mlp_gain[None], block_deal, freq, query_weight, key_weight, value_weight, output_weight,
        gate_weight, up_weight, down_weight, cotangent[0],
    )
    mixed, tokens_grad, *grads, first_gain, second_gain = finish(
        mixed, tokens_grad, query_grad, kv_grad, o_grad, gu_grads, dn_grad, gain_grads
    )
    return (mixed[None], tokens_grad[None], first_gain[0], *grads[:4], second_gain[0], *grads[4:])


def solution(mesh):
    held = P("fsdp", "ctx", None)
    rows = P("fsdp", None)
    return jax.shard_map(
        on_device,
        mesh=mesh,
        in_specs=(held, P(), P("fsdp"), rows, rows, rows, rows, P("fsdp"), rows, rows, rows, held),
        out_specs=(held, held, P("fsdp"), rows, rows, rows, rows, P("fsdp"), rows, rows, rows),
        check_vma=False,
    )
```

```python
import functools

import jax
import jax.numpy as jnp
from jax import lax
from jax.experimental import pallas as pl
from jax.experimental.pallas import tpu as pltpu
from jax.sharding import PartitionSpec as P
import numpy as np

MESH = pl.DeviceIdType.MESH
BF = jnp.bfloat16
F32 = jnp.float32
ANY = pl.BlockSpec(memory_space=pl.ANY)
VMEM = pl.BlockSpec(memory_space=pltpu.VMEM)

HEAD_DIM = 64
EPS = 1e-05
SCALE = 0.125
BASE = 10000.0

SLOT = {(0, 0): 0, (0, 1): 1, (1, 0): 2, (3, 0): 3, (1, 1): 4, (3, 1): 5, (2, 0): 6, (2, 1): 7}
STEPS = (0, 0, 1, 3, 1, 3, 2, 2)
PAIRS = (0, 1, 0, 0, 1, 1, 0, 1)


def slot_of(dr, dp):
    return SLOT[(dr % 4, dp % 2)]


class Place:
    def __init__(self):
        self.c = lax.axis_index("ctx")
        self.f = lax.axis_index("fsdp")
        self.y, self.zl = lax.div(self.c, 2), lax.rem(self.c, 2)
        self.j, self.co = lax.div(self.f, 2), lax.rem(self.f, 2)
        self.x, self.zh = lax.div(self.j, 2), lax.rem(self.j, 2)

    def ctx_at(self, dr, dp):
        return lax.rem(self.y + dr % 4, 4) * 2 + lax.rem(self.zl + dp, 2)

    def chip_at(self, dr, dp):
        return lax.rem(self.x + dr % 4, 4) * 2 + lax.rem(self.zh + dp, 2)

    def fsdp_at(self, dr, dp):
        return self.chip_at(dr, dp) * 2 + self.co

    def across_y(self, dr, dp):
        return {"ctx": self.ctx_at(dr, dp), "fsdp": self.f}

    def across_x(self, dr, dp):
        return {"ctx": self.c, "fsdp": self.fsdp_at(dr, dp)}

    def sibling(self):
        return {"ctx": self.c, "fsdp": self.f + 1 - 2 * self.co}


def chip_of(me, t):
    dr = jnp.where(t < 2, 0, jnp.where(t >= 6, 2, 1 + 2 * lax.rem(t, 2)))
    dp = jnp.where(t < 2, t, jnp.where(t >= 6, t - 6, lax.div(t, 4)))
    return lax.rem(me.x + dr, 4) * 2 + lax.rem(me.zh + dp, 2)


def greet(devices):
    barrier = pltpu.get_barrier_semaphore()
    for device in devices:
        pl.semaphore_signal(barrier, 1, device_id=device, device_id_type=MESH)
    pl.semaphore_wait(barrier, len(devices))


class Swap:
    def __init__(self, me, src, dst, sems, local):
        self.moved = me.c != me.j
        self.to = {"ctx": me.j, "fsdp": 2 * me.c + me.co}
        self.copy = pltpu.make_async_remote_copy(
            src, dst, sems[0], sems[1], device_id=self.to, device_id_type=MESH
        )
        self.keep = pltpu.make_async_copy(src, dst, local)

    def start(self):
        pl.when(self.moved)(self.copy.start)
        pl.when(jnp.logical_not(self.moved))(self.keep.start)

    def wait(self):
        pl.when(self.moved)(self.copy.wait)
        pl.when(jnp.logical_not(self.moved))(self.keep.wait)


def greet_all(me, plane=False):
    barrier = pltpu.get_barrier_semaphore()
    others = near(me.across_x) + [me.sibling()]
    others += [me.across_y(STEPS[s], PAIRS[s]) for s in range(1, 8)] if plane else near(me.across_y)
    for device in others:
        pl.semaphore_signal(barrier, 1, device_id=device, device_id_type=MESH)
    moved = me.c != me.j

    @pl.when(moved)
    def _():
        to = {"ctx": me.j, "fsdp": 2 * me.c + me.co}
        pl.semaphore_signal(barrier, 1, device_id=to, device_id_type=MESH)

    pl.semaphore_wait(barrier, len(others) + jnp.where(moved, 1, 0))


def near(dev):
    return [dev(1, 0), dev(-1, 0), dev(0, 1)]


def send(src, dst, sems, index, device):
    return pltpu.make_async_remote_copy(
        src, dst, sems[0].at[index], sems[1].at[index], device_id=device, device_id_type=MESH
    )


class Gather:
    MOVES = (
        ((0, 0), (0, 1), None),
        ((0, 0), (1, 0), None),
        ((0, 0), (-1, 0), None),
        ((0, 1), (1, 0), None),
        ((0, 1), (-1, 0), None),
        ((-1, 0), (1, 0), 0),
        ((-1, 1), (1, 0), 0),
        ((1, 0), (-1, 0), 1),
        ((1, 1), (-1, 0), 1),
    )

    def __init__(self, dev, own, loc, sems, row, sibling=None, sibling_sems=None):
        self.loc = loc
        self.copies = []
        for index, (block, to, half) in enumerate(self.MOVES):
            src = own if block == (0, 0) else loc(*block, 0, 0, half)
            dst = loc(*block, *to, half)
            self.copies.append(send(src, dst, sems, (row, index), dev(*to)))
        self.passed = {}
        if sibling is not None:
            self.passed[9] = send(own, loc(0, 0, 0, 0, None), sibling_sems, (row, 9), sibling)
            for index, ((dr, dp), (er, ep), half) in enumerate(self.MOVES):
                ref = loc(dr - er, dp + ep, 0, 0, half)
                self.passed[index] = send(ref, ref, sibling_sems, (row, index), sibling)
        self.own = own

    def _pass(self, index):
        if self.passed:
            self.passed[index].start()

    def _got(self, index):
        self.copies[index].wait_recv()
        self._pass(index)

    def start(self):
        for index in (0, 1, 2):
            self.copies[index].start()
        self._pass(9)

    def pair(self):
        self._got(0)
        self.copies[3].start()
        self.copies[4].start()

    def turn(self, dp):
        for got, on in (((1, 5), (2, 7)) if dp == 0 else ((3, 6), (4, 8))):
            self._got(got)
            self.copies[on].start()

    def last(self, dp):
        for got in ((5, 7) if dp == 0 else (6, 8)):
            self._got(got)

    def sync(self):
        for copy in self.passed.values():
            copy.wait()

    def end(self):
        for copy in self.copies:
            copy.wait_send()


class RingFirst:
    MOVES = (
        ((0, 0), (0, 1), None),
        ((0, 0), (1, 0), None),
        ((0, 0), (-1, 0), None),
        ((-1, 0), (1, 0), 0),
        ((1, 0), (-1, 0), 1),
        ((-1, 0), (0, 1), None),
        ((1, 0), (0, 1), None),
        ((2, 0), (0, 1), 0),
        ((2, 0), (0, 1), 1),
    )

    def __init__(self, dev, own, loc, sems, row):
        self.own, self.loc = own, loc
        self.copies = []
        for index, (block, to, half) in enumerate(self.MOVES):
            src = own if block == (0, 0) else loc(*block, 0, 0, half)
            self.copies.append(send(src, loc(*block, *to, half), sems, (row, index), dev(*to)))

    def go(self, *indices):
        for index in indices:
            self.copies[index].start()

    def got(self, *indices):
        for index in indices:
            self.copies[index].wait_recv()

    def end(self):
        for copy in self.copies:
            copy.wait_send()


def row_half(half, rows):
    return pl.ds(0, rows) if half is None else pl.ds(half * (rows // 2), rows // 2)


def add_into(ref, rows, others, step=16):
    step = min(step, rows)

    @pl.loop(0, rows // step)
    def _(i):
        at = pl.ds(pl.multiple_of(i * step, step), step)
        total = ref[at].astype(F32)
        for other in others:
            total = total + other[at].astype(F32)
        ref[at] = total.astype(ref.dtype)


class Scatter:
    def __init__(self, dev, part, rows, halves, fulls, paired, sems, row, cut=None):
        self.part, self.rows, self.cut = part, rows, cut
        self.halves, self.fulls, self.paired = halves, fulls, paired
        self.first, self.second = {}, {}
        for dp in (0, 1):
            for way, sign in ((0, 1), (1, -1)):
                self.first[way, dp] = send(
                    self._half(part(slot_of(2, dp)), way), halves.at[way, dp], sems, (row, way * 2 + dp), dev(sign, 0)
                )
                self.second[way, dp] = send(
                    part(slot_of(sign, dp)), fulls.at[way, dp], sems, (row, 4 + way * 2 + dp), dev(sign, 0)
                )
        self.third = send(part(slot_of(0, 1)), paired, sems, (row, 8), dev(0, 1))

    def _half(self, ref, way):
        if self.cut is None:
            return ref.at[pl.ds(way * (self.rows // 2), self.rows // 2)]
        return ref.at[:, pl.ds(way * (self.cut // 2), self.cut // 2)]

    def start(self):
        for dp in (1, 0):
            for way in (0, 1):
                self.first[way, dp].start()

    def turn(self, dp):
        for way, sign in ((0, 1), (1, -1)):
            self.first[way, dp].wait_recv()
            block = self._half(self.part(slot_of(sign, dp)), way)
            add_into(block, block.shape[0], [self.halves.at[way, dp]])
            self.second[way, dp].start()

    def pair(self):
        for way in (0, 1):
            self.second[way, 1].wait_recv()
        add_into(self.part(slot_of(0, 1)), self.rows, [self.fulls.at[0, 1], self.fulls.at[1, 1]])
        self.third.start()

    def finish(self, out, extra=()):
        for way in (0, 1):
            self.second[way, 0].wait_recv()
        self.third.wait_recv()
        own = self.part(0)
        terms = [own, self.fulls.at[0, 0], self.fulls.at[1, 0], self.paired, *extra]

        @pl.loop(0, self.rows // 16)
        def _(i):
            at = pl.ds(pl.multiple_of(i * 16, 16), 16)
            total = terms[0][at].astype(F32)
            for term in terms[1:]:
                total = total + term[at].astype(F32)
            out[at] = total.astype(out.dtype)

    def end(self):
        for copy in (*self.first.values(), *self.second.values(), self.third):
            copy.wait_send()


def mirror(slot):
    return slot_of(-STEPS[slot], PAIRS[slot])


class Trade:
    def __init__(self, dev, what, where, sems, row):
        self.copies = [
            pltpu.make_async_remote_copy(
                what(slot), where(slot), sems[0].at[row, slot], sems[1].at[row, mirror(slot)],
                device_id=dev(STEPS[slot], PAIRS[slot]), device_id_type=MESH,
            )
            for slot in range(1, 8)
        ]

    def start(self):
        for copy in self.copies:
            copy.start()

    def got(self):
        for copy in self.copies:
            copy.wait_recv()

    def end(self):
        for copy in self.copies:
            copy.wait_send()


def scatter_buffers(rows, columns, dtype=BF, cut=False):
    half = (rows, columns // 2) if cut else (rows // 2, columns)
    return [
        pltpu.VMEM((2, 2, *half), dtype),
        pltpu.VMEM((2, 2, rows, columns), dtype),
        pltpu.VMEM((rows, columns), dtype),
    ]


def dma_sems(rows, count):
    return [pltpu.SemaphoreType.DMA((rows, count)), pltpu.SemaphoreType.DMA((rows, count))]


def params(collective_id, vmem=56):
    return pltpu.CompilerParams(
        collective_id=collective_id, has_side_effects=True, vmem_limit_bytes=vmem << 20
    )


def dot_in(left, right):
    return jnp.dot(left, right, preferred_element_type=F32)


def dot_back(left, right):
    return lax.dot_general(left, right, (((1,), (1,)), ((), ())), preferred_element_type=F32)


def dot_rows(left, right):
    return lax.dot_general(left, right, (((0,), (0,)), ((), ())), preferred_element_type=F32)


def load(src, dst, sem):
    copy = pltpu.make_async_copy(src, dst, sem)
    copy.start()
    return copy


def turned(values):
    lane = lax.broadcasted_iota(jnp.int32, values.shape, 1)
    low = lax.rem(lane, 64) < 32
    return jnp.where(low, pltpu.roll(values, 96, 1), pltpu.roll(values, 32, 1))


def pile(out, values, half):
    for h in range(8):
        out[pl.ds(64 * h, 64), :] = values[64 * half : 64 * half + 64, 64 * h : 64 * h + 64]


def unpile(values):
    flat = values.T
    return [
        jnp.concatenate([flat[128 * m : 128 * m + 64], flat[128 * m + 64 : 128 * m + 128]], axis=1)
        for m in range(4)
    ]


def norm_scale(ref, out):
    values = ref[...].astype(F32)
    out[...] = lax.rsqrt(jnp.mean(values * values, axis=1, keepdims=True) + EPS)


def place_tables(me, deal, freq, cosine, sine, bias_p, bias_c):
    def block(slot, part):
        return deal[me.ctx_at(STEPS[slot], PAIRS[slot]), part, me.f]

    first, second = block(0, 0), block(0, 1)
    odd = lax.rem(second, 2)
    row = lax.broadcasted_iota(jnp.int32, (128, 128), 0)
    lane = lax.broadcasted_iota(jnp.int32, (128, 128), 1)
    position = jnp.where(row < 64, first * 64 + row, 448 + odd * 64 + row)
    angle = position.astype(F32) * freq[...]
    cosine[...] = jnp.cos(angle)
    sine[...] = jnp.where(lax.rem(lane, 64) < 32, -jnp.sin(angle), jnp.sin(angle))
    row, lane = row[:64], lax.rem(lane[:64], 64)
    mate = jnp.int32(0)
    for slot in range(8):
        seen = block(slot, 0) * 64 + row <= first * 64 + lane
        bias_p[pl.ds(64 * slot, 64), :] = jnp.where(seen, 0.0, -1e30)
        if slot:
            mate = mate + jnp.where(block(slot, 1) == second + 1 - 2 * odd, slot, 0)
    bias_c[pl.ds(0, 64), :] = jnp.where(odd + 0 * row == 1, 0.0, -1e30)
    bias_c[pl.ds(64, 64), :] = jnp.where(row <= lane, 0.0, -1e30)
    return mate


def layer_kernel(
    x_in, attn_gain, mlp_gain, deal, freq, q_in, key_in, value_in, wo_in, gate_in, up_in, dn_in, dy_in,
    mixed, tokens_grad, q_grad, kv_grad, o_grad, gains_out, gu_all, dn_all,
    q_saved, kw_saved, wo_saved, mpart, m_half, m_full, m_pair,
    x, gains, a1s, atts, qst, kst, vst, lse, h1, cosine, sine, bias_p, bias_c,
    qw, kw, wo, kv_own, kv, sT, pT, dT, dsT, scale, gu_win, dnp, acts, gu, wd, dy, hid,
    grecv, gdrecv, g_pair, da2, datts, dqkvs, grow, gown_rows, gsib_rows, dn_moved,
    n_half, n_full, n_pair, e_half, e_full, e_pair, gp, ggot, g_sum, o_got, q_got, k_got,
    s0, s1, t0, t1, y0, y1, u0, u1, r0, r1, z0, z1, c0, c1, w0, w1, v0, v1, credit, local,
):
    me = Place()
    greet_all(me, plane=True)
    own, other = pl.ds(0, 128), pl.ds(128, 128)
    slots = iter(range(64))

    def load(src, dst):
        copy = pltpu.make_async_copy(src, dst, local.at[next(slots)])
        copy.start()
        return copy

    def later(src, dst):
        return pltpu.make_async_copy(src, dst, local.at[next(slots)])

    def aligned(index, step):
        return index if isinstance(index, int) else pl.multiple_of(index, step)

    def gains_at(dr, dp, er, ep, half):
        return gains.at[me.fsdp_at(dr, dp), row_half(half, 16)]

    def slot_at(ref, rows):
        def loc(dr, dp, er, ep, half):
            return ref.at[slot_of(dr - er, dp + ep), row_half(half, rows)]

        return loc

    def acts_at(dr, dp, er, ep, half):
        slot = slot_of(dr - er, dp + ep)
        return acts.at[slot // 2, slot % 2, row_half(half, 128)]

    def columns(first, index):
        return pl.ds(pl.multiple_of(first + index * 128, 128), 128)

    def plain(ref, count):
        def loc(dr, dp, er, ep, half):
            return ref.at[me.chip_at(dr, dp), me.co, row_half(half, 128), pl.ds(0, count)]

        return loc

    def strip_x(ref, first):
        def loc(dr, dp, er, ep, half):
            return ref.at[me.chip_at(dr, dp), me.co, row_half(half, 128), columns(first, me.c)]

        return loc

    def strip_y(ref, first):
        def loc(dr, dp, er, ep, half):
            chips = pl.ds(0, 8) if half is None else pl.ds(4 * half, 4)
            return ref.at[chips, me.co, :, columns(first, me.ctx_at(dr, dp))]

        return loc

    def wd_at(dr, dp, er, ep, half):
        size = 352 if half is None else 176
        first = me.co * 352 + (0 if half is None else half * size)
        return wd.at[
            pl.ds(pl.multiple_of(first, 16), size),
            pl.ds(pl.multiple_of(me.chip_at(dr, dp) * 256, 256), 256),
        ]

    def gu_at(dr, dp, er, ep, half):
        size = 128 if half is None else 64
        first = me.fsdp_at(dr, dp) * 128 + (0 if half is None else half * size)
        return gu.at[pl.ds(pl.multiple_of(first, size), size)]

    def over_x(own, loc, row, both=True):
        own = loc(0, 0, 0, 0, None) if own is None else own
        return Gather(me.across_x, own, loc, (s0, s1), row, me.sibling() if both else None, (t0, t1))

    def over_y(own, loc, row, both=True):
        own = loc(0, 0, 0, 0, None) if own is None else own
        return Gather(me.across_y, own, loc, (y0, y1), row, me.sibling() if both else None, (u0, u1))

    g = over_x(None, gains_at, 0)
    k = over_x(None, plain(kw, 512), 1)
    q = over_x(q_in.at[:, pl.ds(0, 1024)], plain(qw, 1024), 2)
    qx = over_x(q_in.at[:, columns(1024, me.c)], strip_x(qw, 1024), 3, both=False)
    o = over_x(wo_in.at[:, pl.ds(0, 1024)], plain(wo, 1024), 4)
    ox = over_x(wo_in.at[:, columns(1024, me.c)], strip_x(wo, 1024), 5, both=False)
    m = over_x(None, gu_at, 6)
    dn = over_x(dnp, wd_at, 7)
    qy = over_y(None, strip_y(qw, 1024), 0)
    oy = over_y(None, strip_y(wo, 1024), 1)
    dy_task = over_y(dy_in, slot_at(dy, 128), 2, both=False)
    kv_task = over_y(kv_own, slot_at(kv, 128), 3, both=False)
    a = over_y(None, acts_at, 4, both=False)
    swap = Swap(me, dn_in.at[:, pl.ds(pl.multiple_of(me.c * 256, 256), 256)], dnp, (w0, w1), local.at[next(slots)])

    own_kw = plain(kw, 512)(0, 0, 0, 0, None)
    x_load = load(x_in, x)
    loads = [load(key_in, own_kw.at[:, pl.ds(0, 256)]), load(value_in, own_kw.at[:, pl.ds(256, 256)])]
    kept = {task: load(task.own, task.loc(0, 0, 0, 0, None)) for task in (q, qx, o, ox, dy_task)}
    window = pl.ds(pl.multiple_of(me.y * 1408 + me.zl * 640, 128), 768)
    loads.append(load(gate_in.at[:, window], gu_win.at[0]))
    loads.append(load(up_in.at[:, window], gu_win.at[1]))
    gains[me.f] = jnp.zeros((16, 128), F32)
    gains[me.f, pl.ds(0, 1), :] = attn_gain[...].astype(F32)
    gains[me.f, pl.ds(8, 1), :] = mlp_gain[...].astype(F32)

    dpart = op = wo.at[:, 0]
    qp = wo.at[:, 1]
    dgu = wo.at[:, 1, :, pl.ds(0, 1536)]
    kvp = kv
    packed = gu.at[pl.ds(1024, 128), pl.ds(0, 1408)]

    def gsib(t):
        return gu.at[pl.ds(aligned(128 * t, 128), 128)]

    def gown(t):
        return gu.at[pl.ds(aligned(1024 + 128 * t, 128), 128)]

    def kp(t):
        return gu.at[pl.ds(aligned(128 * t, 128), 128), pl.ds(0, 512)]

    def gd(t):
        return wd.at[:, pl.ds(aligned(256 * t, 256), 256)]

    def gd_own(t):
        return gd(t).at[pl.ds(pl.multiple_of(me.co * 352, 16), 352)]

    def dost(n, half):
        return grecv.at[pl.ds(0, 4), :, pl.ds(pl.multiple_of(512 + 128 * (2 * n + half), 128), 128)]

    saved = []

    def put_gate_up():
        loads[2].wait()
        loads[3].wait()

        @pl.loop(0, 8)
        def _(i):
            rows = pl.ds(pl.multiple_of(16 * i, 16), 16)
            out = pl.ds(pl.multiple_of(me.f * 128 + 16 * i, 16), 16)
            for w in (0, 1):
                values = gu_win[w, rows].astype(F32)
                values = jnp.where(me.zl == 1, pltpu.roll(values, 704, 1), values)
                lane = lax.broadcasted_iota(jnp.int32, values.shape, 1)
                gu[out, 768 * w : 768 * w + 768] = jnp.where(lane < 704, values, 0.0).astype(BF)

        wd[pl.ds(704, 64)] = jnp.zeros((64, 2048), BF)

    def normed():
        norm_scale(x, scale)

        @pl.loop(0, 16)
        def _(i):
            at = pl.ds(pl.multiple_of(i * 128, 128), 128)
            a1s[own, at] = (x[:, at].astype(F32) * scale[...] * gains[i, pl.ds(0, 1), :]).astype(BF)

    def project_kv():
        raw = dot_in(a1s[own], kw[...].reshape(2048, 512))
        for i in range(2):
            part = raw[:, 128 * i : 128 * i + 128]
            kv_own[:, 128 * i : 128 * i + 128] = (part * cosine[...] + turned(part) * sine[...]).astype(BF)
        kv_own[:, 256:] = raw[:, 256:].astype(BF)
        kv[0] = kv_own[...]

    def project_q():
        @pl.loop(0, 4)
        def _(n):
            raw = dot_in(a1s[own], qw[:, :, :, pl.ds(pl.multiple_of(512 * n, 512), 512)].reshape(2048, 512))
            for i in range(4):
                part = raw[:, 128 * i : 128 * i + 128]
                part = ((part * cosine[...] + turned(part) * sine[...]).astype(BF).astype(F32) * SCALE).astype(BF)
                for half in (0, 1):
                    for e in (0, 1):
                        rows = pl.ds(64 * (2 * i + e), 64)
                        qst[n, half, rows, :] = part[64 * half : 64 * half + 64, 64 * e : 64 * e + 64]

    def collect_kv(mate):
        beside = kv[mate]
        for out, base in ((kst, 0), (vst, 256)):
            for n in range(4):
                first = base + 64 * n
                for slot in range(8):
                    out[n, pl.ds(64 * slot, 64), :] = kv[slot, 0:64, first : first + 64]
                out[n, pl.ds(512, 64), :] = beside[64:128, first : first + 64]
                out[n, pl.ds(576, 64), :] = kv_own[64:128, first : first + 64]

    def attend(n, half):
        count = 512 if half == 0 else 640
        keys = pl.ds(0, count)
        sT[keys] = dot_back(kst[n, keys, :], qst[n, half])
        for i in range(4):
            at = pl.ds(128 * i, 128)
            if half == 0:
                scores = sT[keys, at] + bias_p[...]
                peak = jnp.max(scores, axis=0, keepdims=True)
                raised = jnp.exp(scores - peak)
                total = jnp.sum(raised, axis=0, keepdims=True)
                pT[keys, at] = (raised * (1.0 / total)).astype(BF)
            else:
                first = sT[0:512, at]
                rest = sT[512:640, at] + bias_c[...]
                peak = jnp.maximum(
                    jnp.max(first, axis=0, keepdims=True), jnp.max(rest, axis=0, keepdims=True)
                )
                first = jnp.exp(first - peak)
                rest = jnp.exp(rest - peak)
                total = jnp.sum(first, axis=0, keepdims=True) + jnp.sum(rest, axis=0, keepdims=True)
                pT[0:512, at] = (first * (1.0 / total)).astype(BF)
                pT[512:640, at] = (rest * (1.0 / total)).astype(BF)
            lse[2 * n + half, :, at] = peak + jnp.log(total)
        for i, block in enumerate(unpile(dot_rows(vst[n, keys, :], pT[keys]))):
            first = pl.multiple_of(512 * n + 128 * i, 128)
            atts[pl.ds(64 * half, 64), pl.ds(first, 128)] = block.astype(BF)

    def project_o():
        @pl.loop(0, 4)
        def _(n):
            at = pl.ds(pl.multiple_of(512 * n, 512), 512)
            h1[:, at] = x[:, at].astype(F32) + dot_in(atts[own], wo[:, :, :, at].reshape(2048, 512))

    def normed_two():
        norm_scale(h1, scale)

        @pl.loop(0, 16)
        def _(i):
            at = pl.ds(pl.multiple_of(i * 128, 128), 128)
            acts[0, 0, :, at] = (h1[:, at] * scale[...] * gains[i, pl.ds(8, 1), :]).astype(BF)

    def mpart_copy(n):
        return [
            pltpu.make_async_copy(
                kv.at[pl.ds(2 * i, 2)], mpart.at[pl.ds(2 * n, 2), :, pl.ds(512 * i, 512)], local.at[60 + i]
            )
            for i in range(4)
        ]

    def group(n):
        at = pl.ds(2 * n, 2)
        rows = pl.ds(pl.multiple_of(256 * n, 256), 256)
        for h in range(3):
            first, second = pl.ds(256 * h, 256), pl.ds(768 + 256 * h, 256)
            here = acts[n].reshape(256, 2048)
            gate = dot_in(here, gu[:, first])
            up = dot_in(here, gu[:, second])
            back = dot_back(dy[at].reshape(256, 2048), wd[first, :])
            curve = 1.0 / (1.0 + jnp.exp(-gate))
            silu = gate * curve
            hid[rows, first] = (silu * up).astype(BF)
            dgu[at, :, first] = (back * up * (curve + silu * (1.0 - curve))).astype(BF).reshape(2, 128, 256)
            dgu[at, :, second] = (back * silu).astype(BF).reshape(2, 128, 256)

        @pl.when(n > 0)
        def _():
            for copy in mpart_copy(n - 1):
                copy.wait()

        for i in range(4):
            wide = pl.ds(512 * i, 512)
            grads = dgu[at].reshape(256, 1536)
            dpart[at, :, wide] = dot_back(grads, gu[wide, :]).astype(BF).reshape(2, 128, 512)
            kv[pl.ds(2 * i, 2)] = dot_in(hid[rows, :], wd[:, wide]).astype(BF).reshape(2, 128, 512)
        for copy in mpart_copy(n):
            copy.start()

    def group_half(slot):
        rows = pl.ds(128 * slot, 128)
        here = acts[slot // 2, slot % 2]
        for h in range(3):
            first, second = pl.ds(256 * h, 256), pl.ds(768 + 256 * h, 256)
            gate = dot_in(here, gu[:, first])
            up = dot_in(here, gu[:, second])
            back = dot_back(dy[slot], wd[first, :])
            curve = 1.0 / (1.0 + jnp.exp(-gate))
            silu = gate * curve
            hid[rows, first] = (silu * up).astype(BF)
            dgu[slot, :, first] = (back * up * (curve + silu * (1.0 - curve))).astype(BF)
            dgu[slot, :, second] = (back * silu).astype(BF)
        for i in range(4):
            wide = pl.ds(512 * i, 512)
            dpart[slot, :, wide] = dot_back(dgu[slot], gu[wide, :]).astype(BF)

    def group_out():
        for copy in mpart_copy(2):
            copy.wait()
        for i in range(4):
            wide = pl.ds(512 * i, 512)
            kv[pl.ds(2 * i, 2)] = dot_in(hid[pl.ds(768, 256), :], wd[:, wide]).astype(BF).reshape(2, 128, 512)
        for copy in mpart_copy(3):
            copy.start()

    class Views:
        def __init__(self, pick):
            self.pick = pick

        @property
        def at(self):
            return self

        def __getitem__(self, index):
            return self.pick(index)

    def scatter(dev, part, place, columns, row, pair=None):
        wide = pl.ds(0, columns)
        halves = Views(lambda index: place.at[4 + index[0], pl.ds(64 * index[1], 64), wide])
        fulls = Views(lambda index: place.at[2 * index[0] + index[1], :, wide])
        paired = place.at[6, :, wide] if pair is None else pair
        return Scatter(dev, part, 128, halves, fulls, paired, (r0, r1), row)

    first_bay, second_bay = qw.at[:, 0], qw.at[:, 1]
    d = scatter(me.across_y, lambda slot: dpart.at[slot], second_bay, 2048, 0)
    gjob = scatter(me.across_x, gown, first_bay, 1536, 1, g_pair)
    n_job = Scatter(me.across_x, gd_own, 352, n_half, n_full, n_pair, (r0, r1), 2)
    o_job = scatter(me.across_x, lambda slot: op.at[slot], second_bay, 2048, 3)
    q_job = scatter(me.across_x, lambda slot: qp.at[slot], first_bay, 2048, 4)
    k_job = scatter(me.across_x, kp, kw.at[:, 0], 512, 5)
    e_job = Scatter(me.across_x, lambda slot: gp.at[slot], 16, e_half, e_full, e_pair, (r0, r1), 6)
    d_job = scatter(me.across_y, lambda slot: kvp.at[slot], kw.at[:, 1], 512, 7)

    def weight_terms(t, core):
        at = pl.multiple_of((chip_of(me, t) * 2 + core) * 128, 128)
        left = acts[:, :, :, pl.ds(at, 128)].reshape(1024, 128)
        return dot_rows(left, dgu[...].reshape(1024, 1536))

    def gu_to(t):
        return send(gsib(t), grecv.at[t], (c0, c1), 8 + t, me.sibling())

    def down_to(t):
        mine = pl.ds(pl.multiple_of((1 - me.co) * 352, 16), 352)
        return send(gd(t).at[mine], gdrecv.at[t], (c0, c1), t, me.sibling())

    def terms_for_sibling(start):
        @pl.loop(start, start + 2)
        def _(i):
            gsib(7 - i)[...] = weight_terms(7 - i, 1 - me.co).astype(BF)
            gu_to(7 - i).start()

    def sibling_has_terms():
        @pl.loop(0, 8)
        def _(t):
            gu_to(t).wait_send()

    def own_terms(start):
        @pl.loop(start, start + 2)
        def _(i):
            gu_to(7 - i).wait_recv()
            gown(7 - i)[...] = (weight_terms(7 - i, me.co) + grecv[7 - i].astype(F32)).astype(BF)

    def down_terms():
        @pl.loop(0, 8)
        def _(t):
            at = pl.multiple_of(chip_of(me, t) * 256, 256)
            gd(t)[...] = dot_rows(hid[...], dy[:, :, pl.ds(at, 256)].reshape(1024, 256)).astype(BF)
            down_to(t).start()

    def down_sums():
        @pl.loop(0, 8)
        def _(t):
            down_to(t).wait_recv()

            @pl.loop(0, 22)
            def _(i):
                at = pl.ds(pl.multiple_of(i * 16, 16), 16)
                mine = gd(t).at[pl.ds(pl.multiple_of(me.co * 352 + i * 16, 16), 16)]
                mine[...] = (mine[...].astype(F32) + gdrecv[t, at].astype(F32)).astype(BF)

    m_first, m_second = {}, {}
    for dp in (0, 1):
        for way, sign in ((0, 1), (1, -1)):
            m_first[way, dp] = send(
                mpart.at[slot_of(2, dp), pl.ds(64 * way, 64)], m_half.at[way, dp], (r0, r1), (8, way * 2 + dp),
                me.across_y(sign, 0),
            )
            m_second[way, dp] = send(
                dy.at[1 + 2 * way + dp], m_full.at[way, dp], (r0, r1), (8, 4 + way * 2 + dp), me.across_y(sign, 0)
            )
    m_third = send(dy.at[5], m_pair, (r0, r1), (8, 8), me.across_y(0, 1))

    def m_start():
        dy_task.end()
        for copy in mpart_copy(3):
            copy.wait()
        for dp in (1, 0):
            for way in (0, 1):
                m_first[way, dp].start()

    m_parts = {(way, dp): later(mpart.at[slot_of(1 - 2 * way, dp)], dy.at[1 + 2 * way + dp]) for way in (0, 1) for dp in (0, 1)}
    m_halves = {(way, dp): later(m_half.at[way, dp], dy.at[6 + way, pl.ds(0, 64)]) for way in (0, 1) for dp in (0, 1)}
    m_fulls = {(way, dp): later(m_full.at[way, dp], dy.at[6 + way]) for way in (0, 1) for dp in (0, 1)}
    m_mine, m_near, m_last = later(mpart.at[0], dy.at[1]), later(mpart.at[1], dy.at[5]), later(m_pair, dy.at[2])
    m_out = later(dy.at[1], mixed)

    def m_turn(dp):
        for way in (0, 1):
            m_parts[way, dp].start()
        for way in (0, 1):
            m_first[way, dp].wait_recv()
            m_halves[way, dp].start()
        for way in (0, 1):
            m_parts[way, dp].wait()
            m_halves[way, dp].wait()
            add_into(dy.at[1 + 2 * way + dp, pl.ds(64 * way, 64)], 64, [dy.at[6 + way, pl.ds(0, 64)]])
            m_second[way, dp].start()

    def m_pair_up():
        m_near.start()
        for way in (0, 1):
            m_second[way, 1].wait_recv()
            m_fulls[way, 1].start()
        m_near.wait()
        for way in (0, 1):
            m_fulls[way, 1].wait()
        add_into(dy.at[5], 128, [dy.at[6], dy.at[7]])
        m_third.start()

    def m_finish():
        for dp in (0, 1):
            m_second[0, dp].wait_send()
        m_mine.start()
        for way in (0, 1):
            m_second[way, 0].wait_recv()
            m_fulls[way, 0].start()
        m_third.wait_recv()
        m_last.start()
        m_mine.wait()
        for way in (0, 1):
            m_fulls[way, 0].wait()
        m_last.wait()

        @pl.loop(0, 8)
        def _(i):
            at = pl.ds(pl.multiple_of(i * 16, 16), 16)
            total = h1[at]
            for slot in (1, 2, 6, 7):
                total = total + dy[slot, at].astype(F32)
            dy[1, at] = total.astype(BF)

        m_out.start()

    def wo_load(n):
        return pltpu.make_async_copy(
            wo_saved.at[pl.ds(2 * n, 2)], acts.at[pl.ds(2 * (n % 2), 2)], local.at[56 + n % 2]
        )

    def q_load(n):
        return pltpu.make_async_copy(q_saved.at[pl.ds(2 * n, 2)], acts.at[pl.ds(2 * (n % 2), 2)], local.at[58 + n % 2])

    def kw_load():
        return [
            load(kw_saved.at[chip], grecv.at[pl.ds(2 * (chip % 4), 2), :, pl.ds(512 * (chip // 4), 512)])
            for chip in range(8)
        ]

    def at_ctx(ref):
        def loc(dr, dp, er, ep, half):
            return ref.at[me.ctx_at(dr, dp), row_half(half, ref.shape[1])]

        return loc

    def dn_at(dr, dp, er, ep, half):
        first = pl.multiple_of(me.ctx_at(dr, dp) * 256, 256)
        return dn_all.at[row_half(half, 352), pl.ds(first, 256)]

    gu_task = over_y(packed, at_ctx(gu_all), 5, both=False)
    dn_task = over_y(dn_moved, dn_at, 6, both=False)
    dn_swap = Swap(me, gd_own(0), dn_moved, (v0, v1), local.at[next(slots)])
    gu_keep = later(packed, gu_all.at[me.c])
    dn_keep = later(dn_moved, dn_at(0, 0, 0, 0, None))
    dn_local = later(dnp, wd_at(0, 0, 0, 0, None))
    tokens_out = later(datts.at[own], tokens_grad)

    def block_at(ref, slot):
        first = pl.multiple_of(me.ctx_at(STEPS[slot], PAIRS[slot]) * 16, 16)
        return ref.at[pl.ds(first, 16)]

    def sum_over_ctx(total, got, row):
        return Trade(
            me.across_y, lambda slot: block_at(total, slot), lambda slot: got.at[mirror(slot)], (z0, z1), row
        )

    def spread(out, row):
        return Trade(me.across_y, lambda slot: block_at(out, 0), lambda slot: block_at(out, 0), (z0, z1), row)

    def sum_up(total, got, out):
        value = block_at(total, 0)[...].astype(F32)
        for slot in range(1, 8):
            value = value + got[slot].astype(F32)
        block_at(out, 0)[...] = value.astype(BF)

    o_sum, q_sum, kv_sum = op.at[0], qp.at[0], kp(0)
    o_sums = sum_over_ctx(o_sum, o_got, 0)
    q_sums = sum_over_ctx(q_sum, q_got, 1)
    k_sums = sum_over_ctx(kv_sum, k_got, 2)
    o_spread = spread(o_grad, 3)
    q_spread = spread(q_grad, 4)
    k_spread = spread(kv_grad, 5)
    e_task = Trade(me.across_y, lambda slot: g_sum, lambda slot: ggot.at[me.c], (z0, z1), 6)

    def to_sibling(src, dst, index):
        return send(src, dst, (c0, c1), 16 + index, me.sibling())

    att_swap = to_sibling(atts.at[own], atts.at[other], 0)
    datt_swap = to_sibling(datts.at[own], datts.at[other], 1)
    a1_swap = to_sibling(a1s.at[own], a1s.at[other], 2)
    queries, rest = pl.ds(0, 2048), pl.ds(2048, 512)
    dq_swap = to_sibling(dqkvs.at[own, queries], dqkvs.at[other, queries], 3)
    dkv_swap = to_sibling(dqkvs.at[own, rest], dqkvs.at[other, rest], 4)
    gain_swap = to_sibling(gown_rows, gsib_rows, 5)

    def norm_two_back():
        for i in range(16):
            grow[0, :, 128 * i : 128 * i + 128] = gains[i, 0:1, :]
            grow[1, :, 128 * i : 128 * i + 128] = gains[i, 8:9, :]
        grow[2] = jnp.zeros((1, 2048), F32)
        grow[3] = jnp.zeros((1, 2048), F32)

        @pl.loop(0, 8)
        def _(i):
            at = pl.ds(pl.multiple_of(16 * i, 16), 16)
            values, grad = h1[at], da2[at]
            scale = lax.rsqrt(jnp.mean(values * values, axis=1, keepdims=True) + EPS)
            grow[3] += jnp.sum(grad * values * scale, axis=0, keepdims=True)
            grad = grad * grow[1]
            level = jnp.mean(grad * values, axis=1, keepdims=True) * scale * scale * scale
            total = dy[0, at].astype(F32) + scale * grad - values * level
            da2[at] = total
            datts[at] = total.astype(BF)

        datt_swap.start()

    def heads_back():
        for n in range(4):
            wo_load(n).wait()
            part = dot_back(datts[own], acts[2 * (n % 2) : 2 * (n % 2) + 2].reshape(512, 2048)).astype(BF)
            for half in (0, 1):
                place = dost(n, half)
                for h in range(8):
                    place[h // 2, pl.ds(64 * (h % 2), 64), pl.ds(0, 64)] = part[
                        64 * half : 64 * half + 64, 64 * h : 64 * h + 64
                    ]
            if n < 2:
                wo_load(n + 2).start()
        for n in range(2):
            q_load(n).start()

    def terms(left, right, out, job):
        @pl.loop(0, 8)
        def _(i):
            at = pl.multiple_of((chip_of(me, 7 - i) * 2 + me.co) * 128, 128)
            out(7 - i)[...] = dot_rows(left[:, pl.ds(at, 128)], right[...]).astype(BF)

            @pl.when(i == 1)
            def _():
                job.start()

    def output_terms():
        att_swap.wait_recv()
        datt_swap.wait_recv()
        pl.semaphore_wait(credit, 3)
        terms(atts, datts, lambda t: op.at[t], o_job)

    def query_terms():
        a1_swap.wait_recv()
        dq_swap.wait_recv()
        terms(a1s, dqkvs.at[:, pl.ds(0, 2048)], lambda t: qp.at[t], q_job)

    def kv_terms():
        dkv_swap.wait_recv()
        terms(a1s, dqkvs.at[:, pl.ds(2048, 512)], kp, k_job)

    def kv_blocks(mate):
        for part, base in ((0, 0), (64, 256)):
            for n in range(4):
                first = base + 64 * n
                block = grecv[0:5, :, 128 * n : 128 * n + 128].reshape(640, 128)[:, part : part + 64]
                for slot in range(8):
                    kvp[slot, 0:64, first : first + 64] = block[64 * slot : 64 * slot + 64]
                    if slot == 0:
                        late = block[576:640]
                    else:
                        late = jnp.where(mate == slot, block[512:576], jnp.zeros((64, 64), BF))
                    kvp[slot, 64:128, first : first + 64] = late

    def kv_back():
        for i in range(2):
            at = slice(128 * i, 128 * i + 128)
            block = sT[512:640, at]
            dqkvs[own, 2048 + 128 * i : 2176 + 128 * i] = (block * cosine[...] - turned(block) * sine[...]).astype(BF)
        dqkvs[own, 2304:2560] = sT[512:640, 256:512].astype(BF)
        dkv_swap.start()

    def inputs_back():
        for copy in kw_back:
            copy.wait()
        for n in range(4):
            q_load(n).wait()
            block = dot_back(dqkvs[own, queries], acts[2 * (n % 2) : 2 * (n % 2) + 2].reshape(512, 2048))
            four, wide = pl.ds(4 * (n % 2), 4), pl.ds(512 * (n // 2), 512)
            block = block + dot_back(dqkvs[own, rest], grecv[four, :, wide].reshape(512, 512))
            sT[pl.ds(128 * n, 128)] = block
            if n < 2:
                q_load(n + 2).start()

    def norm_one_back():
        datt_swap.wait_send()

        @pl.loop(0, 8)
        def _(i):
            at = pl.ds(pl.multiple_of(16 * i, 16), 16)
            values = x[at].astype(F32)
            grad = jnp.concatenate([sT[pl.ds(pl.multiple_of(128 * n + 16 * i, 16), 16)] for n in range(4)], axis=1)
            scale = lax.rsqrt(jnp.mean(values * values, axis=1, keepdims=True) + EPS)
            grow[2] += jnp.sum(grad * values * scale, axis=0, keepdims=True)
            grad = grad * grow[0]
            level = jnp.mean(grad * values, axis=1, keepdims=True) * scale * scale * scale
            datts[at] = (da2[at] + scale * grad - values * level).astype(BF)

        tokens_out.start()

        gown_rows[...] = jnp.zeros((16, 16, 128), F32)
        for i in range(16):
            gown_rows[i, 0:1, :] = grow[2, :, 128 * i : 128 * i + 128]
            gown_rows[i, 8:9, :] = grow[3, :, 128 * i : 128 * i + 128]
        gain_swap.start()

    def gain_terms():
        gain_swap.wait_recv()
        for slot in range(8):
            block = me.fsdp_at(STEPS[slot], PAIRS[slot])
            gp[slot] = gown_rows[block] + gsib_rows[block]

    def dn_begin():
        dn_swap.wait()
        dn_task.start()
        dn_keep.start()

    def gu_begin():
        pack()
        gu_keep.start()
        gu_task.start()

    def e_begin():
        e_task.start()
        ggot[me.c] = g_sum[...]

    def attend_back(n, half):
        count = 512 if half == 0 else 640
        keys = pl.ds(0, count)
        key, query, out = kst[n, keys, :], qst[n, half], dost(n, half)[...].reshape(512, 128)[:, 0:64]
        sT[keys] = dot_back(key, query)
        dT[keys] = dot_back(vst[n, keys, :], out)
        for i in range(4):
            at = pl.ds(128 * i, 128)
            parts = []
            for first, size in ((0, 512), (512, 128))[: 1 + half]:
                scores = sT[first : first + size, at]
                if half == 0:
                    scores = scores + bias_p[...]
                elif first:
                    scores = scores + bias_c[...]
                probs = jnp.exp(scores - lse[2 * n + half, :, at])
                grad = dT[first : first + size, at]
                parts.append((first, size, probs, grad))
            level = sum(jnp.sum(probs * grad, axis=0, keepdims=True) for _, _, probs, grad in parts)
            for first, size, probs, grad in parts:
                pT[first : first + size, at] = probs.astype(BF)
                dsT[first : first + size, at] = (probs * (grad - level)).astype(BF)
        rows = slice(64 * half, 64 * half + 64)
        for i, block in enumerate(unpile(dot_rows(key, dsT[keys]) * SCALE)):
            block = block * cosine[rows] - turned(block) * sine[rows]
            first = pl.multiple_of(512 * n + 128 * i, 128)
            dqkvs[rows, pl.ds(first, 128)] = block.astype(BF)
        return dot_in(dsT[keys], query), dot_in(pT[keys], out)

    def pack():
        @pl.loop(0, 8)
        def _(i):
            here = pl.ds(pl.multiple_of(1024 + 16 * i, 16), 16)
            gate = gu[here, 0:768].astype(F32)
            up = pltpu.roll(gu[here, 768:1536].astype(F32), 64, 1)
            gu[here, 0:640] = gate[:, 0:640].astype(BF)
            gu[here, 640:768] = (gate[:, 640:768] + up[:, 0:128]).astype(BF)
            gu[here, 768:1408] = up[:, 128:768].astype(BF)

    def keep_kv_grads(n, one, two):
        keys = jnp.concatenate([one[0] + two[0][0:512], two[0][512:640]], axis=0)
        values = jnp.concatenate([one[1] + two[1][0:512], two[1][512:640]], axis=0)
        both = jnp.concatenate([keys, values], axis=1).astype(BF)
        grecv[pl.ds(0, 5), :, pl.ds(pl.multiple_of(128 * n, 128), 128)] = both.reshape(5, 128, 128)

    qx.start()
    dy_task.start()
    g.start()
    loads[0].wait()
    loads[1].wait()
    k.start()
    g.turn(0)
    qx.turn(0)
    qx.pair()
    ox.start()
    qx.last(0)
    qx.turn(1)
    o.start()
    swap.start()
    qx.last(1)
    kept[qx].wait()
    qy.start()
    mate = place_tables(me, deal, freq, cosine, sine, bias_p, bias_c)
    q.start()
    g.pair()
    dy_task.pair()
    k.pair()
    qy.turn(0)
    g.turn(1)
    g.last(0)
    k.turn(0)
    ox.turn(0)
    k.turn(1)
    q.turn(0)
    ox.pair()
    g.last(1)
    k.last(0)
    qy.pair()
    k.last(1)
    o.pair()
    ox.turn(1)
    g.sync()
    k.sync()
    x_load.wait()
    normed()
    project_kv()
    qy.last(0)
    ox.last(0)
    kv_task.start()
    q.pair()
    ox.last(1)
    qy.turn(1)
    swap.wait()
    dn_local.start()
    dn.start()
    kv_task.pair()
    kept[ox].wait()
    oy.start()
    kv_task.turn(0)
    q.turn(1)
    o.turn(0)
    qy.last(1)
    kv_task.turn(1)
    o.turn(1)
    put_gate_up()
    qy.sync()
    m.start()
    q.last(1)
    q.last(0)
    oy.pair()
    q.sync()
    oy.turn(0)
    kv_task.last(0)
    kept[q].wait()
    saved.append(load(qw, q_saved))
    saved.append(load(kw, kw_saved))
    project_q()
    kv_task.last(1)
    collect_kv(mate)
    a1_swap.start()
    o.last(1)

    @pl.loop(0, 4)
    def _(n):
        attend(n, 0)
        attend(n, 1)

        @pl.when(n == 0)
        def _():
            oy.turn(1)
            dn.turn(0)
            dn.pair()
            o.last(0)

        @pl.when(n == 1)
        def _():
            dy_task.turn(0)
            oy.last(0)

        @pl.when(n == 2)
        def _():
            dy_task.turn(1)
            oy.last(1)
            m.pair()

    o.sync()
    oy.sync()
    kept[o].wait()
    saved.append(load(wo, wo_saved))
    project_o()
    normed_two()
    for task in (k, q, qx, qy):
        task.end()
    saved[0].wait()
    saved[1].wait()
    a.start()
    m.turn(0)
    dn.last(0)
    m.turn(1)
    dn.turn(1)
    m.last(1)
    m.last(0)
    a.pair()
    dn.last(1)
    m.sync()
    att_swap.start()
    dy_task.last(1)
    dy_task.last(0)
    dn.sync()

    for task in (o, ox, oy, kv_task):
        task.end()
    saved[2].wait()
    dn_local.wait()
    kept[dy_task].wait()

    @pl.loop(0, 3)
    def _(n):
        group(n)

        @pl.when(n == 0)
        def _():
            a.turn(0)

        @pl.when(n == 1)
        def _():
            a.turn(1)

    a.last(0)
    group_half(6)
    a.last(1)
    group_half(7)
    d.start()
    m.end()
    terms_for_sibling(0)
    terms_for_sibling(2)
    own_terms(0)
    gjob.start()
    terms_for_sibling(4)
    terms_for_sibling(6)
    d.turn(1)
    own_terms(2)
    own_terms(4)
    group_out()
    gjob.turn(1)
    dn.end()
    down_terms()
    down_sums()
    n_job.start()
    d.turn(0)
    d.pair()
    n_job.turn(1)
    gjob.turn(0)
    n_job.turn(0)
    m_start()
    own_terms(6)
    a.end()
    wo_load(0).start()
    wo_load(1).start()
    n_job.pair()
    d.finish(da2)
    norm_two_back()
    for device in near(me.across_x):
        pl.semaphore_signal(credit, 1, device_id=device, device_id_type=MESH)
    gjob.pair()
    m_turn(1)
    d.end()
    output_terms()
    heads_back()
    gjob.finish(gown(0))
    gu_begin()

    @pl.loop(0, 4)
    def _(n):
        one, two = attend_back(n, 0), attend_back(n, 1)
        keep_kv_grads(n, one, two)

        @pl.when(n == 0)
        def _():
            o_job.turn(1)
            m_pair_up()

        @pl.when(n == 2)
        def _():
            gu_task.pair()
            o_job.turn(0)

    kv_blocks(mate)
    kw_back = kw_load()
    dq_swap.start()
    d_job.start()
    n_job.finish(gd_own(0))
    dn_swap.start()
    o_job.pair()
    query_terms()
    gu_task.turn(0)
    d_job.turn(1)
    d_job.turn(0)
    gu_task.last(0)
    gu_task.turn(1)
    d_job.pair()
    o_job.finish(o_sum)
    o_sums.start()
    q_job.turn(1)
    d_job.finish(sT.at[pl.ds(512, 128)])
    kv_back()
    m_turn(0)
    dn_begin()
    inputs_back()
    o_sums.got()
    sum_up(o_sum, o_got, o_grad)
    sibling_has_terms()
    kv_terms()
    o_spread.start()
    q_job.pair()
    dn_task.pair()
    gu_task.last(1)
    k_job.turn(1)
    q_job.turn(0)
    m_finish()
    norm_one_back()
    gain_terms()
    dn_task.turn(0)
    k_job.turn(0)
    k_job.pair()
    e_job.start()
    dn_task.turn(1)
    q_job.finish(q_sum)
    q_sums.start()
    e_job.turn(0)
    e_job.turn(1)
    k_job.finish(kv_sum)
    e_job.pair()
    k_sums.start()
    dn_task.last(0)
    q_sums.got()
    sum_up(q_sum, q_got, q_grad)
    q_spread.start()
    e_job.finish(g_sum)
    e_begin()
    k_sums.got()
    sum_up(kv_sum, k_got, kv_grad)
    k_spread.start()
    o_spread.got()
    q_spread.got()
    e_task.got()
    dn_task.last(1)
    k_spread.got()
    total = ggot[0]
    for index in range(1, 8):
        total = total + ggot[index]
    gains_out[...] = total
    for job in (g, gjob, n_job, o_job, q_job, k_job, e_job, d_job, gu_task, dn_task):
        job.end()
    for job in (o_sums, q_sums, k_sums, o_spread, q_spread, k_spread, e_task):
        job.end()
    for copy in (*m_first.values(), m_second[1, 0], m_second[1, 1], m_third):
        copy.wait_send()
    m_out.wait()
    tokens_out.wait()
    gu_keep.wait()
    dn_keep.wait()
    for copy in (att_swap, a1_swap, dq_swap, dkv_swap, gain_swap):
        copy.wait_send()

    @pl.loop(0, 8)
    def _(t):
        down_to(t).wait_send()


def layer(x, attn_gain, mlp_gain, deal, freq, q, key, value, wo, gate, up, dn, dy):
    shape = jax.ShapeDtypeStruct
    smem = pl.BlockSpec(memory_space=pltpu.SMEM)
    vmem = pltpu.VMEM
    outs = pl.pallas_call(
        layer_kernel,
        out_shape=(
            shape((128, 2048), BF),
            shape((128, 2048), BF),
            shape((128, 2048), BF),
            shape((128, 512), BF),
            shape((128, 2048), BF),
            shape((16, 128), F32),
            shape((8, 128, 1408), BF),
            shape((352, 2048), BF),
            shape((8, 2, 128, 2048), BF),
            shape((8, 2, 128, 512), BF),
            shape((8, 2, 128, 2048), BF),
            shape((8, 128, 2048), BF),
            shape((2, 2, 64, 2048), BF),
            shape((2, 2, 128, 2048), BF),
            shape((128, 2048), BF),
        ),
        in_specs=[ANY] + [VMEM] * 2 + [smem, VMEM] + [ANY] * 8,
        out_specs=[ANY] * 2 + [VMEM] * 4 + [ANY] * 9,
        scratch_shapes=[
            vmem((128, 2048), BF),
            vmem((16, 16, 128), F32),
            vmem((256, 2048), BF),
            vmem((256, 2048), BF),
            vmem((4, 2, 512, 64), BF),
            vmem((4, 640, 64), BF),
            vmem((4, 640, 64), BF),
            vmem((8, 1, 512), F32),
            vmem((128, 2048), F32),
            vmem((128, 128), F32),
            vmem((128, 128), F32),
            vmem((512, 128), F32),
            vmem((128, 128), F32),
            vmem((8, 2, 128, 2048), BF),
            vmem((8, 2, 128, 512), BF),
            vmem((8, 2, 128, 2048), BF),
            vmem((128, 512), BF),
            vmem((8, 128, 512), BF),
            vmem((640, 512), F32),
            vmem((640, 512), BF),
            vmem((640, 512), F32),
            vmem((640, 512), BF),
            vmem((128, 1), F32),
            vmem((2, 128, 768), BF),
            vmem((352, 256), BF),
            vmem((4, 2, 128, 2048), BF),
            vmem((2048, 1536), BF),
            vmem((768, 2048), BF),
            vmem((8, 128, 2048), BF),
            vmem((1024, 768), BF),
            vmem((8, 128, 1536), BF),
            vmem((8, 352, 256), BF),
            vmem((128, 1536), BF),
            vmem((128, 2048), F32),
            vmem((256, 2048), BF),
            vmem((256, 2560), BF),
            vmem((4, 1, 2048), F32),
            vmem((16, 16, 128), F32),
            vmem((16, 16, 128), F32),
            vmem((352, 256), BF),
            *scatter_buffers(352, 256),
            *scatter_buffers(16, 128, F32),
            vmem((8, 16, 128), F32),
            vmem((8, 16, 128), F32),
            vmem((16, 128), F32),
            vmem((8, 16, 2048), BF),
            vmem((8, 16, 2048), BF),
            vmem((8, 16, 512), BF),
            *dma_sems(8, 9),
            *dma_sems(8, 10),
            *dma_sems(7, 9),
            *dma_sems(2, 10),
            *dma_sems(9, 9),
            *dma_sems(7, 8),
            pltpu.SemaphoreType.DMA((22,)),
            pltpu.SemaphoreType.DMA((22,)),
            pltpu.SemaphoreType.DMA,
            pltpu.SemaphoreType.DMA,
            pltpu.SemaphoreType.DMA,
            pltpu.SemaphoreType.DMA,
            pltpu.SemaphoreType.REGULAR,
            pltpu.SemaphoreType.DMA((64,)),
        ],
        compiler_params=params(1, 63),
        name="layer",
    )(x, attn_gain, mlp_gain, deal, freq, q, key, value, wo, gate, up, dn, dy)
    return outs[:8]


def finish_kernel(
    mixed_in, tokens_in, q_in, kv_in, o_in, gu_in, dn_in, gains,
    mixed, tokens_grad, q_out, key_out, value_out, o_out, gate_out, up_out, dn_out, first_gain, second_gain,
    b_mixed, b_tokens, b_q, b_kv, b_o, b_gu, b_dn, f_q, f_key, f_value, f_o, f_gate, f_up, f_dn, sems,
):
    slots = iter(range(24))

    def move(src, dst):
        return pltpu.make_async_copy(src, dst, sems.at[next(slots)])

    loads = [
        move(src, dst)
        for src, dst in (
            (q_in, b_q), (o_in, b_o), (dn_in, b_dn), (gu_in.at[pl.ds(0, 4)], b_gu.at[pl.ds(0, 4)]),
            (gu_in.at[pl.ds(4, 4)], b_gu.at[pl.ds(4, 4)]), (kv_in, b_kv), (mixed_in, b_mixed), (tokens_in, b_tokens),
        )
    ]
    for copy in loads:
        copy.start()
    stores = []

    def store(src, dst):
        copy = move(src, dst)
        copy.start()
        stores.append(copy)

    def widen(pair):
        first = 1408 * pair

        @pl.loop(0, 8)
        def _(i):
            rows = pl.ds(pl.multiple_of(16 * i, 16), 16)
            lane = lax.broadcasted_iota(jnp.int32, (16, 128), 1)
            for out, base, turn in ((f_gate, 0, (0, 64)), (f_up, 640, (704, 0))):
                even = b_gu[2 * pair, rows, base : base + 768].astype(F32)
                odd = b_gu[2 * pair + 1, rows, base : base + 768].astype(F32)
                even = pltpu.roll(even, turn[0], 1) if turn[0] else even
                odd = pltpu.roll(odd, turn[1], 1) if turn[1] else odd
                out[rows, first : first + 640] = even[:, 0:640]
                out[rows, first + 640 : first + 768] = jnp.where(lane < 64, even[:, 640:768], odd[:, 0:128])
                out[rows, first + 768 : first + 1408] = odd[:, 128:768]

    def cast(src, dst, rows):
        @pl.loop(0, rows // 32)
        def _(i):
            at = pl.ds(pl.multiple_of(32 * i, 32), 32)
            dst[at] = src[at].astype(F32)

    for index, src, dst, out, rows in (
        (0, b_q, f_q, q_out, 128), (1, b_o, f_o, o_out, 128), (2, b_dn, f_dn, dn_out, 352)
    ):
        loads[index].wait()
        cast(src, dst, rows)
        store(dst, out)
    for half in (0, 1):
        loads[3 + half].wait()
        for pair in (2 * half, 2 * half + 1):
            widen(pair)
            wide = pl.ds(1408 * pair, 1408)
            store(f_gate.at[:, wide], gate_out.at[:, wide])
            store(f_up.at[:, wide], up_out.at[:, wide])
    first_gain[...] = gains[0:1, :]
    second_gain[...] = gains[8:9, :]
    loads[5].wait()
    f_key[...] = b_kv[:, 0:256].astype(F32)
    f_value[...] = b_kv[:, 256:512].astype(F32)
    store(f_key, key_out)
    store(f_value, value_out)
    loads[6].wait()
    store(b_mixed, mixed)
    loads[7].wait()
    store(b_tokens, tokens_grad)
    for copy in stores:
        copy.wait()


def finish(mixed, tokens_grad, q, kv, o, gu, dn, gains):
    shape, vmem = jax.ShapeDtypeStruct, pltpu.VMEM
    wholes = [(128, 2048), (128, 256), (128, 256), (128, 2048), (128, 5632), (128, 5632), (352, 2048)]
    return pl.pallas_call(
        finish_kernel,
        out_shape=(shape((128, 2048), BF), shape((128, 2048), BF), *[shape(dims, F32) for dims in (*wholes, (1, 128), (1, 128))]),
        in_specs=[ANY] * 7 + [VMEM],
        out_specs=[ANY] * 9 + [VMEM] * 2,
        scratch_shapes=[
            vmem((128, 2048), BF),
            vmem((128, 2048), BF),
            vmem((128, 2048), BF),
            vmem((128, 512), BF),
            vmem((128, 2048), BF),
            vmem((8, 128, 1408), BF),
            vmem((352, 2048), BF),
            *[vmem(dims, F32) for dims in wholes],
            pltpu.SemaphoreType.DMA((24,)),
        ],
        compiler_params=pltpu.CompilerParams(vmem_limit_bytes=62 << 20),
        name="finish",
    )(mixed, tokens_grad, q, kv, o, gu, dn, gains)


def on_device(
    tokens,
    block_deal,
    attn_gain,
    query_weight,
    key_weight,
    value_weight,
    output_weight,
    mlp_gain,
    gate_weight,
    up_weight,
    down_weight,
    cotangent,
):
    freq = BASE ** (-(np.arange(HEAD_DIM // 2, dtype=np.float32) * 2.0) / HEAD_DIM)
    freq = np.concatenate([freq] * 4)[None].astype(np.float32)
    mixed, tokens_grad, query_grad, kv_grad, o_grad, gain_grads, gu_grads, dn_grad = layer(
        tokens[0], attn_gain[None], mlp_gain[None], block_deal.transpose(1, 2, 0), freq, query_weight, key_weight, value_weight, output_weight,
        gate_weight, up_weight, down_weight, cotangent[0],
    )
    mixed, tokens_grad, *grads, first_gain, second_gain = finish(
        mixed, tokens_grad, query_grad, kv_grad, o_grad, gu_grads, dn_grad, gain_grads
    )
    return (mixed[None], tokens_grad[None], first_gain[0], *grads[:4], second_gain[0], *grads[4:])


def solution(mesh):
    held = P("fsdp", "ctx", None)
    rows = P("fsdp", None)
    return jax.shard_map(
        on_device,
        mesh=mesh,
        in_specs=(held, P(), P("fsdp"), rows, rows, rows, rows, P("fsdp"), rows, rows, rows, held),
        out_specs=(held, held, P("fsdp"), rows, rows, rows, rows, P("fsdp"), rows, rows, rows),
        check_vma=False,
    )
```

```python
import functools

import jax
import jax.numpy as jnp
from jax import lax
from jax.experimental import pallas as pl
from jax.experimental.pallas import tpu as pltpu
from jax.sharding import PartitionSpec as P
import numpy as np

MESH = pl.DeviceIdType.MESH
BF = jnp.bfloat16
F32 = jnp.float32
ANY = pl.BlockSpec(memory_space=pl.ANY)
VMEM = pl.BlockSpec(memory_space=pltpu.VMEM)

HEAD_DIM = 64
EPS = 1e-05
SCALE = 0.125
BASE = 10000.0

SLOT = {(0, 0): 0, (0, 1): 1, (1, 0): 2, (3, 0): 3, (1, 1): 4, (3, 1): 5, (2, 0): 6, (2, 1): 7}
STEPS = (0, 0, 1, 3, 1, 3, 2, 2)
PAIRS = (0, 1, 0, 0, 1, 1, 0, 1)


def slot_of(dr, dp):
    return SLOT[(dr % 4, dp % 2)]


class Place:
    def __init__(self):
        self.c = lax.axis_index("ctx")
        self.f = lax.axis_index("fsdp")
        self.y, self.zl = lax.div(self.c, 2), lax.rem(self.c, 2)
        self.j, self.co = lax.div(self.f, 2), lax.rem(self.f, 2)
        self.x, self.zh = lax.div(self.j, 2), lax.rem(self.j, 2)

    def ctx_at(self, dr, dp):
        return lax.rem(self.y + dr % 4, 4) * 2 + lax.rem(self.zl + dp, 2)

    def chip_at(self, dr, dp):
        return lax.rem(self.x + dr % 4, 4) * 2 + lax.rem(self.zh + dp, 2)

    def fsdp_at(self, dr, dp):
        return self.chip_at(dr, dp) * 2 + self.co

    def across_y(self, dr, dp):
        return {"ctx": self.ctx_at(dr, dp), "fsdp": self.f}

    def across_x(self, dr, dp):
        return {"ctx": self.c, "fsdp": self.fsdp_at(dr, dp)}

    def sibling(self):
        return {"ctx": self.c, "fsdp": self.f + 1 - 2 * self.co}


def chip_of(me, t):
    dr = jnp.where(t < 2, 0, jnp.where(t >= 6, 2, 1 + 2 * lax.rem(t, 2)))
    dp = jnp.where(t < 2, t, jnp.where(t >= 6, t - 6, lax.div(t, 4)))
    return lax.rem(me.x + dr, 4) * 2 + lax.rem(me.zh + dp, 2)


def greet(devices):
    barrier = pltpu.get_barrier_semaphore()
    for device in devices:
        pl.semaphore_signal(barrier, 1, device_id=device, device_id_type=MESH)
    pl.semaphore_wait(barrier, len(devices))


class Swap:
    def __init__(self, me, src, dst, sems, local):
        self.moved = me.c != me.j
        self.to = {"ctx": me.j, "fsdp": 2 * me.c + me.co}
        self.copy = pltpu.make_async_remote_copy(
            src, dst, sems[0], sems[1], device_id=self.to, device_id_type=MESH
        )
        self.keep = pltpu.make_async_copy(src, dst, local)

    def start(self):
        pl.when(self.moved)(self.copy.start)
        pl.when(jnp.logical_not(self.moved))(self.keep.start)

    def wait(self):
        pl.when(self.moved)(self.copy.wait)
        pl.when(jnp.logical_not(self.moved))(self.keep.wait)


def greet_all(me, plane=False):
    barrier = pltpu.get_barrier_semaphore()
    others = near(me.across_x) + [me.sibling()]
    others += [me.across_y(STEPS[s], PAIRS[s]) for s in range(1, 8)] if plane else near(me.across_y)
    for device in others:
        pl.semaphore_signal(barrier, 1, device_id=device, device_id_type=MESH)
    moved = me.c != me.j

    @pl.when(moved)
    def _():
        to = {"ctx": me.j, "fsdp": 2 * me.c + me.co}
        pl.semaphore_signal(barrier, 1, device_id=to, device_id_type=MESH)

    pl.semaphore_wait(barrier, len(others) + jnp.where(moved, 1, 0))


def near(dev):
    return [dev(1, 0), dev(-1, 0), dev(0, 1)]


def send(src, dst, sems, index, device):
    return pltpu.make_async_remote_copy(
        src, dst, sems[0].at[index], sems[1].at[index], device_id=device, device_id_type=MESH
    )


class Gather:
    MOVES = (
        ((0, 0), (0, 1), None),
        ((0, 0), (1, 0), None),
        ((0, 0), (-1, 0), None),
        ((0, 1), (1, 0), None),
        ((0, 1), (-1, 0), None),
        ((-1, 0), (1, 0), 0),
        ((-1, 1), (1, 0), 0),
        ((1, 0), (-1, 0), 1),
        ((1, 1), (-1, 0), 1),
    )

    def __init__(self, dev, own, loc, sems, row, sibling=None, sibling_sems=None):
        self.loc = loc
        self.copies = []
        for index, (block, to, half) in enumerate(self.MOVES):
            src = own if block == (0, 0) else loc(*block, 0, 0, half)
            dst = loc(*block, *to, half)
            self.copies.append(send(src, dst, sems, (row, index), dev(*to)))
        self.passed = {}
        if sibling is not None:
            self.passed[9] = send(own, loc(0, 0, 0, 0, None), sibling_sems, (row, 9), sibling)
            for index, ((dr, dp), (er, ep), half) in enumerate(self.MOVES):
                ref = loc(dr - er, dp + ep, 0, 0, half)
                self.passed[index] = send(ref, ref, sibling_sems, (row, index), sibling)
        self.own = own

    def _pass(self, index):
        if self.passed:
            self.passed[index].start()

    def _got(self, index):
        self.copies[index].wait_recv()
        self._pass(index)

    def start(self):
        for index in (0, 1, 2):
            self.copies[index].start()
        self._pass(9)

    def pair(self):
        self._got(0)
        self.copies[3].start()
        self.copies[4].start()

    def turn(self, dp):
        for got, on in (((1, 5), (2, 7)) if dp == 0 else ((3, 6), (4, 8))):
            self._got(got)
            self.copies[on].start()

    def last(self, dp):
        for got in ((5, 7) if dp == 0 else (6, 8)):
            self._got(got)

    def sync(self):
        for copy in self.passed.values():
            copy.wait()

    def end(self):
        for copy in self.copies:
            copy.wait_send()


class RingFirst:
    MOVES = (
        ((0, 0), (0, 1), None),
        ((0, 0), (1, 0), None),
        ((0, 0), (-1, 0), None),
        ((-1, 0), (1, 0), 0),
        ((1, 0), (-1, 0), 1),
        ((-1, 0), (0, 1), None),
        ((1, 0), (0, 1), None),
        ((2, 0), (0, 1), 0),
        ((2, 0), (0, 1), 1),
    )

    def __init__(self, dev, own, loc, sems, row):
        self.own, self.loc = own, loc
        self.copies = []
        for index, (block, to, half) in enumerate(self.MOVES):
            src = own if block == (0, 0) else loc(*block, 0, 0, half)
            self.copies.append(send(src, loc(*block, *to, half), sems, (row, index), dev(*to)))

    def go(self, *indices):
        for index in indices:
            self.copies[index].start()

    def got(self, *indices):
        for index in indices:
            self.copies[index].wait_recv()

    def end(self):
        for copy in self.copies:
            copy.wait_send()


def row_half(half, rows):
    return pl.ds(0, rows) if half is None else pl.ds(half * (rows // 2), rows // 2)


def add_into(ref, rows, others, step=16):
    step = min(step, rows)

    @pl.loop(0, rows // step)
    def _(i):
        at = pl.ds(pl.multiple_of(i * step, step), step)
        total = ref[at].astype(F32)
        for other in others:
            total = total + other[at].astype(F32)
        ref[at] = total.astype(ref.dtype)


class Scatter:
    def __init__(self, dev, part, rows, halves, fulls, paired, sems, row, cut=None):
        self.part, self.rows, self.cut = part, rows, cut
        self.halves, self.fulls, self.paired = halves, fulls, paired
        self.first, self.second = {}, {}
        for dp in (0, 1):
            for way, sign in ((0, 1), (1, -1)):
                self.first[way, dp] = send(
                    self._half(part(slot_of(2, dp)), way), halves.at[way, dp], sems, (row, way * 2 + dp), dev(sign, 0)
                )
                self.second[way, dp] = send(
                    part(slot_of(sign, dp)), fulls.at[way, dp], sems, (row, 4 + way * 2 + dp), dev(sign, 0)
                )
        self.third = send(part(slot_of(0, 1)), paired, sems, (row, 8), dev(0, 1))

    def _half(self, ref, way):
        if self.cut is None:
            return ref.at[pl.ds(way * (self.rows // 2), self.rows // 2)]
        return ref.at[:, pl.ds(way * (self.cut // 2), self.cut // 2)]

    def start(self):
        for dp in (1, 0):
            for way in (0, 1):
                self.first[way, dp].start()

    def turn(self, dp):
        for way, sign in ((0, 1), (1, -1)):
            self.first[way, dp].wait_recv()
            block = self._half(self.part(slot_of(sign, dp)), way)
            add_into(block, block.shape[0], [self.halves.at[way, dp]])
            self.second[way, dp].start()

    def pair(self):
        for way in (0, 1):
            self.second[way, 1].wait_recv()
        add_into(self.part(slot_of(0, 1)), self.rows, [self.fulls.at[0, 1], self.fulls.at[1, 1]])
        self.third.start()

    def finish(self, out, extra=()):
        for way in (0, 1):
            self.second[way, 0].wait_recv()
        self.third.wait_recv()
        own = self.part(0)
        terms = [own, self.fulls.at[0, 0], self.fulls.at[1, 0], self.paired, *extra]

        @pl.loop(0, self.rows // 16)
        def _(i):
            at = pl.ds(pl.multiple_of(i * 16, 16), 16)
            total = terms[0][at].astype(F32)
            for term in terms[1:]:
                total = total + term[at].astype(F32)
            out[at] = total.astype(out.dtype)

    def end(self):
        for copy in (*self.first.values(), *self.second.values(), self.third):
            copy.wait_send()


def mirror(slot):
    return slot_of(-STEPS[slot], PAIRS[slot])


class Trade:
    def __init__(self, dev, what, where, sems, row):
        self.copies = [
            pltpu.make_async_remote_copy(
                what(slot), where(slot), sems[0].at[row, slot], sems[1].at[row, mirror(slot)],
                device_id=dev(STEPS[slot], PAIRS[slot]), device_id_type=MESH,
            )
            for slot in range(1, 8)
        ]

    def start(self):
        for copy in self.copies:
            copy.start()

    def got(self):
        for copy in self.copies:
            copy.wait_recv()

    def end(self):
        for copy in self.copies:
            copy.wait_send()


def scatter_buffers(rows, columns, dtype=BF, cut=False):
    half = (rows, columns // 2) if cut else (rows // 2, columns)
    return [
        pltpu.VMEM((2, 2, *half), dtype),
        pltpu.VMEM((2, 2, rows, columns), dtype),
        pltpu.VMEM((rows, columns), dtype),
    ]


def dma_sems(rows, count):
    return [pltpu.SemaphoreType.DMA((rows, count)), pltpu.SemaphoreType.DMA((rows, count))]


def params(collective_id, vmem=56):
    return pltpu.CompilerParams(
        collective_id=collective_id, has_side_effects=True, vmem_limit_bytes=vmem << 20
    )


def dot_in(left, right):
    return jnp.dot(left, right, preferred_element_type=F32)


def dot_back(left, right):
    return lax.dot_general(left, right, (((1,), (1,)), ((), ())), preferred_element_type=F32)


def dot_rows(left, right):
    return lax.dot_general(left, right, (((0,), (0,)), ((), ())), preferred_element_type=F32)


def load(src, dst, sem):
    copy = pltpu.make_async_copy(src, dst, sem)
    copy.start()
    return copy


def turned(values):
    lane = lax.broadcasted_iota(jnp.int32, values.shape, 1)
    low = lax.rem(lane, 64) < 32
    return jnp.where(low, pltpu.roll(values, 96, 1), pltpu.roll(values, 32, 1))


def pile(out, values, half):
    for h in range(8):
        out[pl.ds(64 * h, 64), :] = values[64 * half : 64 * half + 64, 64 * h : 64 * h + 64]


def unpile(values):
    flat = values.T
    return [
        jnp.concatenate([flat[128 * m : 128 * m + 64], flat[128 * m + 64 : 128 * m + 128]], axis=1)
        for m in range(4)
    ]


def norm_scale(ref, out):
    values = ref[...].astype(F32)
    out[...] = lax.rsqrt(jnp.mean(values * values, axis=1, keepdims=True) + EPS)


def place_tables(me, deal, freq, cosine, sine, bias_p, bias_c):
    def block(slot, part):
        return deal[me.ctx_at(STEPS[slot], PAIRS[slot]), part, me.f]

    first, second = block(0, 0), block(0, 1)
    odd = lax.rem(second, 2)
    row = lax.broadcasted_iota(jnp.int32, (128, 128), 0)
    lane = lax.broadcasted_iota(jnp.int32, (128, 128), 1)
    position = jnp.where(row < 64, first * 64 + row, 448 + odd * 64 + row)
    angle = position.astype(F32) * freq[...]
    cosine[...] = jnp.cos(angle)
    sine[...] = jnp.where(lax.rem(lane, 64) < 32, -jnp.sin(angle), jnp.sin(angle))
    row, lane = row[:64], lax.rem(lane[:64], 64)
    mate = jnp.int32(0)
    for slot in range(8):
        seen = block(slot, 0) * 64 + row <= first * 64 + lane
        bias_p[pl.ds(64 * slot, 64), :] = jnp.where(seen, 0.0, -1e30)
        if slot:
            mate = mate + jnp.where(block(slot, 1) == second + 1 - 2 * odd, slot, 0)
    bias_c[pl.ds(0, 64), :] = jnp.where(odd + 0 * row == 1, 0.0, -1e30)
    bias_c[pl.ds(64, 64), :] = jnp.where(row <= lane, 0.0, -1e30)
    return mate


def layer_kernel(
    x_in, attn_gain, mlp_gain, deal, freq, q_in, key_in, value_in, wo_in, gate_in, up_in, dn_in, dy_in,
    mixed, tokens_grad, q_grad, kv_grad, o_grad, gains_out, gu_all, dn_all,
    q_saved, kw_saved, wo_saved, mpart, m_half, m_full, m_pair,
    x, gains, a1s, atts, qst, kst, vst, lse, h1, cosine, sine, bias_p, bias_c,
    qw, kw, wo, kv_own, kv, sT, pT, dT, dsT, scale, gu_win, dnp, acts, gu, wd, dy, hid,
    grecv, gdrecv, g_pair, da2, datts, dqkvs, grow, gown_rows, gsib_rows, dn_moved,
    n_half, n_full, n_pair, e_half, e_full, e_pair, gp, ggot, g_sum, o_got, q_got, k_got,
    s0, s1, t0, t1, y0, y1, u0, u1, r0, r1, z0, z1, c0, c1, w0, w1, v0, v1, credit, local,
):
    me = Place()
    greet_all(me, plane=True)
    own, other = pl.ds(0, 128), pl.ds(128, 128)
    slots = iter(range(64))

    def load(src, dst):
        copy = pltpu.make_async_copy(src, dst, local.at[next(slots)])
        copy.start()
        return copy

    def later(src, dst):
        return pltpu.make_async_copy(src, dst, local.at[next(slots)])

    def aligned(index, step):
        return index if isinstance(index, int) else pl.multiple_of(index, step)

    def gains_at(dr, dp, er, ep, half):
        return gains.at[me.fsdp_at(dr, dp), row_half(half, 16)]

    def slot_at(ref, rows):
        def loc(dr, dp, er, ep, half):
            return ref.at[slot_of(dr - er, dp + ep), row_half(half, rows)]

        return loc

    def acts_at(dr, dp, er, ep, half):
        slot = slot_of(dr - er, dp + ep)
        return acts.at[slot // 2, slot % 2, row_half(half, 128)]

    def columns(first, index):
        return pl.ds(pl.multiple_of(first + index * 128, 128), 128)

    def plain(ref, count):
        def loc(dr, dp, er, ep, half):
            return ref.at[me.chip_at(dr, dp), me.co, row_half(half, 128), pl.ds(0, count)]

        return loc

    def strip_x(ref, first):
        def loc(dr, dp, er, ep, half):
            return ref.at[me.chip_at(dr, dp), me.co, row_half(half, 128), columns(first, me.c)]

        return loc

    def strip_y(ref, first):
        def loc(dr, dp, er, ep, half):
            chips = pl.ds(0, 8) if half is None else pl.ds(4 * half, 4)
            return ref.at[chips, me.co, :, columns(first, me.ctx_at(dr, dp))]

        return loc

    def wd_at(dr, dp, er, ep, half):
        size = 352 if half is None else 176
        first = me.co * 352 + (0 if half is None else half * size)
        return wd.at[
            pl.ds(pl.multiple_of(first, 16), size),
            pl.ds(pl.multiple_of(me.chip_at(dr, dp) * 256, 256), 256),
        ]

    def gu_at(dr, dp, er, ep, half):
        size = 128 if half is None else 64
        first = me.fsdp_at(dr, dp) * 128 + (0 if half is None else half * size)
        return gu.at[pl.ds(pl.multiple_of(first, size), size)]

    def over_x(own, loc, row, both=True):
        own = loc(0, 0, 0, 0, None) if own is None else own
        return Gather(me.across_x, own, loc, (s0, s1), row, me.sibling() if both else None, (t0, t1))

    def over_y(own, loc, row, both=True):
        own = loc(0, 0, 0, 0, None) if own is None else own
        return Gather(me.across_y, own, loc, (y0, y1), row, me.sibling() if both else None, (u0, u1))

    g = over_x(None, gains_at, 0)
    k = over_x(None, plain(kw, 512), 1)
    q = over_x(q_in.at[:, pl.ds(0, 1024)], plain(qw, 1024), 2)
    qx = over_x(q_in.at[:, columns(1024, me.c)], strip_x(qw, 1024), 3, both=False)
    o = over_x(wo_in.at[:, pl.ds(0, 1024)], plain(wo, 1024), 4)
    ox = over_x(wo_in.at[:, columns(1024, me.c)], strip_x(wo, 1024), 5, both=False)
    m = over_x(None, gu_at, 6)
    dn = over_x(dnp, wd_at, 7)
    qy = over_y(None, strip_y(qw, 1024), 0)
    oy = over_y(None, strip_y(wo, 1024), 1)
    dy_task = over_y(dy_in, slot_at(dy, 128), 2, both=False)
    kv_task = over_y(kv_own, slot_at(kv, 128), 3, both=False)
    a = over_y(None, acts_at, 4, both=False)
    swap = Swap(me, dn_in.at[:, pl.ds(pl.multiple_of(me.c * 256, 256), 256)], dnp, (w0, w1), local.at[next(slots)])

    own_kw = plain(kw, 512)(0, 0, 0, 0, None)
    x_load = load(x_in, x)
    loads = [load(key_in, own_kw.at[:, pl.ds(0, 256)]), load(value_in, own_kw.at[:, pl.ds(256, 256)])]
    kept = {task: load(task.own, task.loc(0, 0, 0, 0, None)) for task in (q, qx, o, ox, dy_task)}
    window = pl.ds(pl.multiple_of(me.y * 1408 + me.zl * 640, 128), 768)
    loads.append(load(gate_in.at[:, window], gu_win.at[0]))
    loads.append(load(up_in.at[:, window], gu_win.at[1]))
    gains[me.f] = jnp.zeros((16, 128), F32)
    gains[me.f, pl.ds(0, 1), :] = attn_gain[...].astype(F32)
    gains[me.f, pl.ds(8, 1), :] = mlp_gain[...].astype(F32)

    dpart = op = wo.at[:, 0]
    qp = wo.at[:, 1]
    dgu = wo.at[:, 1, :, pl.ds(0, 1536)]
    kvp = kv
    packed = gu.at[pl.ds(1024, 128), pl.ds(0, 1408)]

    def gsib(t):
        return gu.at[pl.ds(aligned(128 * t, 128), 128)]

    def gown(t):
        return gu.at[pl.ds(aligned(1024 + 128 * t, 128), 128)]

    def kp(t):
        return gu.at[pl.ds(aligned(128 * t, 128), 128), pl.ds(0, 512)]

    def gd(t):
        return wd.at[:, pl.ds(aligned(256 * t, 256), 256)]

    def gd_own(t):
        return gd(t).at[pl.ds(pl.multiple_of(me.co * 352, 16), 352)]

    def dost(n, half):
        return grecv.at[pl.ds(0, 4), :, pl.ds(pl.multiple_of(512 + 128 * (2 * n + half), 128), 128)]

    saved = []

    def put_gate_up():
        loads[2].wait()
        loads[3].wait()

        @pl.loop(0, 8)
        def _(i):
            rows = pl.ds(pl.multiple_of(16 * i, 16), 16)
            out = pl.ds(pl.multiple_of(me.f * 128 + 16 * i, 16), 16)
            for w in (0, 1):
                values = gu_win[w, rows].astype(F32)
                values = jnp.where(me.zl == 1, pltpu.roll(values, 704, 1), values)
                lane = lax.broadcasted_iota(jnp.int32, values.shape, 1)
                gu[out, 768 * w : 768 * w + 768] = jnp.where(lane < 704, values, 0.0).astype(BF)

        wd[pl.ds(704, 64)] = jnp.zeros((64, 2048), BF)

    def normed():
        norm_scale(x, scale)

        @pl.loop(0, 16)
        def _(i):
            at = pl.ds(pl.multiple_of(i * 128, 128), 128)
            a1s[own, at] = (x[:, at].astype(F32) * scale[...] * gains[i, pl.ds(0, 1), :]).astype(BF)

    def project_kv():
        raw = dot_in(a1s[own], kw[...].reshape(2048, 512))
        for i in range(2):
            part = raw[:, 128 * i : 128 * i + 128]
            kv_own[:, 128 * i : 128 * i + 128] = (part * cosine[...] + turned(part) * sine[...]).astype(BF)
        kv_own[:, 256:] = raw[:, 256:].astype(BF)
        kv[0] = kv_own[...]

    def project_q():
        @pl.loop(0, 4)
        def _(n):
            raw = dot_in(a1s[own], qw[:, :, :, pl.ds(pl.multiple_of(512 * n, 512), 512)].reshape(2048, 512))
            for i in range(4):
                part = raw[:, 128 * i : 128 * i + 128]
                part = ((part * cosine[...] + turned(part) * sine[...]).astype(BF).astype(F32) * SCALE).astype(BF)
                for half in (0, 1):
                    for e in (0, 1):
                        rows = pl.ds(64 * (2 * i + e), 64)
                        qst[n, half, rows, :] = part[64 * half : 64 * half + 64, 64 * e : 64 * e + 64]

    def collect_kv(mate):
        beside = kv[mate]
        for out, base in ((kst, 0), (vst, 256)):
            for n in range(4):
                first = base + 64 * n
                for slot in range(8):
                    out[n, pl.ds(64 * slot, 64), :] = kv[slot, 0:64, first : first + 64]
                out[n, pl.ds(512, 64), :] = beside[64:128, first : first + 64]
                out[n, pl.ds(576, 64), :] = kv_own[64:128, first : first + 64]

    def attend(n, half):
        count = 512 if half == 0 else 640
        keys = pl.ds(0, count)
        sT[keys] = dot_back(kst[n, keys, :], qst[n, half])
        for i in range(4):
            at = pl.ds(128 * i, 128)
            if half == 0:
                scores = sT[keys, at] + bias_p[...]
                peak = jnp.max(scores, axis=0, keepdims=True)
                raised = jnp.exp(scores - peak)
                total = jnp.sum(raised, axis=0, keepdims=True)
                pT[keys, at] = (raised * (1.0 / total)).astype(BF)
            else:
                first = sT[0:512, at]
                rest = sT[512:640, at] + bias_c[...]
                peak = jnp.maximum(
                    jnp.max(first, axis=0, keepdims=True), jnp.max(rest, axis=0, keepdims=True)
                )
                first = jnp.exp(first - peak)
                rest = jnp.exp(rest - peak)
                total = jnp.sum(first, axis=0, keepdims=True) + jnp.sum(rest, axis=0, keepdims=True)
                pT[0:512, at] = (first * (1.0 / total)).astype(BF)
                pT[512:640, at] = (rest * (1.0 / total)).astype(BF)
            lse[2 * n + half, :, at] = peak + jnp.log(total)
        for i, block in enumerate(unpile(dot_rows(vst[n, keys, :], pT[keys]))):
            first = pl.multiple_of(512 * n + 128 * i, 128)
            atts[pl.ds(64 * half, 64), pl.ds(first, 128)] = block.astype(BF)

    def project_o():
        @pl.loop(0, 4)
        def _(n):
            at = pl.ds(pl.multiple_of(512 * n, 512), 512)
            h1[:, at] = x[:, at].astype(F32) + dot_in(atts[own], wo[:, :, :, at].reshape(2048, 512))

    def normed_two():
        norm_scale(h1, scale)

        @pl.loop(0, 16)
        def _(i):
            at = pl.ds(pl.multiple_of(i * 128, 128), 128)
            acts[0, 0, :, at] = (h1[:, at] * scale[...] * gains[i, pl.ds(8, 1), :]).astype(BF)

    def mpart_copy(n):
        return [
            pltpu.make_async_copy(
                kv.at[pl.ds(2 * i, 2)], mpart.at[pl.ds(2 * n, 2), :, pl.ds(512 * i, 512)], local.at[60 + i]
            )
            for i in range(4)
        ]

    def group(n):
        at = pl.ds(2 * n, 2)
        rows = pl.ds(pl.multiple_of(256 * n, 256), 256)
        for h in range(3):
            first, second = pl.ds(256 * h, 256), pl.ds(768 + 256 * h, 256)
            here = acts[n].reshape(256, 2048)
            gate = dot_in(here, gu[:, first])
            up = dot_in(here, gu[:, second])
            back = dot_back(dy[at].reshape(256, 2048), wd[first, :])
            curve = 1.0 / (1.0 + jnp.exp(-gate))
            silu = gate * curve
            hid[rows, first] = (silu * up).astype(BF)
            dgu[at, :, first] = (back * up * (curve + silu * (1.0 - curve))).astype(BF).reshape(2, 128, 256)
            dgu[at, :, second] = (back * silu).astype(BF).reshape(2, 128, 256)

        @pl.when(n > 0)
        def _():
            for copy in mpart_copy(n - 1):
                copy.wait()

        for i in range(4):
            wide = pl.ds(512 * i, 512)
            grads = dgu[at].reshape(256, 1536)
            dpart[at, :, wide] = dot_back(grads, gu[wide, :]).astype(BF).reshape(2, 128, 512)
            kv[pl.ds(2 * i, 2)] = dot_in(hid[rows, :], wd[:, wide]).astype(BF).reshape(2, 128, 512)
        for copy in mpart_copy(n):
            copy.start()

    def group_half(slot):
        rows = pl.ds(128 * slot, 128)
        here = acts[slot // 2, slot % 2]
        for h in range(3):
            first, second = pl.ds(256 * h, 256), pl.ds(768 + 256 * h, 256)
            gate = dot_in(here, gu[:, first])
            up = dot_in(here, gu[:, second])
            back = dot_back(dy[slot], wd[first, :])
            curve = 1.0 / (1.0 + jnp.exp(-gate))
            silu = gate * curve
            hid[rows, first] = (silu * up).astype(BF)
            dgu[slot, :, first] = (back * up * (curve + silu * (1.0 - curve))).astype(BF)
            dgu[slot, :, second] = (back * silu).astype(BF)
        for i in range(4):
            wide = pl.ds(512 * i, 512)
            dpart[slot, :, wide] = dot_back(dgu[slot], gu[wide, :]).astype(BF)

    def group_out():
        for copy in mpart_copy(2):
            copy.wait()
        for i in range(4):
            wide = pl.ds(512 * i, 512)
            kv[pl.ds(2 * i, 2)] = dot_in(hid[pl.ds(768, 256), :], wd[:, wide]).astype(BF).reshape(2, 128, 512)
        for copy in mpart_copy(3):
            copy.start()

    class Views:
        def __init__(self, pick):
            self.pick = pick

        @property
        def at(self):
            return self

        def __getitem__(self, index):
            return self.pick(index)

    def scatter(dev, part, place, columns, row, pair=None):
        wide = pl.ds(0, columns)
        halves = Views(lambda index: place.at[4 + index[0], pl.ds(64 * index[1], 64), wide])
        fulls = Views(lambda index: place.at[2 * index[0] + index[1], :, wide])
        paired = place.at[6, :, wide] if pair is None else pair
        return Scatter(dev, part, 128, halves, fulls, paired, (r0, r1), row)

    first_bay, second_bay = qw.at[:, 0], qw.at[:, 1]
    d = scatter(me.across_y, lambda slot: dpart.at[slot], second_bay, 2048, 0)
    gjob = scatter(me.across_x, gown, first_bay, 1536, 1, g_pair)
    n_job = Scatter(me.across_x, gd_own, 352, n_half, n_full, n_pair, (r0, r1), 2)
    o_job = scatter(me.across_x, lambda slot: op.at[slot], second_bay, 2048, 3)
    q_job = scatter(me.across_x, lambda slot: qp.at[slot], first_bay, 2048, 4)
    k_job = scatter(me.across_x, kp, kw.at[:, 0], 512, 5)
    e_job = Scatter(me.across_x, lambda slot: gp.at[slot], 16, e_half, e_full, e_pair, (r0, r1), 6)
    d_job = scatter(me.across_y, lambda slot: kvp.at[slot], kw.at[:, 1], 512, 7)

    def weight_terms(t, core):
        at = pl.multiple_of((chip_of(me, t) * 2 + core) * 128, 128)
        left = acts[:, :, :, pl.ds(at, 128)].reshape(1024, 128)
        return dot_rows(left, dgu[...].reshape(1024, 1536))

    def gu_to(t):
        return send(gsib(t), grecv.at[t], (c0, c1), 8 + t, me.sibling())

    def down_to(t):
        mine = pl.ds(pl.multiple_of((1 - me.co) * 352, 16), 352)
        return send(gd(t).at[mine], gdrecv.at[t], (c0, c1), t, me.sibling())

    def terms_for_sibling(start):
        @pl.loop(start, start + 2)
        def _(i):
            gsib(7 - i)[...] = weight_terms(7 - i, 1 - me.co).astype(BF)
            gu_to(7 - i).start()

    def sibling_has_terms():
        @pl.loop(0, 8)
        def _(t):
            gu_to(t).wait_send()

    def own_terms(start):
        @pl.loop(start, start + 2)
        def _(i):
            gu_to(7 - i).wait_recv()
            gown(7 - i)[...] = (weight_terms(7 - i, me.co) + grecv[7 - i].astype(F32)).astype(BF)

    def down_terms():
        @pl.loop(0, 8)
        def _(t):
            at = pl.multiple_of(chip_of(me, t) * 256, 256)
            gd(t)[...] = dot_rows(hid[...], dy[:, :, pl.ds(at, 256)].reshape(1024, 256)).astype(BF)
            down_to(t).start()

    def down_sums():
        @pl.loop(0, 8)
        def _(t):
            down_to(t).wait_recv()

            @pl.loop(0, 22)
            def _(i):
                at = pl.ds(pl.multiple_of(i * 16, 16), 16)
                mine = gd(t).at[pl.ds(pl.multiple_of(me.co * 352 + i * 16, 16), 16)]
                mine[...] = (mine[...].astype(F32) + gdrecv[t, at].astype(F32)).astype(BF)

    m_first, m_second = {}, {}
    for dp in (0, 1):
        for way, sign in ((0, 1), (1, -1)):
            m_first[way, dp] = send(
                mpart.at[slot_of(2, dp), pl.ds(64 * way, 64)], m_half.at[way, dp], (r0, r1), (8, way * 2 + dp),
                me.across_y(sign, 0),
            )
            m_second[way, dp] = send(
                dy.at[1 + 2 * way + dp], m_full.at[way, dp], (r0, r1), (8, 4 + way * 2 + dp), me.across_y(sign, 0)
            )
    m_third = send(dy.at[5], m_pair, (r0, r1), (8, 8), me.across_y(0, 1))

    def m_start():
        dy_task.end()
        for copy in mpart_copy(3):
            copy.wait()
        for dp in (1, 0):
            for way in (0, 1):
                m_first[way, dp].start()

    m_parts = {(way, dp): later(mpart.at[slot_of(1 - 2 * way, dp)], dy.at[1 + 2 * way + dp]) for way in (0, 1) for dp in (0, 1)}
    m_halves = {(way, dp): later(m_half.at[way, dp], dy.at[6 + way, pl.ds(0, 64)]) for way in (0, 1) for dp in (0, 1)}
    m_fulls = {(way, dp): later(m_full.at[way, dp], dy.at[6 + way]) for way in (0, 1) for dp in (0, 1)}
    m_mine, m_near, m_last = later(mpart.at[0], dy.at[1]), later(mpart.at[1], dy.at[5]), later(m_pair, dy.at[2])
    m_out = later(dy.at[1], mixed)

    def m_turn(dp):
        for way in (0, 1):
            m_parts[way, dp].start()
        for way in (0, 1):
            m_first[way, dp].wait_recv()
            m_halves[way, dp].start()
        for way in (0, 1):
            m_parts[way, dp].wait()
            m_halves[way, dp].wait()
            add_into(dy.at[1 + 2 * way + dp, pl.ds(64 * way, 64)], 64, [dy.at[6 + way, pl.ds(0, 64)]])
            m_second[way, dp].start()

    def m_pair_up():
        m_near.start()
        for way in (0, 1):
            m_second[way, 1].wait_recv()
            m_fulls[way, 1].start()
        m_near.wait()
        for way in (0, 1):
            m_fulls[way, 1].wait()
        add_into(dy.at[5], 128, [dy.at[6], dy.at[7]])
        m_third.start()

    def m_finish():
        for dp in (0, 1):
            m_second[0, dp].wait_send()
        m_mine.start()
        for way in (0, 1):
            m_second[way, 0].wait_recv()
            m_fulls[way, 0].start()
        m_third.wait_recv()
        m_last.start()
        m_mine.wait()
        for way in (0, 1):
            m_fulls[way, 0].wait()
        m_last.wait()

        @pl.loop(0, 8)
        def _(i):
            at = pl.ds(pl.multiple_of(i * 16, 16), 16)
            total = h1[at]
            for slot in (1, 2, 6, 7):
                total = total + dy[slot, at].astype(F32)
            dy[1, at] = total.astype(BF)

        m_out.start()

    def wo_load(n):
        return pltpu.make_async_copy(
            wo_saved.at[pl.ds(2 * n, 2)], acts.at[pl.ds(2 * (n % 2), 2)], local.at[56 + n % 2]
        )

    def q_load(n):
        return pltpu.make_async_copy(q_saved.at[pl.ds(2 * n, 2)], acts.at[pl.ds(2 * (n % 2), 2)], local.at[58 + n % 2])

    def kw_load():
        return [
            load(kw_saved.at[chip], grecv.at[pl.ds(2 * (chip % 4), 2), :, pl.ds(512 * (chip // 4), 512)])
            for chip in range(8)
        ]

    def at_ctx(ref):
        def loc(dr, dp, er, ep, half):
            return ref.at[me.ctx_at(dr, dp), row_half(half, ref.shape[1])]

        return loc

    def dn_at(dr, dp, er, ep, half):
        first = pl.multiple_of(me.ctx_at(dr, dp) * 256, 256)
        return dn_all.at[row_half(half, 352), pl.ds(first, 256)]

    gu_task = over_y(packed, at_ctx(gu_all), 5, both=False)
    dn_task = over_y(dn_moved, dn_at, 6, both=False)
    dn_swap = Swap(me, gd_own(0), dn_moved, (v0, v1), local.at[next(slots)])
    gu_keep = later(packed, gu_all.at[me.c])
    dn_keep = later(dn_moved, dn_at(0, 0, 0, 0, None))
    dn_local = later(dnp, wd_at(0, 0, 0, 0, None))
    tokens_out = later(datts.at[own], tokens_grad)

    def block_at(ref, slot):
        first = pl.multiple_of(me.ctx_at(STEPS[slot], PAIRS[slot]) * 16, 16)
        return ref.at[pl.ds(first, 16)]

    def sum_over_ctx(total, got, row):
        return Trade(
            me.across_y, lambda slot: block_at(total, slot), lambda slot: got.at[mirror(slot)], (z0, z1), row
        )

    def spread(out, row):
        return Trade(me.across_y, lambda slot: block_at(out, 0), lambda slot: block_at(out, 0), (z0, z1), row)

    def sum_up(total, got, out):
        value = block_at(total, 0)[...].astype(F32)
        for slot in range(1, 8):
            value = value + got[slot].astype(F32)
        block_at(out, 0)[...] = value.astype(BF)

    o_sum, q_sum, kv_sum = op.at[0], qp.at[0], kp(0)
    o_sums = sum_over_ctx(o_sum, o_got, 0)
    q_sums = sum_over_ctx(q_sum, q_got, 1)
    k_sums = sum_over_ctx(kv_sum, k_got, 2)
    o_spread = spread(o_grad, 3)
    q_spread = spread(q_grad, 4)
    k_spread = spread(kv_grad, 5)
    e_task = Trade(me.across_y, lambda slot: g_sum, lambda slot: ggot.at[me.c], (z0, z1), 6)

    def to_sibling(src, dst, index):
        return send(src, dst, (c0, c1), 16 + index, me.sibling())

    att_swap = to_sibling(atts.at[own], atts.at[other], 0)
    datt_swap = to_sibling(datts.at[own], datts.at[other], 1)
    a1_swap = to_sibling(a1s.at[own], a1s.at[other], 2)
    queries, rest = pl.ds(0, 2048), pl.ds(2048, 512)
    dq_swap = to_sibling(dqkvs.at[own, queries], dqkvs.at[other, queries], 3)
    dkv_swap = to_sibling(dqkvs.at[own, rest], dqkvs.at[other, rest], 4)
    gain_swap = to_sibling(gown_rows, gsib_rows, 5)

    def norm_two_back():
        for i in range(16):
            grow[0, :, 128 * i : 128 * i + 128] = gains[i, 0:1, :]
            grow[1, :, 128 * i : 128 * i + 128] = gains[i, 8:9, :]
        grow[2] = jnp.zeros((1, 2048), F32)
        grow[3] = jnp.zeros((1, 2048), F32)

        @pl.loop(0, 8)
        def _(i):
            at = pl.ds(pl.multiple_of(16 * i, 16), 16)
            values, grad = h1[at], da2[at]
            scale = lax.rsqrt(jnp.mean(values * values, axis=1, keepdims=True) + EPS)
            grow[3] += jnp.sum(grad * values * scale, axis=0, keepdims=True)
            grad = grad * grow[1]
            level = jnp.mean(grad * values, axis=1, keepdims=True) * scale * scale * scale
            total = dy[0, at].astype(F32) + scale * grad - values * level
            da2[at] = total
            datts[at] = total.astype(BF)

        datt_swap.start()

    def heads_back():
        for n in range(4):
            wo_load(n).wait()
            part = dot_back(datts[own], acts[2 * (n % 2) : 2 * (n % 2) + 2].reshape(512, 2048)).astype(BF)
            for half in (0, 1):
                place = dost(n, half)
                for h in range(8):
                    place[h // 2, pl.ds(64 * (h % 2), 64), pl.ds(0, 64)] = part[
                        64 * half : 64 * half + 64, 64 * h : 64 * h + 64
                    ]
            if n < 2:
                wo_load(n + 2).start()
        for n in range(2):
            q_load(n).start()

    def terms(left, right, out, job):
        @pl.loop(0, 8)
        def _(i):
            at = pl.multiple_of((chip_of(me, 7 - i) * 2 + me.co) * 128, 128)
            out(7 - i)[...] = dot_rows(left[:, pl.ds(at, 128)], right[...]).astype(BF)

            @pl.when(i == 1)
            def _():
                job.start()

    def output_terms():
        att_swap.wait_recv()
        datt_swap.wait_recv()
        pl.semaphore_wait(credit, 3)
        terms(atts, datts, lambda t: op.at[t], o_job)

    def query_terms():
        a1_swap.wait_recv()
        dq_swap.wait_recv()
        terms(a1s, dqkvs.at[:, pl.ds(0, 2048)], lambda t: qp.at[t], q_job)

    def kv_terms():
        dkv_swap.wait_recv()
        terms(a1s, dqkvs.at[:, pl.ds(2048, 512)], kp, k_job)

    def kv_blocks(mate):
        for part, base in ((0, 0), (64, 256)):
            for n in range(4):
                first = base + 64 * n
                block = grecv[0:5, :, 128 * n : 128 * n + 128].reshape(640, 128)[:, part : part + 64]
                for slot in range(8):
                    kvp[slot, 0:64, first : first + 64] = block[64 * slot : 64 * slot + 64]
                    if slot == 0:
                        late = block[576:640]
                    else:
                        late = jnp.where(mate == slot, block[512:576], jnp.zeros((64, 64), BF))
                    kvp[slot, 64:128, first : first + 64] = late

    def kv_back():
        for i in range(2):
            at = slice(128 * i, 128 * i + 128)
            block = sT[512:640, at]
            dqkvs[own, 2048 + 128 * i : 2176 + 128 * i] = (block * cosine[...] - turned(block) * sine[...]).astype(BF)
        dqkvs[own, 2304:2560] = sT[512:640, 256:512].astype(BF)
        dkv_swap.start()

    def inputs_back():
        for copy in kw_back:
            copy.wait()
        for n in range(4):
            q_load(n).wait()
            block = dot_back(dqkvs[own, queries], acts[2 * (n % 2) : 2 * (n % 2) + 2].reshape(512, 2048))
            four, wide = pl.ds(4 * (n % 2), 4), pl.ds(512 * (n // 2), 512)
            block = block + dot_back(dqkvs[own, rest], grecv[four, :, wide].reshape(512, 512))
            sT[pl.ds(128 * n, 128)] = block
            if n < 2:
                q_load(n + 2).start()

    def norm_one_back():
        datt_swap.wait_send()

        @pl.loop(0, 8)
        def _(i):
            at = pl.ds(pl.multiple_of(16 * i, 16), 16)
            values = x[at].astype(F32)
            grad = jnp.concatenate([sT[pl.ds(pl.multiple_of(128 * n + 16 * i, 16), 16)] for n in range(4)], axis=1)
            scale = lax.rsqrt(jnp.mean(values * values, axis=1, keepdims=True) + EPS)
            grow[2] += jnp.sum(grad * values * scale, axis=0, keepdims=True)
            grad = grad * grow[0]
            level = jnp.mean(grad * values, axis=1, keepdims=True) * scale * scale * scale
            datts[at] = (da2[at] + scale * grad - values * level).astype(BF)

        tokens_out.start()

        gown_rows[...] = jnp.zeros((16, 16, 128), F32)
        for i in range(16):
            gown_rows[i, 0:1, :] = grow[2, :, 128 * i : 128 * i + 128]
            gown_rows[i, 8:9, :] = grow[3, :, 128 * i : 128 * i + 128]
        gain_swap.start()

    def gain_terms():
        gain_swap.wait_recv()
        for slot in range(8):
            block = me.fsdp_at(STEPS[slot], PAIRS[slot])
            gp[slot] = gown_rows[block] + gsib_rows[block]

    def dn_begin():
        dn_swap.wait()
        dn_task.start()
        dn_keep.start()

    def gu_begin():
        pack()
        gu_keep.start()
        gu_task.start()

    def e_begin():
        e_task.start()
        ggot[me.c] = g_sum[...]

    def attend_back(n, half):
        count = 512 if half == 0 else 640
        keys = pl.ds(0, count)
        key, query, out = kst[n, keys, :], qst[n, half], dost(n, half)[...].reshape(512, 128)[:, 0:64]
        sT[keys] = dot_back(key, query)
        dT[keys] = dot_back(vst[n, keys, :], out)
        for i in range(4):
            at = pl.ds(128 * i, 128)
            parts = []
            for first, size in ((0, 512), (512, 128))[: 1 + half]:
                scores = sT[first : first + size, at]
                if half == 0:
                    scores = scores + bias_p[...]
                elif first:
                    scores = scores + bias_c[...]
                probs = jnp.exp(scores - lse[2 * n + half, :, at])
                grad = dT[first : first + size, at]
                parts.append((first, size, probs, grad))
            level = sum(jnp.sum(probs * grad, axis=0, keepdims=True) for _, _, probs, grad in parts)
            for first, size, probs, grad in parts:
                pT[first : first + size, at] = probs.astype(BF)
                dsT[first : first + size, at] = (probs * (grad - level)).astype(BF)
        rows = slice(64 * half, 64 * half + 64)
        for i, block in enumerate(unpile(dot_rows(key, dsT[keys]) * SCALE)):
            block = block * cosine[rows] - turned(block) * sine[rows]
            first = pl.multiple_of(512 * n + 128 * i, 128)
            dqkvs[rows, pl.ds(first, 128)] = block.astype(BF)
        return dot_in(dsT[keys], query), dot_in(pT[keys], out)

    def pack():
        @pl.loop(0, 8)
        def _(i):
            here = pl.ds(pl.multiple_of(1024 + 16 * i, 16), 16)
            gate = gu[here, 0:768].astype(F32)
            up = pltpu.roll(gu[here, 768:1536].astype(F32), 64, 1)
            gu[here, 0:640] = gate[:, 0:640].astype(BF)
            gu[here, 640:768] = (gate[:, 640:768] + up[:, 0:128]).astype(BF)
            gu[here, 768:1408] = up[:, 128:768].astype(BF)

    def keep_kv_grads(n, one, two):
        keys = jnp.concatenate([one[0] + two[0][0:512], two[0][512:640]], axis=0)
        values = jnp.concatenate([one[1] + two[1][0:512], two[1][512:640]], axis=0)
        both = jnp.concatenate([keys, values], axis=1).astype(BF)
        grecv[pl.ds(0, 5), :, pl.ds(pl.multiple_of(128 * n, 128), 128)] = both.reshape(5, 128, 128)

    qx.start()
    dy_task.start()
    loads[0].wait()
    loads[1].wait()
    k.start()
    qx.pair()
    qx.turn(0)
    ox.start()
    put_gate_up()
    k.turn(0)
    qx.turn(1)
    g.start()
    q.start()
    qx.last(0)
    qx.last(1)
    kept[qx].wait()
    qy.start()
    g.turn(0)
    o.start()
    dy_task.pair()
    k.pair()
    swap.start()
    k.last(0)
    ox.pair()
    mate = place_tables(me, deal, freq, cosine, sine, bias_p, bias_c)
    g.last(0)
    g.pair()
    ox.turn(0)
    q.turn(0)
    k.turn(1)
    g.turn(1)
    qy.turn(0)
    q.pair()
    swap.wait()
    dn_local.start()
    dn.start()
    ox.last(0)
    qy.pair()
    g.last(1)
    k.last(1)
    g.sync()
    k.sync()
    ox.turn(1)
    x_load.wait()
    normed()
    project_kv()
    q.turn(1)
    kv_task.start()
    qy.turn(1)
    o.pair()
    kv_task.pair()
    q.last(0)
    ox.last(1)
    q.last(1)
    dn.pair()
    qy.last(0)
    kept[ox].wait()
    oy.start()
    qy.last(1)
    o.turn(1)
    kv_task.turn(0)
    kv_task.turn(1)
    o.turn(0)
    q.sync()
    dn.turn(1)
    oy.pair()
    qy.sync()
    kept[q].wait()
    saved.append(load(qw, q_saved))
    saved.append(load(kw, kw_saved))
    project_q()
    oy.turn(0)
    m.start()
    kv_task.last(1)
    kv_task.last(0)
    collect_kv(mate)

    @pl.loop(0, 4)
    def _(n):
        attend(n, 0)
        attend(n, 1)

        @pl.when(n == 0)
        def _():
            o.last(0)

        @pl.when(n == 1)
        def _():
            oy.turn(1)
            o.last(1)
            a1_swap.start()
            dy_task.turn(0)
            dn.last(1)
            oy.last(0)

        @pl.when(n == 2)
        def _():
            oy.last(1)
            dy_task.turn(1)
            m.pair()
            o.sync()
            dn.turn(0)

    oy.sync()
    kept[o].wait()
    saved.append(load(wo, wo_saved))
    project_o()
    normed_two()
    for task in (k, q, qx, qy):
        task.end()
    saved[0].wait()
    saved[1].wait()
    a.start()
    m.turn(0)
    m.turn(1)
    m.last(0)
    dn.last(0)
    a.pair()
    m.last(1)
    m.sync()
    a.turn(0)
    dn.sync()

    for task in (o, ox, oy, kv_task):
        task.end()
    saved[2].wait()
    dn_local.wait()
    kept[dy_task].wait()

    @pl.loop(0, 3)
    def _(n):
        group(n)

        @pl.when(n == 1)
        def _():
            dy_task.last(0)
            a.turn(1)

    dy_task.last(1)
    a.last(0)
    group_half(6)
    a.last(1)
    group_half(7)
    d.start()
    m.end()
    terms_for_sibling(0)
    terms_for_sibling(2)
    terms_for_sibling(4)
    own_terms(0)
    gjob.start()
    own_terms(2)
    d.turn(1)
    group_out()
    own_terms(4)
    gjob.turn(1)
    att_swap.start()
    d.turn(0)
    m_start()
    dn.end()
    down_terms()
    gjob.turn(0)
    terms_for_sibling(6)
    down_sums()
    d.pair()
    own_terms(6)
    a.end()
    wo_load(0).start()
    wo_load(1).start()
    n_job.start()
    n_job.turn(1)
    n_job.turn(0)
    d.finish(da2)
    norm_two_back()
    for device in near(me.across_x):
        pl.semaphore_signal(credit, 1, device_id=device, device_id_type=MESH)
    gjob.pair()
    m_turn(1)
    d.end()
    output_terms()
    n_job.pair()
    heads_back()

    @pl.loop(0, 4)
    def _(n):
        one, two = attend_back(n, 0), attend_back(n, 1)
        keep_kv_grads(n, one, two)

        @pl.when(n == 0)
        def _():
            gjob.finish(gown(0))
            gu_begin()
            o_job.turn(1)

        @pl.when(n == 1)
        def _():
            m_pair_up()
            m_turn(0)

    n_job.finish(gd_own(0))
    dq_swap.start()
    o_job.turn(0)
    o_job.pair()
    kv_blocks(mate)
    kw_back = kw_load()
    d_job.start()
    query_terms()
    d_job.turn(1)
    gu_task.turn(0)
    dn_swap.start()
    d_job.pair()
    d_job.turn(0)
    o_job.finish(o_sum)
    dn_begin()
    q_job.turn(1)
    o_sums.start()
    d_job.finish(sT.at[pl.ds(512, 128)])
    kv_back()
    inputs_back()
    dn_task.pair()
    gu_task.pair()
    sibling_has_terms()
    kv_terms()
    norm_one_back()
    o_sums.got()
    sum_up(o_sum, o_got, o_grad)
    o_spread.start()
    gain_terms()
    e_job.start()
    k_job.turn(1)
    q_job.pair()
    dn_task.turn(1)
    gu_task.last(0)
    dn_task.turn(0)
    e_job.turn(1)
    q_job.turn(0)
    gu_task.turn(1)
    k_job.turn(0)
    k_job.pair()
    e_job.pair()
    q_job.finish(q_sum)
    q_sums.start()
    m_finish()
    k_job.finish(kv_sum)
    e_job.turn(0)
    e_job.finish(g_sum)
    gu_task.last(1)
    dn_task.last(0)
    e_begin()
    dn_task.last(1)
    k_sums.start()
    q_sums.got()
    sum_up(q_sum, q_got, q_grad)
    q_spread.start()
    k_sums.got()
    sum_up(kv_sum, k_got, kv_grad)
    k_spread.start()
    o_spread.got()
    q_spread.got()
    e_task.got()
    k_spread.got()
    total = ggot[0]
    for index in range(1, 8):
        total = total + ggot[index]
    gains_out[...] = total
    for job in (g, gjob, n_job, o_job, q_job, k_job, e_job, d_job, gu_task, dn_task):
        job.end()
    for job in (o_sums, q_sums, k_sums, o_spread, q_spread, k_spread, e_task):
        job.end()
    for copy in (*m_first.values(), m_second[1, 0], m_second[1, 1], m_third):
        copy.wait_send()
    m_out.wait()
    tokens_out.wait()
    gu_keep.wait()
    dn_keep.wait()
    for copy in (att_swap, a1_swap, dq_swap, dkv_swap, gain_swap):
        copy.wait_send()

    @pl.loop(0, 8)
    def _(t):
        down_to(t).wait_send()


def layer(x, attn_gain, mlp_gain, deal, freq, q, key, value, wo, gate, up, dn, dy):
    shape = jax.ShapeDtypeStruct
    smem = pl.BlockSpec(memory_space=pltpu.SMEM)
    vmem = pltpu.VMEM
    outs = pl.pallas_call(
        layer_kernel,
        out_shape=(
            shape((128, 2048), BF),
            shape((128, 2048), BF),
            shape((128, 2048), BF),
            shape((128, 512), BF),
            shape((128, 2048), BF),
            shape((16, 128), F32),
            shape((8, 128, 1408), BF),
            shape((352, 2048), BF),
            shape((8, 2, 128, 2048), BF),
            shape((8, 2, 128, 512), BF),
            shape((8, 2, 128, 2048), BF),
            shape((8, 128, 2048), BF),
            shape((2, 2, 64, 2048), BF),
            shape((2, 2, 128, 2048), BF),
            shape((128, 2048), BF),
        ),
        in_specs=[ANY] + [VMEM] * 2 + [smem, VMEM] + [ANY] * 8,
        out_specs=[ANY] * 2 + [VMEM] * 4 + [ANY] * 9,
        scratch_shapes=[
            vmem((128, 2048), BF),
            vmem((16, 16, 128), F32),
            vmem((256, 2048), BF),
            vmem((256, 2048), BF),
            vmem((4, 2, 512, 64), BF),
            vmem((4, 640, 64), BF),
            vmem((4, 640, 64), BF),
            vmem((8, 1, 512), F32),
            vmem((128, 2048), F32),
            vmem((128, 128), F32),
            vmem((128, 128), F32),
            vmem((512, 128), F32),
            vmem((128, 128), F32),
            vmem((8, 2, 128, 2048), BF),
            vmem((8, 2, 128, 512), BF),
            vmem((8, 2, 128, 2048), BF),
            vmem((128, 512), BF),
            vmem((8, 128, 512), BF),
            vmem((640, 512), F32),
            vmem((640, 512), BF),
            vmem((640, 512), F32),
            vmem((640, 512), BF),
            vmem((128, 1), F32),
            vmem((2, 128, 768), BF),
            vmem((352, 256), BF),
            vmem((4, 2, 128, 2048), BF),
            vmem((2048, 1536), BF),
            vmem((768, 2048), BF),
            vmem((8, 128, 2048), BF),
            vmem((1024, 768), BF),
            vmem((8, 128, 1536), BF),
            vmem((8, 352, 256), BF),
            vmem((128, 1536), BF),
            vmem((128, 2048), F32),
            vmem((256, 2048), BF),
            vmem((256, 2560), BF),
            vmem((4, 1, 2048), F32),
            vmem((16, 16, 128), F32),
            vmem((16, 16, 128), F32),
            vmem((352, 256), BF),
            *scatter_buffers(352, 256),
            *scatter_buffers(16, 128, F32),
            vmem((8, 16, 128), F32),
            vmem((8, 16, 128), F32),
            vmem((16, 128), F32),
            vmem((8, 16, 2048), BF),
            vmem((8, 16, 2048), BF),
            vmem((8, 16, 512), BF),
            *dma_sems(8, 9),
            *dma_sems(8, 10),
            *dma_sems(7, 9),
            *dma_sems(2, 10),
            *dma_sems(9, 9),
            *dma_sems(7, 8),
            pltpu.SemaphoreType.DMA((22,)),
            pltpu.SemaphoreType.DMA((22,)),
            pltpu.SemaphoreType.DMA,
            pltpu.SemaphoreType.DMA,
            pltpu.SemaphoreType.DMA,
            pltpu.SemaphoreType.DMA,
            pltpu.SemaphoreType.REGULAR,
            pltpu.SemaphoreType.DMA((64,)),
        ],
        compiler_params=params(1, 63),
        name="layer",
    )(x, attn_gain, mlp_gain, deal, freq, q, key, value, wo, gate, up, dn, dy)
    return outs[:8]


def finish_kernel(
    mixed_in, tokens_in, q_in, kv_in, o_in, gu_in, dn_in, gains,
    mixed, tokens_grad, q_out, key_out, value_out, o_out, gate_out, up_out, dn_out, first_gain, second_gain,
    b_mixed, b_tokens, b_q, b_kv, b_o, b_gu, b_dn, f_q, f_key, f_value, f_o, f_gate, f_up, f_dn, sems,
):
    slots = iter(range(28))

    def move(src, dst):
        return pltpu.make_async_copy(src, dst, sems.at[next(slots)])

    loads = [
        move(src, dst)
        for src, dst in (
            *[(gu_in.at[pl.ds(2 * pair, 2)], b_gu.at[pl.ds(2 * pair, 2)]) for pair in range(4)],
            (dn_in, b_dn), (q_in, b_q), (o_in, b_o), (kv_in, b_kv), (mixed_in, b_mixed), (tokens_in, b_tokens),
        )
    ]
    for copy in loads:
        copy.start()
    stores = []

    def store(src, dst):
        copy = move(src, dst)
        copy.start()
        stores.append(copy)

    def widen(pair):
        first = 1408 * pair

        @pl.loop(0, 8)
        def _(i):
            rows = pl.ds(pl.multiple_of(16 * i, 16), 16)
            lane = lax.broadcasted_iota(jnp.int32, (16, 128), 1)
            for out, base, turn in ((f_gate, 0, (0, 64)), (f_up, 640, (704, 0))):
                even = b_gu[2 * pair, rows, base : base + 768].astype(F32)
                odd = b_gu[2 * pair + 1, rows, base : base + 768].astype(F32)
                even = pltpu.roll(even, turn[0], 1) if turn[0] else even
                odd = pltpu.roll(odd, turn[1], 1) if turn[1] else odd
                out[rows, first : first + 640] = even[:, 0:640]
                out[rows, first + 640 : first + 768] = jnp.where(lane < 64, even[:, 640:768], odd[:, 0:128])
                out[rows, first + 768 : first + 1408] = odd[:, 128:768]

    def cast(src, dst, rows):
        @pl.loop(0, rows // 32)
        def _(i):
            at = pl.ds(pl.multiple_of(32 * i, 32), 32)
            dst[at] = src[at].astype(F32)

    for pair in range(4):
        loads[pair].wait()
        widen(pair)
        wide = pl.ds(1408 * pair, 1408)
        store(f_gate.at[:, wide], gate_out.at[:, wide])
        store(f_up.at[:, wide], up_out.at[:, wide])
    for index, src, dst, out, rows in (
        (4, b_dn, f_dn, dn_out, 352), (5, b_q, f_q, q_out, 128), (6, b_o, f_o, o_out, 128)
    ):
        loads[index].wait()
        cast(src, dst, rows)
        store(dst, out)
    first_gain[...] = gains[0:1, :]
    second_gain[...] = gains[8:9, :]
    loads[7].wait()
    f_key[...] = b_kv[:, 0:256].astype(F32)
    f_value[...] = b_kv[:, 256:512].astype(F32)
    store(f_key, key_out)
    store(f_value, value_out)
    loads[8].wait()
    store(b_mixed, mixed)
    loads[9].wait()
    store(b_tokens, tokens_grad)
    for copy in stores:
        copy.wait()


def finish(mixed, tokens_grad, q, kv, o, gu, dn, gains):
    shape, vmem = jax.ShapeDtypeStruct, pltpu.VMEM
    wholes = [(128, 2048), (128, 256), (128, 256), (128, 2048), (128, 5632), (128, 5632), (352, 2048)]
    return pl.pallas_call(
        finish_kernel,
        out_shape=(shape((128, 2048), BF), shape((128, 2048), BF), *[shape(dims, F32) for dims in (*wholes, (1, 128), (1, 128))]),
        in_specs=[ANY] * 7 + [VMEM],
        out_specs=[ANY] * 9 + [VMEM] * 2,
        scratch_shapes=[
            vmem((128, 2048), BF),
            vmem((128, 2048), BF),
            vmem((128, 2048), BF),
            vmem((128, 512), BF),
            vmem((128, 2048), BF),
            vmem((8, 128, 1408), BF),
            vmem((352, 2048), BF),
            *[vmem(dims, F32) for dims in wholes],
            pltpu.SemaphoreType.DMA((28,)),
        ],
        compiler_params=pltpu.CompilerParams(vmem_limit_bytes=62 << 20),
        name="finish",
    )(mixed, tokens_grad, q, kv, o, gu, dn, gains)


def on_device(
    tokens,
    block_deal,
    attn_gain,
    query_weight,
    key_weight,
    value_weight,
    output_weight,
    mlp_gain,
    gate_weight,
    up_weight,
    down_weight,
    cotangent,
):
    freq = BASE ** (-(np.arange(HEAD_DIM // 2, dtype=np.float32) * 2.0) / HEAD_DIM)
    freq = np.concatenate([freq] * 4)[None].astype(np.float32)
    mixed, tokens_grad, query_grad, kv_grad, o_grad, gain_grads, gu_grads, dn_grad = layer(
        tokens[0], attn_gain[None], mlp_gain[None], block_deal.transpose(1, 2, 0), freq, query_weight, key_weight, value_weight, output_weight,
        gate_weight, up_weight, down_weight, cotangent[0],
    )
    mixed, tokens_grad, *grads, first_gain, second_gain = finish(
        mixed, tokens_grad, query_grad, kv_grad, o_grad, gu_grads, dn_grad, gain_grads
    )
    return (mixed[None], tokens_grad[None], first_gain[0], *grads[:4], second_gain[0], *grads[4:])


def solution(mesh):
    held = P("fsdp", "ctx", None)
    rows = P("fsdp", None)
    return jax.shard_map(
        on_device,
        mesh=mesh,
        in_specs=(held, P(), P("fsdp"), rows, rows, rows, rows, P("fsdp"), rows, rows, rows, held),
        out_specs=(held, held, P("fsdp"), rows, rows, rows, rows, P("fsdp"), rows, rows, rows),
        check_vma=False,
    )
```
